32 devices in a mesh: wide: 8 (over z, x), narrow: 4 (over y, core).
Axes of the slice: x: 2, y: 2, z: 4, core: 2. Of those that a mesh axis runs over, the one named last changes fastest.
Arguments:
- inputs: bfloat16 [16384, 768], P(('wide', 'narrow')), may hold values from -6 to 6
- segment_ids: int32 [64, 256], P(('wide', 'narrow')), may hold values from 0 to 9, as said below
- pre_attn_gain: bfloat16 [768], P(('wide', 'narrow')), may hold values from 0.5 to 1.5
- pre_attn_bias: bfloat16 [768], P(('wide', 'narrow')), may hold values from -2 to 2
- w_qkv: bfloat16 [768, 2304], P(('wide', 'narrow')), may hold values from -0.21875 to 0.21875
- b_query: bfloat16 [768], P(('wide', 'narrow')), may hold values from -2 to 2
- b_value: bfloat16 [768], P(('wide', 'narrow')), may hold values from -2 to 2
- w_out: bfloat16 [768, 768], P(('wide', 'narrow')), may hold values from -0.875 to 0.875
- b_out: bfloat16 [768], P(('wide', 'narrow')), may hold values from -2 to 2
- pre_mlp_gain: bfloat16 [768], P(('wide', 'narrow')), may hold values from 0.5 to 1.5
- pre_mlp_bias: bfloat16 [768], P(('wide', 'narrow')), may hold values from -2 to 2
- w_up: bfloat16 [768, 3072], P(('wide', 'narrow')), may hold values from -0.21875 to 0.21875
- b_up: bfloat16 [3072], P(('wide', 'narrow')), may hold values from -2 to 2
- w_down: bfloat16 [3072, 768], P(('wide', 'narrow')), may hold values from -0.109375 to 0.109375
- b_down: bfloat16 [768], P(('wide', 'narrow')), may hold values from -2 to 2
- cotangent: bfloat16 [16384, 768], P(('wide', 'narrow')), may hold values from -6 to 6
Outputs:
- layer_out: bfloat16 [16384, 768], P(('wide', 'narrow'))
- input_grad: bfloat16 [16384, 768], P(('wide', 'narrow'))
- grad_attn_gain: float32 [768], P(('wide', 'narrow'))
- grad_attn_shift: float32 [768], P(('wide', 'narrow'))
- grad_w_qkv: float32 [768, 2304], P(('wide', 'narrow'))
- grad_b_query: float32 [768], P(('wide', 'narrow'))
- grad_b_value: float32 [768], P(('wide', 'narrow'))
- grad_w_out: float32 [768, 768], P(('wide', 'narrow'))
- grad_b_out: float32 [768], P(('wide', 'narrow'))
- grad_mlp_gain: float32 [768], P(('wide', 'narrow'))
- grad_mlp_shift: float32 [768], P(('wide', 'narrow'))
- grad_w_up: float32 [768, 3072], P(('wide', 'narrow'))
- grad_b_up: float32 [3072], P(('wide', 'narrow'))
- grad_w_down: float32 [3072, 768], P(('wide', 'narrow'))
- grad_b_down: float32 [768], P(('wide', 'narrow'))
The draws below stay inside these ranges and needn't reach their ends.
Inputs may be any that keep to these rules, and one draw needn't show every extreme that they name: `segment_ids`: in every row of 256 positions the ids count up from 1 without falling, one id for each caption of 1 to 64 positions, the first caption of each row has exactly 64; the last 1 to 8 positions of every row are 0 (padding). Ids are compared only within a row.
All inputs are finite; a program needn't handle non-finite values.
Results may differ from the reference program's by a relative error of at most 0.012.
The reference program's roundings to bfloat16 on the way count: a program that leaves them out, or rounds other values in their place, can miss the bound.
Values may be sent and summed in bfloat16 or wider, within the bound.
No kernel may reach another device: no remote copies, remote signals or barrier semaphores. Data moves between devices by JAX's collectives and lax.ppermute only.
A program may use at most 128 MiB of HBM per device.

```python
import jax
import jax.numpy as jnp
from jax import lax

HEADS = 12
HEAD_DIM = 64
D = 768
FF = 3072
ROW_LEN = 256
CAP_MAX = 64
PAD_MAX = 8
ROWS = 64
TOKENS = 16384


def draw_segment_ids(key, part):
    shortest = CAP_MAX * 3 // 8
    captions = ROW_LEN // shortest + 1
    key_len, key_pad = jax.random.split(key)
    row_index = jnp.arange(ROWS, dtype=jnp.int32)[:, None]
    lengths = jax.random.randint(key_len, (ROWS, captions - 1), shortest, CAP_MAX + 1).astype(jnp.int32)
    lengths = jnp.where(row_index == 0, shortest, lengths).astype(jnp.int32)
    lengths = jnp.concatenate([jnp.full((ROWS, 1), CAP_MAX, jnp.int32), lengths], axis=1)
    bounds = jnp.cumsum(lengths, axis=1)
    positions = jnp.arange(ROW_LEN, dtype=jnp.int32)
    labels = 1 + jnp.sum((bounds[:, None, :] <= positions[None, :, None]).astype(jnp.int32), axis=2)
    padding = jax.random.randint(key_pad, (ROWS, 1), 1, PAD_MAX + 1).astype(jnp.int32)
    padding = jnp.where(row_index == 0, 1, padding).astype(jnp.int32)
    return jnp.where(positions[None, :] >= ROW_LEN - padding, 0, labels).astype(jnp.int32)


def with_spikes(values, own_key, source, target, blocks, factor):
    owner, partner = [(jnp.arange(values.shape[axis_at]) // (values.shape[axis_at] // blocks)).reshape([-1 if axis == axis_at else 1 for axis in range(values.ndim)]) for axis_at in (source, target)]
    chosen = jax.random.permutation(own_key, blocks)[partner]
    strong = (owner == chosen) | (owner == (partner + blocks // 2) % blocks)
    return jnp.where(strong, factor * values, values)


def block_levels(stream_key, extent, cuts, least, largest):
    def one(axis_at, shards_of):
        steps = jax.random.uniform(jax.random.fold_in(jax.random.fold_in(stream_key, 6), axis_at), (shards_of,), jnp.float32, least / len(cuts), largest / len(cuts))
        return jnp.repeat(jnp.exp(steps), extent[axis_at] // shards_of).reshape((-1,) + (1,) * (len(extent) - axis_at - 1))

    gain = one(*cuts[0])
    for cut in cuts[1:]:
        gain = gain * one(*cut)
    return gain


def normal_values(key, dims, scale, reach, shards=(), kind=jnp.bfloat16):
    gain = block_levels(key, dims, shards, -0.22, 0.18) if shards else 1.0
    entries = jax.random.normal(key, dims, jnp.float32) * scale * gain
    return jnp.minimum(jnp.maximum(entries, -reach), reach).astype(kind)


def heavy_noise(key, extent, deviation, limit, cuts, heavy, held_as=jnp.bfloat16):
    array = deviation * jax.random.normal(key, extent, jnp.float32)
    if cuts:
        array = array * block_levels(key, extent, cuts, -0.22, 0.18)
    return jnp.clip(with_spikes(array, jax.random.fold_in(key, 3), *heavy), -limit, limit).astype(held_as)


def setup_inputs(seed: int = 0) -> dict:
    arg_keys = jax.random.split(jax.random.key(seed), 17)
    inputs = heavy_noise(arg_keys[0], (TOKENS, D), 1.0, 6.0, ((0, 32),), (0, 1, 32, 2.75))
    segment_ids = draw_segment_ids(jax.random.fold_in(arg_keys[16], 71), 0)
    pre_attn_gain = jnp.clip(1.0 + 0.1 * jax.random.normal(arg_keys[2], (D,), jnp.float32), 0.5, 1.5).astype(jnp.bfloat16)
    pre_attn_bias = normal_values(arg_keys[3], (D,), 0.3, 2.0, ((0, 32),))
    w_qkv = normal_values(arg_keys[4], (D, 3 * D), D ** -0.5, 0.21875, ((0, 32),))
    b_query = normal_values(arg_keys[5], (D,), 0.3, 2.0, ((0, 32),))
    b_value = normal_values(arg_keys[6], (D,), 0.3, 2.0, ((0, 32),))
    w_out = normal_values(arg_keys[7], (D, D), (D // 16) ** -0.5, 0.875, ((0, 32),))
    b_out = normal_values(arg_keys[8], (D,), 0.3, 2.0, ((0, 32),))
    pre_mlp_gain = jnp.clip(1.0 + 0.1 * jax.random.normal(arg_keys[9], (D,), jnp.float32), 0.5, 1.5).astype(jnp.bfloat16)
    pre_mlp_bias = normal_values(arg_keys[10], (D,), 0.3, 2.0, ((0, 32),))
    w_up = normal_values(arg_keys[11], (D, FF), D ** -0.5, 0.21875, ((0, 32),))
    b_up = normal_values(arg_keys[12], (FF,), 0.3, 2.0, ((0, 32),))
    w_down = normal_values(arg_keys[13], (FF, D), FF ** -0.5, 0.109375, ((0, 32),))
    b_down = normal_values(arg_keys[14], (D,), 0.3, 2.0, ((0, 32),))
    cotangent = normal_values(arg_keys[15], (TOKENS, D), 1.0, 6.0, ((0, 32),))
    return {"inputs": inputs, "segment_ids": segment_ids, "pre_attn_gain": pre_attn_gain, "pre_attn_bias": pre_attn_bias, "w_qkv": w_qkv, "b_query": b_query, "b_value": b_value, "w_out": w_out, "b_out": b_out, "pre_mlp_gain": pre_mlp_gain, "pre_mlp_bias": pre_mlp_bias, "w_up": w_up, "b_up": b_up, "w_down": w_down, "b_down": b_down, "cotangent": cotangent}


@jax.custom_vjp
def low(v):
    return lax.optimization_barrier(v.astype(jnp.bfloat16)).astype(jnp.float32)

@jax.custom_vjp
def low_back(v):
    return v

def low_keep(v):
    return (low(v), None)

def low_pass(kept, grad):
    return (grad,)

def back_keep(v):
    return (v, None)

def back_low(kept, grad):
    return (low(grad),)
low.defvjp(low_keep, low_pass)
low_back.defvjp(back_keep, back_low)
epsilon = 1e-06
highest = lax.Precision.HIGHEST

def matmul(left, right):
    return jnp.dot(left, right, precision=highest, preferred_element_type=jnp.float32)

def layer_norm(values, gain_row, shift_row):
    centre = lax.optimization_barrier(jnp.mean(values, axis=-1, keepdims=True))
    centred = values - centre
    variance = lax.optimization_barrier(jnp.mean(centred * centred, axis=-1, keepdims=True))
    return centred * lax.rsqrt(variance + epsilon) * gain_row + shift_row

def attend(qkv_rows, segments):
    rows_here = qkv_rows.shape[0]
    split_heads = qkv_rows.reshape(rows_here, ROW_LEN, 3, HEADS, HEAD_DIM)
    queries = split_heads[:, :, 0]
    key_rows = split_heads[:, :, 1]
    value_rows = split_heads[:, :, 2]
    raw_scores = jnp.einsum('rqhd,rkhd->rhqk', queries, key_rows, precision=highest) * HEAD_DIM ** (-0.5)
    raw_scores = low_back(raw_scores)
    same_caption = (segments[:, :, None] == segments[:, None, :]) & (segments[:, None, :] != 0)
    own_place = jnp.eye(ROW_LEN, dtype=bool)
    allowed = (same_caption | own_place[None])[:, None]
    scores = jnp.where(allowed, raw_scores, -1e+30)
    soft_weights = low(jax.nn.softmax(scores, axis=-1))
    mixed_heads = jnp.einsum('rhqk,rkhd->rqhd', soft_weights, value_rows, precision=highest)
    return low(low_back(mixed_heads.reshape(rows_here, ROW_LEN, D)))

def forward(resid_in, segments, attn_gain, attn_shift, w_qkv, b_query, b_value, w_out, b_out, mlp_gain, mlp_shift, w_up, b_up, w_down, b_down):
    normed_one = low(layer_norm(resid_in, attn_gain, attn_shift))
    bias_qkv = jnp.concatenate([b_query, jnp.zeros_like(b_query), b_value])
    qkv_rows = low(low_back(matmul(normed_one, w_qkv) + bias_qkv))
    mixed_rows = attend(qkv_rows, segments)
    branch = low_back(matmul(mixed_rows, w_out) + b_out)
    resid_mid = resid_in + branch
    normed_two = low(layer_norm(resid_mid, mlp_gain, mlp_shift))
    pre_act = low_back(matmul(normed_two, w_up) + b_up)
    activated = low(jax.nn.gelu(pre_act, approximate=True))
    mlp_branch = low_back(matmul(activated, w_down) + b_down)
    return resid_mid + mlp_branch

def reference(inputs, segment_ids, pre_attn_gain, pre_attn_bias, w_qkv, b_query, b_value, w_out, b_out, pre_mlp_gain, pre_mlp_bias, w_up, b_up, w_down, b_down, cotangent):
    params = (pre_attn_gain.astype(jnp.float32), pre_attn_bias.astype(jnp.float32), w_qkv.astype(jnp.float32), b_query.astype(jnp.float32), b_value.astype(jnp.float32), w_out.astype(jnp.float32), b_out.astype(jnp.float32), pre_mlp_gain.astype(jnp.float32), pre_mlp_bias.astype(jnp.float32), w_up.astype(jnp.float32), b_up.astype(jnp.float32), w_down.astype(jnp.float32), b_down.astype(jnp.float32))
    group_rows = 16
    blocks_count = ROWS // group_rows
    resid_all = inputs.astype(jnp.float32).reshape(blocks_count, group_rows, ROW_LEN, D)
    segment_all = segment_ids.reshape(blocks_count, group_rows, ROW_LEN)
    valid_mask = (segment_ids != 0).astype(jnp.float32).reshape(blocks_count, group_rows, ROW_LEN, 1)
    grad_all = cotangent.astype(jnp.float32).reshape(blocks_count, group_rows, ROW_LEN, D) * valid_mask

    def advance(totals, block_data):
        resid_block, segment_block, grad_block = block_data

        def run_block(resid_value, *weights):
            return forward(resid_value, segment_block, *weights)
        result, pullback = jax.vjp(run_block, resid_block, *params)
        gradients = pullback(grad_block)
        totals = tuple((total + gradient for total, gradient in zip(totals, gradients[1:])))
        return (totals, (result, gradients[0]))
    start_totals = tuple((jnp.zeros_like(tensor) for tensor in params))
    totals, (results, input_grads) = lax.scan(advance, start_totals, (resid_all, segment_all, grad_all))
    layer_out = results.reshape(TOKENS, D).astype(jnp.bfloat16)
    input_grad = input_grads.reshape(TOKENS, D).astype(jnp.bfloat16)
    return (layer_out, input_grad, totals[0], totals[1], totals[2], totals[3], totals[4], totals[5], totals[6], totals[7], totals[8], totals[9], totals[10], totals[11], totals[12])
```

```python
import functools

import jax
import jax.numpy as jnp
from jax import lax
from jax.experimental import pallas as pl
from jax.experimental.pallas import tpu as pltpu
from jax.sharding import PartitionSpec as P

HEADS = 12
HEAD_DIM = 64
D = 768
FF = 3072
ROW_LEN = 256
HALF = 384
CHIPS = 16
BLK = 48
PAIRS = HEADS // 2
AXES = ("wide", "narrow")

EPS = 1e-06
MASKED = -1e30
F32 = jnp.float32
BF16 = jnp.bfloat16

BIT_Y, BIT_X, BIT_Z0, BIT_Z1 = 1, 2, 4, 8


def xor_order(bits):
    order = [0]
    for bit in bits:
        order = order + [o ^ bit for o in order]
    return order


GATHER = (
    xor_order((BIT_Z0, BIT_Z1, BIT_Y, BIT_X)),
    xor_order((BIT_Z0, BIT_Z1, BIT_X, BIT_Y)),
)
SCATTER = GATHER


def nt(a, b):
    return lax.dot_general(a, b, (((1,), (1,)), ((), ())), preferred_element_type=F32)


def tn(a, b):
    return lax.dot_general(a, b, (((0,), (0,)), ((), ())), preferred_element_type=F32)


def nn(a, b):
    return lax.dot_general(a, b, (((1,), (0,)), ((), ())), preferred_element_type=F32)


def chunks(tokens, step, body):
    def one(i, carry):
        body(pl.ds(pl.multiple_of(i * step, step), step))
        return carry

    lax.fori_loop(0, tokens // step, one, 0)


def norm_parts(v):
    centre = jnp.mean(v, axis=-1, keepdims=True)
    centred = v - centre
    scale = lax.rsqrt(jnp.mean(centred * centred, axis=-1, keepdims=True) + EPS)
    return centred * scale, scale


def whole_wait(ref, sem):
    pltpu.make_async_copy(ref, ref, sem).wait()


def each_block(pos_ref, stream, pieces):
    me, core = pos_ref[0], pos_ref[1]
    own0, own1, sib0, sib1 = pieces
    for half, first, second in ((core, own0, own1), (1 - core, sib0, sib1)):
        for p in range(CHIPS):
            yield (first, second)[p // 8], p % 8, me ^ GATHER[stream][p], half


def rows_at(chip, size, extra=0):
    return pl.ds(pl.multiple_of(chip * size + extra, 16), BLK if size == BLK else size // 2)


def fetch_qk(pos_ref, pieces, w_qkv, sem):
    for ref, b, chip, half in each_block(pos_ref, 0, pieces):
        pltpu.make_async_copy(
            ref.at[b], w_qkv.at[pl.ds(0, 2), half, rows_at(chip, BLK)], sem
        ).start()


def fetch_v(pos_ref, pieces, w_qkv, sem):
    for ref, b, chip, half in each_block(pos_ref, 1, pieces):
        pltpu.make_async_copy(
            ref.at[b, pl.ds(0, BLK)], w_qkv.at[2, half, rows_at(chip, BLK)], sem
        ).start()


def fetch_out(pos_ref, pieces, w_out, sem):
    for ref, b, chip, half in each_block(pos_ref, 1, pieces):
        pltpu.make_async_copy(
            ref.at[b, pl.ds(BLK, BLK)], w_out.at[half, rows_at(chip, BLK)], sem
        ).start()


def fetch_small(pos_ref, pieces, small, sem):
    for ref, b, chip, half in each_block(pos_ref, 1, pieces):
        pltpu.make_async_copy(
            ref.at[b, pl.ds(2 * BLK, 16)], small.at[half, chip], sem
        ).start()


def fetch_up(pos_ref, pieces, w_up, sem):
    for s in range(2):
        for ref, b, chip, half in each_block(pos_ref, s, pieces[4 * s : 4 * s + 4]):
            pltpu.make_async_copy(
                ref.at[b], w_up.at[half, pl.ds(2 * s, 2), rows_at(chip, BLK)], sem
            ).start()


def fetch_down(pos_ref, pieces, w_down, sem):
    for s in range(2):
        for ref, b, chip, half in each_block(pos_ref, s, pieces[4 * s : 4 * s + 4]):
            pltpu.make_async_copy(
                ref.at[b], w_down.at[half, rows_at(chip, 4 * BLK, 2 * BLK * s)], sem
            ).start()


def attn_forward_kernel(
    pos_ref, x_ref, segr_ref, segc_ref, qk0, qk1, qk2, qk3, vo0, vo1, vo2, vo3,
    n1_ref, qkv_ref, soft_ref, mixed_ref, mid_ref, n2_ref, vec_ref,
    w_qkv, w_out, small, bias, sems,
):
    tokens = x_ref.shape[0]
    vo = (vo0, vo1, vo2, vo3)
    fetch_small(pos_ref, vo, small, sems.at[0])
    fetch_qk(pos_ref, (qk0, qk1, qk2, qk3), w_qkv, sems.at[1])
    fetch_v(pos_ref, vo, w_qkv, sems.at[1])
    fetch_out(pos_ref, vo, w_out, sems.at[2])
    for r in range(tokens // ROW_LEN):
        same = segc_ref[r * ROW_LEN : (r + 1) * ROW_LEN] == segr_ref[r]
        bias[r] = jnp.where(same, 0.0, MASKED)
    whole_wait(small, sems.at[0])
    for h in range(2):
        vec_ref[:, h * HALF : (h + 1) * HALF] = jnp.sum(small[h].astype(F32), axis=0)

    def norm_one(rows):
        xhat, _ = norm_parts(x_ref[rows, :].astype(F32))
        n1_ref[rows, :] = (xhat * vec_ref[0:1, :] + vec_ref[1:2, :]).astype(BF16)

    chunks(tokens, 64, norm_one)
    whole_wait(w_qkv, sems.at[1])
    for t in range(3):
        for h in range(2):
            cols = slice(t * D + h * HALF, t * D + (h + 1) * HALF)
            y = nn(n1_ref[...], w_qkv[t, h]) + vec_ref[2 + t : 3 + t, h * HALF : (h + 1) * HALF]
            y = y.astype(BF16)
            if t == 0:
                y = y * BF16(HEAD_DIM**-0.5)
            qkv_ref[:, cols] = y

    lane = lax.broadcasted_iota(jnp.int32, (1, 2 * HEAD_DIM), 1)
    low = (lane < HEAD_DIM).astype(F32).astype(BF16)
    high = (lane >= HEAD_DIM).astype(F32).astype(BF16)
    for r in range(tokens // ROW_LEN):
        rows = slice(r * ROW_LEN, (r + 1) * ROW_LEN)

        def pair(i, carry):
            q = qkv_ref[rows, pl.ds(pl.multiple_of(i * 128, 128), 128)]
            k = qkv_ref[rows, pl.ds(pl.multiple_of(D + i * 128, 128), 128)]
            v = qkv_ref[rows, pl.ds(pl.multiple_of(2 * D + i * 128, 128), 128)]
            mixed = jnp.zeros((ROW_LEN, 128), F32)
            for hh, keep in enumerate((low, high)):
                s = nt(q, k * keep) + bias[r]
                e = jnp.exp(s - jnp.max(s, axis=-1, keepdims=True))
                p = (e * (1.0 / jnp.sum(e, axis=-1, keepdims=True))).astype(BF16)
                soft_ref[r * HEADS + 2 * i + hh] = p
                mixed = mixed + nn(p, v * keep)
            mixed_ref[rows, pl.ds(pl.multiple_of(i * 128, 128), 128)] = mixed.astype(BF16)
            return carry

        lax.fori_loop(0, PAIRS, pair, 0)
    whole_wait(w_out, sems.at[2])
    for h in range(2):
        cols = slice(h * HALF, (h + 1) * HALF)
        mid_ref[:, cols] = (
            x_ref[:, cols].astype(F32) + nn(mixed_ref[...], w_out[h]) + vec_ref[5:6, cols]
        )

    def norm_two(rows):
        xhat, _ = norm_parts(mid_ref[rows, :])
        n2_ref[rows, :] = (xhat * vec_ref[6:7, :] + vec_ref[7:8, :]).astype(BF16)

    chunks(tokens, 64, norm_two)


GELU_A = 0.7978845608028654
GELU_B = 0.044715


def mlp_up_kernel(
    pos_ref, n2_ref, cot_ref, segc_ref, vec_ref, up0, up1, up2, up3, up4, up5, up6, up7,
    act_ref, slope_ref, gout_ref, gb_ref, am, at, bm, bt,
    w_up, grad, sems,
):
    tokens = n2_ref.shape[0]
    fetch_up(pos_ref, (up0, up1, up2, up3, up4, up5, up6, up7), w_up, sems.at[0])
    valid = segc_ref[...] > 0
    gout_ref[...] = jnp.where(valid, cot_ref[...].astype(F32), 0.0).astype(BF16)
    gb_ref[...] = jnp.broadcast_to(
        jnp.sum(gout_ref[...].astype(F32), axis=0, keepdims=True), gb_ref.shape
    )
    whole_wait(w_up, sems.at[0])
    for h in range(2):
        for k in range(4):
            f = h * 1536 + k * HALF
            cols = slice(f, f + HALF)
            row, lane = 8 + f // D, f % D
            b_up = vec_ref[row : row + 1, lane : lane + HALF]

            def part(rows):
                u = nn(n2_ref[rows, :], w_up[h, k]) + b_up
                sq = u * u
                t = jnp.tanh(u * (GELU_A + GELU_A * GELU_B * sq))
                half_up = 0.5 + 0.5 * t
                act_ref[rows, cols] = (u * half_up).astype(BF16)
                slope_ref[rows, cols] = (
                    half_up
                    + 0.5 * u * (1.0 - t * t) * (GELU_A + 3.0 * GELU_A * GELU_B * sq)
                ).astype(BF16)

            chunks(tokens, 128, part)
    for f in range(0, FF, HALF):
        g = tn(act_ref[:, f : f + HALF], gout_ref[...]).astype(BF16)
        grad[0, f : f + HALF, :] = g[:, :HALF]
        grad[1, f : f + HALF, :] = g[:, HALF:]
    me, core = pos_ref[0], pos_ref[1]
    for s, outs in enumerate(((am, at), (bm, bt))):
        for out, half in zip(outs, (core, 1 - core)):
            for p in range(CHIPS):
                chip = me ^ SCATTER[s][p]
                pltpu.make_async_copy(
                    grad.at[half, rows_at(chip, 4 * BLK, 2 * BLK * s)], out.at[p], sems.at[1]
                ).start()
    whole_wait(grad, sems.at[1])


def mlp_down_kernel(
    pos_ref, gout_ref, slope_ref, n2_ref, dn0, dn1, dn2, dn3, dn4, dn5, dn6, dn7,
    gpre_ref, gb_ref, am, at, bm, bt,
    w_down, grad, n2t, sems,
):
    fetch_down(pos_ref, (dn0, dn1, dn2, dn3, dn4, dn5, dn6, dn7), w_down, sems.at[0])
    n2t[...] = n2_ref[...].T
    gb_ref[...] = jnp.zeros(gb_ref.shape, F32)
    whole_wait(w_down, sems.at[0])
    for h in range(2):
        for k in range(4):
            f = h * 1536 + k * HALF
            cols = slice(f, f + HALF)
            row, lane = f // D, f % D
            ga = nt(gout_ref[:, :HALF], w_down[0, cols, :]) + nt(gout_ref[:, HALF:], w_down[1, cols, :])
            gp = (ga * slope_ref[:, cols].astype(F32)).astype(BF16)
            gpre_ref[:, cols] = gp
            gb_ref[row : row + 1, lane : lane + HALF] = jnp.sum(gp.astype(F32), axis=0, keepdims=True)
            grad[h, k] = nn(n2t[...], gp).astype(BF16)
    me, core = pos_ref[0], pos_ref[1]
    for s, outs in enumerate(((am, at), (bm, bt))):
        for out, half in zip(outs, (core, 1 - core)):
            for p in range(CHIPS):
                chip = me ^ SCATTER[s][p]
                pltpu.make_async_copy(
                    grad.at[half, pl.ds(2 * s, 2), rows_at(chip, BLK)], out.at[p], sems.at[1]
                ).start()
    whole_wait(grad, sems.at[1])


def norm_back(grad, xhat, scale, gain):
    gn = grad * gain
    mean_gn = jnp.mean(gn, axis=-1, keepdims=True)
    mean_gx = jnp.mean(gn * xhat, axis=-1, keepdims=True)
    return scale * (gn - mean_gn - xhat * mean_gx)


def attn_backward_kernel(
    pos_ref, gpre_ref, gout_ref, mid_ref, vec_ref, mixed_ref, qkv_ref, soft_ref, n1_ref, x_ref,
    gbd_ref, gbu_ref,
    up0, up1, up2, up3, up4, up5, up6, up7, qk0, qk1, qk2, qk3, vo0, vo1, vo2, vo3,
    igrad_ref, am, at, bm, bt,
    w_up, w_qkv, w_out, acc, gmid, gbr, gmixed, gqkv, tr, grad_qkv, grad_out, sums, small, sems,
):
    tokens = x_ref.shape[0]
    vo = (vo0, vo1, vo2, vo3)
    fetch_up(pos_ref, (up0, up1, up2, up3, up4, up5, up6, up7), w_up, sems.at[0])
    fetch_out(pos_ref, vo, w_out, sems.at[1])
    fetch_qk(pos_ref, (qk0, qk1, qk2, qk3), w_qkv, sems.at[2])
    fetch_v(pos_ref, vo, w_qkv, sems.at[2])
    sums[...] = jnp.zeros(sums.shape, F32)
    sums[8:12, :] = gbu_ref[0:4, :]
    sums[12:13, :] = gbd_ref[0:1, :]
    whole_wait(w_up, sems.at[0])
    for h in range(2):
        for k in range(4):
            f = h * 1536 + k * HALF
            part = nt(gpre_ref[:, f : f + HALF], w_up[h, k])
            acc[...] = part if f == 0 else acc[...] + part

    def back_two(rows):
        xhat, scale = norm_parts(mid_ref[rows, :])
        g = acc[rows, :]
        sums[6:7, :] += jnp.sum(g * xhat, axis=0, keepdims=True)
        sums[7:8, :] += jnp.sum(g, axis=0, keepdims=True)
        gm = gout_ref[rows, :].astype(F32) + norm_back(g, xhat, scale, vec_ref[6:7, :])
        gmid[rows, :] = gm
        low = gm.astype(BF16)
        gbr[rows, :] = low
        sums[5:6, :] += jnp.sum(low.astype(F32), axis=0, keepdims=True)

    chunks(tokens, 64, back_two)
    tr[...] = mixed_ref[...].T
    for h in range(2):
        grad_out[h] = nn(tr[...], gbr[:, h * HALF : (h + 1) * HALF]).astype(BF16)
    whole_wait(w_out, sems.at[1])
    gmixed[...] = (nt(gbr[:, :HALF], w_out[0]) + nt(gbr[:, HALF:], w_out[1])).astype(BF16)

    lane = lax.broadcasted_iota(jnp.int32, (1, 2 * HEAD_DIM), 1)
    first = (lane < HEAD_DIM).astype(F32).astype(BF16)
    second = (lane >= HEAD_DIM).astype(F32).astype(BF16)
    for r in range(tokens // ROW_LEN):
        rows = slice(r * ROW_LEN, (r + 1) * ROW_LEN)

        def pair(i, carry):
            at_q = pl.ds(pl.multiple_of(i * 128, 128), 128)
            at_k = pl.ds(pl.multiple_of(D + i * 128, 128), 128)
            at_v = pl.ds(pl.multiple_of(2 * D + i * 128, 128), 128)
            q, k, v = qkv_ref[rows, at_q], qkv_ref[rows, at_k], qkv_ref[rows, at_v]
            gm = gmixed[rows, at_q]
            dq = jnp.zeros((ROW_LEN, 128), F32)
            dk = jnp.zeros((ROW_LEN, 128), F32)
            dv = jnp.zeros((ROW_LEN, 128), F32)
            for hh, keep in enumerate((first, second)):
                p_low = soft_ref[r * HEADS + 2 * i + hh]
                p = p_low.astype(F32)
                gmk = gm * keep
                gs = nt(gmk, v)
                inner = jnp.sum(p * gs, axis=-1, keepdims=True)
                ds = (p * (gs - inner)).astype(BF16)
                dq = dq + nn(ds, k * keep)
                dk = dk + tn(ds, q * keep)
                dv = dv + tn(p_low, gmk)
            gqkv[rows, at_q] = (dq * (HEAD_DIM**-0.5)).astype(BF16)
            gqkv[rows, at_k] = dk.astype(BF16)
            gqkv[rows, at_v] = dv.astype(BF16)
            return carry

        lax.fori_loop(0, PAIRS, pair, 0)
    tr[...] = n1_ref[...].T
    whole_wait(w_qkv, sems.at[2])
    for t in range(3):
        for h in range(2):
            f = t * D + h * HALF
            g = gqkv[:, f : f + HALF]
            if t != 1:
                sums[2 + t : 3 + t, h * HALF : (h + 1) * HALF] = jnp.sum(
                    g.astype(F32), axis=0, keepdims=True
                )
            grad_qkv[t, h] = nn(tr[...], g).astype(BF16)
            part = nt(g, w_qkv[t, h])
            acc[...] = part if f == 0 else acc[...] + part

    def back_one(rows):
        xhat, scale = norm_parts(x_ref[rows, :].astype(F32))
        g = acc[rows, :]
        sums[0:1, :] += jnp.sum(g * xhat, axis=0, keepdims=True)
        sums[1:2, :] += jnp.sum(g, axis=0, keepdims=True)
        igrad_ref[rows, :] = (
            gmid[rows, :] + norm_back(g, xhat, scale, vec_ref[0:1, :])
        ).astype(BF16)

    chunks(tokens, 64, back_one)
    small[0] = sums[:, :HALF].astype(BF16)
    small[1] = sums[:, HALF:].astype(BF16)
    me, core = pos_ref[0], pos_ref[1]
    for out, half in ((am, core), (at, 1 - core)):
        for p in range(CHIPS):
            chip = me ^ SCATTER[0][p]
            pltpu.make_async_copy(
                grad_qkv.at[pl.ds(0, 2), half, rows_at(chip, BLK)], out.at[p], sems.at[3]
            ).start()
    for out, half in ((bm, core), (bt, 1 - core)):
        for p in range(CHIPS):
            chip = me ^ SCATTER[1][p]
            pltpu.make_async_copy(
                grad_qkv.at[2, half, rows_at(chip, BLK)], out.at[p, pl.ds(0, BLK)], sems.at[3]
            ).start()
            pltpu.make_async_copy(
                grad_out.at[half, rows_at(chip, BLK)], out.at[p, pl.ds(BLK, BLK)], sems.at[4]
            ).start()
            pltpu.make_async_copy(
                small.at[half], out.at[p, pl.ds(2 * BLK, 16)], sems.at[5 + p]
            ).start()
        for p in range(CHIPS):
            pltpu.make_async_copy(
                small.at[half], out.at[p, pl.ds(2 * BLK, 16)], sems.at[5 + p]
            ).wait()
    whole_wait(grad_qkv, sems.at[3])
    whole_wait(grad_out, sems.at[4])


def layer_out_kernel(
    pos_ref, act_ref, mid_ref, vec_ref, dn0, dn1, dn2, dn3, dn4, dn5, dn6, dn7, out_ref, w_down, sems
):
    fetch_down(pos_ref, (dn0, dn1, dn2, dn3, dn4, dn5, dn6, dn7), w_down, sems.at[0])
    whole_wait(w_down, sems.at[0])
    for h in range(2):
        cols = slice(h * HALF, (h + 1) * HALF)
        out_ref[:, cols] = (
            mid_ref[:, cols] + nn(act_ref[...], w_down[h]) + vec_ref[12:13, cols]
        ).astype(BF16)


def call(kernel, name, inputs, anywhere, outs, scratch, flops, any_outs=0):
    vmem = pl.BlockSpec(memory_space=pltpu.VMEM)
    anyspec = pl.BlockSpec(memory_space=pl.ANY)
    moved = sum(a.size * a.dtype.itemsize for a in tuple(inputs) + tuple(anywhere)) + sum(
        a.size * a.dtype.itemsize for a in outs
    )
    return pl.pallas_call(
        kernel,
        out_shape=outs,
        in_specs=[pl.BlockSpec(memory_space=pltpu.SMEM)]
        + [vmem] * (len(inputs) - 1)
        + [anyspec] * len(anywhere),
        out_specs=[vmem] * (len(outs) - any_outs) + [anyspec] * any_outs,
        scratch_shapes=scratch,
        compiler_params=pltpu.CompilerParams(vmem_limit_bytes=56 << 20),
        cost_estimate=pl.CostEstimate(flops=flops, bytes_accessed=moved, transcendentals=0),
        name=name,
    )(*inputs, *anywhere)


def swap(value, chip_bit):
    flip = chip_bit * 2 if chip_bit else 1
    return lax.ppermute(value, AXES, [(i, i ^ flip) for i in range(2 * CHIPS)])


def gather_group(block, cut):
    near = swap(block, BIT_Z0)
    far = swap(jnp.stack([block, near]), BIT_Z1)
    pieces = []
    for rows, bits in ((slice(0, cut), (BIT_Y, BIT_X)), (slice(cut, None), (BIT_X, BIT_Y))):
        four = jnp.stack([block[rows], near[rows], far[0, rows], far[1, rows]])
        eight = jnp.concatenate([four, swap(four, bits[0])])
        other = swap(eight, bits[1])
        pieces.append((eight, other, swap(eight, 0), swap(other, 0)))
    return pieces


def scatter_group(parts):
    fours = []
    for (mine, theirs), bits in zip(parts, ((BIT_X, BIT_Y), (BIT_Y, BIT_X))):
        total = mine.astype(F32) + swap(theirs, 0).astype(F32)
        got = swap(total[8:].astype(BF16), bits[0])
        total = total[:8] + got.astype(F32)
        got = swap(total[4:].astype(BF16), bits[1])
        fours.append(total[:4] + got.astype(F32))
    total = jnp.concatenate(fours, axis=1)
    got = swap(total[2:].astype(BF16), BIT_Z1)
    total = total[:2] + got.astype(F32)
    got = swap(total[1].astype(BF16), BIT_Z0)
    return total[0] + got.astype(F32)


def small_rows(place, values):
    gain1, bias1, bq, bv, bo, gain2, bias2, bu, bd = values
    per = gain1.shape[0]
    zero = jnp.zeros_like(gain1)
    eight = jnp.stack([gain1, bias1, bq, zero, bv, bo, gain2, bias2])
    rows = jnp.zeros((16, D), BF16)
    rows = lax.dynamic_update_slice(rows, eight, (0, place * per))
    at = place * bu.shape[0]
    rows = lax.dynamic_update_slice(rows, bu[None], (8 + at // D, at % D))
    return lax.dynamic_update_slice(rows, bd[None], (12, place * per))


def small_grads(sums, place, per, per_up):
    eight = lax.dynamic_slice(sums, (0, place * per), (8, per))
    at = place * per_up
    up = lax.dynamic_slice(sums, (8 + at // D, at % D), (1, per_up))[0]
    down = lax.dynamic_slice(sums, (12, place * per), (1, per))[0]
    return eight, up, down


def halves(w_qkv, w_out, w_up, w_down):
    rows = w_qkv.shape[0]
    qkv = w_qkv.reshape(rows, 3, 2, HALF)
    up = w_up.reshape(rows, 2, 4, HALF)
    for h in range(2):
        cols = slice(h * HALF, (h + 1) * HALF)
        yield (
            jnp.concatenate([qkv[:, :, h].transpose(1, 0, 2), w_out[None, :, cols]]),
            up[:, h].transpose(1, 0, 2),
            w_down[:, cols],
        )


def gather_by_swaps(wide, narrow, weights, values):
    core = narrow & 1
    place = wide * 4 + narrow
    rows = small_rows(place, values)
    packed = [
        (a, u, d, rows[:, h * HALF : (h + 1) * HALF]) for h, (a, u, d) in enumerate(halves(*weights))
    ]
    mine = [jnp.where(core == 0, p, q) for p, q in zip(*packed)]
    theirs = [jnp.where(core == 0, q, p) for p, q in zip(*packed)]
    got = [swap(t, 0) for t in theirs]

    def both(m, g, axis):
        return jnp.where(
            core == 0, jnp.concatenate([m, g], axis), jnp.concatenate([g, m], axis)
        )

    attn = both(mine[0], got[0], 1).reshape(4 * BLK, HALF)
    up = both(mine[1], got[1], 1).reshape(4 * BLK, HALF)
    down = both(mine[2], got[2], 0)
    small = mine[3] + got[3]
    one = gather_group(jnp.concatenate([attn, small]), 2 * BLK)
    two = gather_group(up, 2 * BLK)
    three = gather_group(down, 2 * BLK)
    return one, two, three


def gather_plain(weights, values):
    def whole(w):
        return lax.all_gather(w, AXES, axis=0, tiled=True)

    gain1, bias1, bq, bv, bo, gain2, bias2, bu, bd = [whole(v) for v in values]
    rest = jnp.zeros((3, D), BF16)
    small = jnp.stack([gain1, bias1, bq, jnp.zeros_like(bq), bv, bo, gain2, bias2])
    small = jnp.concatenate([small, bu.reshape(4, D), bd[None], rest])
    groups = ([], [], [])
    for h, (attn, up, down) in enumerate(halves(*[whole(w) for w in weights])):
        attn = attn.reshape(4, CHIPS, BLK, HALF).transpose(1, 0, 2, 3).reshape(CHIPS, 4 * BLK, HALF)
        up = up.reshape(4, CHIPS, BLK, HALF).transpose(1, 0, 2, 3).reshape(CHIPS, 4 * BLK, HALF)
        down = down.reshape(CHIPS, 4 * BLK, HALF)
        extra = jnp.zeros((CHIPS, 16, HALF), BF16).at[0].set(small[:, h * HALF : (h + 1) * HALF])
        for group, blocks in zip(groups, (jnp.concatenate([attn, extra], axis=1), up, down)):
            streams = []
            for s, rows in enumerate((slice(0, 2 * BLK), slice(2 * BLK, None))):
                ordered = jnp.stack([blocks[o, rows] for o in GATHER[s]])
                streams.append((ordered[:8], ordered[8:]))
            group.append(streams)
    return tuple([own + sib for own, sib in zip(*group)] for group in groups)


def scatter_plain(parts, group):
    whole = []
    for s, pair in enumerate(parts):
        back = [SCATTER[s].index(chip) for chip in range(CHIPS)]
        whole.append([jnp.stack([part[p] for p in back]) for part in pair])
    both = [jnp.concatenate([whole[0][h], whole[1][h]], axis=1) for h in range(2)]

    def scatter(v):
        return lax.psum_scatter(v.astype(F32), AXES, scatter_dimension=0, tiled=True)

    def matrix(first, units):
        cut = [
            b[:, first * BLK : (first + units) * BLK].reshape(CHIPS, units, BLK, HALF) for b in both
        ]
        return jnp.stack(cut, axis=3).transpose(0, 2, 1, 3, 4).reshape(D, units, 2, HALF)

    if group == "attn":
        sums = jnp.concatenate([b[0, 4 * BLK :] for b in both], axis=1)
        return (
            scatter(matrix(0, 3).reshape(D, 3 * D)),
            scatter(matrix(3, 1).reshape(D, D)),
            lax.psum(sums.astype(F32), AXES),
        )
    if group == "up":
        return scatter(matrix(0, 4).transpose(0, 2, 1, 3).reshape(D, FF))
    return scatter(jnp.concatenate([b.reshape(FF, HALF) for b in both], axis=1))


def per_device(tuned, *args):
    (
        inputs, segment_ids, pre_attn_gain, pre_attn_bias, w_qkv, b_query, b_value, w_out, b_out,
        pre_mlp_gain, pre_mlp_bias, w_up, b_up, w_down, b_down, cotangent,
    ) = args
    tokens = inputs.shape[0]
    n_rows = tokens // ROW_LEN
    wide, narrow = lax.axis_index("wide"), lax.axis_index("narrow")
    weights = (w_qkv, w_out, w_up, w_down)
    values = (
        pre_attn_gain, pre_attn_bias, b_query, b_value, b_out, pre_mlp_gain, pre_mlp_bias, b_up, b_down,
    )
    if tuned:
        place = wide * 4 + narrow
        pos = jnp.stack([wide * 2 + (narrow >> 1), narrow & 1]).astype(jnp.int32)
        groups = gather_by_swaps(wide, narrow, weights, values)
    else:
        place = wide * lax.axis_size("narrow") + narrow
        pos = jnp.zeros((2,), jnp.int32)
        groups = gather_plain(weights, values)
    (qk, vo), up, down = groups
    per_block = (
        [a.reshape(8, 2, BLK, HALF) for a in qk],
        list(vo),
        [a.reshape(8, 2, BLK, HALF) for s in up for a in s],
        [a for s in down for a in s],
    )
    qk, vo, up, down = per_block

    position = jnp.arange(ROW_LEN, dtype=jnp.int32)[None]
    own_id = jnp.where(segment_ids != 0, segment_ids, -1 - position)
    segr = own_id.reshape(n_rows, 1, ROW_LEN)
    segc = own_id.reshape(tokens, 1)

    def shape(dims, kind=BF16):
        return jax.ShapeDtypeStruct(dims, kind)

    def dma(n):
        return pltpu.SemaphoreType.DMA((n,))

    n1, qkv, soft, mixed, mid, n2, vec = call(
        attn_forward_kernel, "attn_forward", (pos, inputs, segr, segc), qk + vo,
        (
            shape((tokens, D)), shape((tokens, 3 * D)), shape((n_rows * HEADS, ROW_LEN, ROW_LEN)),
            shape((tokens, D)), shape((tokens, D), F32), shape((tokens, D)), shape((16, D), F32),
        ),
        [
            pltpu.VMEM((3, 2, D, HALF), BF16), pltpu.VMEM((2, D, HALF), BF16),
            pltpu.VMEM((2, CHIPS, 16, HALF), BF16), pltpu.VMEM((n_rows, ROW_LEN, ROW_LEN), F32), dma(3),
        ],
        2 * tokens * D * D * 4 + 8 * tokens * D * ROW_LEN,
    )
    blocks_a = shape((CHIPS, 2, BLK, HALF))
    act, slope, gout, gb_down, *g_down = call(
        mlp_up_kernel, "mlp_up", (pos, n2, cotangent, segc, vec), up,
        (shape((tokens, FF)), shape((tokens, FF)), shape((tokens, D)), shape((8, D), F32))
        + (shape((CHIPS, 2 * BLK, HALF)),) * 4,
        [pltpu.VMEM((2, 4, D, HALF), BF16), pltpu.VMEM((2, FF, HALF), BF16), dma(2)],
        4 * tokens * D * FF, 4,
    )
    gpre, gb_up, *g_up = call(
        mlp_down_kernel, "mlp_down", (pos, gout, slope, n2), down,
        (shape((tokens, FF)), shape((8, D), F32)) + (blocks_a,) * 4,
        [
            pltpu.VMEM((2, FF, HALF), BF16), pltpu.VMEM((2, 4, D, HALF), BF16),
            pltpu.VMEM((D, tokens), BF16), dma(2),
        ],
        4 * tokens * D * FF, 4,
    )
    input_grad, *g_attn = call(
        attn_backward_kernel, "attn_backward",
        (pos, gpre, gout, mid, vec, mixed, qkv, soft, n1, inputs, gb_down, gb_up), up + qk + vo,
        (shape((tokens, D)), blocks_a, blocks_a)
        + (shape((CHIPS, 2 * BLK + 16, HALF)),) * 2,
        [
            pltpu.VMEM((2, 4, D, HALF), BF16), pltpu.VMEM((3, 2, D, HALF), BF16),
            pltpu.VMEM((2, D, HALF), BF16), pltpu.VMEM((tokens, D), F32), pltpu.VMEM((tokens, D), F32),
            pltpu.VMEM((tokens, D), BF16), pltpu.VMEM((tokens, D), BF16), pltpu.VMEM((tokens, 3 * D), BF16),
            pltpu.VMEM((D, tokens), BF16), pltpu.VMEM((3, 2, D, HALF), BF16), pltpu.VMEM((2, D, HALF), BF16),
            pltpu.VMEM((16, D), F32), pltpu.VMEM((2, 16, HALF), BF16), dma(5 + CHIPS),
        ],
        2 * tokens * D * (FF + 8 * D) + 20 * tokens * D * ROW_LEN, 4,
    )
    (layer_out,) = call(
        layer_out_kernel, "layer_out", (pos, act, mid, vec), down, (shape((tokens, D)),),
        [pltpu.VMEM((2, FF, HALF), BF16), dma(1)], 2 * tokens * D * FF,
    )

    g_up = [g.reshape(CHIPS, 2 * BLK, HALF) for g in g_up]
    g_attn = [g.reshape(CHIPS, -1, HALF) for g in g_attn]
    pairs = [((g[0], g[1]), (g[2], g[3])) for g in (g_down, g_up, g_attn)]
    per, per_up = pre_attn_gain.shape[0], b_up.shape[0]
    if tuned:
        grad_down, grad_up, grad_attn = [scatter_group(p) for p in pairs]
        core = pos[1]

        def exchange(blocks, axis):
            first, second = jnp.split(blocks, 2, axis=axis)
            keep = jnp.where(core == 0, first, second)
            got = swap(jnp.where(core == 0, second, first), 0)
            return jnp.where(core == 0, keep, got), jnp.where(core == 0, got, keep)

        lo, hi = exchange(grad_attn[: 4 * BLK].reshape(4, BLK, HALF), 1)
        wide_rows = jnp.stack([lo, hi]).transpose(2, 1, 0, 3)
        grad_w_qkv = wide_rows[:, :3].reshape(per, 3 * D)
        grad_w_out = wide_rows[:, 3].reshape(per, D)
        lo, hi = exchange(grad_up.reshape(4, BLK, HALF), 1)
        grad_w_up = jnp.stack([lo, hi]).transpose(2, 0, 1, 3).reshape(per, FF)
        grad_w_down = jnp.concatenate(exchange(grad_down, 0), axis=1)
        own = grad_attn[4 * BLK :]
        got = swap(own, 0)
        sums = jnp.where(
            core == 0, jnp.concatenate([own, got], 1), jnp.concatenate([got, own], 1)
        )
    else:
        grad_w_down = scatter_plain(pairs[0], "down")
        grad_w_up = scatter_plain(pairs[1], "up")
        grad_w_qkv, grad_w_out, sums = scatter_plain(pairs[2], "attn")
    eight, grad_b_up, grad_b_down = small_grads(sums, place, per, per_up)
    return (
        layer_out, input_grad, eight[0], eight[1], grad_w_qkv, eight[2], eight[4], grad_w_out, eight[5],
        eight[6], eight[7], grad_w_up, grad_b_up, grad_w_down, grad_b_down,
    )


def solution(mesh):
    both = P(AXES, None)
    one = P(AXES)
    tuned = dict(mesh.shape) == {"wide": 8, "narrow": 4}
    in_specs = (both, both, one, one, both, one, one, both, one, one, one, both, one, both, one, both)
    out_specs = (both, both, one, one, both, one, one, both, one, one, one, both, one, both, one)
    return jax.shard_map(
        functools.partial(per_device, tuned),
        mesh=mesh,
        in_specs=in_specs,
        out_specs=out_specs,
        check_vma=False,
    )
```

```python
import functools

import jax
import jax.numpy as jnp
from jax import lax
from jax.experimental import pallas as pl
from jax.experimental.pallas import tpu as pltpu
from jax.sharding import PartitionSpec as P

HEADS = 12
HEAD_DIM = 64
D = 768
FF = 3072
ROW_LEN = 256
HALF = 384
CHIPS = 16
BLK = 48
PAIRS = HEADS // 2
AXES = ("wide", "narrow")

EPS = 1e-06
MASKED = -1e30
F32 = jnp.float32
BF16 = jnp.bfloat16

BIT_Y, BIT_X, BIT_Z0, BIT_Z1 = 1, 2, 4, 8


def xor_order(bits):
    order = [0]
    for bit in bits:
        order = order + [o ^ bit for o in order]
    return order


GATHER = (
    xor_order((BIT_Z0, BIT_Z1, BIT_Y, BIT_X)),
    xor_order((BIT_Z0, BIT_Z1, BIT_X, BIT_Y)),
)
SCATTER = GATHER


def nt(a, b):
    return lax.dot_general(a, b, (((1,), (1,)), ((), ())), preferred_element_type=F32)


def tn(a, b):
    return lax.dot_general(a, b, (((0,), (0,)), ((), ())), preferred_element_type=F32)


def nn(a, b):
    return lax.dot_general(a, b, (((1,), (0,)), ((), ())), preferred_element_type=F32)


def chunks(tokens, step, body):
    def one(i, carry):
        body(pl.ds(pl.multiple_of(i * step, step), step))
        return carry

    lax.fori_loop(0, tokens // step, one, 0)


def norm_parts(v):
    centre = jnp.mean(v, axis=-1, keepdims=True)
    centred = v - centre
    scale = lax.rsqrt(jnp.mean(centred * centred, axis=-1, keepdims=True) + EPS)
    return centred * scale, scale


def start(src, dst, sem):
    copy = pltpu.make_async_copy(src, dst, sem)
    copy.start()
    return copy


def whole_wait(ref, sem):
    pltpu.make_async_copy(ref, ref, sem).wait()


def each_block(pos_ref, stream, pieces):
    me = pos_ref[0]
    own0, own1, sib0, sib1 = pieces
    for other, first, second in ((0, own0, own1), (1, sib0, sib1)):
        for p in range(CHIPS):
            offset = GATHER[stream][p]
            yield (first, second)[p // 8], p % 8, me ^ offset, other, offset


def chip_rows(chip, size, count, extra=0):
    return pl.ds(pl.multiple_of(chip * size + extra, 16), count)


def half_cols(pos_ref, other):
    return pl.ds(pl.multiple_of((pos_ref[1] ^ other) * HALF, 128), HALF)


def fetch_qk(pos_ref, pieces, w_qkv, sem):
    for ref, b, chip, other, _ in each_block(pos_ref, 0, pieces):
        dst = w_qkv.at[pl.ds(0, 2), chip_rows(chip, BLK, BLK), half_cols(pos_ref, other)]
        start(ref.at[b], dst, sem)


def fetch_v(pos_ref, pieces, w_qkv, sem):
    for ref, b, chip, other, _ in each_block(pos_ref, 1, pieces):
        dst = w_qkv.at[2, chip_rows(chip, BLK, BLK), half_cols(pos_ref, other)]
        start(ref.at[b, pl.ds(0, BLK)], dst, sem)


def fetch_out(pos_ref, pieces, w_out, sem):
    for ref, b, chip, other, _ in each_block(pos_ref, 1, pieces):
        dst = w_out.at[chip_rows(chip, BLK, BLK), half_cols(pos_ref, other)]
        start(ref.at[b, pl.ds(BLK, BLK)], dst, sem)


def fetch_small(pos_ref, pieces, small, sem):
    for ref, b, chip, other, _ in each_block(pos_ref, 1, pieces):
        start(ref.at[b, pl.ds(2 * BLK, 16)], small.at[pos_ref[1] ^ other, chip], sem)


def fetch_up(pos_ref, pieces, w_up, sems):
    for s in range(2):
        for ref, b, chip, other, _ in each_block(pos_ref, s, pieces[4 * s : 4 * s + 4]):
            for u in range(2):
                dst = w_up.at[other, s, chip_rows(chip, BLK, BLK), pl.ds(u * HALF, HALF)]
                start(ref.at[b, u], dst, sems.at[2 * other + s])


def fetch_down(pos_ref, pieces, w_down, sems):
    for q in range(4):
        for s in range(2):
            for ref, b, chip, other, offset in each_block(pos_ref, s, pieces[4 * s : 4 * s + 4]):
                if offset // 4 == q:
                    rows = chip_rows(chip, 4 * BLK, 2 * BLK, 2 * BLK * s)
                    start(ref.at[b], w_down.at[rows, half_cols(pos_ref, other)], sems.at[q])


def scatter_place(pos_ref, stream, chip):
    o = pos_ref[0] ^ chip
    y, x, z0, z1 = o & 1, (o >> 1) & 1, (o >> 2) & 1, (o >> 3) & 1
    return (x * 8 + y * 4 if stream == 0 else y * 8 + x * 4) + z1 * 2 + z0


def attn_forward_kernel(
    pos_ref, segr_ref, segc_ref, x_any, qk0, qk1, qk2, qk3, vo0, vo1, vo2, vo3,
    vec_ref, n1_any, qkv_any, soft_any, mixed_any, mid_any, n2_any,
    x_ref, n1_ref, qkv_ref, soft_ref, mixed_ref, mid_ref, n2_ref, w_qkv, w_out, small, bias, sems,
):
    tokens = x_ref.shape[0]
    vo = (vo0, vo1, vo2, vo3)
    load_x = start(x_any, x_ref, sems.at[0])
    fetch_small(pos_ref, vo, small, sems.at[1])
    fetch_qk(pos_ref, (qk0, qk1, qk2, qk3), w_qkv, sems.at[2])
    fetch_v(pos_ref, vo, w_qkv, sems.at[3])
    fetch_out(pos_ref, vo, w_out, sems.at[4])
    for r in range(tokens // ROW_LEN):
        same = segc_ref[r * ROW_LEN : (r + 1) * ROW_LEN] == segr_ref[r]
        bias[r] = jnp.where(same, 0.0, MASKED)
    whole_wait(small, sems.at[1])
    for h in range(2):
        vec_ref[:, h * HALF : (h + 1) * HALF] = jnp.sum(small[h].astype(F32), axis=0)
    load_x.wait()

    def norm_one(rows):
        xhat, _ = norm_parts(x_ref[rows, :].astype(F32))
        n1_ref[rows, :] = (xhat * vec_ref[0:1, :] + vec_ref[1:2, :]).astype(BF16)

    chunks(tokens, 128, norm_one)
    stores = [start(n1_ref, n1_any, sems.at[5])]
    whole_wait(w_qkv.at[pl.ds(0, 2)], sems.at[2])
    for t in range(3):
        if t == 2:
            whole_wait(w_qkv.at[2], sems.at[3])
        y = (nn(n1_ref[...], w_qkv[t]) + vec_ref[2 + t : 3 + t, :]).astype(BF16)
        if t == 0:
            y = y * BF16(HEAD_DIM**-0.5)
        qkv_ref[:, t * D : (t + 1) * D] = y
    stores.append(start(qkv_ref, qkv_any, sems.at[6]))

    lane = lax.broadcasted_iota(jnp.int32, (1, 2 * HEAD_DIM), 1)
    low = (lane < HEAD_DIM).astype(F32).astype(BF16)
    high = (lane >= HEAD_DIM).astype(F32).astype(BF16)
    for r in range(tokens // ROW_LEN):
        rows = slice(r * ROW_LEN, (r + 1) * ROW_LEN)

        def pair(i, carry):
            q = qkv_ref[rows, pl.ds(pl.multiple_of(i * 128, 128), 128)]
            k = qkv_ref[rows, pl.ds(pl.multiple_of(D + i * 128, 128), 128)]
            v = qkv_ref[rows, pl.ds(pl.multiple_of(2 * D + i * 128, 128), 128)]
            mixed = jnp.zeros((ROW_LEN, 128), F32)
            for hh, keep in enumerate((low, high)):
                s = nt(q, k * keep) + bias[r]
                e = jnp.exp(s - jnp.max(s, axis=-1, keepdims=True))
                p = (e * (1.0 / jnp.sum(e, axis=-1, keepdims=True))).astype(BF16)
                soft_ref[r * HEADS + 2 * i + hh] = p
                mixed = mixed + nn(p, v * keep)
            mixed_ref[rows, pl.ds(pl.multiple_of(i * 128, 128), 128)] = mixed.astype(BF16)
            at = pl.ds(r * HEADS + 2 * i, 2)
            start(soft_ref.at[at], soft_any.at[at], sems.at[7])
            return carry

        lax.fori_loop(0, PAIRS, pair, 0)
    stores.append(start(mixed_ref, mixed_any, sems.at[8]))
    whole_wait(w_out, sems.at[4])
    mid_ref[...] = x_ref[...].astype(F32) + nn(mixed_ref[...], w_out[...]) + vec_ref[5:6, :]
    stores.append(start(mid_ref, mid_any, sems.at[9]))

    def norm_two(rows):
        xhat, _ = norm_parts(mid_ref[rows, :])
        n2_ref[rows, :] = (xhat * vec_ref[6:7, :] + vec_ref[7:8, :]).astype(BF16)

    chunks(tokens, 128, norm_two)
    stores.append(start(n2_ref, n2_any, sems.at[10]))
    whole_wait(soft_ref, sems.at[7])
    for store in stores:
        store.wait()


GELU_A = 0.7978845608028654
GELU_B = 0.044715


def mlp_up_kernel(
    pos_ref, segc_ref, vec_ref, n2_any, cot_any, up0, up1, up2, up3, up4, up5, up6, up7,
    gb_ref, act_any, slope_any, gout_any, am, at, bm, bt,
    n2_ref, cot_ref, act_ref, slope_ref, gout_ref, w_up, grad, sems,
):
    tokens = n2_ref.shape[0]
    load_n2 = start(n2_any, n2_ref, sems.at[4])
    load_cot = start(cot_any, cot_ref, sems.at[5])
    fetch_up(pos_ref, (up0, up1, up2, up3, up4, up5, up6, up7), w_up, sems)
    load_cot.wait()
    valid = segc_ref[...] > 0
    gout = jnp.where(valid, cot_ref[...].astype(F32), 0.0)
    gout_ref[...] = gout.astype(BF16)
    gb_ref[...] = jnp.broadcast_to(jnp.sum(gout, axis=0, keepdims=True), gb_ref.shape)
    stores = [start(gout_ref, gout_any, sems.at[6])]
    load_n2.wait()
    outs = ((am, at), (bm, bt))
    for other in range(2):
        for s in range(2):
            whole_wait(w_up.at[other, s], sems.at[2 * other + s])
            half = pos_ref[1] ^ other
            f = half * (2 * D) + s * D
            b_up = vec_ref[pl.ds(8 + 2 * half + s, 1), :]

            def part(rows):
                u = nn(n2_ref[rows, :], w_up[other, s]) + b_up
                sq = u * u
                t = jnp.tanh(u * (GELU_A + GELU_A * GELU_B * sq))
                half_up = 0.5 + 0.5 * t
                act_ref[other, s, rows, :] = (u * half_up).astype(BF16)
                slope_ref[other, s, rows, :] = (
                    half_up + u * (0.5 - 0.5 * t * t) * (GELU_A + 3.0 * GELU_A * GELU_B * sq)
                ).astype(BF16)

            chunks(tokens, 256, part)
            cols = pl.ds(pl.multiple_of(f, 128), D)
            stores.append(start(act_ref.at[other, s], act_any.at[:, cols], sems.at[7 + 2 * other + s]))
            stores.append(
                start(slope_ref.at[other, s], slope_any.at[:, cols], sems.at[11 + 2 * other + s])
            )
            grad[other, s] = tn(act_ref[other, s], gout_ref[...]).astype(BF16)
            for j in range(4):
                chip = 4 * (2 * half + s) + j
                for stream in range(2):
                    rows = pl.ds(j * 4 * BLK + stream * 2 * BLK, 2 * BLK)
                    for oc in range(2):
                        start(
                            grad.at[other, s, rows, half_cols(pos_ref, oc)],
                            outs[stream][oc].at[scatter_place(pos_ref, stream, chip)],
                            sems.at[15],
                        )
    whole_wait(grad, sems.at[15])
    for store in stores:
        store.wait()


def mlp_down_kernel(
    pos_ref, gout_any, slope_any, n2_any, dn0, dn1, dn2, dn3, dn4, dn5, dn6, dn7,
    gb_ref, gpre_any, am, at, bm, bt,
    gout_ref, slope_ref, n2_ref, gpre_ref, n2t, w_down, grad, sems,
):
    load_n2 = start(n2_any, n2_ref, sems.at[4])
    load_gout = start(gout_any, gout_ref, sems.at[5])
    fetch_down(pos_ref, (dn0, dn1, dn2, dn3, dn4, dn5, dn6, dn7), w_down, sems)
    loads = {}
    for other in range(2):
        for s in range(2):
            f = (pos_ref[1] ^ other) * (2 * D) + s * D
            cols = pl.ds(pl.multiple_of(f, 128), D)
            loads[other, s] = start(
                slope_any.at[:, cols], slope_ref.at[other, s], sems.at[6 + 2 * other + s]
            )
    gb_ref[...] = jnp.zeros(gb_ref.shape, F32)
    load_n2.wait()
    n2t[...] = n2_ref[...].T
    load_gout.wait()
    outs = ((am, at), (bm, bt))
    stores = []
    for other in range(2):
        for s in range(2):
            z = (pos_ref[1] ^ other) * 2 + s
            rows = pl.ds(pl.multiple_of(z * D, 128), D)
            whole_wait(w_down.at[rows], sems.at[z ^ (pos_ref[0] >> 2)])
            loads[other, s].wait()
            ga = nt(gout_ref[...], w_down[rows, :])
            gp = (ga * slope_ref[other, s].astype(F32)).astype(BF16)
            gpre_ref[other, s] = gp
            stores.append(
                start(gpre_ref.at[other, s], gpre_any.at[:, rows], sems.at[10 + 2 * other + s])
            )
            gb_ref[pl.ds(z, 1), :] = jnp.sum(gp.astype(F32), axis=0, keepdims=True)
            grad[other, s] = nn(n2t[...], gpre_ref[other, s]).astype(BF16)
            for chip in range(CHIPS):
                for u in range(2):
                    start(
                        grad.at[other, s, pl.ds(chip * BLK, BLK), pl.ds(u * HALF, HALF)],
                        outs[s][other].at[scatter_place(pos_ref, s, chip), u],
                        sems.at[14],
                    )
    whole_wait(grad, sems.at[14])
    for store in stores:
        store.wait()


def norm_back(grad, xhat, scale, gain):
    gn = grad * gain
    mean_gn = jnp.mean(gn, axis=-1, keepdims=True)
    mean_gx = jnp.mean(gn * xhat, axis=-1, keepdims=True)
    return scale * (gn - mean_gn - xhat * mean_gx)


def mid_backward_kernel(
    pos_ref, vec_ref, gbd_ref, gbu_ref, gpre_any, gout_any, mid_any, mixed_any,
    up0, up1, up2, up3, up4, up5, up6, up7, vo0, vo1, vo2, vo3,
    sums, gmid_any, gmixed_any, om, ot,
    gpre_ref, gout_ref, mid_ref, mixed_ref, w_up, w_out, acc, gmid, gbr, gmixed, mixt, grad, sems,
):
    tokens = mid_ref.shape[0]
    fetch_up(pos_ref, (up0, up1, up2, up3, up4, up5, up6, up7), w_up, sems)
    loads = {}
    for other in range(2):
        for s in range(2):
            f = (pos_ref[1] ^ other) * (2 * D) + s * D
            cols = pl.ds(pl.multiple_of(f, 128), D)
            loads[other, s] = start(
                gpre_any.at[:, cols], gpre_ref.at[other, s], sems.at[4 + 2 * other + s]
            )
    load_mixed = start(mixed_any, mixed_ref, sems.at[8])
    load_mid = start(mid_any, mid_ref, sems.at[9])
    load_gout = start(gout_any, gout_ref, sems.at[10])
    fetch_out(pos_ref, (vo0, vo1, vo2, vo3), w_out, sems.at[11])
    sums[...] = jnp.zeros(sums.shape, F32)
    sums[8:12, :] = gbu_ref[0:4, :]
    sums[12:13, :] = gbd_ref[0:1, :]
    load_mixed.wait()
    mixt[...] = mixed_ref[...].T
    for other in range(2):
        for s in range(2):
            whole_wait(w_up.at[other, s], sems.at[2 * other + s])
            loads[other, s].wait()
            part = nt(gpre_ref[other, s], w_up[other, s])
            acc[...] = part if other + s == 0 else acc[...] + part
    load_mid.wait()
    load_gout.wait()

    def back_two(rows):
        xhat, scale = norm_parts(mid_ref[rows, :])
        g = acc[rows, :]
        sums[6:7, :] += jnp.sum(g * xhat, axis=0, keepdims=True)
        sums[7:8, :] += jnp.sum(g, axis=0, keepdims=True)
        gm = gout_ref[rows, :].astype(F32) + norm_back(g, xhat, scale, vec_ref[6:7, :])
        gmid[rows, :] = gm
        low = gm.astype(BF16)
        gbr[rows, :] = low
        sums[5:6, :] += jnp.sum(low.astype(F32), axis=0, keepdims=True)

    chunks(tokens, 128, back_two)
    stores = [start(gmid, gmid_any, sems.at[12])]
    whole_wait(w_out, sems.at[11])
    gmixed[...] = nt(gbr[...], w_out[...]).astype(BF16)
    stores.append(start(gmixed, gmixed_any, sems.at[13]))
    grad[...] = nn(mixt[...], gbr[...]).astype(BF16)
    for chip in range(CHIPS):
        for oc, out in enumerate((om, ot)):
            start(
                grad.at[pl.ds(chip * BLK, BLK), half_cols(pos_ref, oc)],
                out.at[scatter_place(pos_ref, 1, chip)],
                sems.at[14],
            )
    whole_wait(grad, sems.at[14])
    for store in stores:
        store.wait()


def attn_backward_kernel(
    pos_ref, vec_ref, sums_ref, gmid_any, gmixed_any, qkv_any, soft_any, n1_any, x_any,
    qk0, qk1, qk2, qk3, vo0, vo1, vo2, vo3,
    igrad_any, am, at, bm, bt,
    gmid, gmixed, qkv_ref, soft_ref, n1_ref, x_ref, w_qkv, acc, gqkv, n1t, grad, sums, small, igrad, sems,
):
    tokens = x_ref.shape[0]
    load_gmixed = start(gmixed_any, gmixed, sems.at[0])
    load_qkv = start(qkv_any, qkv_ref, sems.at[1])
    per_row = [
        start(soft_any.at[pl.ds(r * HEADS, HEADS)], soft_ref.at[pl.ds(r * HEADS, HEADS)], sems.at[8 + r])
        for r in range(tokens // ROW_LEN)
    ]
    load_n1 = start(n1_any, n1_ref, sems.at[2])
    load_x = start(x_any, x_ref, sems.at[3])
    load_gmid = start(gmid_any, gmid, sems.at[4])
    fetch_qk(pos_ref, (qk0, qk1, qk2, qk3), w_qkv, sems.at[5])
    fetch_v(pos_ref, (vo0, vo1, vo2, vo3), w_qkv, sems.at[5])
    sums[...] = sums_ref[...]
    load_gmixed.wait()
    load_qkv.wait()
    lane = lax.broadcasted_iota(jnp.int32, (1, 2 * HEAD_DIM), 1)
    first = (lane < HEAD_DIM).astype(F32).astype(BF16)
    second = (lane >= HEAD_DIM).astype(F32).astype(BF16)
    for r in range(tokens // ROW_LEN):
        rows = slice(r * ROW_LEN, (r + 1) * ROW_LEN)
        per_row[r].wait()

        def pair(i, carry):
            at_q = pl.ds(pl.multiple_of(i * 128, 128), 128)
            at_k = pl.ds(pl.multiple_of(D + i * 128, 128), 128)
            at_v = pl.ds(pl.multiple_of(2 * D + i * 128, 128), 128)
            q, k, v = qkv_ref[rows, at_q], qkv_ref[rows, at_k], qkv_ref[rows, at_v]
            gm = gmixed[rows, at_q]
            dq = jnp.zeros((ROW_LEN, 128), F32)
            dk = jnp.zeros((ROW_LEN, 128), F32)
            dv = jnp.zeros((ROW_LEN, 128), F32)
            for hh, keep in enumerate((first, second)):
                p_low = soft_ref[r * HEADS + 2 * i + hh]
                p = p_low.astype(F32)
                gmk = gm * keep
                gs = nt(gmk, v)
                inner = jnp.sum(p * gs, axis=-1, keepdims=True)
                ds = (p * (gs - inner)).astype(BF16)
                dq = dq + nn(ds, k * keep)
                dk = dk + tn(ds, q * keep)
                dv = dv + tn(p_low, gmk)
            gqkv[rows, at_q] = (dq * (HEAD_DIM**-0.5)).astype(BF16)
            gqkv[rows, at_k] = dk.astype(BF16)
            gqkv[rows, at_v] = dv.astype(BF16)
            return carry

        lax.fori_loop(0, PAIRS, pair, 0)
    load_n1.wait()
    n1t[...] = n1_ref[...].T
    whole_wait(w_qkv, sems.at[5])
    outs = ((am, at), (bm, bt))
    for t in (0, 1, 2):
        g = gqkv[:, t * D : (t + 1) * D]
        if t != 1:
            sums[2 + t : 3 + t, :] = jnp.sum(g.astype(F32), axis=0, keepdims=True)
        grad[t] = nn(n1t[...], g).astype(BF16)
        stream = 0 if t < 2 else 1
        for chip in range(CHIPS):
            place = scatter_place(pos_ref, stream, chip)
            for oc in range(2):
                src = grad.at[t, pl.ds(chip * BLK, BLK), half_cols(pos_ref, oc)]
                dst = outs[stream][oc].at[place, pl.ds(t * BLK if t < 2 else 0, BLK)]
                start(src, dst, sems.at[6])
        part = nt(g, w_qkv[t])
        acc[...] = part if t == 0 else acc[...] + part
    load_x.wait()
    load_gmid.wait()

    def back_one(rows):
        xhat, scale = norm_parts(x_ref[rows, :].astype(F32))
        g = acc[rows, :]
        sums[0:1, :] += jnp.sum(g * xhat, axis=0, keepdims=True)
        sums[1:2, :] += jnp.sum(g, axis=0, keepdims=True)
        igrad[rows, :] = (gmid[rows, :] + norm_back(g, xhat, scale, vec_ref[0:1, :])).astype(BF16)

    chunks(tokens, 128, back_one)
    store = start(igrad, igrad_any, sems.at[7])
    for p in range(CHIPS):
        small[0, p] = sums[:, :HALF].astype(BF16)
        small[1, p] = sums[:, HALF:].astype(BF16)
    for oc in range(2):
        for p in range(CHIPS):
            start(
                small.at[pos_ref[1] ^ oc, p], outs[1][oc].at[p, pl.ds(BLK, 16)], sems.at[10]
            )
    whole_wait(small, sems.at[10])
    whole_wait(grad, sems.at[6])
    store.wait()


def layer_out_kernel(
    pos_ref, vec_ref, act_any, mid_any, dn0, dn1, dn2, dn3, dn4, dn5, dn6, dn7,
    out_any, act_ref, mid_ref, out_ref, w_down, acc, sems,
):
    fetch_down(pos_ref, (dn0, dn1, dn2, dn3, dn4, dn5, dn6, dn7), w_down, sems)
    loads = []
    own_z = pos_ref[0] >> 2
    for q in range(4):
        cols = pl.ds(pl.multiple_of((own_z ^ q) * D, 128), D)
        loads.append(start(act_any.at[:, cols], act_ref.at[q], sems.at[4 + q]))
    load_mid = start(mid_any, mid_ref, sems.at[8])
    for q in range(4):
        rows = pl.ds(pl.multiple_of((own_z ^ q) * D, 128), D)
        whole_wait(w_down.at[rows], sems.at[q])
        loads[q].wait()
        part = nn(act_ref[q], w_down[rows, :])
        if q == 0:
            load_mid.wait()
            acc[...] = part + (mid_ref[...] + vec_ref[12:13, :])
        elif q < 3:
            acc[...] = acc[...] + part
        else:
            out_ref[...] = (acc[...] + part).astype(BF16)
    start(out_ref, out_any, sems.at[9]).wait()


def call(kernel, name, near, far, near_outs, far_outs, scratch, flops):
    vmem = pl.BlockSpec(memory_space=pltpu.VMEM)
    anyspec = pl.BlockSpec(memory_space=pl.ANY)
    outs = tuple(near_outs) + tuple(far_outs)
    moved = sum(a.size * a.dtype.itemsize for a in tuple(near) + tuple(far) + outs)
    return pl.pallas_call(
        kernel,
        out_shape=outs,
        in_specs=[pl.BlockSpec(memory_space=pltpu.SMEM)]
        + [vmem] * (len(near) - 1)
        + [anyspec] * len(far),
        out_specs=[vmem] * len(near_outs) + [anyspec] * len(far_outs),
        scratch_shapes=scratch,
        compiler_params=pltpu.CompilerParams(vmem_limit_bytes=56 << 20),
        cost_estimate=pl.CostEstimate(flops=flops, bytes_accessed=moved, transcendentals=0),
        name=name,
    )(*near, *far)


def swap(value, chip_bit):
    flip = chip_bit * 2 if chip_bit else 1
    return lax.ppermute(value, AXES, [(i, i ^ flip) for i in range(2 * CHIPS)])


def tie(value, *after):
    return lax.optimization_barrier((value,) + after)[0]


def gather_group(block, cut, after=()):
    near = swap(tie(block, *after[:1]), BIT_Z0)
    far = swap(tie(jnp.stack([block, near]), *after[1:]), BIT_Z1)
    pieces = []
    for rows, bits in ((slice(0, cut), (BIT_Y, BIT_X)), (slice(cut, None), (BIT_X, BIT_Y))):
        four = jnp.stack([block[rows], near[rows], far[0, rows], far[1, rows]])
        eight = jnp.concatenate([four, swap(four, bits[0])])
        other = swap(eight, bits[1])
        pieces.append((eight, other, swap(eight, 0), swap(other, 0)))
    return pieces, (near, far)


def scatter_group(parts):
    fours = []
    for (mine, theirs), bits in zip(parts, ((BIT_X, BIT_Y), (BIT_Y, BIT_X))):
        total = mine.astype(F32) + swap(theirs, 0).astype(F32)
        got = swap(total[8:].astype(BF16), bits[0])
        total = total[:8] + got.astype(F32)
        got = swap(total[4:].astype(BF16), bits[1])
        fours.append(total[:4] + got.astype(F32))
    total = jnp.concatenate(fours, axis=1)
    got = swap(total[2:].astype(BF16), BIT_Z1)
    total = total[:2] + got.astype(F32)
    got = swap(total[1].astype(BF16), BIT_Z0)
    return total[0] + got.astype(F32)


def small_rows(place, values):
    gain1, bias1, bq, bv, bo, gain2, bias2, bu, bd = values
    per = gain1.shape[0]
    zero = jnp.zeros_like(gain1)
    eight = jnp.stack([gain1, bias1, bq, zero, bv, bo, gain2, bias2])
    rows = jnp.zeros((16, D), BF16)
    rows = lax.dynamic_update_slice(rows, eight, (0, place * per))
    at = place * bu.shape[0]
    rows = lax.dynamic_update_slice(rows, bu[None], (8 + at // D, at % D))
    return lax.dynamic_update_slice(rows, bd[None], (12, place * per))


def small_grads(sums, place, per, per_up):
    eight = lax.dynamic_slice(sums, (0, place * per), (8, per))
    at = place * per_up
    up = lax.dynamic_slice(sums, (8 + at // D, at % D), (1, per_up))[0]
    down = lax.dynamic_slice(sums, (12, place * per), (1, per))[0]
    return eight, up, down


def halves(w_qkv, w_out, w_up, w_down):
    rows = w_qkv.shape[0]
    qkv = w_qkv.reshape(rows, 3, 2, HALF)
    up = w_up.reshape(rows, 2, 4, HALF)
    for h in range(2):
        cols = slice(h * HALF, (h + 1) * HALF)
        yield (
            jnp.concatenate([qkv[:, :, h].transpose(1, 0, 2), w_out[None, :, cols]]),
            up[:, h].transpose(1, 0, 2),
            w_down[:, cols],
        )


def gather_by_swaps(wide, narrow, weights, values):
    core = narrow & 1
    place = wide * 4 + narrow
    rows = small_rows(place, values)
    packed = [
        (a, u, d, rows[:, h * HALF : (h + 1) * HALF]) for h, (a, u, d) in enumerate(halves(*weights))
    ]
    mine = [jnp.where(core == 0, p, q) for p, q in zip(*packed)]
    theirs = [jnp.where(core == 0, q, p) for p, q in zip(*packed)]
    got = [swap(t, 0) for t in theirs]

    def both(m, g, axis):
        return jnp.where(
            core == 0, jnp.concatenate([m, g], axis), jnp.concatenate([g, m], axis)
        )

    attn = both(mine[0], got[0], 1).reshape(4 * BLK, HALF)
    up = both(mine[1], got[1], 1).reshape(4 * BLK, HALF)
    down = both(mine[2], got[2], 0)
    small = mine[3] + got[3]
    one, (near1, far1) = gather_group(jnp.concatenate([attn, small]), 2 * BLK)
    two, (_, far2) = gather_group(up, 2 * BLK, (near1, far1))
    three, _ = gather_group(down, 2 * BLK, (far1, far2))
    return one, two, three


def gather_plain(weights, values):
    def whole(w):
        return lax.all_gather(w, AXES, axis=0, tiled=True)

    gain1, bias1, bq, bv, bo, gain2, bias2, bu, bd = [whole(v) for v in values]
    rest = jnp.zeros((3, D), BF16)
    small = jnp.stack([gain1, bias1, bq, jnp.zeros_like(bq), bv, bo, gain2, bias2])
    small = jnp.concatenate([small, bu.reshape(4, D), bd[None], rest])
    groups = ([], [], [])
    for h, (attn, up, down) in enumerate(halves(*[whole(w) for w in weights])):
        attn = attn.reshape(4, CHIPS, BLK, HALF).transpose(1, 0, 2, 3).reshape(CHIPS, 4 * BLK, HALF)
        up = up.reshape(4, CHIPS, BLK, HALF).transpose(1, 0, 2, 3).reshape(CHIPS, 4 * BLK, HALF)
        down = down.reshape(CHIPS, 4 * BLK, HALF)
        extra = jnp.zeros((CHIPS, 16, HALF), BF16).at[0].set(small[:, h * HALF : (h + 1) * HALF])
        for group, blocks in zip(groups, (jnp.concatenate([attn, extra], axis=1), up, down)):
            streams = []
            for s, rows in enumerate((slice(0, 2 * BLK), slice(2 * BLK, None))):
                ordered = jnp.stack([blocks[o, rows] for o in GATHER[s]])
                streams.append((ordered[:8], ordered[8:]))
            group.append(streams)
    return tuple([own + sib for own, sib in zip(*group)] for group in groups)


def scatter_plain(parts, group):
    whole = []
    for s, pair in enumerate(parts):
        back = [SCATTER[s].index(chip) for chip in range(CHIPS)]
        whole.append([jnp.stack([part[p] for p in back]) for part in pair])
    both = [jnp.concatenate([whole[0][h], whole[1][h]], axis=1) for h in range(2)]

    def scatter(v):
        return lax.psum_scatter(v.astype(F32), AXES, scatter_dimension=0, tiled=True)

    def matrix(first, units):
        cut = [
            b[:, first * BLK : (first + units) * BLK].reshape(CHIPS, units, BLK, HALF) for b in both
        ]
        return jnp.stack(cut, axis=3).transpose(0, 2, 1, 3, 4).reshape(D, units, 2, HALF)

    if group == "attn":
        sums = jnp.concatenate([b[0, 4 * BLK :] for b in both], axis=1)
        return (
            scatter(matrix(0, 3).reshape(D, 3 * D)),
            scatter(matrix(3, 1).reshape(D, D)),
            lax.psum(sums.astype(F32), AXES),
        )
    if group == "up":
        return scatter(matrix(0, 4).transpose(0, 2, 1, 3).reshape(D, FF))
    return scatter(jnp.concatenate([b.reshape(FF, HALF) for b in both], axis=1))


def per_device(tuned, *args):
    (
        inputs, segment_ids, pre_attn_gain, pre_attn_bias, w_qkv, b_query, b_value, w_out, b_out,
        pre_mlp_gain, pre_mlp_bias, w_up, b_up, w_down, b_down, cotangent,
    ) = args
    tokens = inputs.shape[0]
    n_rows = tokens // ROW_LEN
    wide, narrow = lax.axis_index("wide"), lax.axis_index("narrow")
    weights = (w_qkv, w_out, w_up, w_down)
    values = (
        pre_attn_gain, pre_attn_bias, b_query, b_value, b_out, pre_mlp_gain, pre_mlp_bias, b_up, b_down,
    )
    if tuned:
        place = wide * 4 + narrow
        pos = jnp.stack([wide * 2 + (narrow >> 1), narrow & 1]).astype(jnp.int32)
        groups = gather_by_swaps(wide, narrow, weights, values)
    else:
        place = wide * lax.axis_size("narrow") + narrow
        pos = jnp.zeros((2,), jnp.int32)
        groups = gather_plain(weights, values)
    (qk, vo), up, down = groups
    per_block = (
        [a.reshape(8, 2, BLK, HALF) for a in qk],
        list(vo),
        [a.reshape(8, 2, BLK, HALF) for s in up for a in s],
        [a for s in down for a in s],
    )
    qk, vo, up, down = per_block

    position = jnp.arange(ROW_LEN, dtype=jnp.int32)[None]
    own_id = jnp.where(segment_ids != 0, segment_ids, -1 - position)
    segr = own_id.reshape(n_rows, 1, ROW_LEN)
    segc = own_id.reshape(tokens, 1)

    def shape(dims, kind=BF16):
        return jax.ShapeDtypeStruct(dims, kind)

    def dma(n):
        return pltpu.SemaphoreType.DMA((n,))

    def vmem(*dims, kind=BF16):
        return pltpu.VMEM(dims, kind)

    wide_act = shape((tokens, FF))
    act_like = shape((tokens, D))
    mid_like = shape((tokens, D), F32)
    quarters = vmem(2, 2, tokens, D)
    one = vmem(tokens, D)
    one_f32 = vmem(tokens, D, kind=F32)
    square = vmem(D, D)
    three = vmem(3, D, D)
    four = vmem(2, 2, D, D)
    soft_dims = (n_rows * HEADS, ROW_LEN, ROW_LEN)
    block_2 = shape((CHIPS, 2, BLK, HALF))
    block_flat = shape((CHIPS, 2 * BLK, HALF))
    block_1 = shape((CHIPS, BLK, HALF))
    block_vs = shape((CHIPS, BLK + 16, HALF))

    vec, n1, qkv, soft, mixed, mid, n2 = call(
        attn_forward_kernel, "attn_forward", (pos, segr, segc), [inputs] + qk + vo,
        (shape((16, D), F32),),
        (act_like, shape((tokens, 3 * D)), shape(soft_dims), act_like, mid_like, act_like),
        [
            one, one, vmem(tokens, 3 * D), vmem(*soft_dims), one, one_f32, one, three, square,
            vmem(2, CHIPS, 16, HALF), vmem(n_rows, ROW_LEN, ROW_LEN, kind=F32), dma(11),
        ],
        2 * tokens * D * D * 4 + 8 * tokens * D * ROW_LEN,
    )
    gb_down, act, slope, gout, *g_down = call(
        mlp_up_kernel, "mlp_up", (pos, segc, vec), [n2, cotangent] + up,
        (shape((8, D), F32),), (wide_act, wide_act, act_like) + (block_flat,) * 4,
        [one, one, quarters, quarters, one, four, four, dma(16)],
        4 * tokens * D * FF,
    )
    gb_up, gpre, *g_up = call(
        mlp_down_kernel, "mlp_down", (pos,), [gout, slope, n2] + down,
        (shape((8, D), F32),), (wide_act,) + (block_2,) * 4,
        [one, quarters, one, quarters, vmem(D, tokens), vmem(FF, D), four, dma(15)],
        4 * tokens * D * FF,
    )
    sums, gmid, gmixed, *g_out = call(
        mid_backward_kernel, "mid_backward", (pos, vec, gb_down, gb_up), [gpre, gout, mid, mixed] + up + vo,
        (shape((16, D), F32),), (mid_like, act_like, block_1, block_1),
        [
            quarters, one, one_f32, one, four, square, one_f32, one_f32, one, one, vmem(D, tokens), square,
            dma(15),
        ],
        2 * tokens * D * (FF + 2 * D),
    )
    input_grad, *g_attn = call(
        attn_backward_kernel, "attn_backward", (pos, vec, sums),
        [gmid, gmixed, qkv, soft, n1, inputs] + qk + vo,
        (), (act_like, block_flat, block_flat, block_vs, block_vs),
        [
            one_f32, one, vmem(tokens, 3 * D), vmem(*soft_dims), one, one, three, one_f32,
            vmem(tokens, 3 * D), vmem(D, tokens), three, vmem(16, D, kind=F32), vmem(2, CHIPS, 16, HALF),
            one, dma(11),
        ],
        2 * tokens * D * 6 * D + 20 * tokens * D * ROW_LEN,
    )
    (layer_out,) = call(
        layer_out_kernel, "layer_out", (pos, vec), [act, mid] + down,
        (), (act_like,),
        [vmem(4, tokens, D), one_f32, one, vmem(FF, D), one_f32, dma(10)],
        2 * tokens * D * FF,
    )

    g_up = [g.reshape(CHIPS, 2 * BLK, HALF) for g in g_up]
    g_vs = [jnp.concatenate([v[:, :BLK], o, v[:, BLK:]], axis=1) for v, o in zip(g_attn[2:], g_out)]
    g_attn = g_attn[:2] + g_vs
    pairs = [((g[0], g[1]), (g[2], g[3])) for g in (g_down, g_up, g_attn)]
    per, per_up = pre_attn_gain.shape[0], b_up.shape[0]
    if tuned:
        grad_down, grad_up, grad_attn = [scatter_group(p) for p in pairs]
        core = pos[1]

        def exchange(blocks, axis):
            first, second = jnp.split(blocks, 2, axis=axis)
            keep = jnp.where(core == 0, first, second)
            got = swap(jnp.where(core == 0, second, first), 0)
            return jnp.where(core == 0, keep, got), jnp.where(core == 0, got, keep)

        lo, hi = exchange(grad_attn[: 4 * BLK].reshape(4, BLK, HALF), 1)
        wide_rows = jnp.stack([lo, hi]).transpose(2, 1, 0, 3)
        grad_w_qkv = wide_rows[:, :3].reshape(per, 3 * D)
        grad_w_out = wide_rows[:, 3].reshape(per, D)
        lo, hi = exchange(grad_up.reshape(4, BLK, HALF), 1)
        grad_w_up = jnp.stack([lo, hi]).transpose(2, 0, 1, 3).reshape(per, FF)
        grad_w_down = jnp.concatenate(exchange(grad_down, 0), axis=1)
        own = grad_attn[4 * BLK :]
        got = swap(own, 0)
        sums = jnp.where(
            core == 0, jnp.concatenate([own, got], 1), jnp.concatenate([got, own], 1)
        )
    else:
        grad_w_down = scatter_plain(pairs[0], "down")
        grad_w_up = scatter_plain(pairs[1], "up")
        grad_w_qkv, grad_w_out, sums = scatter_plain(pairs[2], "attn")
    eight, grad_b_up, grad_b_down = small_grads(sums, place, per, per_up)
    return (
        layer_out, input_grad, eight[0], eight[1], grad_w_qkv, eight[2], eight[4], grad_w_out, eight[5],
        eight[6], eight[7], grad_w_up, grad_b_up, grad_w_down, grad_b_down,
    )


def solution(mesh):
    both = P(AXES, None)
    one = P(AXES)
    tuned = dict(mesh.shape) == {"wide": 8, "narrow": 4}
    in_specs = (both, both, one, one, both, one, one, both, one, one, one, both, one, both, one, both)
    out_specs = (both, both, one, one, both, one, one, both, one, one, one, both, one, both, one)
    return jax.shard_map(
        functools.partial(per_device, tuned),
        mesh=mesh,
        in_specs=in_specs,
        out_specs=out_specs,
        check_vma=False,
    )
```

```python
import functools

import jax
import jax.numpy as jnp
from jax import lax
from jax.experimental import pallas as pl
from jax.experimental.pallas import tpu as pltpu
from jax.sharding import PartitionSpec as P

HEADS = 12
HEAD_DIM = 64
D = 768
FF = 3072
ROW_LEN = 256
HALF = 384
CHIPS = 16
BLK = 48
PAIRS = HEADS // 2
AXES = ("wide", "narrow")

EPS = 1e-06
MASKED = -1e30
F32 = jnp.float32
BF16 = jnp.bfloat16

BIT_Y, BIT_X, BIT_Z0, BIT_Z1 = 1, 2, 4, 8
Z_OFFSETS = (0, 4, 8, 12)

GATHER = (
    Z_OFFSETS,
    tuple(o + BIT_Y for o in Z_OFFSETS),
    tuple(o + BIT_X for o in Z_OFFSETS),
    tuple(o + BIT_X + BIT_Y for o in Z_OFFSETS[:2]),
    tuple(o + BIT_X + BIT_Y for o in Z_OFFSETS[2:]),
)
PIECES = 2 * len(GATHER)

SCATTER = (0, 4, 8, 12, 1, 5, 10, 14, 9, 13, 11, 15, 2, 6, 3, 7)


def nt(a, b):
    return lax.dot_general(a, b, (((1,), (1,)), ((), ())), preferred_element_type=F32)


def tn(a, b):
    return lax.dot_general(a, b, (((0,), (0,)), ((), ())), preferred_element_type=F32)


def nn(a, b):
    return lax.dot_general(a, b, (((1,), (0,)), ((), ())), preferred_element_type=F32)


def chunks(tokens, step, body):
    def one(i, carry):
        body(pl.ds(pl.multiple_of(i * step, step), step))
        return carry

    lax.fori_loop(0, tokens // step, one, 0)


def norm_parts(v):
    centre = jnp.mean(v, axis=-1, keepdims=True)
    centred = v - centre
    scale = lax.rsqrt(jnp.mean(centred * centred, axis=-1, keepdims=True) + EPS)
    return centred * scale, scale


def start(src, dst, sem):
    copy = pltpu.make_async_copy(src, dst, sem)
    copy.start()
    return copy


def whole_wait(ref, sem):
    pltpu.make_async_copy(ref, ref, sem).wait()


def each_block(pos_ref, pieces):
    for other in range(2):
        for ref, offsets in zip(pieces[other * len(GATHER) :], GATHER):
            for b, offset in enumerate(offsets):
                yield ref, b, pos_ref[0] ^ offset, other, offset


def chip_rows(chip, size):
    return pl.ds(pl.multiple_of(chip * size, 16), size)


def half_cols(pos_ref, other):
    return pl.ds(pl.multiple_of((pos_ref[1] ^ other) * HALF, 128), HALF)


def fetch_qkv(pos_ref, pieces, w_qkv, sems):
    for t in range(3):
        for ref, b, chip, other, _ in each_block(pos_ref, pieces):
            dst = w_qkv.at[t, chip_rows(chip, BLK), half_cols(pos_ref, other)]
            start(ref.at[b, pl.ds(t * BLK, BLK)], dst, sems.at[t])


def fetch_out(pos_ref, pieces, w_out, sem):
    for ref, b, chip, other, _ in each_block(pos_ref, pieces):
        dst = w_out.at[chip_rows(chip, BLK), half_cols(pos_ref, other)]
        start(ref.at[b, pl.ds(3 * BLK, BLK)], dst, sem)


def fetch_small(pos_ref, pieces, small, sem):
    for ref, b, chip, other, _ in each_block(pos_ref, pieces):
        start(ref.at[b, pl.ds(4 * BLK, 16)], small.at[pos_ref[1] ^ other, chip], sem)


def fetch_up(pos_ref, pieces, w_up, sems):
    for ref, b, chip, other, _ in each_block(pos_ref, pieces):
        for u in range(2):
            dst = w_up.at[other, pl.ds(0, 2), chip_rows(chip, BLK), pl.ds(u * HALF, HALF)]
            start(ref.at[b, pl.ds(2 * u, 2)], dst, sems.at[other])


def fetch_down(pos_ref, pieces, w_down, sems):
    for q in range(4):
        for ref, b, chip, other, offset in each_block(pos_ref, pieces):
            if offset // 4 == q:
                dst = w_down.at[chip_rows(chip, 4 * BLK), half_cols(pos_ref, other)]
                start(ref.at[b], dst, sems.at[q])


def scatter_place(pos_ref, chip):
    offset = pos_ref[0] ^ chip
    xy, z = offset & 3, offset >> 2
    near = jnp.where(xy == 1, 4, jnp.where(xy == 2, 12, 14)) + z
    far = jnp.where(xy == 1, 6, jnp.where(xy == 2, 4, 8)) + z
    return jnp.where(xy == 0, z, jnp.where(z < 2, near, far))


def attn_forward_kernel(pos_ref, segr_ref, segc_ref, x_any, *refs):
    pieces, refs = refs[:PIECES], refs[PIECES:]
    vec_ref, n1_any, qkv_any, soft_any, mixed_any, mid_any, n2_any, *refs = refs
    x_ref, n1_ref, qkv_ref, soft_ref, mixed_ref, mid_ref, n2_ref, w_qkv, w_out, small, bias, sems = refs
    tokens = x_ref.shape[0]
    load_x = start(x_any, x_ref, sems.at[0])
    fetch_small(pos_ref, pieces, small, sems.at[1])
    fetch_qkv(pos_ref, pieces, w_qkv, sems.at[pl.ds(2, 3)])
    fetch_out(pos_ref, pieces, w_out, sems.at[11])
    for r in range(tokens // ROW_LEN):
        same = segc_ref[r * ROW_LEN : (r + 1) * ROW_LEN] == segr_ref[r]
        bias[r] = jnp.where(same, 0.0, MASKED)
    whole_wait(small, sems.at[1])
    for h in range(2):
        vec_ref[:, h * HALF : (h + 1) * HALF] = jnp.sum(small[h].astype(F32), axis=0)
    load_x.wait()

    def norm_one(rows):
        xhat, _ = norm_parts(x_ref[rows, :].astype(F32))
        n1_ref[rows, :] = (xhat * vec_ref[0:1, :] + vec_ref[1:2, :]).astype(BF16)

    chunks(tokens, 128, norm_one)
    stores = [start(n1_ref, n1_any, sems.at[5])]
    for t in range(3):
        whole_wait(w_qkv.at[t], sems.at[2 + t])
        y = (nn(n1_ref[...], w_qkv[t]) + vec_ref[2 + t : 3 + t, :]).astype(BF16)
        if t == 0:
            y = y * BF16(HEAD_DIM**-0.5)
        qkv_ref[:, t * D : (t + 1) * D] = y
    stores.append(start(qkv_ref, qkv_any, sems.at[6]))

    lane = lax.broadcasted_iota(jnp.int32, (1, 2 * HEAD_DIM), 1)
    low = (lane < HEAD_DIM).astype(F32).astype(BF16)
    high = (lane >= HEAD_DIM).astype(F32).astype(BF16)
    for r in range(tokens // ROW_LEN):
        rows = slice(r * ROW_LEN, (r + 1) * ROW_LEN)

        def pair(i, carry):
            q = qkv_ref[rows, pl.ds(pl.multiple_of(i * 128, 128), 128)]
            k = qkv_ref[rows, pl.ds(pl.multiple_of(D + i * 128, 128), 128)]
            v = qkv_ref[rows, pl.ds(pl.multiple_of(2 * D + i * 128, 128), 128)]
            mixed = jnp.zeros((ROW_LEN, 128), F32)
            for hh, keep in enumerate((low, high)):
                s = nt(q, k * keep) + bias[r]
                e = jnp.exp(s - jnp.max(s, axis=-1, keepdims=True))
                p = (e * (1.0 / jnp.sum(e, axis=-1, keepdims=True))).astype(BF16)
                soft_ref[r * HEADS + 2 * i + hh] = p
                mixed = mixed + nn(p, v * keep)
            mixed_ref[rows, pl.ds(pl.multiple_of(i * 128, 128), 128)] = mixed.astype(BF16)
            at = pl.ds(r * HEADS + 2 * i, 2)
            start(soft_ref.at[at], soft_any.at[at], sems.at[7])
            return carry

        lax.fori_loop(0, PAIRS, pair, 0)
    stores.append(start(mixed_ref, mixed_any, sems.at[8]))
    whole_wait(w_out, sems.at[11])
    mid_ref[...] = x_ref[...].astype(F32) + nn(mixed_ref[...], w_out[...]) + vec_ref[5:6, :]
    stores.append(start(mid_ref, mid_any, sems.at[9]))

    def norm_two(rows):
        xhat, _ = norm_parts(mid_ref[rows, :])
        n2_ref[rows, :] = (xhat * vec_ref[6:7, :] + vec_ref[7:8, :]).astype(BF16)

    chunks(tokens, 128, norm_two)
    stores.append(start(n2_ref, n2_any, sems.at[10]))
    whole_wait(soft_ref, sems.at[7])
    for store in stores:
        store.wait()


GELU_A = 0.7978845608028654
GELU_B = 0.044715


def quarter(pos_ref, other, s):
    return (pos_ref[1] ^ other) * 2 + s


def quarter_cols(z):
    return pl.ds(pl.multiple_of(z * D, 128), D)


QUARTERS = ((0, 0), (0, 1), (1, 0), (1, 1))


def mlp_up_kernel(pos_ref, segc_ref, vec_ref, n2_any, cot_any, *refs):
    pieces, refs = refs[:PIECES], refs[PIECES:]
    gb_ref, act_any, slope_any, gout_any, *refs = refs
    n2_ref, cot_ref, act_ref, slope_ref, gout_ref, w_up, sems = refs
    tokens = n2_ref.shape[0]
    load_n2 = start(n2_any, n2_ref, sems.at[2])
    fetch_up(pos_ref, pieces, w_up, sems)
    load_cot = start(cot_any, cot_ref, sems.at[3])
    load_n2.wait()
    stores = []
    for other, s in QUARTERS:
        if s == 0:
            whole_wait(w_up.at[other], sems.at[other])
        z = quarter(pos_ref, other, s)
        b_up = vec_ref[pl.ds(8 + z, 1), :]

        def part(rows):
            u = nn(n2_ref[rows, :], w_up[other, s]) + b_up
            sq = u * u
            t = jnp.tanh(u * (GELU_A + GELU_A * GELU_B * sq))
            half_up = 0.5 + 0.5 * t
            act_ref[other, s, rows, :] = (u * half_up).astype(BF16)
            slope_ref[other, s, rows, :] = (
                half_up + u * (0.5 - 0.5 * t * t) * (GELU_A + 3.0 * GELU_A * GELU_B * sq)
            ).astype(BF16)

        chunks(tokens, 256, part)
        k = 2 * other + s
        stores.append(start(act_ref.at[other, s], act_any.at[:, quarter_cols(z)], sems.at[5 + k]))
        stores.append(start(slope_ref.at[other, s], slope_any.at[:, quarter_cols(z)], sems.at[9 + k]))
    load_cot.wait()
    valid = segc_ref[...] > 0
    gout = jnp.where(valid, cot_ref[...].astype(F32), 0.0)
    gout_ref[...] = gout.astype(BF16)
    gb_ref[...] = jnp.broadcast_to(jnp.sum(gout, axis=0, keepdims=True), gb_ref.shape)
    stores.append(start(gout_ref, gout_any, sems.at[4]))
    for store in stores:
        store.wait()


def down_grad_kernel(pos_ref, act_any, gout_any, mine, theirs, act_ref, gout_ref, grad, sems):
    load_gout = start(gout_any, gout_ref, sems.at[0])
    loads = [
        start(act_any.at[:, pl.ds(z * D, D)], act_ref.at[z], sems.at[2 + z]) for z in range(4)
    ]
    load_gout.wait()
    for z in range(4):
        loads[z].wait()
        grad[z] = tn(act_ref[z], gout_ref[...]).astype(BF16)
        for j in range(4):
            place = scatter_place(pos_ref, 4 * z + j)
            for other, out in enumerate((mine, theirs)):
                src = grad.at[z, pl.ds(j * 4 * BLK, 4 * BLK), half_cols(pos_ref, other)]
                start(src, out.at[place], sems.at[1])
    whole_wait(grad, sems.at[1])


def mlp_down_kernel(pos_ref, gout_any, slope_any, n2_any, *refs):
    pieces, refs = refs[:PIECES], refs[PIECES:]
    gb_ref, gpre_any, mine, theirs, *refs = refs
    gout_ref, slope_ref, n2_ref, gpre_ref, n2t, w_down, grad, sems = refs
    load_n2 = start(n2_any, n2_ref, sems.at[4])
    load_gout = start(gout_any, gout_ref, sems.at[5])
    fetch_down(pos_ref, pieces, w_down, sems)
    loads = {
        (other, s): start(
            slope_any.at[:, quarter_cols(quarter(pos_ref, other, s))],
            slope_ref.at[other, s],
            sems.at[6 + 2 * other + s],
        )
        for other, s in QUARTERS
    }
    gb_ref[...] = jnp.zeros(gb_ref.shape, F32)
    load_n2.wait()
    n2t[...] = n2_ref[...].T
    load_gout.wait()
    stores = []
    for other, s in QUARTERS:
        z = quarter(pos_ref, other, s)
        rows = quarter_cols(z)
        whole_wait(w_down.at[rows], sems.at[z ^ (pos_ref[0] >> 2)])
        loads[other, s].wait()
        ga = nt(gout_ref[...], w_down[rows, :])
        gp = (ga * slope_ref[other, s].astype(F32)).astype(BF16)
        gpre_ref[other, s] = gp
        stores.append(start(gpre_ref.at[other, s], gpre_any.at[:, rows], sems.at[10 + 2 * other + s]))
        gb_ref[pl.ds(z, 1), :] = jnp.sum(gp.astype(F32), axis=0, keepdims=True)
        grad[other, s] = nn(n2t[...], gpre_ref[other, s]).astype(BF16)
        if s == 1:
            for chip in range(CHIPS):
                place = scatter_place(pos_ref, chip)
                for u in range(2):
                    src = grad.at[other, pl.ds(0, 2), pl.ds(chip * BLK, BLK), pl.ds(u * HALF, HALF)]
                    start(src, (mine, theirs)[other].at[place, pl.ds(2 * u, 2)], sems.at[14])
    whole_wait(grad, sems.at[14])
    for store in stores:
        store.wait()


def norm_back(grad, xhat, scale, gain):
    gn = grad * gain
    mean_gn = jnp.mean(gn, axis=-1, keepdims=True)
    mean_gx = jnp.mean(gn * xhat, axis=-1, keepdims=True)
    return scale * (gn - mean_gn - xhat * mean_gx)


def mid_backward_kernel(
    pos_ref, vec_ref, gbd_ref, gbu_ref, gpre_any, gout_any, mid_any, mixed_any, *refs
):
    pieces_up, pieces_attn, refs = refs[:PIECES], refs[PIECES : 2 * PIECES], refs[2 * PIECES :]
    sums, gmid_any, gmixed_any, mine, theirs, *refs = refs
    gpre_ref, gout_ref, mid_ref, mixed_ref, w_up, w_out, acc, gmid, gbr, gmixed, mixt, grad, sems = refs
    tokens = mid_ref.shape[0]
    load_mixed = start(mixed_any, mixed_ref, sems.at[8])
    fetch_up(pos_ref, pieces_up, w_up, sems)
    loads = {
        (other, s): start(
            gpre_any.at[:, quarter_cols(quarter(pos_ref, other, s))],
            gpre_ref.at[other, s],
            sems.at[4 + 2 * other + s],
        )
        for other, s in QUARTERS
    }
    load_mid = start(mid_any, mid_ref, sems.at[9])
    load_gout = start(gout_any, gout_ref, sems.at[10])
    fetch_out(pos_ref, pieces_attn, w_out, sems.at[11])
    sums[...] = jnp.zeros(sums.shape, F32)
    sums[8:12, :] = gbu_ref[0:4, :]
    sums[12:13, :] = gbd_ref[0:1, :]
    load_mixed.wait()
    mixt[...] = mixed_ref[...].T
    for other, s in QUARTERS:
        if s == 0:
            whole_wait(w_up.at[other], sems.at[other])
        loads[other, s].wait()
        part = nt(gpre_ref[other, s], w_up[other, s])
        acc[...] = part if other + s == 0 else acc[...] + part
    load_mid.wait()
    load_gout.wait()

    def back_two(rows):
        xhat, scale = norm_parts(mid_ref[rows, :])
        g = acc[rows, :]
        sums[6:7, :] += jnp.sum(g * xhat, axis=0, keepdims=True)
        sums[7:8, :] += jnp.sum(g, axis=0, keepdims=True)
        gm = gout_ref[rows, :].astype(F32) + norm_back(g, xhat, scale, vec_ref[6:7, :])
        gmid[rows, :] = gm
        low = gm.astype(BF16)
        gbr[rows, :] = low
        sums[5:6, :] += jnp.sum(low.astype(F32), axis=0, keepdims=True)

    chunks(tokens, 128, back_two)
    stores = [start(gmid, gmid_any, sems.at[12])]
    whole_wait(w_out, sems.at[11])
    gmixed[...] = nt(gbr[...], w_out[...]).astype(BF16)
    stores.append(start(gmixed, gmixed_any, sems.at[13]))
    grad[...] = nn(mixt[...], gbr[...]).astype(BF16)
    for chip in range(CHIPS):
        place = scatter_place(pos_ref, chip)
        for other, out in enumerate((mine, theirs)):
            src = grad.at[pl.ds(chip * BLK, BLK), half_cols(pos_ref, other)]
            start(src, out.at[place, pl.ds(3 * BLK, BLK)], sems.at[14])
    whole_wait(grad, sems.at[14])
    for store in stores:
        store.wait()


def attn_backward_kernel(
    pos_ref, gmixed_any, qkv_any, soft_any, gb_ref, gqkv_any, gmixed, qkv_ref, soft_ref, gqkv, sems
):
    tokens = gmixed.shape[0]
    load_gmixed = start(gmixed_any, gmixed, sems.at[0])
    load_qkv = start(qkv_any, qkv_ref, sems.at[1])
    n_rows = tokens // ROW_LEN
    per_row = [
        start(
            soft_any.at[pl.ds(r * HEADS, HEADS)], soft_ref.at[pl.ds(r * HEADS, HEADS)], sems.at[4 + r]
        )
        for r in range(n_rows)
    ]
    load_gmixed.wait()
    load_qkv.wait()
    lane = lax.broadcasted_iota(jnp.int32, (1, 2 * HEAD_DIM), 1)
    first = (lane < HEAD_DIM).astype(F32).astype(BF16)
    second = (lane >= HEAD_DIM).astype(F32).astype(BF16)
    for r in range(n_rows):
        rows = slice(r * ROW_LEN, (r + 1) * ROW_LEN)
        per_row[r].wait()

        def pair(i, carry):
            at_q = pl.ds(pl.multiple_of(i * 128, 128), 128)
            at_k = pl.ds(pl.multiple_of(D + i * 128, 128), 128)
            at_v = pl.ds(pl.multiple_of(2 * D + i * 128, 128), 128)
            q, k, v = qkv_ref[rows, at_q], qkv_ref[rows, at_k], qkv_ref[rows, at_v]
            gm = gmixed[rows, at_q]
            dq = jnp.zeros((ROW_LEN, 128), F32)
            dk = jnp.zeros((ROW_LEN, 128), F32)
            dv = jnp.zeros((ROW_LEN, 128), F32)
            for hh, keep in enumerate((first, second)):
                p_low = soft_ref[r * HEADS + 2 * i + hh]
                p = p_low.astype(F32)
                gmk = gm * keep
                gs = nt(gmk, v)
                inner = jnp.sum(p * gs, axis=-1, keepdims=True)
                ds = (p * (gs - inner)).astype(BF16)
                dq = dq + nn(ds, k * keep)
                dk = dk + tn(ds, q * keep)
                dv = dv + tn(p_low, gmk)
            gqkv[rows, at_q] = (dq * (HEAD_DIM**-0.5)).astype(BF16)
            gqkv[rows, at_k] = dk.astype(BF16)
            gqkv[rows, at_v] = dv.astype(BF16)
            return carry

        lax.fori_loop(0, PAIRS, pair, 0)
    store = start(gqkv, gqkv_any, sems.at[2])
    gb_ref[...] = jnp.zeros(gb_ref.shape, F32)
    gb_ref[0:1, :] = jnp.sum(gqkv[:, :D].astype(F32), axis=0, keepdims=True)
    gb_ref[2:3, :] = jnp.sum(gqkv[:, 2 * D :].astype(F32), axis=0, keepdims=True)
    store.wait()


def qkv_grad_kernel(
    pos_ref, vec_ref, sums_ref, gbq_ref, gmid_any, gqkv_any, n1_any, x_any, *refs
):
    pieces, refs = refs[:PIECES], refs[PIECES + 2 :]
    igrad_any, mine, theirs, *refs = refs
    gmid, gqkv, n1_ref, x_ref, w_qkv, acc, n1t, grad, sums, small, igrad, sems = refs
    tokens = x_ref.shape[0]
    load_n1 = start(n1_any, n1_ref, sems.at[0])
    loads = [
        start(gqkv_any.at[:, pl.ds(t * D, D)], gqkv.at[t], sems.at[1 + t]) for t in range(3)
    ]
    fetch_qkv(pos_ref, pieces, w_qkv, sems.at[pl.ds(4, 3)])
    load_x = start(x_any, x_ref, sems.at[7])
    load_gmid = start(gmid_any, gmid, sems.at[8])
    sums[...] = sums_ref[...]
    sums[2:3, :] = gbq_ref[0:1, :]
    sums[4:5, :] = gbq_ref[2:3, :]
    load_n1.wait()
    n1t[...] = n1_ref[...].T
    for t in range(3):
        loads[t].wait()
        grad[t] = nn(n1t[...], gqkv[t]).astype(BF16)
        for chip in range(CHIPS):
            place = scatter_place(pos_ref, chip)
            for other, out in enumerate((mine, theirs)):
                src = grad.at[t, pl.ds(chip * BLK, BLK), half_cols(pos_ref, other)]
                start(src, out.at[place, pl.ds(t * BLK, BLK)], sems.at[9])
    for t in range(3):
        whole_wait(w_qkv.at[t], sems.at[4 + t])
        part = nt(gqkv[t], w_qkv[t])
        acc[...] = part if t == 0 else acc[...] + part
    load_x.wait()
    load_gmid.wait()

    def back_one(rows):
        xhat, scale = norm_parts(x_ref[rows, :].astype(F32))
        g = acc[rows, :]
        sums[0:1, :] += jnp.sum(g * xhat, axis=0, keepdims=True)
        sums[1:2, :] += jnp.sum(g, axis=0, keepdims=True)
        igrad[rows, :] = (gmid[rows, :] + norm_back(g, xhat, scale, vec_ref[0:1, :])).astype(BF16)

    chunks(tokens, 128, back_one)
    store = start(igrad, igrad_any, sems.at[10])
    for p in range(CHIPS):
        small[0, p] = sums[:, :HALF].astype(BF16)
        small[1, p] = sums[:, HALF:].astype(BF16)
    for other, out in enumerate((mine, theirs)):
        for p in range(CHIPS):
            start(small.at[pos_ref[1] ^ other, p], out.at[p, pl.ds(4 * BLK, 16)], sems.at[11])
    whole_wait(small, sems.at[11])
    whole_wait(grad, sems.at[9])
    store.wait()


def layer_out_kernel(pos_ref, vec_ref, act_any, mid_any, *refs):
    pieces, refs = refs[:PIECES], refs[PIECES:]
    out_any, act_ref, mid_ref, out_ref, w_down, acc, sems = refs
    own_z = pos_ref[0] >> 2
    load_mid = start(mid_any, mid_ref, sems.at[8])
    loads = [
        start(act_any.at[:, quarter_cols(own_z ^ q)], act_ref.at[q], sems.at[4 + q]) for q in range(4)
    ]
    fetch_down(pos_ref, pieces, w_down, sems)
    for q in range(4):
        rows = quarter_cols(own_z ^ q)
        loads[q].wait()
        whole_wait(w_down.at[rows], sems.at[q])
        part = nn(act_ref[q], w_down[rows, :])
        if q == 0:
            load_mid.wait()
            acc[...] = part + (mid_ref[...] + vec_ref[12:13, :])
        elif q < 3:
            acc[...] = acc[...] + part
        else:
            out_ref[...] = (acc[...] + part).astype(BF16)
    start(out_ref, out_any, sems.at[9]).wait()


def call(kernel, name, near, far, near_outs, far_outs, scratch, flops, aliases=None):
    vmem = pl.BlockSpec(memory_space=pltpu.VMEM)
    anyspec = pl.BlockSpec(memory_space=pl.ANY)
    outs = tuple(near_outs) + tuple(far_outs)
    moved = sum(a.size * a.dtype.itemsize for a in tuple(near) + tuple(far) + outs)
    return pl.pallas_call(
        kernel,
        out_shape=outs,
        in_specs=[pl.BlockSpec(memory_space=pltpu.SMEM)]
        + [vmem] * (len(near) - 1)
        + [anyspec] * len(far),
        out_specs=[vmem] * len(near_outs) + [anyspec] * len(far_outs),
        scratch_shapes=scratch,
        input_output_aliases=aliases or {},
        compiler_params=pltpu.CompilerParams(vmem_limit_bytes=56 << 20),
        cost_estimate=pl.CostEstimate(flops=flops, bytes_accessed=moved, transcendentals=0),
        name=name,
    )(*near, *far)


def swap(value, chip_bit):
    flip = chip_bit * 2 if chip_bit else 1
    return lax.ppermute(value, AXES, [(i, i ^ flip) for i in range(2 * CHIPS)])


def tie(value, *after):
    return lax.optimization_barrier((value,) + after)[0]


def gathered(own, y, x, d0, d1, *after):
    own_half = (own, y, x, d0, d1)
    return list(own_half) + [swap(tie(piece, *after) if after else piece, 0) for piece in own_half]


def rounded_sum(*terms):
    total = terms[0].astype(F32)
    for term in terms[1:]:
        total = total + term.astype(F32)
    return total.astype(BF16)


def small_rows(place, values):
    gain1, bias1, bq, bv, bo, gain2, bias2, bu, bd = values
    per = gain1.shape[0]
    zero = jnp.zeros_like(gain1)
    eight = jnp.stack([gain1, bias1, bq, zero, bv, bo, gain2, bias2])
    rows = jnp.zeros((16, D), BF16)
    rows = lax.dynamic_update_slice(rows, eight, (0, place * per))
    at = place * bu.shape[0]
    rows = lax.dynamic_update_slice(rows, bu[None], (8 + at // D, at % D))
    return lax.dynamic_update_slice(rows, bd[None], (12, place * per))


def small_grads(sums, place, per, per_up):
    eight = lax.dynamic_slice(sums, (0, place * per), (8, per))
    at = place * per_up
    up = lax.dynamic_slice(sums, (8 + at // D, at % D), (1, per_up))[0]
    down = lax.dynamic_slice(sums, (12, place * per), (1, per))[0]
    return eight, up, down


def halves(w_qkv, w_out, w_up, w_down):
    rows = w_qkv.shape[0]
    qkv = w_qkv.reshape(rows, 3, 2, HALF)
    up = w_up.reshape(rows, 2, 4, HALF)
    for h in range(2):
        cols = slice(h * HALF, (h + 1) * HALF)
        yield (
            jnp.concatenate([qkv[:, :, h].transpose(1, 0, 2), w_out[None, :, cols]]),
            up[:, h].reshape(rows, 2, 2, HALF).transpose(2, 1, 0, 3).reshape(4, rows, HALF),
            w_down[:, cols],
        )


def chip_blocks(wide, narrow, weights, values):
    core = narrow & 1
    place = wide * 4 + narrow
    rows = small_rows(place, values)
    packed = [
        (a, u, d, rows[:, h * HALF : (h + 1) * HALF]) for h, (a, u, d) in enumerate(halves(*weights))
    ]
    mine = [jnp.where(core == 0, p, q) for p, q in zip(*packed)]
    theirs = [jnp.where(core == 0, q, p) for p, q in zip(*packed)]
    got = [swap(t, 0) for t in theirs]

    def both(m, g, axis):
        return jnp.where(
            core == 0, jnp.concatenate([m, g], axis), jnp.concatenate([g, m], axis)
        )

    attn = both(mine[0], got[0], 1).reshape(4 * BLK, HALF)
    up = both(mine[1], got[1], 1).reshape(4 * BLK, HALF)
    down = both(mine[2], got[2], 0)
    small = mine[3] + got[3]
    return jnp.concatenate([attn, small]), up, down


def gather_plain(weights, values):
    def whole(w):
        return lax.all_gather(w, AXES, axis=0, tiled=True)

    gain1, bias1, bq, bv, bo, gain2, bias2, bu, bd = [whole(v) for v in values]
    rest = jnp.zeros((3, D), BF16)
    small = jnp.stack([gain1, bias1, bq, jnp.zeros_like(bq), bv, bo, gain2, bias2])
    small = jnp.concatenate([small, bu.reshape(4, D), bd[None], rest])
    groups = ([], [], [])
    for h, (attn, up, down) in enumerate(halves(*[whole(w) for w in weights])):
        attn = attn.reshape(4, CHIPS, BLK, HALF).transpose(1, 0, 2, 3).reshape(CHIPS, 4 * BLK, HALF)
        up = up.reshape(4, CHIPS, BLK, HALF).transpose(1, 0, 2, 3).reshape(CHIPS, 4 * BLK, HALF)
        down = down.reshape(CHIPS, 4 * BLK, HALF)
        extra = jnp.zeros((CHIPS, 16, HALF), BF16).at[0].set(small[:, h * HALF : (h + 1) * HALF])
        for group, blocks in zip(groups, (jnp.concatenate([attn, extra], axis=1), up, down)):
            group.extend(jnp.stack([blocks[o] for o in piece]) for piece in GATHER)
    return groups


def scatter_plain(pair, group):
    both = [jnp.stack([part[SCATTER.index(chip)] for chip in range(CHIPS)]) for part in pair]

    def scatter(v):
        return lax.psum_scatter(v.astype(F32), AXES, scatter_dimension=0, tiled=True)

    def matrix(first, units):
        cut = [
            b[:, first * BLK : (first + units) * BLK].reshape(CHIPS, units, BLK, HALF) for b in both
        ]
        return jnp.stack(cut, axis=3).transpose(0, 2, 1, 3, 4).reshape(D, units, 2, HALF)

    if group == "attn":
        sums = jnp.concatenate([b[0, 4 * BLK :] for b in both], axis=1)
        return (
            scatter(matrix(0, 3).reshape(D, 3 * D)),
            scatter(matrix(3, 1).reshape(D, D)),
            lax.psum(sums.astype(F32), AXES),
        )
    if group == "up":
        return scatter(matrix(0, 4).reshape(D, 2, 2, 2, HALF).transpose(0, 3, 2, 1, 4).reshape(D, FF))
    return scatter(jnp.concatenate([b.reshape(FF, HALF) for b in both], axis=1))


def shape(dims, kind=BF16):
    return jax.ShapeDtypeStruct(dims, kind)


def dma(n):
    return pltpu.SemaphoreType.DMA((n,))


def vmem(*dims, kind=BF16):
    return pltpu.VMEM(dims, kind)


class Layer:
    def __init__(self, tokens):
        self.tokens = tokens
        self.rows = tokens // ROW_LEN
        self.wide = shape((tokens, FF))
        self.act = shape((tokens, D))
        self.mid = shape((tokens, D), F32)
        self.qkv = shape((tokens, 3 * D))
        self.soft = shape((self.rows * HEADS, ROW_LEN, ROW_LEN))
        self.quarters = vmem(2, 2, tokens, D)
        self.one = vmem(tokens, D)
        self.one_f32 = vmem(tokens, D, kind=F32)
        self.turned = vmem(D, tokens)
        self.square = vmem(D, D)
        self.three = vmem(3, D, D)
        self.four = vmem(2, 2, D, D)
        self.sums = shape((8, D), F32)
        self.vec = shape((16, D), F32)

    def attn_forward(self, pos, segr, segc, inputs, attn):
        one, t = self.one, self.tokens
        return call(
            attn_forward_kernel, "attn_forward", (pos, segr, segc), [inputs] + attn,
            (self.vec,), (self.act, self.qkv, self.soft, self.act, self.mid, self.act),
            [
                one, one, vmem(t, 3 * D), vmem(*self.soft.shape), one, self.one_f32, one, self.three,
                self.square, vmem(2, CHIPS, 16, HALF), vmem(self.rows, ROW_LEN, ROW_LEN, kind=F32), dma(12),
            ],
            2 * t * D * D * 4 + 8 * t * D * ROW_LEN,
        )

    def mlp_up(self, pos, segc, vec, n2, cotangent, up):
        one, quarters = self.one, self.quarters
        return call(
            mlp_up_kernel, "mlp_up", (pos, segc, vec), [n2, cotangent] + up,
            (self.sums,), (self.wide, self.wide, self.act),
            [one, one, quarters, quarters, one, self.four, dma(13)],
            2 * self.tokens * D * FF,
        )

    def down_grad(self, pos, act, gout):
        buffer = shape((CHIPS, 4 * BLK, HALF))
        return call(
            down_grad_kernel, "down_grad", (pos,), [act, gout], (), (buffer, buffer),
            [vmem(4, self.tokens, D), self.one, vmem(4, D, D), dma(6)],
            2 * self.tokens * D * FF,
        )

    def mlp_down(self, pos, gout, slope, n2, down):
        one, quarters = self.one, self.quarters
        buffer = shape((CHIPS, 4, BLK, HALF))
        gb, gpre, mine, theirs = call(
            mlp_down_kernel, "mlp_down", (pos,), [gout, slope, n2] + down,
            (self.sums,), (self.wide, buffer, buffer),
            [one, quarters, one, quarters, self.turned, vmem(FF, D), self.four, dma(15)],
            4 * self.tokens * D * FF,
        )
        flat = (CHIPS, 4 * BLK, HALF)
        return gb, gpre, mine.reshape(flat), theirs.reshape(flat)

    def mid_backward(self, pos, vec, gbd, gbu, gpre, gout, mid, mixed, up, attn):
        one, wide = self.one, self.one_f32
        buffer = shape((CHIPS, 4 * BLK + 16, HALF))
        return call(
            mid_backward_kernel, "mid_backward", (pos, vec, gbd, gbu), [gpre, gout, mid, mixed] + up + attn,
            (self.vec,), (self.mid, self.act, buffer, buffer),
            [
                self.quarters, one, wide, one, self.four, self.square, wide, wide, one, one, self.turned,
                self.square, dma(15),
            ],
            2 * self.tokens * D * (FF + 2 * D),
        )

    def attn_backward(self, pos, gmixed, qkv, soft):
        t = self.tokens
        return call(
            attn_backward_kernel, "attn_backward", (pos,), [gmixed, qkv, soft], (self.sums,), (self.qkv,),
            [self.one, vmem(t, 3 * D), vmem(*self.soft.shape), vmem(t, 3 * D), dma(4 + self.rows)],
            20 * t * D * ROW_LEN,
        )

    def qkv_grad(self, pos, vec, sums, gbq, gmid, gqkv, n1, inputs, attn, mine, theirs):
        one, wide = self.one, self.one_f32
        buffer = shape(mine.shape)
        far = [gmid, gqkv, n1, inputs] + attn + [mine, theirs]
        return call(
            qkv_grad_kernel, "qkv_grad", (pos, vec, sums, gbq), far, (), (self.act, buffer, buffer),
            [
                wide, vmem(3, self.tokens, D), one, one, self.three, wide, self.turned, self.three,
                vmem(16, D, kind=F32), vmem(2, CHIPS, 16, HALF), one, dma(12),
            ],
            2 * self.tokens * D * 6 * D,
            {4 + len(far) - 2: 1, 4 + len(far) - 1: 2},
        )

    def layer_out(self, pos, vec, act, mid, down):
        wide = self.one_f32
        (out,) = call(
            layer_out_kernel, "layer_out", (pos, vec), [act, mid] + down, (), (self.act,),
            [vmem(4, self.tokens, D), wide, self.one, vmem(FF, D), wide, dma(10)],
            2 * self.tokens * D * FF,
        )
        return out


class Scatter:
    def __init__(self, mine, theirs, *after):
        self.mine = mine
        self.got = swap(tie(theirs, *after), 0)

    def part(self, first, last):
        return self.mine[first:last], self.got[first:last]

    def first(self, *after):
        got = tie(self.got, *after) if after else self.got
        self.got = got
        self.out_y = rounded_sum(*self.part(8, 12))
        self.out_x = rounded_sum(*self.part(12, 16))
        self.in_y = swap(self.out_y, BIT_Y)
        self.in_x = swap(self.out_x, BIT_X)

    def second(self, *after):
        if after:
            self.in_y, self.in_x = lax.optimization_barrier((self.in_y, self.in_x) + after)[:2]
        self.out_y2 = rounded_sum(*self.part(4, 6), self.in_x[2:])
        self.out_x2 = rounded_sum(*self.part(6, 8), self.in_y[2:])
        self.in_y2 = swap(self.out_y2, BIT_Y)
        self.in_x2 = swap(self.out_x2, BIT_X)

    def third(self, *after):
        if after:
            self.in_y2, self.in_x2 = lax.optimization_barrier((self.in_y2, self.in_x2) + after)[:2]
        self.low = (*self.part(0, 2), self.in_x[:2], self.in_y2)
        self.out_z1 = rounded_sum(*self.part(2, 4), self.in_y[:2], self.in_x2)
        self.in_z1 = swap(self.out_z1, BIT_Z1)

    def fourth(self, *after):
        if after:
            self.in_z1 = tie(self.in_z1, *after)
        self.low = self.low + (self.in_z1,)
        self.out_z0 = rounded_sum(*[t[1] for t in self.low])
        self.in_z0 = swap(self.out_z0, BIT_Z0)

    def result(self, *after):
        total = self.in_z0.astype(F32) if not after else tie(self.in_z0, *after).astype(F32)
        for term in self.low:
            total = total + term[0].astype(F32)
        return total


def per_device(tuned, *args):
    (
        inputs, segment_ids, pre_attn_gain, pre_attn_bias, w_qkv, b_query, b_value, w_out, b_out,
        pre_mlp_gain, pre_mlp_bias, w_up, b_up, w_down, b_down, cotangent,
    ) = args
    tokens = inputs.shape[0]
    n_rows = tokens // ROW_LEN
    wide, narrow = lax.axis_index("wide"), lax.axis_index("narrow")
    weights = (w_qkv, w_out, w_up, w_down)
    values = (
        pre_attn_gain, pre_attn_bias, b_query, b_value, b_out, pre_mlp_gain, pre_mlp_bias, b_up, b_down,
    )
    per, per_up = pre_attn_gain.shape[0], b_up.shape[0]
    position = jnp.arange(ROW_LEN, dtype=jnp.int32)[None]
    own_id = jnp.where(segment_ids != 0, segment_ids, -1 - position)
    segr = own_id.reshape(n_rows, 1, ROW_LEN)
    segc = own_id.reshape(tokens, 1)
    layer = Layer(tokens)

    def four_units(pieces):
        return [p.reshape(p.shape[0], 4, BLK, HALF) for p in pieces]

    if not tuned:
        place = wide * lax.axis_size("narrow") + narrow
        pos = jnp.zeros((2,), jnp.int32)
        attn, up, down = gather_plain(weights, values)
        up = four_units(up)
        vec, n1, qkv, soft, mixed, mid, n2 = layer.attn_forward(pos, segr, segc, inputs, attn)
        gbd, act, slope, gout = layer.mlp_up(pos, segc, vec, n2, cotangent, up)
        pair_down = layer.down_grad(pos, act, gout)
        gbu, gpre, *pair_up = layer.mlp_down(pos, gout, slope, n2, down)
        sums, gmid, gmixed, *pair_attn = layer.mid_backward(
            pos, vec, gbd, gbu, gpre, gout, mid, mixed, up, attn
        )
        gbq, gqkv = layer.attn_backward(pos, gmixed, qkv, soft)
        input_grad, *pair_attn = layer.qkv_grad(
            pos, vec, sums, gbq, gmid, gqkv, n1, inputs, attn, *pair_attn
        )
        layer_out = layer.layer_out(pos, vec, act, mid, down)
        grad_w_down = scatter_plain(pair_down, "down")
        grad_w_up = scatter_plain(pair_up, "up")
        grad_w_qkv, grad_w_out, sums = scatter_plain(pair_attn, "attn")
    else:
        place = wide * 4 + narrow
        core = (narrow & 1).astype(jnp.int32)
        pos = jnp.stack([wide * 2 + (narrow >> 1), core]).astype(jnp.int32)
        block1, block2, block3 = chip_blocks(wide, narrow, weights, values)

        def column(block, near, far):
            return jnp.stack([block, near, far[0], far[1]])

        def z_pair(block, near, *after):
            both = jnp.stack([block, near])
            return swap(tie(both, *after) if after else both, BIT_Z1)

        near1 = swap(block1, BIT_Z0)
        far1 = z_pair(block1, near1)
        near2 = swap(tie(block2, near1), BIT_Z0)
        own1 = column(block1, near1, far1)
        y1, x1 = swap(own1, BIT_Y), swap(own1, BIT_X)
        far2 = z_pair(block2, near2, far1)
        near3 = swap(tie(block3, far1), BIT_Z0)
        d0_1, d1_1 = swap(y1[:2], BIT_X), swap(x1[2:], BIT_Y)
        own2 = tie(column(block2, near2, far2), y1, x1)
        far3 = z_pair(block3, near3, far2)
        y2, x2 = swap(own2, BIT_Y), swap(own2, BIT_X)
        attn = gathered(own1, y1, x1, d0_1, d1_1)
        vec, n1, qkv, soft, mixed, mid, n2 = layer.attn_forward(
            tie(pos, own2, near3), segr, segc, inputs, attn
        )
        y2, x2, far3 = lax.optimization_barrier((y2, x2, far3, vec))[:3]
        d0_2, d1_2 = swap(y2[:2], BIT_X), swap(x2[2:], BIT_Y)
        own3 = column(block3, near3, far3)
        y3, x3 = swap(own3, BIT_Y), swap(own3, BIT_X)
        up = four_units(gathered(own2, y2, x2, d0_2, d1_2))
        gbd, act, slope, gout = layer.mlp_up(tie(pos, own3), segc, vec, n2, cotangent, up)
        y3, x3 = lax.optimization_barrier((y3, x3, gbd))[:2]
        to_x, to_y = y3[:2], x3[2:]
        d0_3, d1_3 = swap(to_x, BIT_X), swap(to_y, BIT_Y)
        pair_down = layer.down_grad(tie(pos, to_x, to_y), act, gout)
        d0_3, d1_3 = lax.optimization_barrier((d0_3, d1_3, pair_down[0]))[:2]
        down = gathered(own3, y3, x3, d0_3, d1_3)
        scatter1 = Scatter(*pair_down, d0_3, d1_3)
        scatter1.first()

        gbu, gpre, *pair_up = layer.mlp_down(
            tie(pos, scatter1.out_y, scatter1.out_x), gout, slope, n2, down
        )
        scatter1.second(gbu)
        scatter2 = Scatter(*pair_up, scatter1.in_y, scatter1.in_x)
        sums, gmid, gmixed, *pair_attn = layer.mid_backward(
            tie(pos, scatter1.out_y2, scatter1.out_x2), vec, gbd, gbu, gpre, gout, mid, mixed, up, attn
        )
        scatter2.first(sums)
        scatter1.third(sums)
        gbq, gqkv = layer.attn_backward(
            tie(pos, scatter2.out_y, scatter2.out_x, scatter1.out_z1), gmixed, qkv, soft
        )
        scatter2.second(gbq)
        scatter1.fourth(gbq)
        input_grad, *pair_attn = layer.qkv_grad(
            tie(pos, scatter2.out_y2, scatter2.out_x2, scatter1.out_z0),
            vec, sums, gbq, gmid, gqkv, n1, inputs, attn, *pair_attn,
        )
        scatter2.third(input_grad)
        scatter3 = Scatter(*pair_attn, scatter2.in_y2, scatter2.in_x2, scatter1.in_z0)
        scatter3.first()
        layer_out = layer.layer_out(tie(pos, scatter3.out_y, scatter3.out_x), vec, act, mid, down)
        scatter3.second(layer_out)
        scatter2.fourth(layer_out)
        scatter3.third()
        scatter3.fourth()

        def exchange(blocks, axis):
            first, second = jnp.split(blocks, 2, axis=axis)
            keep = jnp.where(core == 0, first, second)
            got = swap(jnp.where(core == 0, second, first), 0)
            return jnp.where(core == 0, keep, got), jnp.where(core == 0, got, keep)

        grad_w_down = jnp.concatenate(exchange(scatter1.result(input_grad, layer_out), 0), axis=1)
        lo, hi = exchange(scatter2.result(layer_out).reshape(4, BLK, HALF), 1)
        grad_w_up = jnp.stack([lo, hi]).reshape(2, 2, 2, per, HALF).transpose(3, 0, 2, 1, 4).reshape(per, FF)
        grad_attn = scatter3.result()
        lo, hi = exchange(grad_attn[: 4 * BLK].reshape(4, BLK, HALF), 1)
        wide_rows = jnp.stack([lo, hi]).transpose(2, 1, 0, 3)
        grad_w_qkv = wide_rows[:, :3].reshape(per, 3 * D)
        grad_w_out = wide_rows[:, 3].reshape(per, D)
        own = grad_attn[4 * BLK :]
        got = swap(own, 0)
        sums = jnp.where(
            core == 0, jnp.concatenate([own, got], 1), jnp.concatenate([got, own], 1)
        )
    eight, grad_b_up, grad_b_down = small_grads(sums, place, per, per_up)
    return (
        layer_out, input_grad, eight[0], eight[1], grad_w_qkv, eight[2], eight[4], grad_w_out, eight[5],
        eight[6], eight[7], grad_w_up, grad_b_up, grad_w_down, grad_b_down,
    )


def solution(mesh):
    both = P(AXES, None)
    one = P(AXES)
    tuned = dict(mesh.shape) == {"wide": 8, "narrow": 4}
    in_specs = (both, both, one, one, both, one, one, both, one, one, one, both, one, both, one, both)
    out_specs = (both, both, one, one, both, one, one, both, one, one, one, both, one, both, one)
    return jax.shard_map(
        functools.partial(per_device, tuned),
        mesh=mesh,
        in_specs=in_specs,
        out_specs=out_specs,
        check_vma=False,
    )
```

```python
import functools

import jax
import jax.numpy as jnp
from jax import lax
from jax.experimental import pallas as pl
from jax.experimental.pallas import tpu as pltpu
from jax.sharding import PartitionSpec as P

HEADS = 12
HEAD_DIM = 64
D = 768
FF = 3072
ROW_LEN = 256
HALF = 384
CHIPS = 16
BLK = 48
PAIRS = HEADS // 2
AXES = ("wide", "narrow")

EPS = 1e-06
MASKED = -1e30
F32 = jnp.float32
BF16 = jnp.bfloat16

BIT_Y, BIT_X, BIT_Z0, BIT_Z1 = 1, 2, 4, 8
Z_OFFSETS = (0, 4, 8, 12)

GATHER = tuple((o + z, o + z + BIT_Z0) for o in (0, BIT_Y, BIT_X, BIT_X + BIT_Y) for z in (0, BIT_Z1))
PIECES = 2 * len(GATHER)

SCATTER = (0, 4, 8, 12, 1, 5, 10, 14, 9, 13, 11, 15, 2, 6, 3, 7)


def nt(a, b):
    return lax.dot_general(a, b, (((1,), (1,)), ((), ())), preferred_element_type=F32)


def tn(a, b):
    return lax.dot_general(a, b, (((0,), (0,)), ((), ())), preferred_element_type=F32)


def nn(a, b):
    return lax.dot_general(a, b, (((1,), (0,)), ((), ())), preferred_element_type=F32)


def chunks(tokens, step, body):
    def one(i, carry):
        body(pl.ds(pl.multiple_of(i * step, step), step))
        return carry

    lax.fori_loop(0, tokens // step, one, 0)


def norm_parts(v):
    centre = jnp.mean(v, axis=-1, keepdims=True)
    centred = v - centre
    scale = lax.rsqrt(jnp.mean(centred * centred, axis=-1, keepdims=True) + EPS)
    return centred * scale, scale


def start(src, dst, sem):
    copy = pltpu.make_async_copy(src, dst, sem)
    copy.start()
    return copy


def whole_wait(ref, sem):
    pltpu.make_async_copy(ref, ref, sem).wait()


def each_block(pos_ref, pieces):
    for other in range(2):
        for ref, offsets in zip(pieces[other * len(GATHER) :], GATHER):
            for b, offset in enumerate(offsets):
                yield ref, b, pos_ref[0] ^ offset, other, offset


def chip_rows(chip, size):
    return pl.ds(pl.multiple_of(chip * size, 16), size)


def half_cols(pos_ref, other):
    return pl.ds(pl.multiple_of((pos_ref[1] ^ other) * HALF, 128), HALF)


def fetch_qkv(pos_ref, pieces, w_qkv, sems):
    for t in range(3):
        for ref, b, chip, other, _ in each_block(pos_ref, pieces):
            dst = w_qkv.at[t, chip_rows(chip, BLK), half_cols(pos_ref, other)]
            start(ref.at[b, pl.ds(t * BLK, BLK)], dst, sems.at[t])


def fetch_out(pos_ref, pieces, w_out, sem):
    for ref, b, chip, other, _ in each_block(pos_ref, pieces):
        dst = w_out.at[chip_rows(chip, BLK), half_cols(pos_ref, other)]
        start(ref.at[b, 4], dst, sem)


def fetch_small(pos_ref, pieces, small, sem):
    for ref, b, chip, other, _ in each_block(pos_ref, pieces):
        start(ref.at[b, pl.ds(3 * BLK, 16)], small.at[pos_ref[1] ^ other, chip], sem)


def fetch_up(pos_ref, pieces, w_up, sems):
    for ref, b, chip, other, _ in each_block(pos_ref, pieces):
        for u in range(2):
            dst = w_up.at[other, pl.ds(0, 2), chip_rows(chip, BLK), pl.ds(u * HALF, HALF)]
            start(ref.at[b, pl.ds(2 * u, 2)], dst, sems.at[other])


def fetch_down(pos_ref, pieces, w_down, sems):
    for q in range(4):
        for ref, b, chip, other, offset in each_block(pos_ref, pieces):
            if offset // 4 == q:
                dst = w_down.at[chip_rows(chip, 4 * BLK), half_cols(pos_ref, other)]
                start(ref.at[b], dst, sems.at[q])


def scatter_place(pos_ref, chip):
    offset = pos_ref[0] ^ chip
    xy, z = offset & 3, offset >> 2
    near = jnp.where(xy == 1, 4, jnp.where(xy == 2, 12, 14)) + z
    far = jnp.where(xy == 1, 6, jnp.where(xy == 2, 4, 8)) + z
    return jnp.where(xy == 0, z, jnp.where(z < 2, near, far))


def qkv_forward_kernel(pos_ref, x_any, *refs):
    pieces, refs = refs[:PIECES], refs[PIECES:]
    vec_ref, n1_any, qkv_any, x_ref, n1_ref, qkv_ref, w_qkv, small, sems = refs
    tokens = x_ref.shape[0]
    load_x = start(x_any, x_ref, sems.at[0])
    fetch_small(pos_ref, pieces, small, sems.at[1])
    fetch_qkv(pos_ref, pieces, w_qkv, sems.at[pl.ds(2, 3)])
    whole_wait(small, sems.at[1])
    for h in range(2):
        vec_ref[:, h * HALF : (h + 1) * HALF] = jnp.sum(small[h].astype(F32), axis=0)
    load_x.wait()

    def norm_one(rows):
        xhat, _ = norm_parts(x_ref[rows, :].astype(F32))
        n1_ref[rows, :] = (xhat * vec_ref[0:1, :] + vec_ref[1:2, :]).astype(BF16)

    chunks(tokens, 128, norm_one)
    stores = [start(n1_ref, n1_any, sems.at[5])]
    for t in range(3):
        whole_wait(w_qkv.at[t], sems.at[2 + t])
        y = (nn(n1_ref[...], w_qkv[t]) + vec_ref[2 + t : 3 + t, :]).astype(BF16)
        if t == 0:
            y = y * BF16(HEAD_DIM**-0.5)
        qkv_ref[:, t * D : (t + 1) * D] = y
        cols = pl.ds(t * D, D)
        stores.append(start(qkv_ref.at[:, cols], qkv_any.at[:, cols], sems.at[6 + t]))
    for store in stores:
        store.wait()


def attention_kernel(
    pos_ref, segr_ref, segc_ref, qkv_any, soft_any, mixed_any, qkv_ref, soft_ref, mixed_ref, bias, sems
):
    tokens = qkv_ref.shape[0]
    n_rows = tokens // ROW_LEN
    loads = []
    for r in range(n_rows):
        rows = pl.ds(r * ROW_LEN, ROW_LEN)
        loads.append(start(qkv_any.at[rows], qkv_ref.at[rows], sems.at[2 + r]))
    for r in range(n_rows):
        same = segc_ref[r * ROW_LEN : (r + 1) * ROW_LEN] == segr_ref[r]
        bias[r] = jnp.where(same, 0.0, MASKED)
    lane = lax.broadcasted_iota(jnp.int32, (1, 2 * HEAD_DIM), 1)
    low = (lane < HEAD_DIM).astype(F32).astype(BF16)
    high = (lane >= HEAD_DIM).astype(F32).astype(BF16)
    for r in range(n_rows):
        rows = slice(r * ROW_LEN, (r + 1) * ROW_LEN)
        loads[r].wait()

        def pair(i, carry):
            q = qkv_ref[rows, pl.ds(pl.multiple_of(i * 128, 128), 128)]
            k = qkv_ref[rows, pl.ds(pl.multiple_of(D + i * 128, 128), 128)]
            v = qkv_ref[rows, pl.ds(pl.multiple_of(2 * D + i * 128, 128), 128)]
            mixed = jnp.zeros((ROW_LEN, 128), F32)
            for hh, keep in enumerate((low, high)):
                s = nt(q, k * keep) + bias[r]
                e = jnp.exp(s - jnp.max(s, axis=-1, keepdims=True))
                p = (e * (1.0 / jnp.sum(e, axis=-1, keepdims=True))).astype(BF16)
                soft_ref[r * HEADS + 2 * i + hh] = p
                mixed = mixed + nn(p, v * keep)
            mixed_ref[rows, pl.ds(pl.multiple_of(i * 128, 128), 128)] = mixed.astype(BF16)
            at = pl.ds(r * HEADS + 2 * i, 2)
            start(soft_ref.at[at], soft_any.at[at], sems.at[0])
            return carry

        lax.fori_loop(0, PAIRS, pair, 0)
    store = start(mixed_ref, mixed_any, sems.at[1])
    whole_wait(soft_ref, sems.at[0])
    store.wait()


GELU_A = 0.7978845608028654
GELU_B = 0.044715


def quarter(pos_ref, other, s):
    return (pos_ref[1] ^ other) * 2 + s


def quarter_cols(z):
    return pl.ds(pl.multiple_of(z * D, 128), D)


QUARTERS = ((0, 0), (0, 1), (1, 0), (1, 1))


def mlp_up_kernel(pos_ref, segc_ref, vec_ref, x_any, mixed_any, cot_any, *refs):
    pieces, refs = refs[:PIECES], refs[PIECES:]
    gb_ref, n2_any, mid_any, act_any, slope_any, gout_any, *refs = refs
    x_ref, mixed_ref, cot_ref, n2_ref, mid_ref, act_ref, slope_ref, gout_ref, w_out, w_up, sems = refs
    tokens = n2_ref.shape[0]
    load_x = start(x_any, x_ref, sems.at[2])
    load_mixed = start(mixed_any, mixed_ref, sems.at[13])
    fetch_out(pos_ref, pieces, w_out, sems.at[14])
    fetch_up(pos_ref, pieces, w_up, sems)
    load_cot = start(cot_any, cot_ref, sems.at[3])
    load_x.wait()
    load_mixed.wait()
    whole_wait(w_out, sems.at[14])
    mid_ref[...] = x_ref[...].astype(F32) + nn(mixed_ref[...], w_out[...]) + vec_ref[5:6, :]

    def norm_two(rows):
        xhat, _ = norm_parts(mid_ref[rows, :])
        n2_ref[rows, :] = (xhat * vec_ref[6:7, :] + vec_ref[7:8, :]).astype(BF16)

    chunks(tokens, 128, norm_two)
    stores = [start(mid_ref, mid_any, sems.at[15]), start(n2_ref, n2_any, sems.at[16])]
    for other, s in QUARTERS:
        if s == 0:
            whole_wait(w_up.at[other], sems.at[other])
        z = quarter(pos_ref, other, s)
        b_up = vec_ref[pl.ds(8 + z, 1), :]

        def part(rows):
            u = nn(n2_ref[rows, :], w_up[other, s]) + b_up
            sq = u * u
            t = jnp.tanh(u * (GELU_A + GELU_A * GELU_B * sq))
            half_up = 0.5 + 0.5 * t
            act_ref[other, s, rows, :] = (u * half_up).astype(BF16)
            slope_ref[other, s, rows, :] = (
                half_up + u * (0.5 - 0.5 * t * t) * (GELU_A + 3.0 * GELU_A * GELU_B * sq)
            ).astype(BF16)

        chunks(tokens, 256, part)
        k = 2 * other + s
        stores.append(start(act_ref.at[other, s], act_any.at[:, quarter_cols(z)], sems.at[5 + k]))
        stores.append(start(slope_ref.at[other, s], slope_any.at[:, quarter_cols(z)], sems.at[9 + k]))
    load_cot.wait()
    valid = segc_ref[...] > 0
    gout = jnp.where(valid, cot_ref[...].astype(F32), 0.0)
    gout_ref[...] = gout.astype(BF16)
    gb_ref[...] = jnp.broadcast_to(jnp.sum(gout, axis=0, keepdims=True), gb_ref.shape)
    stores.append(start(gout_ref, gout_any, sems.at[4]))
    for store in stores:
        store.wait()


def down_grad_kernel(pos_ref, act_any, gout_any, mine, theirs, act_ref, gout_ref, grad, sems):
    load_gout = start(gout_any, gout_ref, sems.at[0])
    loads = [
        start(act_any.at[:, pl.ds(z * D, D)], act_ref.at[z], sems.at[2 + z]) for z in range(4)
    ]
    load_gout.wait()
    for z in range(4):
        loads[z].wait()
        grad[z] = tn(act_ref[z], gout_ref[...]).astype(BF16)
        for j in range(4):
            place = scatter_place(pos_ref, 4 * z + j)
            for other, out in enumerate((mine, theirs)):
                src = grad.at[z, pl.ds(j * 4 * BLK, 4 * BLK), half_cols(pos_ref, other)]
                start(src, out.at[place], sems.at[1])
    whole_wait(grad, sems.at[1])


def mlp_down_kernel(pos_ref, gout_any, slope_any, n2_any, *refs):
    pieces, refs = refs[:PIECES], refs[PIECES:]
    gb_ref, gpre_any, mine, theirs, *refs = refs
    gout_ref, slope_ref, n2_ref, gpre_ref, n2t, w_down, grad, sems = refs
    load_n2 = start(n2_any, n2_ref, sems.at[4])
    load_gout = start(gout_any, gout_ref, sems.at[5])
    fetch_down(pos_ref, pieces, w_down, sems)
    loads = {
        (other, s): start(
            slope_any.at[:, quarter_cols(quarter(pos_ref, other, s))],
            slope_ref.at[other, s],
            sems.at[6 + 2 * other + s],
        )
        for other, s in QUARTERS
    }
    gb_ref[...] = jnp.zeros(gb_ref.shape, F32)
    load_n2.wait()
    n2t[...] = n2_ref[...].T
    load_gout.wait()
    stores = []
    for other, s in QUARTERS:
        z = quarter(pos_ref, other, s)
        rows = quarter_cols(z)
        whole_wait(w_down.at[rows], sems.at[z ^ (pos_ref[0] >> 2)])
        loads[other, s].wait()
        ga = nt(gout_ref[...], w_down[rows, :])
        gp = (ga * slope_ref[other, s].astype(F32)).astype(BF16)
        gpre_ref[other, s] = gp
        stores.append(start(gpre_ref.at[other, s], gpre_any.at[:, rows], sems.at[10 + 2 * other + s]))
        gb_ref[pl.ds(z, 1), :] = jnp.sum(gp.astype(F32), axis=0, keepdims=True)
        grad[other, s] = nn(n2t[...], gpre_ref[other, s]).astype(BF16)
        if s == 1:
            for chip in range(CHIPS):
                place = scatter_place(pos_ref, chip)
                for u in range(2):
                    src = grad.at[other, pl.ds(0, 2), pl.ds(chip * BLK, BLK), pl.ds(u * HALF, HALF)]
                    start(src, (mine, theirs)[other].at[place, pl.ds(2 * u, 2)], sems.at[14])
    whole_wait(grad, sems.at[14])
    for store in stores:
        store.wait()


def norm_back(grad, xhat, scale, gain):
    gn = grad * gain
    mean_gn = jnp.mean(gn, axis=-1, keepdims=True)
    mean_gx = jnp.mean(gn * xhat, axis=-1, keepdims=True)
    return scale * (gn - mean_gn - xhat * mean_gx)


def mid_backward_kernel(
    pos_ref, vec_ref, gbd_ref, gbu_ref, gpre_any, gout_any, mid_any, mixed_any, *refs
):
    pieces, refs = refs[:PIECES], refs[PIECES + 2 :]
    sums, gmid_any, gmixed_any, mine, theirs, *refs = refs
    gpre_ref, gout_ref, mid_ref, mixed_ref, w_up, w_out, acc, gmid, gbr, gmixed, mixt, grad, sems = refs
    tokens = mid_ref.shape[0]
    load_mixed = start(mixed_any, mixed_ref, sems.at[8])
    fetch_up(pos_ref, pieces, w_up, sems)
    loads = {
        (other, s): start(
            gpre_any.at[:, quarter_cols(quarter(pos_ref, other, s))],
            gpre_ref.at[other, s],
            sems.at[4 + 2 * other + s],
        )
        for other, s in QUARTERS
    }
    load_mid = start(mid_any, mid_ref, sems.at[9])
    load_gout = start(gout_any, gout_ref, sems.at[10])
    fetch_out(pos_ref, pieces, w_out, sems.at[11])
    sums[...] = jnp.zeros(sums.shape, F32)
    sums[8:12, :] = gbu_ref[0:4, :]
    sums[12:13, :] = gbd_ref[0:1, :]
    load_mixed.wait()
    mixt[...] = mixed_ref[...].T
    for other, s in QUARTERS:
        if s == 0:
            whole_wait(w_up.at[other], sems.at[other])
        loads[other, s].wait()
        part = nt(gpre_ref[other, s], w_up[other, s])
        acc[...] = part if other + s == 0 else acc[...] + part
    load_mid.wait()
    load_gout.wait()

    def back_two(rows):
        xhat, scale = norm_parts(mid_ref[rows, :])
        g = acc[rows, :]
        sums[6:7, :] += jnp.sum(g * xhat, axis=0, keepdims=True)
        sums[7:8, :] += jnp.sum(g, axis=0, keepdims=True)
        gm = gout_ref[rows, :].astype(F32) + norm_back(g, xhat, scale, vec_ref[6:7, :])
        gmid[rows, :] = gm
        low = gm.astype(BF16)
        gbr[rows, :] = low
        sums[5:6, :] += jnp.sum(low.astype(F32), axis=0, keepdims=True)

    chunks(tokens, 128, back_two)
    stores = [start(gmid, gmid_any, sems.at[12])]
    whole_wait(w_out, sems.at[11])
    gmixed[...] = nt(gbr[...], w_out[...]).astype(BF16)
    stores.append(start(gmixed, gmixed_any, sems.at[13]))
    grad[...] = nn(mixt[...], gbr[...]).astype(BF16)
    for chip in range(CHIPS):
        place = scatter_place(pos_ref, chip)
        for other, out in enumerate((mine, theirs)):
            src = grad.at[pl.ds(chip * BLK, BLK), half_cols(pos_ref, other)]
            start(src, out.at[place, 4], sems.at[14])
    whole_wait(grad, sems.at[14])
    for store in stores:
        store.wait()


def attn_backward_kernel(
    pos_ref, gmixed_any, qkv_any, soft_any, gb_ref, gqkv_any, gmixed, qkv_ref, soft_ref, gqkv, sems
):
    tokens = gmixed.shape[0]
    load_gmixed = start(gmixed_any, gmixed, sems.at[0])
    load_qkv = start(qkv_any, qkv_ref, sems.at[1])
    n_rows = tokens // ROW_LEN
    per_row = [
        start(
            soft_any.at[pl.ds(r * HEADS, HEADS)], soft_ref.at[pl.ds(r * HEADS, HEADS)], sems.at[4 + r]
        )
        for r in range(n_rows)
    ]
    load_gmixed.wait()
    load_qkv.wait()
    lane = lax.broadcasted_iota(jnp.int32, (1, 2 * HEAD_DIM), 1)
    first = (lane < HEAD_DIM).astype(F32).astype(BF16)
    second = (lane >= HEAD_DIM).astype(F32).astype(BF16)
    for r in range(n_rows):
        rows = slice(r * ROW_LEN, (r + 1) * ROW_LEN)
        per_row[r].wait()

        def pair(i, carry):
            at_q = pl.ds(pl.multiple_of(i * 128, 128), 128)
            at_k = pl.ds(pl.multiple_of(D + i * 128, 128), 128)
            at_v = pl.ds(pl.multiple_of(2 * D + i * 128, 128), 128)
            q, k, v = qkv_ref[rows, at_q], qkv_ref[rows, at_k], qkv_ref[rows, at_v]
            gm = gmixed[rows, at_q]
            dq = jnp.zeros((ROW_LEN, 128), F32)
            dk = jnp.zeros((ROW_LEN, 128), F32)
            dv = jnp.zeros((ROW_LEN, 128), F32)
            for hh, keep in enumerate((first, second)):
                p_low = soft_ref[r * HEADS + 2 * i + hh]
                p = p_low.astype(F32)
                gmk = gm * keep
                gs = nt(gmk, v)
                inner = jnp.sum(p * gs, axis=-1, keepdims=True)
                ds = (p * (gs - inner)).astype(BF16)
                dq = dq + nn(ds, k * keep)
                dk = dk + tn(ds, q * keep)
                dv = dv + tn(p_low, gmk)
            gqkv[rows, at_q] = (dq * (HEAD_DIM**-0.5)).astype(BF16)
            gqkv[rows, at_k] = dk.astype(BF16)
            gqkv[rows, at_v] = dv.astype(BF16)
            return carry

        lax.fori_loop(0, PAIRS, pair, 0)
    store = start(gqkv, gqkv_any, sems.at[2])
    gb_ref[...] = jnp.zeros(gb_ref.shape, F32)
    gb_ref[0:1, :] = jnp.sum(gqkv[:, :D].astype(F32), axis=0, keepdims=True)
    gb_ref[2:3, :] = jnp.sum(gqkv[:, 2 * D :].astype(F32), axis=0, keepdims=True)
    store.wait()


def qkv_grad_kernel(
    pos_ref, vec_ref, sums_ref, gbq_ref, gmid_any, gqkv_any, n1_any, x_any, *refs
):
    pieces, refs = refs[:PIECES], refs[PIECES:]
    igrad_any, mine, theirs, *refs = refs
    gmid, gqkv, n1_ref, x_ref, w_qkv, acc, n1t, grad, sums, small, igrad, sems = refs
    tokens = x_ref.shape[0]
    load_n1 = start(n1_any, n1_ref, sems.at[0])
    loads = [
        start(gqkv_any.at[:, pl.ds(t * D, D)], gqkv.at[t], sems.at[1 + t]) for t in range(3)
    ]
    fetch_qkv(pos_ref, pieces, w_qkv, sems.at[pl.ds(4, 3)])
    load_x = start(x_any, x_ref, sems.at[7])
    load_gmid = start(gmid_any, gmid, sems.at[8])
    sums[...] = sums_ref[...]
    sums[2:3, :] = gbq_ref[0:1, :]
    sums[4:5, :] = gbq_ref[2:3, :]
    load_n1.wait()
    n1t[...] = n1_ref[...].T
    for t in range(3):
        loads[t].wait()
        grad[t] = nn(n1t[...], gqkv[t]).astype(BF16)
        for chip in range(CHIPS):
            place = scatter_place(pos_ref, chip)
            for other, out in enumerate((mine, theirs)):
                src = grad.at[t, pl.ds(chip * BLK, BLK), half_cols(pos_ref, other)]
                start(src, out.at[place, pl.ds(t * BLK, BLK)], sems.at[9])
    for t in range(3):
        whole_wait(w_qkv.at[t], sems.at[4 + t])
        part = nt(gqkv[t], w_qkv[t])
        acc[...] = part if t == 0 else acc[...] + part
    load_x.wait()
    load_gmid.wait()

    def back_one(rows):
        xhat, scale = norm_parts(x_ref[rows, :].astype(F32))
        g = acc[rows, :]
        sums[0:1, :] += jnp.sum(g * xhat, axis=0, keepdims=True)
        sums[1:2, :] += jnp.sum(g, axis=0, keepdims=True)
        igrad[rows, :] = (gmid[rows, :] + norm_back(g, xhat, scale, vec_ref[0:1, :])).astype(BF16)

    chunks(tokens, 128, back_one)
    store = start(igrad, igrad_any, sems.at[10])
    for p in range(CHIPS):
        small[0, p] = sums[:, :HALF].astype(BF16)
        small[1, p] = sums[:, HALF:].astype(BF16)
    for other, out in enumerate((mine, theirs)):
        for p in range(CHIPS):
            start(small.at[pos_ref[1] ^ other, p], out.at[p, pl.ds(3 * BLK, 16)], sems.at[11])
    whole_wait(small, sems.at[11])
    whole_wait(grad, sems.at[9])
    store.wait()


def layer_out_kernel(pos_ref, vec_ref, act_any, mid_any, *refs):
    pieces, refs = refs[:PIECES], refs[PIECES:]
    out_any, act_ref, mid_ref, out_ref, w_down, acc, sems = refs
    own_z = pos_ref[0] >> 2
    load_mid = start(mid_any, mid_ref, sems.at[8])
    loads = [
        start(act_any.at[:, quarter_cols(own_z ^ q)], act_ref.at[q], sems.at[4 + q]) for q in range(4)
    ]
    fetch_down(pos_ref, pieces, w_down, sems)
    for q in range(4):
        rows = quarter_cols(own_z ^ q)
        loads[q].wait()
        whole_wait(w_down.at[rows], sems.at[q])
        part = nn(act_ref[q], w_down[rows, :])
        if q == 0:
            load_mid.wait()
            acc[...] = part + (mid_ref[...] + vec_ref[12:13, :])
        elif q < 3:
            acc[...] = acc[...] + part
        else:
            out_ref[...] = (acc[...] + part).astype(BF16)
    start(out_ref, out_any, sems.at[9]).wait()


PER = D // (2 * CHIPS)
SEND_ROWS = (3 * PER, 16, 5 * PER, 4 * PER)


def pack_kernel(pos_ref, w_qkv, w_out, w_up, w_down, bu_ref, *refs):
    values, (mine, theirs, rows, last, wide) = refs[:8], refs[8:]
    place = pos_ref[0] * 2 + pos_ref[1]
    rows[...] = jnp.zeros(rows.shape, F32)
    last[...] = jnp.zeros(last.shape, F32)
    for r, value in zip((0, 1, 2, 4, 5, 6, 7, 12), values):
        rows[r : r + 1, 0:PER] = value[...].astype(F32)
    last[0:1, 0 : 4 * PER] = bu_ref[...].astype(F32)
    at = place * (4 * PER)
    up = pltpu.roll(last[...], at % D, 1)[0:1]
    here = lax.broadcasted_iota(jnp.int32, (16, 1), 0) == 8 + at // D
    rows[...] = pltpu.roll(rows[...], place * PER, 1) + jnp.where(here, up, 0.0)
    for out, other in ((mine, 0), (theirs, 1)):
        half = pos_ref[1] ^ other

        def cols(first):
            return pl.ds(pl.multiple_of(first + half * HALF, 128), HALF)

        at = 0
        for t in range(3):
            wide[at : at + PER, :] = w_qkv[:, cols(t * D)].astype(F32)
            at += PER
        wide[at : at + 16, :] = rows[:, cols(0)]
        at += 16
        for n in range(4):
            u, s = n // 2, n % 2
            first = pl.multiple_of(half * (2 * D) + s * D + u * HALF, 128)
            wide[at : at + PER, :] = w_up[:, pl.ds(first, HALF)].astype(F32)
            at += PER
        wide[at : at + PER, :] = w_out[:, cols(0)].astype(F32)
        at += PER
        wide[at : at + 4 * PER, :] = w_down[:, cols(0)].astype(F32)
        out[...] = wide[...].astype(BF16)


def combine_kernel(pos_ref, mine, got, one, two, three, upper, lower, wide):
    first = pos_ref[1] == 0
    m, g = mine[...].astype(F32), got[...].astype(F32)
    upper[...] = jnp.where(first, m, g)
    lower[...] = jnp.where(first, g, m)

    def pair(at, size):
        wide[0:size, :] = upper[at : at + size, :]
        wide[size : 2 * size, :] = lower[at : at + size, :]
        return wide[0 : 2 * size, :].astype(BF16)

    for t in range(3):
        one[t * BLK : (t + 1) * BLK, :] = pair(t * PER, PER)
    at = 3 * PER
    one[3 * BLK :, :] = (upper[at : at + 16, :] + lower[at : at + 16, :]).astype(BF16)
    at += 16
    for n in range(5):
        two[n] = pair(at + n * PER, PER)
    three[...] = pair(at + 5 * PER, 4 * PER)


def finish_kernel(pos_ref, last, mine, got, in_y, in_x, in_z, keep, send):
    total = last[...].astype(F32)
    for ref in (mine, got, in_y, in_x, in_z):
        total = total + ref[0].astype(F32)
    first = pos_ref[1] == 0
    for t in range(3):
        upper, lower = total[t * BLK : t * BLK + PER], total[t * BLK + PER : (t + 1) * BLK]
        keep[t * PER : (t + 1) * PER, :] = jnp.where(first, upper, lower)
        send[t * PER : (t + 1) * PER, :] = jnp.where(first, lower, upper)
    keep[3 * PER :, :] = total[3 * BLK :]
    send[3 * PER :, :] = total[3 * BLK :]


def spread_kernel(pos_ref, keep, got, w_ref, eight_ref, up_ref, down_ref, rows):
    place = pos_ref[0] * 2 + pos_ref[1]
    for ref, other in ((keep, 0), (got, 1)):
        half = pos_ref[1] ^ other
        for t in range(3):
            cols = pl.ds(pl.multiple_of(t * D + half * HALF, 128), HALF)
            w_ref[:, cols] = ref[t * PER : (t + 1) * PER, :]
        rows[:, pl.ds(pl.multiple_of(half * HALF, 128), HALF)] = ref[3 * PER :, :]
    mine = pltpu.roll(rows[...], lax.rem(D - place * PER, D), 1)
    eight_ref[...] = mine[0:8, 0:PER]
    down_ref[...] = mine[12:13, 0:PER]
    at = place * (4 * PER)
    here = lax.broadcasted_iota(jnp.int32, (16, 1), 0) == 8 + at // D
    row = jnp.sum(jnp.where(here, rows[...], 0.0), axis=0, keepdims=True)
    turned = pltpu.roll(jnp.broadcast_to(row, (8, D)), lax.rem(D - at % D, D), 1)
    up_ref[...] = turned[0:1, 0 : 4 * PER]


def call(kernel, name, near, far, near_outs, far_outs, scratch, flops, aliases=None):
    vmem = pl.BlockSpec(memory_space=pltpu.VMEM)
    anyspec = pl.BlockSpec(memory_space=pl.ANY)
    outs = tuple(near_outs) + tuple(far_outs)
    moved = sum(a.size * a.dtype.itemsize for a in tuple(near) + tuple(far) + outs)
    return pl.pallas_call(
        kernel,
        out_shape=outs,
        in_specs=[pl.BlockSpec(memory_space=pltpu.SMEM)]
        + [vmem] * (len(near) - 1)
        + [anyspec] * len(far),
        out_specs=[vmem] * len(near_outs) + [anyspec] * len(far_outs),
        scratch_shapes=scratch,
        input_output_aliases=aliases or {},
        compiler_params=pltpu.CompilerParams(vmem_limit_bytes=56 << 20),
        cost_estimate=pl.CostEstimate(flops=flops, bytes_accessed=moved, transcendentals=0),
        name=name,
    )(*near, *far)


def swap(value, chip_bit):
    flip = chip_bit * 2 if chip_bit else 1
    return lax.ppermute(value, AXES, [(i, i ^ flip) for i in range(2 * CHIPS)])


def tie(value, *after):
    return lax.optimization_barrier((value,) + after)[0]


def gathered(*own_half):
    return list(own_half) + [swap(piece, 0) for piece in own_half]


def hold(pieces, after):
    return lax.optimization_barrier((*pieces, after))[: len(pieces)]


def rounded_sum(*terms):
    total = terms[0].astype(F32)
    for term in terms[1:]:
        total = total + term.astype(F32)
    return total.astype(BF16)


def small_grads(sums, place, per, per_up):
    eight = lax.dynamic_slice(sums, (0, place * per), (8, per))
    at = place * per_up
    up = lax.dynamic_slice(sums, (8 + at // D, at % D), (1, per_up))[0]
    down = lax.dynamic_slice(sums, (12, place * per), (1, per))[0]
    return eight, up, down


def halves(w_qkv, w_out, w_up, w_down):
    rows = w_qkv.shape[0]
    qkv = w_qkv.reshape(rows, 3, 2, HALF)
    up = w_up.reshape(rows, 2, 4, HALF)
    for h in range(2):
        cols = slice(h * HALF, (h + 1) * HALF)
        up_h = up[:, h].reshape(rows, 2, 2, HALF).transpose(2, 1, 0, 3).reshape(4, rows, HALF)
        yield (
            qkv[:, :, h].transpose(1, 0, 2),
            jnp.concatenate([up_h, w_out[None, :, cols]]),
            w_down[:, cols],
        )


def gather_plain(weights, values):
    def whole(w):
        return lax.all_gather(w, AXES, axis=0, tiled=True)

    gain1, bias1, bq, bv, bo, gain2, bias2, bu, bd = [whole(v) for v in values]
    rest = jnp.zeros((3, D), BF16)
    small = jnp.stack([gain1, bias1, bq, jnp.zeros_like(bq), bv, bo, gain2, bias2])
    small = jnp.concatenate([small, bu.reshape(4, D), bd[None], rest])
    groups = ([], [], [])
    for h, (attn, up, down) in enumerate(halves(*[whole(w) for w in weights])):
        attn = attn.reshape(3, CHIPS, BLK, HALF).transpose(1, 0, 2, 3).reshape(CHIPS, 3 * BLK, HALF)
        up = up.reshape(5, CHIPS, BLK, HALF).transpose(1, 0, 2, 3)
        down = down.reshape(CHIPS, 4 * BLK, HALF)
        extra = jnp.zeros((CHIPS, 16, HALF), BF16).at[0].set(small[:, h * HALF : (h + 1) * HALF])
        for group, blocks in zip(groups, (jnp.concatenate([attn, extra], axis=1), up, down)):
            group.extend(jnp.stack([blocks[o] for o in piece]) for piece in GATHER)
    return groups


def scatter_plain(pair, group):
    both = [jnp.stack([part[SCATTER.index(chip)] for chip in range(CHIPS)]) for part in pair]

    def scatter(v):
        return lax.psum_scatter(v.astype(F32), AXES, scatter_dimension=0, tiled=True)

    def matrix(units):
        return jnp.stack(units, axis=3).transpose(0, 2, 1, 3, 4).reshape(D, -1, 2, HALF)

    if group == "attn":
        sums = jnp.concatenate([b[0, 3 * BLK :] for b in both], axis=1)
        qkv = matrix([b[:, : 3 * BLK].reshape(CHIPS, 3, BLK, HALF) for b in both])
        return scatter(qkv.reshape(D, 3 * D)), lax.psum(sums.astype(F32), AXES)
    if group == "up":
        up = matrix(both)
        order = up[:, :4].reshape(D, 2, 2, 2, HALF).transpose(0, 3, 2, 1, 4)
        return scatter(order.reshape(D, FF)), scatter(up[:, 4].reshape(D, D))
    return scatter(jnp.concatenate([b.reshape(FF, HALF) for b in both], axis=1))


def shape(dims, kind=BF16):
    return jax.ShapeDtypeStruct(dims, kind)


def dma(n):
    return pltpu.SemaphoreType.DMA((n,))


def vmem(*dims, kind=BF16):
    return pltpu.VMEM(dims, kind)


class Layer:
    def __init__(self, tokens):
        self.tokens = tokens
        self.rows = tokens // ROW_LEN
        self.wide = shape((tokens, FF))
        self.act = shape((tokens, D))
        self.mid = shape((tokens, D), F32)
        self.qkv = shape((tokens, 3 * D))
        self.soft = shape((self.rows * HEADS, ROW_LEN, ROW_LEN))
        self.quarters = vmem(2, 2, tokens, D)
        self.one = vmem(tokens, D)
        self.one_f32 = vmem(tokens, D, kind=F32)
        self.turned = vmem(D, tokens)
        self.square = vmem(D, D)
        self.three = vmem(3, D, D)
        self.four = vmem(2, 2, D, D)
        self.sums = shape((8, D), F32)
        self.vec = shape((16, D), F32)

    def chip_blocks(self, pos, weights, values):
        *rest, bu, bd = [v.reshape(1, -1) for v in values]
        sent = shape((sum(SEND_ROWS), HALF))
        wide = vmem(sum(SEND_ROWS), HALF, kind=F32)
        mine, theirs = call(
            pack_kernel, "pack", (pos, *weights, bu, *rest, bd), (), (sent, sent), (),
            [vmem(16, D, kind=F32), vmem(8, D, kind=F32), wide], 0,
        )
        return call(
            combine_kernel, "combine", (pos, mine, swap(theirs, 0)), (),
            (shape((3 * BLK + 16, HALF)), shape((5, BLK, HALF)), shape((4 * BLK, HALF))), (),
            [wide, wide, vmem(4 * BLK, HALF, kind=F32)], 0,
        )

    def finish(self, pos, last, low):
        sent = shape((3 * PER + 16, HALF), F32)
        keep, send = call(finish_kernel, "finish", (pos, last, *low), (), (sent, sent), (), [], 0)
        return call(
            spread_kernel, "spread", (pos, keep, swap(send, 0)), (),
            (shape((PER, 3 * D), F32), shape((8, PER), F32), shape((1, 4 * PER), F32), shape((1, PER), F32)),
            (), [vmem(16, D, kind=F32)], 0,
        )

    def qkv_forward(self, pos, inputs, attn):
        t = self.tokens
        return call(
            qkv_forward_kernel, "qkv_forward", (pos,), [inputs] + attn, (self.vec,), (self.act, self.qkv),
            [self.one, self.one, vmem(t, 3 * D), self.three, vmem(2, CHIPS, 16, HALF), dma(9)],
            2 * t * D * D * 3,
        )

    def attention(self, pos, segr, segc, qkv):
        t = self.tokens
        return call(
            attention_kernel, "attention", (pos, segr, segc), [qkv], (), (self.soft, self.act),
            [
                vmem(t, 3 * D), vmem(*self.soft.shape), self.one,
                vmem(self.rows, ROW_LEN, ROW_LEN, kind=F32), dma(2 + self.rows),
            ],
            8 * t * D * ROW_LEN,
        )

    def mlp_up(self, pos, segc, vec, inputs, mixed, cotangent, up):
        one, quarters = self.one, self.quarters
        return call(
            mlp_up_kernel, "mlp_up", (pos, segc, vec), [inputs, mixed, cotangent] + up,
            (self.sums,), (self.act, self.mid, self.wide, self.wide, self.act),
            [one, one, one, one, self.one_f32, quarters, quarters, one, self.square, self.four, dma(17)],
            2 * self.tokens * D * (FF + D),
        )

    def down_grad(self, pos, act, gout):
        buffer = shape((CHIPS, 4 * BLK, HALF))
        return call(
            down_grad_kernel, "down_grad", (pos,), [act, gout], (), (buffer, buffer),
            [vmem(4, self.tokens, D), self.one, vmem(4, D, D), dma(6)],
            2 * self.tokens * D * FF,
        )

    def mlp_down(self, pos, gout, slope, n2, down):
        one, quarters = self.one, self.quarters
        buffer = shape((CHIPS, 5, BLK, HALF))
        return call(
            mlp_down_kernel, "mlp_down", (pos,), [gout, slope, n2] + down,
            (self.sums,), (self.wide, buffer, buffer),
            [one, quarters, one, quarters, self.turned, vmem(FF, D), self.four, dma(15)],
            4 * self.tokens * D * FF,
        )

    def mid_backward(self, pos, vec, gbd, gbu, gpre, gout, mid, mixed, up, mine, theirs):
        one, wide = self.one, self.one_f32
        buffer = shape(mine.shape)
        far = [gpre, gout, mid, mixed] + up + [mine, theirs]
        return call(
            mid_backward_kernel, "mid_backward", (pos, vec, gbd, gbu), far,
            (self.vec,), (self.mid, self.act, buffer, buffer),
            [
                self.quarters, one, wide, one, self.four, self.square, wide, wide, one, one, self.turned,
                self.square, dma(15),
            ],
            2 * self.tokens * D * (FF + 2 * D),
            {4 + len(far) - 2: 3, 4 + len(far) - 1: 4},
        )

    def attn_backward(self, pos, gmixed, qkv, soft):
        t = self.tokens
        return call(
            attn_backward_kernel, "attn_backward", (pos,), [gmixed, qkv, soft], (self.sums,), (self.qkv,),
            [self.one, vmem(t, 3 * D), vmem(*self.soft.shape), vmem(t, 3 * D), dma(4 + self.rows)],
            20 * t * D * ROW_LEN,
        )

    def qkv_grad(self, pos, vec, sums, gbq, gmid, gqkv, n1, inputs, attn):
        one, wide = self.one, self.one_f32
        buffer = shape((CHIPS, 3 * BLK + 16, HALF))
        return call(
            qkv_grad_kernel, "qkv_grad", (pos, vec, sums, gbq), [gmid, gqkv, n1, inputs] + attn,
            (), (self.act, buffer, buffer),
            [
                wide, vmem(3, self.tokens, D), one, one, self.three, wide, self.turned, self.three,
                vmem(16, D, kind=F32), vmem(2, CHIPS, 16, HALF), one, dma(12),
            ],
            2 * self.tokens * D * 6 * D,
        )

    def layer_out(self, pos, vec, act, mid, down):
        wide = self.one_f32
        (out,) = call(
            layer_out_kernel, "layer_out", (pos, vec), [act, mid] + down, (), (self.act,),
            [vmem(4, self.tokens, D), wide, self.one, vmem(FF, D), wide, dma(10)],
            2 * self.tokens * D * FF,
        )
        return out


class Scatter:
    def __init__(self, mine, theirs, *after):
        self.mine = mine
        self.got = swap(tie(theirs, *after), 0)

    def part(self, first, last):
        return self.mine[first:last], self.got[first:last]

    def first(self, *after):
        got = tie(self.got, *after) if after else self.got
        self.got = got
        self.out_y = rounded_sum(*self.part(8, 12))
        self.out_x = rounded_sum(*self.part(12, 16))
        self.in_y = swap(self.out_y, BIT_Y)
        self.in_x = swap(self.out_x, BIT_X)

    def second(self, *after):
        if after:
            self.in_y, self.in_x = lax.optimization_barrier((self.in_y, self.in_x) + after)[:2]
        self.out_y2 = rounded_sum(*self.part(4, 6), self.in_x[2:])
        self.out_x2 = rounded_sum(*self.part(6, 8), self.in_y[2:])
        self.in_y2 = swap(self.out_y2, BIT_Y)
        self.in_x2 = swap(self.out_x2, BIT_X)

    def third(self, *after):
        if after:
            self.in_y2, self.in_x2 = lax.optimization_barrier((self.in_y2, self.in_x2) + after)[:2]
        self.low = (*self.part(0, 2), self.in_x[:2], self.in_y2)
        self.out_z1 = rounded_sum(*self.part(2, 4), self.in_y[:2], self.in_x2)
        self.in_z1 = swap(self.out_z1, BIT_Z1)

    def diagonal(self):
        self.out_y, self.out_x = rounded_sum(*self.part(10, 12)), rounded_sum(*self.part(14, 16))
        self.in_y, self.in_x = swap(self.out_y, BIT_Y), swap(self.out_x, BIT_X)

    def hi(self):
        in_x = swap(rounded_sum(*self.part(6, 8), self.in_y), BIT_X)
        in_y = swap(rounded_sum(*self.part(8, 10)), BIT_Y)
        self.out_z1 = rounded_sum(*self.part(2, 4), in_x, in_y)
        self.in_z1 = swap(self.out_z1, BIT_Z1)

    def lo(self):
        self.out_y2 = tie(rounded_sum(*self.part(4, 6), self.in_x), self.out_z1)
        self.out_x2 = tie(rounded_sum(*self.part(12, 14)), self.out_z1)
        self.in_y2, self.in_x2 = swap(self.out_y2, BIT_Y), swap(self.out_x2, BIT_X)

    def last(self, after):
        self.in_y2, self.in_x2 = lax.optimization_barrier((self.in_y2, self.in_x2, after))[:2]
        self.low = (*self.part(0, 2), self.in_y2, self.in_x2)
        self.fourth(after)

    def fourth(self, *after):
        if after:
            self.in_z1 = tie(self.in_z1, *after)
        self.low = self.low + (self.in_z1,)
        self.out_z0 = rounded_sum(*[t[1] for t in self.low])
        self.in_z0 = swap(self.out_z0, BIT_Z0)

    def result(self, *after):
        total = self.in_z0.astype(F32) if not after else tie(self.in_z0, *after).astype(F32)
        for term in self.low:
            total = total + term[0].astype(F32)
        return total


def per_device(tuned, *args):
    (
        inputs, segment_ids, pre_attn_gain, pre_attn_bias, w_qkv, b_query, b_value, w_out, b_out,
        pre_mlp_gain, pre_mlp_bias, w_up, b_up, w_down, b_down, cotangent,
    ) = args
    tokens = inputs.shape[0]
    n_rows = tokens // ROW_LEN
    wide, narrow = lax.axis_index("wide"), lax.axis_index("narrow")
    weights = (w_qkv, w_out, w_up, w_down)
    values = (
        pre_attn_gain, pre_attn_bias, b_query, b_value, b_out, pre_mlp_gain, pre_mlp_bias, b_up, b_down,
    )
    per, per_up = pre_attn_gain.shape[0], b_up.shape[0]
    position = jnp.arange(ROW_LEN, dtype=jnp.int32)[None]
    own_id = jnp.where(segment_ids != 0, segment_ids, -1 - position)
    segr = own_id.reshape(n_rows, 1, ROW_LEN)
    segc = own_id.reshape(tokens, 1)
    layer = Layer(tokens)

    if not tuned:
        place = wide * lax.axis_size("narrow") + narrow
        pos = jnp.zeros((2,), jnp.int32)
        attn, up, down = gather_plain(weights, values)
        vec, n1, qkv = layer.qkv_forward(pos, inputs, attn)
        soft, mixed = layer.attention(pos, segr, segc, qkv)
        gbd, n2, mid, act, slope, gout = layer.mlp_up(pos, segc, vec, inputs, mixed, cotangent, up)
        pair_down = layer.down_grad(pos, act, gout)
        gbu, gpre, *pair_up = layer.mlp_down(pos, gout, slope, n2, down)
        sums, gmid, gmixed, *pair_up = layer.mid_backward(
            pos, vec, gbd, gbu, gpre, gout, mid, mixed, up, *pair_up
        )
        gbq, gqkv = layer.attn_backward(pos, gmixed, qkv, soft)
        input_grad, *pair_attn = layer.qkv_grad(pos, vec, sums, gbq, gmid, gqkv, n1, inputs, attn)
        layer_out = layer.layer_out(pos, vec, act, mid, down)
        grad_w_down = scatter_plain(pair_down, "down")
        grad_w_up, grad_w_out = scatter_plain(pair_up, "up")
        grad_w_qkv, sums = scatter_plain(pair_attn, "attn")
        eight, grad_b_up, grad_b_down = small_grads(sums, place, per, per_up)
    else:
        core = (narrow & 1).astype(jnp.int32)
        pos = jnp.stack([wide * 2 + (narrow >> 1), core]).astype(jnp.int32)
        block1, block2, block3 = layer.chip_blocks(pos, weights, values)

        near1 = swap(block1, BIT_Z0)
        lo1 = jnp.stack([block1, near1])
        hi1 = swap(lo1, BIT_Z1)
        y_lo1, x_lo1 = swap(lo1, BIT_Y), swap(lo1, BIT_X)
        near2 = swap(tie(block2, near1), BIT_Z0)
        d_lo1 = swap(y_lo1, BIT_X)
        y_hi1, x_hi1 = swap(hi1, BIT_Y), swap(hi1, BIT_X)
        lo2 = jnp.stack([block2, near2])
        hi2 = swap(tie(lo2, hi1), BIT_Z1)
        d_hi1 = swap(x_hi1, BIT_Y)
        near3 = swap(tie(block3, y_hi1, x_hi1), BIT_Z0)
        lo2b = tie(lo2, y_hi1, x_hi1)
        y_lo2, x_lo2 = swap(lo2b, BIT_Y), swap(lo2b, BIT_X)
        attn = gathered(lo1, hi1, y_lo1, y_hi1, x_lo1, x_hi1, d_lo1, d_hi1)
        vec, n1, qkv = layer.qkv_forward(tie(pos, lo2b), inputs, attn)

        y_lo2, x_lo2, hi2, near3 = lax.optimization_barrier((y_lo2, x_lo2, hi2, near3, vec))[:4]
        lo3 = jnp.stack([block3, near3])
        d_lo2 = swap(y_lo2, BIT_X)
        y_hi2, x_hi2 = swap(hi2, BIT_Y), swap(hi2, BIT_X)
        hi3 = swap(tie(lo3, hi2), BIT_Z1)
        soft, mixed = layer.attention(tie(pos, y_lo2, x_lo2, hi2, lo3), segr, segc, qkv)

        y_hi2, x_hi2, d_lo2, hi3 = lax.optimization_barrier((y_hi2, x_hi2, d_lo2, hi3, mixed))[:4]
        d_hi2 = swap(x_hi2, BIT_Y)
        lo3b = tie(lo3, mixed)
        y_lo3, x_lo3 = swap(lo3b, BIT_Y), swap(lo3b, BIT_X)
        lo2, hi2, y_lo2, x_lo2 = hold((lo2, hi2, y_lo2, x_lo2), mixed)
        up = gathered(lo2, hi2, y_lo2, y_hi2, x_lo2, x_hi2, d_lo2, d_hi2)
        hi3b = tie(hi3, d_hi2)
        y_hi3, x_hi3 = swap(hi3b, BIT_Y), swap(hi3b, BIT_X)
        gbd, n2, mid, act, slope, gout = layer.mlp_up(
            tie(pos, hi3b, lo3b), segc, vec, inputs, mixed, cotangent, up
        )
        y_lo3, x_lo3, y_hi3, x_hi3 = lax.optimization_barrier((y_lo3, x_lo3, y_hi3, x_hi3, gbd))[:4]
        d_lo3, d_hi3 = swap(y_lo3, BIT_X), swap(x_hi3, BIT_Y)
        pair_down = layer.down_grad(tie(pos, y_lo3, x_hi3), act, gout)
        d_lo3, d_hi3 = lax.optimization_barrier((d_lo3, d_hi3, pair_down[0]))[:2]
        down = gathered(lo3, hi3, y_lo3, y_hi3, x_lo3, x_hi3, d_lo3, d_hi3)
        scatter1 = Scatter(*pair_down, d_lo3, d_hi3)
        scatter1.first()

        gbu, gpre, *pair_up = layer.mlp_down(
            tie(pos, scatter1.out_y, scatter1.out_x), gout, slope, n2, down
        )
        scatter1.second(gbu)
        sums, gmid, gmixed, *pair_up = layer.mid_backward(
            tie(pos, scatter1.out_y2, scatter1.out_x2),
            vec, gbd, gbu, gpre, gout, mid, mixed, up, *pair_up,
        )
        scatter1.third(sums)
        scatter2 = Scatter(*pair_up, scatter1.in_y2, scatter1.in_x2)
        gbq, gqkv = layer.attn_backward(tie(pos, scatter1.out_z1, pair_up[0]), gmixed, qkv, soft)
        scatter2.first(gbq)
        scatter1.fourth(gbq)
        input_grad, *pair_attn = layer.qkv_grad(
            tie(pos, scatter2.out_y, scatter2.out_x, scatter1.out_z0),
            vec, sums, gbq, gmid, gqkv, n1, inputs, attn,
        )
        scatter2.second(input_grad)
        scatter3 = Scatter(*pair_attn, scatter2.in_y, scatter2.in_x, scatter1.in_z0)
        scatter3.got = tie(scatter3.got, scatter2.out_y2, scatter2.out_x2)
        scatter3.diagonal()
        scatter2.third()
        scatter3.hi()
        scatter3.lo()
        layer_out = layer.layer_out(
            tie(pos, scatter3.out_z1, scatter3.out_y2, scatter3.out_x2, scatter2.out_z1), vec, act, mid, down
        )
        scatter2.fourth(layer_out)
        scatter3.last(layer_out)

        def exchange(blocks, axis):
            first, second = jnp.split(blocks, 2, axis=axis)
            keep = jnp.where(core == 0, first, second)
            got = swap(jnp.where(core == 0, second, first), 0)
            return jnp.where(core == 0, keep, got), jnp.where(core == 0, got, keep)

        grad_w_down = jnp.concatenate(exchange(scatter1.result(input_grad, layer_out), 0), axis=1)
        lo, hi = exchange(scatter2.result(layer_out), 1)
        both = jnp.stack([lo, hi])
        grad_w_up = both[:, :4].reshape(2, 2, 2, per, HALF).transpose(3, 0, 2, 1, 4).reshape(per, FF)
        grad_w_out = both[:, 4].transpose(1, 0, 2).reshape(per, D)
        low = [term[:1] for term in scatter3.low]
        grad_w_qkv, eight, grad_b_up, grad_b_down = layer.finish(pos, scatter3.in_z0, low)
        grad_b_up, grad_b_down = grad_b_up[0], grad_b_down[0]
    return (
        layer_out, input_grad, eight[0], eight[1], grad_w_qkv, eight[2], eight[4], grad_w_out, eight[5],
        eight[6], eight[7], grad_w_up, grad_b_up, grad_w_down, grad_b_down,
    )


def solution(mesh):
    both = P(AXES, None)
    one = P(AXES)
    tuned = dict(mesh.shape) == {"wide": 8, "narrow": 4}
    in_specs = (both, both, one, one, both, one, one, both, one, one, one, both, one, both, one, both)
    out_specs = (both, both, one, one, both, one, one, both, one, one, one, both, one, both, one)
    return jax.shard_map(
        functools.partial(per_device, tuned),
        mesh=mesh,
        in_specs=in_specs,
        out_specs=out_specs,
        check_vma=False,
    )
```

```python
import functools

import jax
import jax.numpy as jnp
from jax import lax
from jax.experimental import pallas as pl
from jax.experimental.pallas import tpu as pltpu
from jax.sharding import PartitionSpec as P

HEADS = 12
HEAD_DIM = 64
D = 768
FF = 3072
ROW_LEN = 256
HALF = 384
CHIPS = 16
BLK = 48
PAIRS = HEADS // 2
AXES = ("wide", "narrow")

EPS = 1e-06
MASKED = -1e30
F32 = jnp.float32
BF16 = jnp.bfloat16

BIT_Y, BIT_X, BIT_Z0, BIT_Z1 = 1, 2, 4, 8
Z_OFFSETS = (0, 4, 8, 12)

GATHER = tuple((o + z, o + z + BIT_Z0) for o in (0, BIT_Y, BIT_X, BIT_X + BIT_Y) for z in (0, BIT_Z1))
PIECES = 2 * len(GATHER)

SCATTER = (0, 4, 12, 8, 1, 5, 14, 10, 13, 9, 15, 11, 2, 6, 3, 7)


def nt(a, b):
    return lax.dot_general(a, b, (((1,), (1,)), ((), ())), preferred_element_type=F32)


def tn(a, b):
    return lax.dot_general(a, b, (((0,), (0,)), ((), ())), preferred_element_type=F32)


def nn(a, b):
    return lax.dot_general(a, b, (((1,), (0,)), ((), ())), preferred_element_type=F32)


def chunks(tokens, step, body):
    def one(i, carry):
        body(pl.ds(pl.multiple_of(i * step, step), step))
        return carry

    lax.fori_loop(0, tokens // step, one, 0)


def norm_parts(v):
    centre = jnp.mean(v, axis=-1, keepdims=True)
    centred = v - centre
    scale = lax.rsqrt(jnp.mean(centred * centred, axis=-1, keepdims=True) + EPS)
    return centred * scale, scale


def start(src, dst, sem):
    copy = pltpu.make_async_copy(src, dst, sem)
    copy.start()
    return copy


def whole_wait(ref, sem):
    pltpu.make_async_copy(ref, ref, sem).wait()


def each_block(pos_ref, pieces):
    for other in range(2):
        for ref, offsets in zip(pieces[other * len(GATHER) :], GATHER):
            for b, offset in enumerate(offsets):
                yield ref, b, pos_ref[0] ^ offset, other, offset


def chip_rows(chip, size):
    return pl.ds(pl.multiple_of(chip * size, 16), size)


def half_cols(pos_ref, other):
    return pl.ds(pl.multiple_of((pos_ref[1] ^ other) * HALF, 128), HALF)


def fetch_qkv(pos_ref, pieces, w_qkv, sems):
    for t in range(3):
        for ref, b, chip, other, _ in each_block(pos_ref, pieces):
            dst = w_qkv.at[t, chip_rows(chip, BLK), half_cols(pos_ref, other)]
            start(ref.at[b, pl.ds(t * BLK, BLK)], dst, sems.at[t])


def fetch_out(pos_ref, pieces, w_out, sem):
    for ref, b, chip, other, _ in each_block(pos_ref, pieces):
        dst = w_out.at[chip_rows(chip, BLK), half_cols(pos_ref, other)]
        start(ref.at[b, 4], dst, sem)


def fetch_small(pos_ref, pieces, small, sem):
    for ref, b, chip, other, _ in each_block(pos_ref, pieces):
        start(ref.at[b, pl.ds(3 * BLK, 16)], small.at[pos_ref[1] ^ other, chip], sem)


def fetch_up(pos_ref, pieces, w_up, sems):
    for ref, b, chip, other, _ in each_block(pos_ref, pieces):
        for u in range(2):
            dst = w_up.at[other, pl.ds(0, 2), chip_rows(chip, BLK), pl.ds(u * HALF, HALF)]
            start(ref.at[b, pl.ds(2 * u, 2)], dst, sems.at[other])


def fetch_down(pos_ref, pieces, w_down, sems):
    for q in range(4):
        for ref, b, chip, other, offset in each_block(pos_ref, pieces):
            if offset // 4 == q:
                dst = w_down.at[chip_rows(chip, 4 * BLK), half_cols(pos_ref, other)]
                start(ref.at[b], dst, sems.at[q])


def ring_place(z):
    return z ^ (z >> 1)


def scatter_place(pos_ref, chip):
    xy = (pos_ref[0] ^ chip) & 3
    z = (ring_place(chip >> 2) - ring_place(pos_ref[0] >> 2)) & 3
    near = jnp.where(xy == 1, 4, jnp.where(xy == 2, 12, 14)) + z
    far = jnp.where(xy == 1, 6, jnp.where(xy == 2, 4, 8)) + z
    return jnp.where(xy == 0, z, jnp.where(z < 2, near, far))


def qkv_forward_kernel(pos_ref, x_any, *refs):
    pieces, refs = refs[:PIECES], refs[PIECES:]
    vec_ref, n1_any, qkv_any, x_ref, n1_ref, qkv_ref, w_qkv, small, sems = refs
    tokens = x_ref.shape[0]
    load_x = start(x_any, x_ref, sems.at[0])
    fetch_small(pos_ref, pieces, small, sems.at[1])
    fetch_qkv(pos_ref, pieces, w_qkv, sems.at[pl.ds(2, 3)])
    whole_wait(small, sems.at[1])
    for h in range(2):
        vec_ref[:, h * HALF : (h + 1) * HALF] = jnp.sum(small[h].astype(F32), axis=0)
    load_x.wait()

    def norm_one(rows):
        xhat, _ = norm_parts(x_ref[rows, :].astype(F32))
        n1_ref[rows, :] = (xhat * vec_ref[0:1, :] + vec_ref[1:2, :]).astype(BF16)

    chunks(tokens, 128, norm_one)
    stores = [start(n1_ref, n1_any, sems.at[5])]
    for t in range(3):
        whole_wait(w_qkv.at[t], sems.at[2 + t])
        y = (nn(n1_ref[...], w_qkv[t]) + vec_ref[2 + t : 3 + t, :]).astype(BF16)
        if t == 0:
            y = y * BF16(HEAD_DIM**-0.5)
        qkv_ref[:, t * D : (t + 1) * D] = y
        cols = pl.ds(t * D, D)
        stores.append(start(qkv_ref.at[:, cols], qkv_any.at[:, cols], sems.at[6 + t]))
    for store in stores:
        store.wait()


def attention_kernel(
    pos_ref, segr_ref, segc_ref, qkv_any, soft_any, mixed_any, qkv_ref, soft_ref, mixed_ref, bias, sems
):
    tokens = qkv_ref.shape[0]
    n_rows = tokens // ROW_LEN
    loads = []
    for r in range(n_rows):
        rows = pl.ds(r * ROW_LEN, ROW_LEN)
        loads.append(start(qkv_any.at[rows], qkv_ref.at[rows], sems.at[2 + r]))
    for r in range(n_rows):
        same = segc_ref[r * ROW_LEN : (r + 1) * ROW_LEN] == segr_ref[r]
        bias[r] = jnp.where(same, 0.0, MASKED)
    lane = lax.broadcasted_iota(jnp.int32, (1, 2 * HEAD_DIM), 1)
    low = (lane < HEAD_DIM).astype(F32).astype(BF16)
    high = (lane >= HEAD_DIM).astype(F32).astype(BF16)
    for r in range(n_rows):
        rows = slice(r * ROW_LEN, (r + 1) * ROW_LEN)
        loads[r].wait()

        def pair(i, carry):
            q = qkv_ref[rows, pl.ds(pl.multiple_of(i * 128, 128), 128)]
            k = qkv_ref[rows, pl.ds(pl.multiple_of(D + i * 128, 128), 128)]
            v = qkv_ref[rows, pl.ds(pl.multiple_of(2 * D + i * 128, 128), 128)]
            mixed = jnp.zeros((ROW_LEN, 128), F32)
            for hh, keep in enumerate((low, high)):
                s = nt(q, k * keep) + bias[r]
                e = jnp.exp(s - jnp.max(s, axis=-1, keepdims=True))
                p = (e * (1.0 / jnp.sum(e, axis=-1, keepdims=True))).astype(BF16)
                soft_ref[r * HEADS + 2 * i + hh] = p
                mixed = mixed + nn(p, v * keep)
            mixed_ref[rows, pl.ds(pl.multiple_of(i * 128, 128), 128)] = mixed.astype(BF16)
            at = pl.ds(r * HEADS + 2 * i, 2)
            start(soft_ref.at[at], soft_any.at[at], sems.at[0])
            return carry

        lax.fori_loop(0, PAIRS, pair, 0)
    store = start(mixed_ref, mixed_any, sems.at[1])
    whole_wait(soft_ref, sems.at[0])
    store.wait()


GELU_A = 0.7978845608028654
GELU_B = 0.044715


def quarter(pos_ref, other, s):
    return (pos_ref[1] ^ other) * 2 + s


def quarter_cols(z):
    return pl.ds(pl.multiple_of(z * D, 128), D)


QUARTERS = ((0, 0), (0, 1), (1, 0), (1, 1))


def mlp_up_kernel(pos_ref, segc_ref, vec_ref, x_any, mixed_any, cot_any, *refs):
    pieces, refs = refs[:PIECES], refs[PIECES:]
    gb_ref, n2_any, mid_any, act_any, slope_any, gout_any, *refs = refs
    x_ref, mixed_ref, cot_ref, n2_ref, mid_ref, act_ref, slope_ref, gout_ref, w_out, w_up, sems = refs
    tokens = n2_ref.shape[0]
    load_x = start(x_any, x_ref, sems.at[2])
    load_mixed = start(mixed_any, mixed_ref, sems.at[13])
    fetch_out(pos_ref, pieces, w_out, sems.at[14])
    fetch_up(pos_ref, pieces, w_up, sems)
    load_cot = start(cot_any, cot_ref, sems.at[3])
    load_x.wait()
    load_mixed.wait()
    whole_wait(w_out, sems.at[14])
    mid_ref[...] = x_ref[...].astype(F32) + nn(mixed_ref[...], w_out[...]) + vec_ref[5:6, :]

    def norm_two(rows):
        xhat, _ = norm_parts(mid_ref[rows, :])
        n2_ref[rows, :] = (xhat * vec_ref[6:7, :] + vec_ref[7:8, :]).astype(BF16)

    chunks(tokens, 128, norm_two)
    stores = [start(mid_ref, mid_any, sems.at[15]), start(n2_ref, n2_any, sems.at[16])]
    for other, s in QUARTERS:
        if s == 0:
            whole_wait(w_up.at[other], sems.at[other])
        z = quarter(pos_ref, other, s)
        b_up = vec_ref[pl.ds(8 + z, 1), :]

        def part(rows):
            u = nn(n2_ref[rows, :], w_up[other, s]) + b_up
            sq = u * u
            t = jnp.tanh(u * (GELU_A + GELU_A * GELU_B * sq))
            half_up = 0.5 + 0.5 * t
            act_ref[other, s, rows, :] = (u * half_up).astype(BF16)
            slope_ref[other, s, rows, :] = (
                half_up + u * (0.5 - 0.5 * t * t) * (GELU_A + 3.0 * GELU_A * GELU_B * sq)
            ).astype(BF16)

        chunks(tokens, 256, part)
        k = 2 * other + s
        stores.append(start(act_ref.at[other, s], act_any.at[:, quarter_cols(z)], sems.at[5 + k]))
        stores.append(start(slope_ref.at[other, s], slope_any.at[:, quarter_cols(z)], sems.at[9 + k]))
    load_cot.wait()
    valid = segc_ref[...] > 0
    gout = jnp.where(valid, cot_ref[...].astype(F32), 0.0)
    gout_ref[...] = gout.astype(BF16)
    gb_ref[...] = jnp.broadcast_to(jnp.sum(gout, axis=0, keepdims=True), gb_ref.shape)
    stores.append(start(gout_ref, gout_any, sems.at[4]))
    for store in stores:
        store.wait()


def down_grad_kernel(pos_ref, act_any, gout_any, mine, theirs, act_ref, gout_ref, grad, sems):
    load_gout = start(gout_any, gout_ref, sems.at[0])
    loads = [
        start(act_any.at[:, pl.ds(z * D, D)], act_ref.at[z], sems.at[2 + z]) for z in range(4)
    ]
    load_gout.wait()
    for z in range(4):
        loads[z].wait()
        grad[z] = tn(act_ref[z], gout_ref[...]).astype(BF16)
        for j in range(4):
            place = scatter_place(pos_ref, 4 * z + j)
            for other, out in enumerate((mine, theirs)):
                src = grad.at[z, pl.ds(j * 4 * BLK, 4 * BLK), half_cols(pos_ref, other)]
                start(src, out.at[place], sems.at[1])
    whole_wait(grad, sems.at[1])


def mlp_down_kernel(pos_ref, gout_any, slope_any, n2_any, *refs):
    pieces, refs = refs[:PIECES], refs[PIECES:]
    gb_ref, gpre_any, mine, theirs, *refs = refs
    gout_ref, slope_ref, n2_ref, gpre_ref, n2t, w_down, grad, sems = refs
    load_n2 = start(n2_any, n2_ref, sems.at[4])
    load_gout = start(gout_any, gout_ref, sems.at[5])
    fetch_down(pos_ref, pieces, w_down, sems)
    loads = {
        (other, s): start(
            slope_any.at[:, quarter_cols(quarter(pos_ref, other, s))],
            slope_ref.at[other, s],
            sems.at[6 + 2 * other + s],
        )
        for other, s in QUARTERS
    }
    gb_ref[...] = jnp.zeros(gb_ref.shape, F32)
    load_n2.wait()
    n2t[...] = n2_ref[...].T
    load_gout.wait()
    stores = []
    for other, s in QUARTERS:
        z = quarter(pos_ref, other, s)
        rows = quarter_cols(z)
        whole_wait(w_down.at[rows], sems.at[z ^ (pos_ref[0] >> 2)])
        loads[other, s].wait()
        ga = nt(gout_ref[...], w_down[rows, :])
        gp = (ga * slope_ref[other, s].astype(F32)).astype(BF16)
        gpre_ref[other, s] = gp
        stores.append(start(gpre_ref.at[other, s], gpre_any.at[:, rows], sems.at[10 + 2 * other + s]))
        gb_ref[pl.ds(z, 1), :] = jnp.sum(gp.astype(F32), axis=0, keepdims=True)
        grad[other, s] = nn(n2t[...], gpre_ref[other, s]).astype(BF16)
        if s == 1:
            for chip in range(CHIPS):
                place = scatter_place(pos_ref, chip)
                for u in range(2):
                    src = grad.at[other, pl.ds(0, 2), pl.ds(chip * BLK, BLK), pl.ds(u * HALF, HALF)]
                    start(src, (mine, theirs)[other].at[place, pl.ds(2 * u, 2)], sems.at[14])
    whole_wait(grad, sems.at[14])
    for store in stores:
        store.wait()


def norm_back(grad, xhat, scale, gain):
    gn = grad * gain
    mean_gn = jnp.mean(gn, axis=-1, keepdims=True)
    mean_gx = jnp.mean(gn * xhat, axis=-1, keepdims=True)
    return scale * (gn - mean_gn - xhat * mean_gx)


def mid_backward_kernel(
    pos_ref, vec_ref, gbd_ref, gbu_ref, gpre_any, gout_any, mid_any, mixed_any, *refs
):
    pieces, refs = refs[:PIECES], refs[PIECES + 2 :]
    sums, gmid_any, gmixed_any, mine, theirs, *refs = refs
    gpre_ref, gout_ref, mid_ref, mixed_ref, w_up, w_out, acc, gmid, gbr, gmixed, mixt, grad, sems = refs
    tokens = mid_ref.shape[0]
    load_mixed = start(mixed_any, mixed_ref, sems.at[8])
    fetch_up(pos_ref, pieces, w_up, sems)
    loads = {
        (other, s): start(
            gpre_any.at[:, quarter_cols(quarter(pos_ref, other, s))],
            gpre_ref.at[other, s],
            sems.at[4 + 2 * other + s],
        )
        for other, s in QUARTERS
    }
    load_mid = start(mid_any, mid_ref, sems.at[9])
    load_gout = start(gout_any, gout_ref, sems.at[10])
    fetch_out(pos_ref, pieces, w_out, sems.at[11])
    sums[...] = jnp.zeros(sums.shape, F32)
    sums[8:12, :] = gbu_ref[0:4, :]
    sums[12:13, :] = gbd_ref[0:1, :]
    load_mixed.wait()
    mixt[...] = mixed_ref[...].T
    for other, s in QUARTERS:
        if s == 0:
            whole_wait(w_up.at[other], sems.at[other])
        loads[other, s].wait()
        part = nt(gpre_ref[other, s], w_up[other, s])
        acc[...] = part if other + s == 0 else acc[...] + part
    load_mid.wait()
    load_gout.wait()

    def back_two(rows):
        xhat, scale = norm_parts(mid_ref[rows, :])
        g = acc[rows, :]
        sums[6:7, :] += jnp.sum(g * xhat, axis=0, keepdims=True)
        sums[7:8, :] += jnp.sum(g, axis=0, keepdims=True)
        gm = gout_ref[rows, :].astype(F32) + norm_back(g, xhat, scale, vec_ref[6:7, :])
        gmid[rows, :] = gm
        low = gm.astype(BF16)
        gbr[rows, :] = low
        sums[5:6, :] += jnp.sum(low.astype(F32), axis=0, keepdims=True)

    chunks(tokens, 128, back_two)
    stores = [start(gmid, gmid_any, sems.at[12])]
    whole_wait(w_out, sems.at[11])
    gmixed[...] = nt(gbr[...], w_out[...]).astype(BF16)
    stores.append(start(gmixed, gmixed_any, sems.at[13]))
    grad[...] = nn(mixt[...], gbr[...]).astype(BF16)
    for chip in range(CHIPS):
        place = scatter_place(pos_ref, chip)
        for other, out in enumerate((mine, theirs)):
            src = grad.at[pl.ds(chip * BLK, BLK), half_cols(pos_ref, other)]
            start(src, out.at[place, 4], sems.at[14])
    whole_wait(grad, sems.at[14])
    for store in stores:
        store.wait()


def attn_backward_kernel(
    pos_ref, gmixed_any, qkv_any, soft_any, gb_ref, gqkv_any, gmixed, qkv_ref, soft_ref, gqkv, sems
):
    tokens = gmixed.shape[0]
    load_gmixed = start(gmixed_any, gmixed, sems.at[0])
    load_qkv = start(qkv_any, qkv_ref, sems.at[1])
    n_rows = tokens // ROW_LEN
    per_row = [
        start(
            soft_any.at[pl.ds(r * HEADS, HEADS)], soft_ref.at[pl.ds(r * HEADS, HEADS)], sems.at[4 + r]
        )
        for r in range(n_rows)
    ]
    load_gmixed.wait()
    load_qkv.wait()
    lane = lax.broadcasted_iota(jnp.int32, (1, 2 * HEAD_DIM), 1)
    first = (lane < HEAD_DIM).astype(F32).astype(BF16)
    second = (lane >= HEAD_DIM).astype(F32).astype(BF16)
    for r in range(n_rows):
        rows = slice(r * ROW_LEN, (r + 1) * ROW_LEN)
        per_row[r].wait()

        def pair(i, carry):
            at_q = pl.ds(pl.multiple_of(i * 128, 128), 128)
            at_k = pl.ds(pl.multiple_of(D + i * 128, 128), 128)
            at_v = pl.ds(pl.multiple_of(2 * D + i * 128, 128), 128)
            q, k, v = qkv_ref[rows, at_q], qkv_ref[rows, at_k], qkv_ref[rows, at_v]
            gm = gmixed[rows, at_q]
            dq = jnp.zeros((ROW_LEN, 128), F32)
            dk = jnp.zeros((ROW_LEN, 128), F32)
            dv = jnp.zeros((ROW_LEN, 128), F32)
            for hh, keep in enumerate((first, second)):
                p_low = soft_ref[r * HEADS + 2 * i + hh]
                p = p_low.astype(F32)
                gmk = gm * keep
                gs = nt(gmk, v)
                inner = jnp.sum(p * gs, axis=-1, keepdims=True)
                ds = (p * (gs - inner)).astype(BF16)
                dq = dq + nn(ds, k * keep)
                dk = dk + tn(ds, q * keep)
                dv = dv + tn(p_low, gmk)
            gqkv[rows, at_q] = (dq * (HEAD_DIM**-0.5)).astype(BF16)
            gqkv[rows, at_k] = dk.astype(BF16)
            gqkv[rows, at_v] = dv.astype(BF16)
            return carry

        lax.fori_loop(0, PAIRS, pair, 0)
    store = start(gqkv, gqkv_any, sems.at[2])
    gb_ref[...] = jnp.zeros(gb_ref.shape, F32)
    gb_ref[0:1, :] = jnp.sum(gqkv[:, :D].astype(F32), axis=0, keepdims=True)
    gb_ref[2:3, :] = jnp.sum(gqkv[:, 2 * D :].astype(F32), axis=0, keepdims=True)
    store.wait()


def qkv_grad_kernel(
    pos_ref, vec_ref, sums_ref, gbq_ref, gmid_any, gqkv_any, n1_any, x_any, *refs
):
    pieces, refs = refs[:PIECES], refs[PIECES:]
    igrad_any, mine, theirs, *refs = refs
    gmid, gqkv, n1_ref, x_ref, w_qkv, acc, n1t, grad, sums, small, igrad, sems = refs
    tokens = x_ref.shape[0]
    load_n1 = start(n1_any, n1_ref, sems.at[0])
    loads = [
        start(gqkv_any.at[:, pl.ds(t * D, D)], gqkv.at[t], sems.at[1 + t]) for t in range(3)
    ]
    fetch_qkv(pos_ref, pieces, w_qkv, sems.at[pl.ds(4, 3)])
    load_x = start(x_any, x_ref, sems.at[7])
    load_gmid = start(gmid_any, gmid, sems.at[8])
    sums[...] = sums_ref[...]
    sums[2:3, :] = gbq_ref[0:1, :]
    sums[4:5, :] = gbq_ref[2:3, :]
    load_n1.wait()
    n1t[...] = n1_ref[...].T
    for t in range(3):
        loads[t].wait()
        grad[t] = nn(n1t[...], gqkv[t]).astype(BF16)
        for chip in range(CHIPS):
            place = scatter_place(pos_ref, chip)
            for other, out in enumerate((mine, theirs)):
                src = grad.at[t, pl.ds(chip * BLK, BLK), half_cols(pos_ref, other)]
                start(src, out.at[place, pl.ds(t * BLK, BLK)], sems.at[9])
    for t in range(3):
        whole_wait(w_qkv.at[t], sems.at[4 + t])
        part = nt(gqkv[t], w_qkv[t])
        acc[...] = part if t == 0 else acc[...] + part
    load_x.wait()
    load_gmid.wait()

    def back_one(rows):
        xhat, scale = norm_parts(x_ref[rows, :].astype(F32))
        g = acc[rows, :]
        sums[0:1, :] += jnp.sum(g * xhat, axis=0, keepdims=True)
        sums[1:2, :] += jnp.sum(g, axis=0, keepdims=True)
        igrad[rows, :] = (gmid[rows, :] + norm_back(g, xhat, scale, vec_ref[0:1, :])).astype(BF16)

    chunks(tokens, 128, back_one)
    store = start(igrad, igrad_any, sems.at[10])
    for p in range(CHIPS):
        small[0, p] = sums[:, :HALF].astype(BF16)
        small[1, p] = sums[:, HALF:].astype(BF16)
    for other, out in enumerate((mine, theirs)):
        for p in range(CHIPS):
            start(small.at[pos_ref[1] ^ other, p], out.at[p, pl.ds(3 * BLK, 16)], sems.at[11])
    whole_wait(small, sems.at[11])
    whole_wait(grad, sems.at[9])
    store.wait()


def layer_out_kernel(pos_ref, vec_ref, act_any, mid_any, *refs):
    pieces, refs = refs[:PIECES], refs[PIECES:]
    out_any, act_ref, mid_ref, out_ref, w_down, acc, sems = refs
    own_z = pos_ref[0] >> 2
    load_mid = start(mid_any, mid_ref, sems.at[8])
    loads = [
        start(act_any.at[:, quarter_cols(own_z ^ q)], act_ref.at[q], sems.at[4 + q]) for q in range(4)
    ]
    fetch_down(pos_ref, pieces, w_down, sems)
    for q in range(4):
        rows = quarter_cols(own_z ^ q)
        loads[q].wait()
        whole_wait(w_down.at[rows], sems.at[q])
        part = nn(act_ref[q], w_down[rows, :])
        if q == 0:
            load_mid.wait()
            acc[...] = part + (mid_ref[...] + vec_ref[12:13, :])
        elif q < 3:
            acc[...] = acc[...] + part
        else:
            out_ref[...] = (acc[...] + part).astype(BF16)
    start(out_ref, out_any, sems.at[9]).wait()


PER = D // (2 * CHIPS)
SEND_ROWS = (3 * PER, 16, 5 * PER, 4 * PER)


def pack_kernel(pos_ref, w_qkv, w_out, w_up, w_down, bu_ref, *refs):
    values, (mine, theirs, rows, last, wide) = refs[:8], refs[8:]
    place = pos_ref[0] * 2 + pos_ref[1]
    rows[...] = jnp.zeros(rows.shape, F32)
    last[...] = jnp.zeros(last.shape, F32)
    for r, value in zip((0, 1, 2, 4, 5, 6, 7, 12), values):
        rows[r : r + 1, 0:PER] = value[...].astype(F32)
    last[0:1, 0 : 4 * PER] = bu_ref[...].astype(F32)
    at = place * (4 * PER)
    up = pltpu.roll(last[...], at % D, 1)[0:1]
    here = lax.broadcasted_iota(jnp.int32, (16, 1), 0) == 8 + at // D
    rows[...] = pltpu.roll(rows[...], place * PER, 1) + jnp.where(here, up, 0.0)
    for out, other in ((mine, 0), (theirs, 1)):
        half = pos_ref[1] ^ other

        def cols(first):
            return pl.ds(pl.multiple_of(first + half * HALF, 128), HALF)

        at = 0
        for t in range(3):
            wide[at : at + PER, :] = w_qkv[:, cols(t * D)].astype(F32)
            at += PER
        wide[at : at + 16, :] = rows[:, cols(0)]
        at += 16
        for n in range(4):
            u, s = n // 2, n % 2
            first = pl.multiple_of(half * (2 * D) + s * D + u * HALF, 128)
            wide[at : at + PER, :] = w_up[:, pl.ds(first, HALF)].astype(F32)
            at += PER
        wide[at : at + PER, :] = w_out[:, cols(0)].astype(F32)
        at += PER
        wide[at : at + 4 * PER, :] = w_down[:, cols(0)].astype(F32)
        out[...] = wide[...].astype(BF16)


def combine_kernel(pos_ref, mine, got, one, two, three, upper, lower, wide):
    first = pos_ref[1] == 0
    m, g = mine[...].astype(F32), got[...].astype(F32)
    upper[...] = jnp.where(first, m, g)
    lower[...] = jnp.where(first, g, m)

    def pair(at, size):
        wide[0:size, :] = upper[at : at + size, :]
        wide[size : 2 * size, :] = lower[at : at + size, :]
        return wide[0 : 2 * size, :].astype(BF16)

    for t in range(3):
        one[t * BLK : (t + 1) * BLK, :] = pair(t * PER, PER)
    at = 3 * PER
    one[3 * BLK :, :] = (upper[at : at + 16, :] + lower[at : at + 16, :]).astype(BF16)
    at += 16
    for n in range(5):
        two[n] = pair(at + n * PER, PER)
    three[...] = pair(at + 5 * PER, 4 * PER)


def finish_kernel(pos_ref, last, *refs):
    terms, (keep, send, held, sems) = refs[:4], refs[4:]
    for i, term in enumerate(terms):
        start(term.at[0], held.at[i], sems.at[i])
    total = last[...].astype(F32)
    for i in range(4):
        whole_wait(held.at[i], sems.at[i])
        total = total + held[i].astype(F32)
    first = pos_ref[1] == 0
    for t in range(3):
        upper, lower = total[t * BLK : t * BLK + PER], total[t * BLK + PER : (t + 1) * BLK]
        keep[t * PER : (t + 1) * PER, :] = jnp.where(first, upper, lower)
        send[t * PER : (t + 1) * PER, :] = jnp.where(first, lower, upper)
    keep[3 * PER :, :] = total[3 * BLK :]
    send[3 * PER :, :] = total[3 * BLK :]


def spread_kernel(pos_ref, keep, got, w_ref, eight_ref, up_ref, down_ref, rows):
    place = pos_ref[0] * 2 + pos_ref[1]
    for ref, other in ((keep, 0), (got, 1)):
        half = pos_ref[1] ^ other
        for t in range(3):
            cols = pl.ds(pl.multiple_of(t * D + half * HALF, 128), HALF)
            w_ref[:, cols] = ref[t * PER : (t + 1) * PER, :]
        rows[:, pl.ds(pl.multiple_of(half * HALF, 128), HALF)] = ref[3 * PER :, :]
    mine = pltpu.roll(rows[...], lax.rem(D - place * PER, D), 1)
    eight_ref[...] = mine[0:8, 0:PER]
    down_ref[...] = mine[12:13, 0:PER]
    at = place * (4 * PER)
    here = lax.broadcasted_iota(jnp.int32, (16, 1), 0) == 8 + at // D
    row = jnp.sum(jnp.where(here, rows[...], 0.0), axis=0, keepdims=True)
    turned = pltpu.roll(jnp.broadcast_to(row, (8, D)), lax.rem(D - at % D, D), 1)
    up_ref[...] = turned[0:1, 0 : 4 * PER]


def call(kernel, name, near, far, near_outs, far_outs, scratch, flops, aliases=None):
    vmem = pl.BlockSpec(memory_space=pltpu.VMEM)
    anyspec = pl.BlockSpec(memory_space=pl.ANY)
    outs = tuple(near_outs) + tuple(far_outs)
    moved = sum(a.size * a.dtype.itemsize for a in tuple(near) + tuple(far) + outs)
    return pl.pallas_call(
        kernel,
        out_shape=outs,
        in_specs=[pl.BlockSpec(memory_space=pltpu.SMEM)]
        + [vmem] * (len(near) - 1)
        + [anyspec] * len(far),
        out_specs=[vmem] * len(near_outs) + [anyspec] * len(far_outs),
        scratch_shapes=scratch,
        input_output_aliases=aliases or {},
        compiler_params=pltpu.CompilerParams(vmem_limit_bytes=56 << 20),
        cost_estimate=pl.CostEstimate(flops=flops, bytes_accessed=moved, transcendentals=0),
        name=name,
    )(*near, *far)


def swap(value, chip_bit):
    flip = chip_bit * 2 if chip_bit else 1
    return lax.ppermute(value, AXES, [(i, i ^ flip) for i in range(2 * CHIPS)])


def ring_step(value):
    follow = (1, 3, 0, 2)
    return lax.ppermute(value, AXES, [(i, follow[i // 8] * 8 + i % 8) for i in range(2 * CHIPS)])


def tie(value, *after):
    return lax.optimization_barrier((value,) + after)[0]


def gathered(*own_half):
    return list(own_half) + [swap(piece, 0) for piece in own_half]


def hold(pieces, *after):
    return lax.optimization_barrier((*pieces, *after))[: len(pieces)] if after else pieces


def rounded_sum(*terms):
    total = terms[0].astype(F32)
    for term in terms[1:]:
        total = total + term.astype(F32)
    return total.astype(BF16)


def small_grads(sums, place, per, per_up):
    eight = lax.dynamic_slice(sums, (0, place * per), (8, per))
    at = place * per_up
    up = lax.dynamic_slice(sums, (8 + at // D, at % D), (1, per_up))[0]
    down = lax.dynamic_slice(sums, (12, place * per), (1, per))[0]
    return eight, up, down


def halves(w_qkv, w_out, w_up, w_down):
    rows = w_qkv.shape[0]
    qkv = w_qkv.reshape(rows, 3, 2, HALF)
    up = w_up.reshape(rows, 2, 4, HALF)
    for h in range(2):
        cols = slice(h * HALF, (h + 1) * HALF)
        up_h = up[:, h].reshape(rows, 2, 2, HALF).transpose(2, 1, 0, 3).reshape(4, rows, HALF)
        yield (
            qkv[:, :, h].transpose(1, 0, 2),
            jnp.concatenate([up_h, w_out[None, :, cols]]),
            w_down[:, cols],
        )


def gather_plain(weights, values):
    def whole(w):
        return lax.all_gather(w, AXES, axis=0, tiled=True)

    gain1, bias1, bq, bv, bo, gain2, bias2, bu, bd = [whole(v) for v in values]
    rest = jnp.zeros((3, D), BF16)
    small = jnp.stack([gain1, bias1, bq, jnp.zeros_like(bq), bv, bo, gain2, bias2])
    small = jnp.concatenate([small, bu.reshape(4, D), bd[None], rest])
    groups = ([], [], [])
    for h, (attn, up, down) in enumerate(halves(*[whole(w) for w in weights])):
        attn = attn.reshape(3, CHIPS, BLK, HALF).transpose(1, 0, 2, 3).reshape(CHIPS, 3 * BLK, HALF)
        up = up.reshape(5, CHIPS, BLK, HALF).transpose(1, 0, 2, 3)
        down = down.reshape(CHIPS, 4 * BLK, HALF)
        extra = jnp.zeros((CHIPS, 16, HALF), BF16).at[0].set(small[:, h * HALF : (h + 1) * HALF])
        for group, blocks in zip(groups, (jnp.concatenate([attn, extra], axis=1), up, down)):
            group.extend(jnp.stack([blocks[o] for o in piece]) for piece in GATHER)
    return groups


def scatter_plain(pair, group):
    both = [jnp.stack([part[SCATTER.index(chip)] for chip in range(CHIPS)]) for part in pair]

    def scatter(v):
        return lax.psum_scatter(v.astype(F32), AXES, scatter_dimension=0, tiled=True)

    def matrix(units):
        return jnp.stack(units, axis=3).transpose(0, 2, 1, 3, 4).reshape(D, -1, 2, HALF)

    if group == "attn":
        sums = jnp.concatenate([b[0, 3 * BLK :] for b in both], axis=1)
        qkv = matrix([b[:, : 3 * BLK].reshape(CHIPS, 3, BLK, HALF) for b in both])
        return scatter(qkv.reshape(D, 3 * D)), lax.psum(sums.astype(F32), AXES)
    if group == "up":
        up = matrix(both)
        order = up[:, :4].reshape(D, 2, 2, 2, HALF).transpose(0, 3, 2, 1, 4)
        return scatter(order.reshape(D, FF)), scatter(up[:, 4].reshape(D, D))
    return scatter(jnp.concatenate([b.reshape(FF, HALF) for b in both], axis=1))


def shape(dims, kind=BF16):
    return jax.ShapeDtypeStruct(dims, kind)


def dma(n):
    return pltpu.SemaphoreType.DMA((n,))


def vmem(*dims, kind=BF16):
    return pltpu.VMEM(dims, kind)


class Layer:
    def __init__(self, tokens):
        self.tokens = tokens
        self.rows = tokens // ROW_LEN
        self.wide = shape((tokens, FF))
        self.act = shape((tokens, D))
        self.mid = shape((tokens, D), F32)
        self.qkv = shape((tokens, 3 * D))
        self.soft = shape((self.rows * HEADS, ROW_LEN, ROW_LEN))
        self.quarters = vmem(2, 2, tokens, D)
        self.one = vmem(tokens, D)
        self.one_f32 = vmem(tokens, D, kind=F32)
        self.turned = vmem(D, tokens)
        self.square = vmem(D, D)
        self.three = vmem(3, D, D)
        self.four = vmem(2, 2, D, D)
        self.sums = shape((8, D), F32)
        self.vec = shape((16, D), F32)

    def chip_blocks(self, pos, weights, values):
        *rest, bu, bd = [v.reshape(1, -1) for v in values]
        sent = shape((sum(SEND_ROWS), HALF))
        wide = vmem(sum(SEND_ROWS), HALF, kind=F32)
        mine, theirs = call(
            pack_kernel, "pack", (pos, *weights, bu, *rest, bd), (), (sent, sent), (),
            [vmem(16, D, kind=F32), vmem(8, D, kind=F32), wide], 0,
        )
        return call(
            combine_kernel, "combine", (pos, mine, swap(theirs, 0)), (),
            (shape((3 * BLK + 16, HALF)), shape((5, BLK, HALF)), shape((4 * BLK, HALF))), (),
            [wide, wide, vmem(4 * BLK, HALF, kind=F32)], 0,
        )

    def finish(self, pos, last, low):
        sent = shape((3 * PER + 16, HALF), F32)
        keep, send = call(
            finish_kernel, "finish", (pos, last), low, (sent, sent), (),
            [vmem(4, 3 * PER * 2 + 16, HALF), dma(4)], 0,
        )
        return call(
            spread_kernel, "spread", (pos, keep, swap(send, 0)), (),
            (shape((PER, 3 * D), F32), shape((8, PER), F32), shape((1, 4 * PER), F32), shape((1, PER), F32)),
            (), [vmem(16, D, kind=F32)], 0,
        )

    def qkv_forward(self, pos, inputs, attn):
        t = self.tokens
        return call(
            qkv_forward_kernel, "qkv_forward", (pos,), [inputs] + attn, (self.vec,), (self.act, self.qkv),
            [self.one, self.one, vmem(t, 3 * D), self.three, vmem(2, CHIPS, 16, HALF), dma(9)],
            2 * t * D * D * 3,
        )

    def attention(self, pos, segr, segc, qkv):
        t = self.tokens
        return call(
            attention_kernel, "attention", (pos, segr, segc), [qkv], (), (self.soft, self.act),
            [
                vmem(t, 3 * D), vmem(*self.soft.shape), self.one,
                vmem(self.rows, ROW_LEN, ROW_LEN, kind=F32), dma(2 + self.rows),
            ],
            8 * t * D * ROW_LEN,
        )

    def mlp_up(self, pos, segc, vec, inputs, mixed, cotangent, up):
        one, quarters = self.one, self.quarters
        return call(
            mlp_up_kernel, "mlp_up", (pos, segc, vec), [inputs, mixed, cotangent] + up,
            (self.sums,), (self.act, self.mid, self.wide, self.wide, self.act),
            [one, one, one, one, self.one_f32, quarters, quarters, one, self.square, self.four, dma(17)],
            2 * self.tokens * D * (FF + D),
        )

    def down_grad(self, pos, act, gout):
        buffer = shape((CHIPS, 4 * BLK, HALF))
        return call(
            down_grad_kernel, "down_grad", (pos,), [act, gout], (), (buffer, buffer),
            [vmem(4, self.tokens, D), self.one, vmem(4, D, D), dma(6)],
            2 * self.tokens * D * FF,
        )

    def mlp_down(self, pos, gout, slope, n2, down):
        one, quarters = self.one, self.quarters
        buffer = shape((CHIPS, 5, BLK, HALF))
        return call(
            mlp_down_kernel, "mlp_down", (pos,), [gout, slope, n2] + down,
            (self.sums,), (self.wide, buffer, buffer),
            [one, quarters, one, quarters, self.turned, vmem(FF, D), self.four, dma(15)],
            4 * self.tokens * D * FF,
        )

    def mid_backward(self, pos, vec, gbd, gbu, gpre, gout, mid, mixed, up, mine, theirs):
        one, wide = self.one, self.one_f32
        buffer = shape(mine.shape)
        far = [gpre, gout, mid, mixed] + up + [mine, theirs]
        return call(
            mid_backward_kernel, "mid_backward", (pos, vec, gbd, gbu), far,
            (self.vec,), (self.mid, self.act, buffer, buffer),
            [
                self.quarters, one, wide, one, self.four, self.square, wide, wide, one, one, self.turned,
                self.square, dma(15),
            ],
            2 * self.tokens * D * (FF + 2 * D),
            {4 + len(far) - 2: 3, 4 + len(far) - 1: 4},
        )

    def attn_backward(self, pos, gmixed, qkv, soft):
        t = self.tokens
        return call(
            attn_backward_kernel, "attn_backward", (pos,), [gmixed, qkv, soft], (self.sums,), (self.qkv,),
            [self.one, vmem(t, 3 * D), vmem(*self.soft.shape), vmem(t, 3 * D), dma(4 + self.rows)],
            20 * t * D * ROW_LEN,
        )

    def qkv_grad(self, pos, vec, sums, gbq, gmid, gqkv, n1, inputs, attn):
        one, wide = self.one, self.one_f32
        buffer = shape((CHIPS, 3 * BLK + 16, HALF))
        return call(
            qkv_grad_kernel, "qkv_grad", (pos, vec, sums, gbq), [gmid, gqkv, n1, inputs] + attn,
            (), (self.act, buffer, buffer),
            [
                wide, vmem(3, self.tokens, D), one, one, self.three, wide, self.turned, self.three,
                vmem(16, D, kind=F32), vmem(2, CHIPS, 16, HALF), one, dma(12),
            ],
            2 * self.tokens * D * 6 * D,
        )

    def layer_out(self, pos, vec, act, mid, down):
        wide = self.one_f32
        (out,) = call(
            layer_out_kernel, "layer_out", (pos, vec), [act, mid] + down, (), (self.act,),
            [vmem(4, self.tokens, D), wide, self.one, vmem(FF, D), wide, dma(10)],
            2 * self.tokens * D * FF,
        )
        return out


class Scatter:
    def __init__(self, mine, theirs, *after):
        self.mine = mine
        self.got = swap(tie(theirs, *after), 0)

    def part(self, first, last):
        return self.mine[first:last], self.got[first:last]

    def first(self, *after):
        self.got = hold((self.got,), *after)[0]
        self.out = (rounded_sum(*self.part(8, 12)), rounded_sum(*self.part(12, 16)))
        self.in_y, self.in_x = swap(self.out[0], BIT_Y), swap(self.out[1], BIT_X)

    def second(self, *after):
        in_y, in_x = hold((self.in_y, self.in_x), *after)
        self.out = (
            rounded_sum(*self.part(4, 6), in_x[2:]),
            rounded_sum(*self.part(6, 8), in_y[2:]),
        )
        self.in_y, self.in_x = in_y, in_x
        self.in_y2, self.in_x2 = swap(self.out[0], BIT_Y), swap(self.out[1], BIT_X)

    def third(self, *after):
        in_y2, in_x2 = hold((self.in_y2, self.in_x2), *after)
        self.near = (*self.part(0, 2), self.in_x[:2], in_y2)
        self.far = (*self.part(2, 4), self.in_y[:2], in_x2)
        self.out = (rounded_sum(*[t[1] for t in self.far]),)
        self.in_z = ring_step(self.out[0])

    def diagonal(self, *after):
        self.got = hold((self.got,), *after)[0]
        self.out = (rounded_sum(*self.part(10, 12)), rounded_sum(*self.part(14, 16)))
        self.in_y, self.in_x = swap(self.out[0], BIT_Y), swap(self.out[1], BIT_X)

    def hi(self, *after):
        in_y, self.in_x = hold((self.in_y, self.in_x), *after)
        self.out = (rounded_sum(*self.part(8, 10)), rounded_sum(*self.part(6, 8), in_y))
        self.in_y2, self.in_x2 = swap(self.out[0], BIT_Y), swap(self.out[1], BIT_X)

    def lo(self, *after):
        in_y2, in_x2 = hold((self.in_y2, self.in_x2), *after)
        self.far = (*self.part(2, 4), in_y2, in_x2)
        ring = rounded_sum(*[t[1] for t in self.far])
        self.in_z = ring_step(ring)
        low_y, low_x = rounded_sum(*self.part(4, 6), self.in_x), rounded_sum(*self.part(12, 14))
        low_y, low_x = hold((low_y, low_x), ring)
        self.out = (ring, low_y, low_x)
        self.near = (*self.part(0, 2), swap(low_y, BIT_Y), swap(low_x, BIT_X))

    def fourth(self, *after):
        in_z = hold((self.in_z,), *after)[0]
        self.out = (rounded_sum(*[t[0] for t in self.far], in_z),)
        self.in_z = ring_step(self.out[0])

    def fifth(self, *after):
        in_z = hold((self.in_z,), *after)[0]
        self.out = (rounded_sum(*[t[1] for t in self.near], in_z),)
        self.in_z = ring_step(self.out[0])

    def result(self, *after):
        total = hold((self.in_z,), *after)[0].astype(F32)
        for term in self.near:
            total = total + term[0].astype(F32)
        return total


def per_device(tuned, *args):
    (
        inputs, segment_ids, pre_attn_gain, pre_attn_bias, w_qkv, b_query, b_value, w_out, b_out,
        pre_mlp_gain, pre_mlp_bias, w_up, b_up, w_down, b_down, cotangent,
    ) = args
    tokens = inputs.shape[0]
    n_rows = tokens // ROW_LEN
    wide, narrow = lax.axis_index("wide"), lax.axis_index("narrow")
    weights = (w_qkv, w_out, w_up, w_down)
    values = (
        pre_attn_gain, pre_attn_bias, b_query, b_value, b_out, pre_mlp_gain, pre_mlp_bias, b_up, b_down,
    )
    per, per_up = pre_attn_gain.shape[0], b_up.shape[0]
    position = jnp.arange(ROW_LEN, dtype=jnp.int32)[None]
    own_id = jnp.where(segment_ids != 0, segment_ids, -1 - position)
    segr = own_id.reshape(n_rows, 1, ROW_LEN)
    segc = own_id.reshape(tokens, 1)
    layer = Layer(tokens)

    if not tuned:
        place = wide * lax.axis_size("narrow") + narrow
        pos = jnp.zeros((2,), jnp.int32)
        attn, up, down = gather_plain(weights, values)
        vec, n1, qkv = layer.qkv_forward(pos, inputs, attn)
        soft, mixed = layer.attention(pos, segr, segc, qkv)
        gbd, n2, mid, act, slope, gout = layer.mlp_up(pos, segc, vec, inputs, mixed, cotangent, up)
        pair_down = layer.down_grad(pos, act, gout)
        gbu, gpre, *pair_up = layer.mlp_down(pos, gout, slope, n2, down)
        sums, gmid, gmixed, *pair_up = layer.mid_backward(
            pos, vec, gbd, gbu, gpre, gout, mid, mixed, up, *pair_up
        )
        gbq, gqkv = layer.attn_backward(pos, gmixed, qkv, soft)
        input_grad, *pair_attn = layer.qkv_grad(pos, vec, sums, gbq, gmid, gqkv, n1, inputs, attn)
        layer_out = layer.layer_out(pos, vec, act, mid, down)
        grad_w_down = scatter_plain(pair_down, "down")
        grad_w_up, grad_w_out = scatter_plain(pair_up, "up")
        grad_w_qkv, sums = scatter_plain(pair_attn, "attn")
        eight, grad_b_up, grad_b_down = small_grads(sums, place, per, per_up)
    else:
        core = (narrow & 1).astype(jnp.int32)
        pos = jnp.stack([wide * 2 + (narrow >> 1), core]).astype(jnp.int32)
        block1, block2, block3 = layer.chip_blocks(pos, weights, values)

        near1 = swap(block1, BIT_Z0)
        lo1 = jnp.stack([block1, near1])
        hi1 = swap(lo1, BIT_Z1)
        y_lo1, x_lo1 = swap(lo1, BIT_Y), swap(lo1, BIT_X)
        near2 = swap(tie(block2, near1), BIT_Z0)
        d_lo1 = swap(y_lo1, BIT_X)
        y_hi1, x_hi1 = swap(hi1, BIT_Y), swap(hi1, BIT_X)
        lo2 = jnp.stack([block2, near2])
        hi2 = swap(tie(lo2, hi1), BIT_Z1)
        d_hi1 = swap(x_hi1, BIT_Y)
        lo2b = tie(lo2, d_lo1, x_hi1)
        y_lo2, x_lo2 = swap(lo2b, BIT_Y), swap(lo2b, BIT_X)
        near3 = swap(tie(block3, d_hi1), BIT_Z0)
        attn = gathered(lo1, hi1, y_lo1, y_hi1, x_lo1, x_hi1, d_lo1, d_hi1)
        lo3 = jnp.stack([block3, near3])
        hi3 = swap(tie(lo3, hi2), BIT_Z1)
        d_lo2 = swap(y_lo2, BIT_X)
        y_hi2, x_hi2 = swap(hi2, BIT_Y), swap(hi2, BIT_X)
        vec, n1, qkv = layer.qkv_forward(tie(pos, hi2, y_lo2, x_lo2, lo3), inputs, attn)

        y_hi2, x_hi2, d_lo2 = hold((y_hi2, x_hi2, d_lo2), vec)
        d_hi2 = swap(x_hi2, BIT_Y)
        lo3b = tie(lo3, y_hi2, x_hi2, d_lo2)
        y_lo3, x_lo3 = swap(lo3b, BIT_Y), swap(lo3b, BIT_X)
        soft, mixed = layer.attention(tie(pos, lo3b), segr, segc, qkv)

        d_hi2, y_lo3, x_lo3, hi3 = hold((d_hi2, y_lo3, x_lo3, hi3), mixed)
        d_lo3 = swap(y_lo3, BIT_X)
        y_hi3, x_hi3 = swap(hi3, BIT_Y), swap(hi3, BIT_X)
        lo2, hi2, y_lo2, y_hi2, x_lo2, x_hi2, d_lo2 = hold(
            (lo2, hi2, y_lo2, y_hi2, x_lo2, x_hi2, d_lo2), x_lo3, hi3
        )
        up = gathered(lo2, hi2, y_lo2, y_hi2, x_lo2, x_hi2, d_lo2, d_hi2)
        gbd, n2, mid, act, slope, gout = layer.mlp_up(
            tie(pos, hi3, y_lo3, x_lo3), segc, vec, inputs, mixed, cotangent, up
        )
        y_hi3, x_hi3, d_lo3 = hold((y_hi3, x_hi3, d_lo3), gbd)
        d_hi3 = swap(x_hi3, BIT_Y)
        pair_down = layer.down_grad(tie(pos, y_hi3, x_hi3, d_lo3), act, gout)
        d_hi3 = tie(d_hi3, pair_down[0])
        down = gathered(lo3, hi3, y_lo3, y_hi3, x_lo3, x_hi3, d_lo3, d_hi3)
        scatter1 = Scatter(*pair_down, *down)
        gbu, gpre, *pair_up = layer.mlp_down(pos, gout, slope, n2, down)
        scatter1.first(gbu)
        sums, gmid, gmixed, *pair_up = layer.mid_backward(
            tie(pos, *scatter1.out), vec, gbd, gbu, gpre, gout, mid, mixed, up, *pair_up
        )
        scatter1.second(sums)
        scatter2 = Scatter(*pair_up, scatter1.in_y, scatter1.in_x)
        gbq, gqkv = layer.attn_backward(tie(pos, *scatter1.out), gmixed, qkv, soft)
        scatter2.first(gbq)
        scatter1.third(gbq)
        input_grad, *pair_attn = layer.qkv_grad(
            tie(pos, *scatter2.out, *scatter1.out), vec, sums, gbq, gmid, gqkv, n1, inputs, attn
        )
        scatter2.second(input_grad)
        scatter1.fourth(input_grad)
        scatter3 = Scatter(*pair_attn, scatter2.in_y, scatter2.in_x, *scatter1.out)
        scatter3.diagonal(*scatter2.out, *scatter1.out)
        layer_out = layer.layer_out(tie(pos, *scatter3.out), vec, act, mid, down)
        scatter2.third(layer_out)
        scatter1.fifth(layer_out)
        scatter3.hi(*scatter2.out)
        scatter2.fourth(*scatter3.out)
        scatter3.lo(*scatter2.out)
        scatter2.fifth(*scatter3.out)
        scatter3.fourth(*scatter2.out)
        scatter3.fifth()

        def exchange(blocks, axis):
            first, second = jnp.split(blocks, 2, axis=axis)
            keep = jnp.where(core == 0, first, second)
            got = swap(jnp.where(core == 0, second, first), 0)
            return jnp.where(core == 0, keep, got), jnp.where(core == 0, got, keep)

        grad_w_down = jnp.concatenate(exchange(scatter1.result(*scatter3.out), 0), axis=1)
        lo, hi = exchange(scatter2.result(*scatter3.out), 1)
        both = jnp.stack([lo, hi])
        grad_w_up = both[:, :4].reshape(2, 2, 2, per, HALF).transpose(3, 0, 2, 1, 4).reshape(per, FF)
        grad_w_out = both[:, 4].transpose(1, 0, 2).reshape(per, D)
        grad_w_qkv, eight, grad_b_up, grad_b_down = layer.finish(pos, scatter3.in_z, scatter3.near)
        grad_b_up, grad_b_down = grad_b_up[0], grad_b_down[0]
    return (
        layer_out, input_grad, eight[0], eight[1], grad_w_qkv, eight[2], eight[4], grad_w_out, eight[5],
        eight[6], eight[7], grad_w_up, grad_b_up, grad_w_down, grad_b_down,
    )


def solution(mesh):
    both = P(AXES, None)
    one = P(AXES)
    tuned = dict(mesh.shape) == {"wide": 8, "narrow": 4}
    in_specs = (both, both, one, one, both, one, one, both, one, one, one, both, one, both, one, both)
    out_specs = (both, both, one, one, both, one, one, both, one, one, one, both, one, both, one)
    return jax.shard_map(
        functools.partial(per_device, tuned),
        mesh=mesh,
        in_specs=in_specs,
        out_specs=out_specs,
        check_vma=False,
    )
```

```python
import functools
import math

import jax
import jax.numpy as jnp
from jax import lax
from jax.experimental import pallas as pl
from jax.experimental.pallas import tpu as pltpu
from jax.sharding import PartitionSpec as P

HEADS = 12
HEAD_DIM = 64
D = 768
FF = 3072
ROW_LEN = 256
HALF = 384
CHIPS = 16
BLK = 48
PAIRS = HEADS // 2
AXES = ("wide", "narrow")

EPS = 1e-06
MASKED = -1e30
F32 = jnp.float32
BF16 = jnp.bfloat16

BIT_Y, BIT_X, BIT_Z0, BIT_Z1 = 1, 2, 4, 8
Z_OFFSETS = (0, 4, 8, 12)

GATHER = tuple((o + z, o + z + BIT_Z0) for o in (0, BIT_Y, BIT_X, BIT_X + BIT_Y) for z in (0, BIT_Z1))
PIECES = 2 * len(GATHER)

SCATTER = (0, 4, 12, 8, 1, 5, 14, 10, 13, 9, 15, 11, 2, 6, 3, 7)


def nt(a, b):
    return lax.dot_general(a, b, (((1,), (1,)), ((), ())), preferred_element_type=F32)


def tn(a, b):
    return lax.dot_general(a, b, (((0,), (0,)), ((), ())), preferred_element_type=F32)


def nn(a, b):
    return lax.dot_general(a, b, (((1,), (0,)), ((), ())), preferred_element_type=F32)


def chunks(tokens, step, body):
    def one(i, carry):
        body(pl.ds(pl.multiple_of(i * step, step), step))
        return carry

    lax.fori_loop(0, tokens // step, one, 0)


def norm_parts(v):
    centre = jnp.mean(v, axis=-1, keepdims=True)
    centred = v - centre
    scale = lax.rsqrt(jnp.mean(centred * centred, axis=-1, keepdims=True) + EPS)
    return centred * scale, scale


def start(src, dst, sem):
    copy = pltpu.make_async_copy(src, dst, sem)
    copy.start()
    return copy


def whole_wait(ref, sem):
    pltpu.make_async_copy(ref, ref, sem).wait()


def each_block(pos_ref, pieces):
    for other in range(2):
        for ref, offsets in zip(pieces[other * len(GATHER) :], GATHER):
            for b, offset in enumerate(offsets):
                yield ref, b, pos_ref[0] ^ offset, other, offset


def chip_rows(chip, size):
    return pl.ds(pl.multiple_of(chip * size, 16), size)


def half_cols(pos_ref, other):
    return pl.ds(pl.multiple_of((pos_ref[1] ^ other) * HALF, 128), HALF)


def fetch_qkv(pos_ref, pieces, w_qkv, sems):
    for t in range(3):
        for ref, b, chip, other, _ in each_block(pos_ref, pieces):
            dst = w_qkv.at[t, chip_rows(chip, BLK), half_cols(pos_ref, other)]
            start(ref.at[b, pl.ds(t * BLK, BLK)], dst, sems.at[t])


def fetch_out(pos_ref, pieces, w_out, sem):
    for ref, b, chip, other, _ in each_block(pos_ref, pieces):
        dst = w_out.at[chip_rows(chip, BLK), half_cols(pos_ref, other)]
        start(ref.at[b, 4], dst, sem)


def fetch_small(pos_ref, pieces, small, sem):
    for ref, b, chip, other, _ in each_block(pos_ref, pieces):
        start(ref.at[b, pl.ds(3 * BLK, 16)], small.at[pos_ref[1] ^ other, chip], sem)


def fetch_up(pos_ref, pieces, w_up, sems):
    for ref, b, chip, other, _ in each_block(pos_ref, pieces):
        for u in range(2):
            dst = w_up.at[other, pl.ds(0, 2), chip_rows(chip, BLK), pl.ds(u * HALF, HALF)]
            start(ref.at[b, pl.ds(2 * u, 2)], dst, sems.at[other])


def fetch_down(pos_ref, pieces, w_down, sems):
    for q in range(4):
        for ref, b, chip, other, offset in each_block(pos_ref, pieces):
            if offset // 4 == q:
                dst = w_down.at[chip_rows(chip, 4 * BLK), half_cols(pos_ref, other)]
                start(ref.at[b], dst, sems.at[q])


def ring_place(z):
    return z ^ (z >> 1)


def scatter_place(pos_ref, chip):
    xy = (pos_ref[0] ^ chip) & 3
    z = (ring_place(chip >> 2) - ring_place(pos_ref[0] >> 2)) & 3
    near = jnp.where(xy == 1, 4, jnp.where(xy == 2, 12, 14)) + z
    far = jnp.where(xy == 1, 6, jnp.where(xy == 2, 4, 8)) + z
    return jnp.where(xy == 0, z, jnp.where(z < 2, near, far))


def qkv_forward_kernel(pos_ref, x_any, *refs):
    pieces, refs = refs[:PIECES], refs[PIECES:]
    vec_ref, n1_ref, qkv_ref, x_ref, w_qkv, small, sems = refs
    load_x = start(x_any, x_ref, sems.at[4])
    fetch_small(pos_ref, pieces, small, sems.at[0])
    fetch_qkv(pos_ref, pieces, w_qkv, sems.at[pl.ds(1, 3)])
    whole_wait(small, sems.at[0])
    for h in range(2):
        vec_ref[:, h * HALF : (h + 1) * HALF] = jnp.sum(small[h].astype(F32), axis=0)
    load_x.wait()

    def norm_one(rows):
        xhat, _ = norm_parts(x_ref[rows, :].astype(F32))
        n1_ref[rows, :] = (xhat * vec_ref[0:1, :] + vec_ref[1:2, :]).astype(BF16)

    chunks(x_ref.shape[0], 128, norm_one)
    for t in range(3):
        whole_wait(w_qkv.at[t], sems.at[1 + t])
        y = (nn(n1_ref[...], w_qkv[t]) + vec_ref[2 + t : 3 + t, :]).astype(BF16)
        if t == 0:
            y = y * BF16(HEAD_DIM**-0.5)
        qkv_ref[:, t * D : (t + 1) * D] = y


def head_masks():
    lane = lax.broadcasted_iota(jnp.int32, (1, 2 * HEAD_DIM), 1)
    return [(lane // HEAD_DIM == hh).astype(F32).astype(BF16) for hh in range(2)]


def pair_cols(t, i):
    return pl.ds(pl.multiple_of(t * D + i * 128, 128), 128)


def attention_kernel(pos_ref, segr_ref, segc_ref, qkv_ref, soft_ref, mixed_ref, bias):
    n_rows = qkv_ref.shape[0] // ROW_LEN
    for r in range(n_rows):
        same = segc_ref[r * ROW_LEN : (r + 1) * ROW_LEN] == segr_ref[r]
        bias[r] = jnp.where(same, 0.0, MASKED)
    masks = head_masks()
    for r in range(n_rows):
        rows = slice(r * ROW_LEN, (r + 1) * ROW_LEN)

        def pair(i, carry):
            q, k, v = (qkv_ref[rows, pair_cols(t, i)] for t in range(3))
            mixed = jnp.zeros((ROW_LEN, 128), F32)
            for hh, keep in enumerate(masks):
                s = nt(q, k * keep) + bias[r]
                e = jnp.exp(s - jnp.max(s, axis=-1, keepdims=True))
                p = (e * (1.0 / jnp.sum(e, axis=-1, keepdims=True))).astype(BF16)
                soft_ref[r * HEADS + 2 * i + hh] = p
                mixed = mixed + nn(p, v * keep)
            mixed_ref[rows, pair_cols(0, i)] = mixed.astype(BF16)
            return carry

        lax.fori_loop(0, PAIRS, pair, 0)


GELU_A = 0.7978845608028654
GELU_B = 0.044715


def quarter(pos_ref, other, s):
    return (pos_ref[1] ^ other) * 2 + s


def quarter_cols(z):
    return pl.ds(pl.multiple_of(z * D, 128), D)


QUARTERS = ((0, 0), (0, 1), (1, 0), (1, 1))


def mlp_up_kernel(pos_ref, segc_ref, vec_ref, mixed_ref, x_any, cot_any, *refs):
    pieces, refs = refs[:PIECES], refs[PIECES:]
    gb_ref, n2_ref, mid_ref, act_ref, slope_ref, gout_ref, x_ref, cot_ref, w_out, w_up, sems = refs
    tokens = n2_ref.shape[0]
    load_cot = start(cot_any, cot_ref, sems.at[3])
    load_x = start(x_any, x_ref, sems.at[4])
    fetch_out(pos_ref, pieces, w_out, sems.at[2])
    fetch_up(pos_ref, pieces, w_up, sems)
    load_cot.wait()
    valid = segc_ref[...] > 0
    gout = jnp.where(valid, cot_ref[...].astype(F32), 0.0)
    gout_ref[...] = gout.astype(BF16)
    gb_ref[...] = jnp.broadcast_to(jnp.sum(gout, axis=0, keepdims=True), gb_ref.shape)
    load_x.wait()
    whole_wait(w_out, sems.at[2])
    mid_ref[...] = x_ref[...].astype(F32) + nn(mixed_ref[...], w_out[...]) + vec_ref[5:6, :]

    def norm_two(rows):
        xhat, _ = norm_parts(mid_ref[rows, :])
        n2_ref[rows, :] = (xhat * vec_ref[6:7, :] + vec_ref[7:8, :]).astype(BF16)

    chunks(tokens, 128, norm_two)
    for other, s in QUARTERS:
        if s == 0:
            whole_wait(w_up.at[other], sems.at[other])
        z = quarter(pos_ref, other, s)
        b_up = vec_ref[pl.ds(8 + z, 1), :]
        cols = quarter_cols(z)

        def part(rows):
            u = nn(n2_ref[rows, :], w_up[other, s]) + b_up
            sq = u * u
            t = jnp.tanh(u * (GELU_A + GELU_A * GELU_B * sq))
            half_up = 0.5 + 0.5 * t
            act_ref[rows, cols] = (u * half_up).astype(BF16)
            slope_ref[rows, cols] = (
                half_up + u * (0.5 - 0.5 * t * t) * (GELU_A + 3.0 * GELU_A * GELU_B * sq)
            ).astype(BF16)

        chunks(tokens, 256, part)


def down_grad_kernel(pos_ref, act_ref, gout_ref, mine, theirs, grad, sem):
    for z in range(4):
        grad[z] = tn(act_ref[:, z * D : (z + 1) * D], gout_ref[...]).astype(BF16)
        for j in range(4):
            place = scatter_place(pos_ref, 4 * z + j)
            for other, out in enumerate((mine, theirs)):
                src = grad.at[z, pl.ds(j * 4 * BLK, 4 * BLK), half_cols(pos_ref, other)]
                start(src, out.at[place], sem.at[0])
    whole_wait(grad, sem.at[0])


def mlp_down_kernel(pos_ref, gout_ref, slope_ref, n2_ref, *refs):
    pieces, refs = refs[:PIECES], refs[PIECES:]
    gb_ref, gpre_ref, mine, theirs, n2t, w_down, grad, sems = refs
    fetch_down(pos_ref, pieces, w_down, sems)
    gb_ref[...] = jnp.zeros(gb_ref.shape, F32)
    n2t[...] = n2_ref[...].T
    for other, s in QUARTERS:
        z = quarter(pos_ref, other, s)
        cols = quarter_cols(z)
        whole_wait(w_down.at[cols], sems.at[z ^ (pos_ref[0] >> 2)])
        ga = nt(gout_ref[...], w_down[cols, :])
        gp = (ga * slope_ref[:, cols].astype(F32)).astype(BF16)
        gpre_ref[:, cols] = gp
        gb_ref[pl.ds(z, 1), :] = jnp.sum(gp.astype(F32), axis=0, keepdims=True)
        grad[other, s] = nn(n2t[...], gp).astype(BF16)
        if s == 1:
            for chip in range(CHIPS):
                place = scatter_place(pos_ref, chip)
                for u in range(2):
                    src = grad.at[other, pl.ds(0, 2), pl.ds(chip * BLK, BLK), pl.ds(u * HALF, HALF)]
                    start(src, (mine, theirs)[other].at[place, pl.ds(2 * u, 2)], sems.at[4])
    whole_wait(grad, sems.at[4])


def norm_back(grad, xhat, scale, gain):
    gn = grad * gain
    mean_gn = jnp.mean(gn, axis=-1, keepdims=True)
    mean_gx = jnp.mean(gn * xhat, axis=-1, keepdims=True)
    return scale * (gn - mean_gn - xhat * mean_gx)


def mid_backward_kernel(
    pos_ref, vec_ref, gbd_ref, gbu_ref, gpre_ref, gout_ref, mid_ref, mixed_ref, *refs
):
    pieces, refs = refs[:PIECES], refs[PIECES + 2 :]
    sums, gmid, gmixed, mine, theirs, w_up, w_out, acc, gbr, mixt, grad, sems = refs
    tokens = mid_ref.shape[0]
    fetch_up(pos_ref, pieces, w_up, sems)
    fetch_out(pos_ref, pieces, w_out, sems.at[2])
    sums[...] = jnp.zeros(sums.shape, F32)
    sums[8:12, :] = gbu_ref[0:4, :]
    sums[12:13, :] = gbd_ref[0:1, :]
    mixt[...] = mixed_ref[...].T
    for other, s in QUARTERS:
        if s == 0:
            whole_wait(w_up.at[other], sems.at[other])
        part = nt(gpre_ref[:, quarter_cols(quarter(pos_ref, other, s))], w_up[other, s])
        acc[...] = part if other + s == 0 else acc[...] + part

    def back_two(rows):
        xhat, scale = norm_parts(mid_ref[rows, :])
        g = acc[rows, :]
        sums[6:7, :] += jnp.sum(g * xhat, axis=0, keepdims=True)
        sums[7:8, :] += jnp.sum(g, axis=0, keepdims=True)
        gm = gout_ref[rows, :].astype(F32) + norm_back(g, xhat, scale, vec_ref[6:7, :])
        gmid[rows, :] = gm
        low = gm.astype(BF16)
        gbr[rows, :] = low
        sums[5:6, :] += jnp.sum(low.astype(F32), axis=0, keepdims=True)

    chunks(tokens, 128, back_two)
    grad[...] = nn(mixt[...], gbr[...]).astype(BF16)
    for chip in range(CHIPS):
        place = scatter_place(pos_ref, chip)
        for other, out in enumerate((mine, theirs)):
            src = grad.at[pl.ds(chip * BLK, BLK), half_cols(pos_ref, other)]
            start(src, out.at[place, 4], sems.at[3])
    whole_wait(w_out, sems.at[2])
    gmixed[...] = nt(gbr[...], w_out[...]).astype(BF16)
    whole_wait(grad, sems.at[3])


def attn_backward_kernel(pos_ref, gmixed, qkv_ref, soft_ref, gb_ref, gqkv):
    masks = head_masks()
    for r in range(gmixed.shape[0] // ROW_LEN):
        rows = slice(r * ROW_LEN, (r + 1) * ROW_LEN)

        def pair(i, carry):
            q, k, v = (qkv_ref[rows, pair_cols(t, i)] for t in range(3))
            gm = gmixed[rows, pair_cols(0, i)]
            dq = jnp.zeros((ROW_LEN, 128), F32)
            dk = jnp.zeros((ROW_LEN, 128), F32)
            dv = jnp.zeros((ROW_LEN, 128), F32)
            for hh, keep in enumerate(masks):
                p_low = soft_ref[r * HEADS + 2 * i + hh]
                p = p_low.astype(F32)
                gmk = gm * keep
                gs = nt(gmk, v)
                inner = jnp.sum(p * gs, axis=-1, keepdims=True)
                ds = (p * (gs - inner)).astype(BF16)
                dq = dq + nn(ds, k * keep)
                dk = dk + tn(ds, q * keep)
                dv = dv + tn(p_low, gmk)
            gqkv[rows, pair_cols(0, i)] = (dq * (HEAD_DIM**-0.5)).astype(BF16)
            gqkv[rows, pair_cols(1, i)] = dk.astype(BF16)
            gqkv[rows, pair_cols(2, i)] = dv.astype(BF16)
            return carry

        lax.fori_loop(0, PAIRS, pair, 0)
    gb_ref[...] = jnp.zeros(gb_ref.shape, F32)
    gb_ref[0:1, :] = jnp.sum(gqkv[:, :D].astype(F32), axis=0, keepdims=True)
    gb_ref[2:3, :] = jnp.sum(gqkv[:, 2 * D :].astype(F32), axis=0, keepdims=True)


def qkv_grad_kernel(
    pos_ref, vec_ref, sums_ref, gbq_ref, gmid, gqkv, n1_ref, x_any, *refs
):
    pieces, refs = refs[:PIECES], refs[PIECES:]
    igrad, mine, theirs, x_ref, w_qkv, acc, n1t, grad, sums, small, sems = refs
    fetch_qkv(pos_ref, pieces, w_qkv, sems.at[pl.ds(0, 3)])
    load_x = start(x_any, x_ref, sems.at[5])
    sums[...] = sums_ref[...]
    sums[2:3, :] = gbq_ref[0:1, :]
    sums[4:5, :] = gbq_ref[2:3, :]
    n1t[...] = n1_ref[...].T
    for t in range(3):
        grad[t] = nn(n1t[...], gqkv[:, t * D : (t + 1) * D]).astype(BF16)
        for chip in range(CHIPS):
            place = scatter_place(pos_ref, chip)
            for other, out in enumerate((mine, theirs)):
                src = grad.at[t, pl.ds(chip * BLK, BLK), half_cols(pos_ref, other)]
                start(src, out.at[place, pl.ds(t * BLK, BLK)], sems.at[3])
    for t in range(3):
        whole_wait(w_qkv.at[t], sems.at[t])
        part = nt(gqkv[:, t * D : (t + 1) * D], w_qkv[t])
        acc[...] = part if t == 0 else acc[...] + part
    load_x.wait()

    def back_one(rows):
        xhat, scale = norm_parts(x_ref[rows, :].astype(F32))
        g = acc[rows, :]
        sums[0:1, :] += jnp.sum(g * xhat, axis=0, keepdims=True)
        sums[1:2, :] += jnp.sum(g, axis=0, keepdims=True)
        igrad[rows, :] = (gmid[rows, :] + norm_back(g, xhat, scale, vec_ref[0:1, :])).astype(BF16)

    chunks(x_ref.shape[0], 128, back_one)
    for p in range(CHIPS):
        small[0, p] = sums[:, :HALF].astype(BF16)
        small[1, p] = sums[:, HALF:].astype(BF16)
    for other, out in enumerate((mine, theirs)):
        for p in range(CHIPS):
            start(small.at[pos_ref[1] ^ other, p], out.at[p, pl.ds(3 * BLK, 16)], sems.at[4])
    whole_wait(small, sems.at[4])
    whole_wait(grad, sems.at[3])


def layer_out_kernel(pos_ref, vec_ref, act_ref, mid_ref, *refs):
    pieces, refs = refs[:PIECES], refs[PIECES:]
    out_ref, w_down, acc, sems = refs
    fetch_down(pos_ref, pieces, w_down, sems)
    for q in range(4):
        rows = quarter_cols((pos_ref[0] >> 2) ^ q)
        whole_wait(w_down.at[rows], sems.at[q])
        part = nn(act_ref[:, rows], w_down[rows, :])
        if q == 0:
            acc[...] = part + (mid_ref[...] + vec_ref[12:13, :])
        elif q < 3:
            acc[...] = acc[...] + part
        else:
            out_ref[...] = (acc[...] + part).astype(BF16)


PER = D // (2 * CHIPS)
SEND_ROWS = (3 * PER, 16, 5 * PER, 4 * PER)


def pack_kernel(pos_ref, w_qkv, w_out, w_up, w_down, bu_ref, *refs):
    values, (mine, theirs, rows, last, wide) = refs[:8], refs[8:]
    place = pos_ref[0] * 2 + pos_ref[1]
    rows[...] = jnp.zeros(rows.shape, F32)
    last[...] = jnp.zeros(last.shape, F32)
    for r, value in zip((0, 1, 2, 4, 5, 6, 7, 12), values):
        rows[r : r + 1, 0:PER] = value[...].astype(F32)
    last[0:1, 0 : 4 * PER] = bu_ref[...].astype(F32)
    at = place * (4 * PER)
    up = pltpu.roll(last[...], at % D, 1)[0:1]
    here = lax.broadcasted_iota(jnp.int32, (16, 1), 0) == 8 + at // D
    rows[...] = pltpu.roll(rows[...], place * PER, 1) + jnp.where(here, up, 0.0)
    for out, other in ((mine, 0), (theirs, 1)):
        half = pos_ref[1] ^ other

        def cols(first):
            return pl.ds(pl.multiple_of(first + half * HALF, 128), HALF)

        at = 0
        for t in range(3):
            wide[at : at + PER, :] = w_qkv[:, cols(t * D)].astype(F32)
            at += PER
        wide[at : at + 16, :] = rows[:, cols(0)]
        at += 16
        for n in range(4):
            u, s = n // 2, n % 2
            first = pl.multiple_of(half * (2 * D) + s * D + u * HALF, 128)
            wide[at : at + PER, :] = w_up[:, pl.ds(first, HALF)].astype(F32)
            at += PER
        wide[at : at + PER, :] = w_out[:, cols(0)].astype(F32)
        at += PER
        wide[at : at + 4 * PER, :] = w_down[:, cols(0)].astype(F32)
        out[...] = wide[...].astype(BF16)


def combine_kernel(pos_ref, mine, got, one, two, three, upper, lower, wide):
    first = pos_ref[1] == 0
    m, g = mine[...].astype(F32), got[...].astype(F32)
    upper[...] = jnp.where(first, m, g)
    lower[...] = jnp.where(first, g, m)

    def pair(at, size):
        wide[0:size, :] = upper[at : at + size, :]
        wide[size : 2 * size, :] = lower[at : at + size, :]
        return wide[0 : 2 * size, :].astype(BF16)

    for t in range(3):
        one[t * BLK : (t + 1) * BLK, :] = pair(t * PER, PER)
    at = 3 * PER
    one[3 * BLK :, :] = (upper[at : at + 16, :] + lower[at : at + 16, :]).astype(BF16)
    at += 16
    for n in range(5):
        two[n] = pair(at + n * PER, PER)
    three[...] = pair(at + 5 * PER, 4 * PER)


def finish_kernel(pos_ref, last, *refs):
    terms, (keep, send, held, sems) = refs[:4], refs[4:]
    for i, term in enumerate(terms):
        start(term.at[0], held.at[i], sems.at[i])
    total = last[...].astype(F32)
    for i in range(4):
        whole_wait(held.at[i], sems.at[i])
        total = total + held[i].astype(F32)
    first = pos_ref[1] == 0
    for t in range(3):
        upper, lower = total[t * BLK : t * BLK + PER], total[t * BLK + PER : (t + 1) * BLK]
        keep[t * PER : (t + 1) * PER, :] = jnp.where(first, upper, lower)
        send[t * PER : (t + 1) * PER, :] = jnp.where(first, lower, upper)
    keep[3 * PER :, :] = total[3 * BLK :]
    send[3 * PER :, :] = total[3 * BLK :]


def spread_kernel(pos_ref, keep, got, w_ref, eight_ref, up_ref, down_ref, rows):
    place = pos_ref[0] * 2 + pos_ref[1]
    for ref, other in ((keep, 0), (got, 1)):
        half = pos_ref[1] ^ other
        for t in range(3):
            cols = pl.ds(pl.multiple_of(t * D + half * HALF, 128), HALF)
            w_ref[:, cols] = ref[t * PER : (t + 1) * PER, :]
        rows[:, pl.ds(pl.multiple_of(half * HALF, 128), HALF)] = ref[3 * PER :, :]
    mine = pltpu.roll(rows[...], lax.rem(D - place * PER, D), 1)
    eight_ref[...] = mine[0:8, 0:PER]
    down_ref[...] = mine[12:13, 0:PER]
    at = place * (4 * PER)
    here = lax.broadcasted_iota(jnp.int32, (16, 1), 0) == 8 + at // D
    row = jnp.sum(jnp.where(here, rows[...], 0.0), axis=0, keepdims=True)
    turned = pltpu.roll(jnp.broadcast_to(row, (8, D)), lax.rem(D - at % D, D), 1)
    up_ref[...] = turned[0:1, 0 : 4 * PER]


def call(kernel, name, near, far, near_outs, far_outs, scratch, flops, aliases=None, limit=26):
    far = [in_hbm(a) for a in far]
    space = pl.BlockSpec(memory_space=pltpu.VMEM)
    anyspec = pl.BlockSpec(memory_space=pl.ANY)
    outs = tuple(near_outs) + tuple(far_outs)
    moved = sum(math.prod(a.shape) * a.dtype.itemsize for a in (*near, *far, *outs))
    return pl.pallas_call(
        kernel,
        out_shape=outs,
        in_specs=[pl.BlockSpec(memory_space=pltpu.SMEM)]
        + [space] * (len(near) - 1)
        + [anyspec] * len(far),
        out_specs=[space] * len(near_outs) + [anyspec] * len(far_outs),
        scratch_shapes=scratch,
        input_output_aliases=aliases or {},
        compiler_params=pltpu.CompilerParams(vmem_limit_bytes=limit << 20),
        cost_estimate=pl.CostEstimate(flops=flops, bytes_accessed=moved, transcendentals=0),
        name=name,
    )(*near, *far)


def in_hbm(array):
    return pltpu.with_memory_space_constraint(array, pltpu.HBM)


def keep(*arrays):
    return [pltpu.with_memory_space_constraint(a, pltpu.VMEM) for a in arrays]


def swap(value, chip_bit):
    flip = chip_bit * 2 if chip_bit else 1
    return lax.ppermute(value, AXES, [(i, i ^ flip) for i in range(2 * CHIPS)])


def ring_step(value):
    follow = (1, 3, 0, 2)
    return lax.ppermute(value, AXES, [(i, follow[i // 8] * 8 + i % 8) for i in range(2 * CHIPS)])


def tie(value, *after):
    return lax.optimization_barrier((value,) + after)[0]


def gathered(*own_half):
    return list(own_half) + [swap(piece, 0) for piece in own_half]


def hold(pieces, *after):
    return lax.optimization_barrier((*pieces, *after))[: len(pieces)] if after else pieces


def rounded_sum(*terms):
    total = terms[0].astype(F32)
    for term in terms[1:]:
        total = total + term.astype(F32)
    return total.astype(BF16)


def small_grads(sums, place, per, per_up):
    eight = lax.dynamic_slice(sums, (0, place * per), (8, per))
    at = place * per_up
    up = lax.dynamic_slice(sums, (8 + at // D, at % D), (1, per_up))[0]
    down = lax.dynamic_slice(sums, (12, place * per), (1, per))[0]
    return eight, up, down


def halves(w_qkv, w_out, w_up, w_down):
    rows = w_qkv.shape[0]
    qkv = w_qkv.reshape(rows, 3, 2, HALF)
    up = w_up.reshape(rows, 2, 4, HALF)
    for h in range(2):
        cols = slice(h * HALF, (h + 1) * HALF)
        up_h = up[:, h].reshape(rows, 2, 2, HALF).transpose(2, 1, 0, 3).reshape(4, rows, HALF)
        yield (
            qkv[:, :, h].transpose(1, 0, 2),
            jnp.concatenate([up_h, w_out[None, :, cols]]),
            w_down[:, cols],
        )


def gather_plain(weights, values):
    def whole(w):
        return lax.all_gather(w, AXES, axis=0, tiled=True)

    gain1, bias1, bq, bv, bo, gain2, bias2, bu, bd = [whole(v) for v in values]
    rest = jnp.zeros((3, D), BF16)
    small = jnp.stack([gain1, bias1, bq, jnp.zeros_like(bq), bv, bo, gain2, bias2])
    small = jnp.concatenate([small, bu.reshape(4, D), bd[None], rest])
    groups = ([], [], [])
    for h, (attn, up, down) in enumerate(halves(*[whole(w) for w in weights])):
        attn = attn.reshape(3, CHIPS, BLK, HALF).transpose(1, 0, 2, 3).reshape(CHIPS, 3 * BLK, HALF)
        up = up.reshape(5, CHIPS, BLK, HALF).transpose(1, 0, 2, 3)
        down = down.reshape(CHIPS, 4 * BLK, HALF)
        extra = jnp.zeros((CHIPS, 16, HALF), BF16).at[0].set(small[:, h * HALF : (h + 1) * HALF])
        for group, blocks in zip(groups, (jnp.concatenate([attn, extra], axis=1), up, down)):
            group.extend(jnp.stack([blocks[o] for o in piece]) for piece in GATHER)
    return groups


def scatter_plain(pair, group):
    both = [jnp.stack([part[SCATTER.index(chip)] for chip in range(CHIPS)]) for part in pair]

    def scatter(v):
        return lax.psum_scatter(v.astype(F32), AXES, scatter_dimension=0, tiled=True)

    def matrix(units):
        return jnp.stack(units, axis=3).transpose(0, 2, 1, 3, 4).reshape(D, -1, 2, HALF)

    if group == "attn":
        sums = jnp.concatenate([b[0, 3 * BLK :] for b in both], axis=1)
        qkv = matrix([b[:, : 3 * BLK].reshape(CHIPS, 3, BLK, HALF) for b in both])
        return scatter(qkv.reshape(D, 3 * D)), lax.psum(sums.astype(F32), AXES)
    if group == "up":
        up = matrix(both)
        order = up[:, :4].reshape(D, 2, 2, 2, HALF).transpose(0, 3, 2, 1, 4)
        return scatter(order.reshape(D, FF)), scatter(up[:, 4].reshape(D, D))
    return scatter(jnp.concatenate([b.reshape(FF, HALF) for b in both], axis=1))


def shape(dims, kind=BF16):
    return jax.ShapeDtypeStruct(dims, kind)


def far_shape(*dims):
    return pltpu.HBM(dims, BF16)


def dma(n):
    return pltpu.SemaphoreType.DMA((n,))


def vmem(*dims, kind=BF16):
    return pltpu.VMEM(dims, kind)


class Layer:
    def __init__(self, tokens):
        self.tokens = tokens
        self.rows = tokens // ROW_LEN
        self.out = shape((tokens, D))
        self.wide = vmem(tokens, FF)
        self.one = vmem(tokens, D)
        self.one_f32 = vmem(tokens, D, kind=F32)
        self.qkv = vmem(tokens, 3 * D)
        self.soft = vmem(self.rows * HEADS, ROW_LEN, ROW_LEN)
        self.turned = vmem(D, tokens)
        self.square = vmem(D, D)
        self.three = vmem(3, D, D)
        self.four = vmem(2, 2, D, D)
        self.sums = vmem(8, D, kind=F32)
        self.vec = vmem(16, D, kind=F32)

    def chip_blocks(self, pos, weights, values):
        *rest, bu, bd = [in_hbm(v.reshape(1, -1)) for v in values]
        weights = [in_hbm(w) for w in weights]
        sent = shape((sum(SEND_ROWS), HALF))
        wide = vmem(sum(SEND_ROWS), HALF, kind=F32)
        mine, theirs = call(
            pack_kernel, "pack", (pos, *weights, bu, *rest, bd), (), (sent, sent), (),
            [vmem(16, D, kind=F32), vmem(8, D, kind=F32), wide], 0,
        )
        return call(
            combine_kernel, "combine", (pos, mine, swap(theirs, 0)), (),
            (shape((3 * BLK + 16, HALF)), shape((5, BLK, HALF)), shape((4 * BLK, HALF))), (),
            [wide, wide, vmem(4 * BLK, HALF, kind=F32)], 0,
        )

    def finish(self, pos, last, low):
        sent = shape((3 * PER + 16, HALF), F32)
        keep, send = call(
            finish_kernel, "finish", (pos, last), low, (sent, sent), (),
            [vmem(4, 3 * PER * 2 + 16, HALF), dma(4)], 0,
        )
        return call(
            spread_kernel, "spread", (pos, keep, swap(send, 0)), (),
            (shape((PER, 3 * D), F32), shape((8, PER), F32), shape((1, 4 * PER), F32), shape((1, PER), F32)),
            (), [vmem(16, D, kind=F32)], 0,
        )

    def qkv_forward(self, pos, inputs, attn):
        return call(
            qkv_forward_kernel, "qkv_forward", (pos,), [inputs] + attn, (self.vec, self.one, self.qkv), (),
            [self.one, self.three, vmem(2, CHIPS, 16, HALF), dma(5)],
            2 * self.tokens * D * D * 3,
        )

    def attention(self, pos, segr, segc, qkv):
        return call(
            attention_kernel, "attention", (pos, segr, segc, *keep(qkv)), [], (self.soft, self.one), (),
            [vmem(self.rows, ROW_LEN, ROW_LEN, kind=F32)],
            8 * self.tokens * D * ROW_LEN,
        )

    def mlp_up(self, pos, segc, vec, inputs, mixed, cotangent, up):
        vec, mixed = keep(vec, mixed)
        return call(
            mlp_up_kernel, "mlp_up", (pos, segc, vec, mixed), [inputs, cotangent] + up,
            (self.sums, self.one, self.one_f32, self.wide, self.wide, self.one), (),
            [self.one, self.one, self.square, self.four, dma(5)],
            2 * self.tokens * D * (FF + D),
        )

    def down_grad(self, pos, act, gout):
        buffer = far_shape(CHIPS, 4 * BLK, HALF)
        return call(
            down_grad_kernel, "down_grad", (pos, *keep(act, gout)), [], (), (buffer, buffer),
            [vmem(4, D, D), dma(1)],
            2 * self.tokens * D * FF,
        )

    def mlp_down(self, pos, gout, slope, n2, down):
        buffer = far_shape(CHIPS, 5, BLK, HALF)
        return call(
            mlp_down_kernel, "mlp_down", (pos, *keep(gout, slope, n2)), down,
            (self.sums, self.wide), (buffer, buffer),
            [self.turned, vmem(FF, D), self.four, dma(5)],
            4 * self.tokens * D * FF,
        )

    def mid_backward(self, pos, vec, gbd, gbu, gpre, gout, mid, mixed, up, mine, theirs):
        buffer = far_shape(*mine.shape)
        far = up + [mine, theirs]
        near = (pos, *keep(vec, gbd, gbu, gpre, gout, mid, mixed))
        return call(
            mid_backward_kernel, "mid_backward", near, far,
            (self.vec, self.one_f32, self.one), (buffer, buffer),
            [self.four, self.square, self.one_f32, self.one, self.turned, self.square, dma(4)],
            2 * self.tokens * D * (FF + 2 * D),
            {len(near) + len(up): 3, len(near) + len(up) + 1: 4},
        )

    def attn_backward(self, pos, gmixed, qkv, soft):
        return call(
            attn_backward_kernel, "attn_backward", (pos, *keep(gmixed, qkv, soft)), [],
            (self.sums, self.qkv), (), [], 20 * self.tokens * D * ROW_LEN,
        )

    def qkv_grad(self, pos, vec, sums, gbq, gmid, gqkv, n1, inputs, attn):
        buffer = far_shape(CHIPS, 3 * BLK + 16, HALF)
        return call(
            qkv_grad_kernel, "qkv_grad", (pos, *keep(vec, sums, gbq, gmid, gqkv, n1)), [inputs] + attn,
            (self.out,), (buffer, buffer),
            [
                self.one, self.three, self.one_f32, self.turned, self.three,
                vmem(16, D, kind=F32), vmem(2, CHIPS, 16, HALF), dma(6),
            ],
            2 * self.tokens * D * 6 * D,
        )

    def layer_out(self, pos, vec, act, mid, down):
        (out,) = call(
            layer_out_kernel, "layer_out", (pos, *keep(vec, act, mid)), down, (self.out,), (),
            [vmem(FF, D), self.one_f32, dma(4)],
            2 * self.tokens * D * FF,
        )
        return out


class Scatter:
    def __init__(self, mine, theirs, *after):
        self.mine = mine
        self.got = swap(tie(theirs, *after), 0)

    def part(self, first, last):
        return self.mine[first:last], self.got[first:last]

    def first(self, *after):
        self.got = hold((self.got,), *after)[0]
        self.out = (rounded_sum(*self.part(8, 12)), rounded_sum(*self.part(12, 16)))
        self.in_y, self.in_x = swap(self.out[0], BIT_Y), swap(self.out[1], BIT_X)

    def second(self, *after):
        in_y, in_x = hold((self.in_y, self.in_x), *after)
        self.out = (
            rounded_sum(*self.part(4, 6), in_x[2:]),
            rounded_sum(*self.part(6, 8), in_y[2:]),
        )
        self.in_y, self.in_x = in_y, in_x
        self.in_y2, self.in_x2 = swap(self.out[0], BIT_Y), swap(self.out[1], BIT_X)

    def third(self, *after):
        in_y2, in_x2 = hold((self.in_y2, self.in_x2), *after)
        self.near = (*self.part(0, 2), self.in_x[:2], in_y2)
        self.far = (*self.part(2, 4), self.in_y[:2], in_x2)
        self.out = (rounded_sum(*[t[1] for t in self.far]),)
        self.in_z = ring_step(self.out[0])

    def diagonal(self, *after):
        self.got = hold((self.got,), *after)[0]
        self.out = (rounded_sum(*self.part(10, 12)), rounded_sum(*self.part(14, 16)))
        self.in_y, self.in_x = swap(self.out[0], BIT_Y), swap(self.out[1], BIT_X)

    def hi(self, *after):
        in_y, self.in_x = hold((self.in_y, self.in_x), *after)
        self.out = (rounded_sum(*self.part(8, 10)), rounded_sum(*self.part(6, 8), in_y))
        self.in_y2, self.in_x2 = swap(self.out[0], BIT_Y), swap(self.out[1], BIT_X)

    def lo(self, *after):
        in_y2, in_x2 = hold((self.in_y2, self.in_x2), *after)
        self.far = (*self.part(2, 4), in_y2, in_x2)
        ring = rounded_sum(*[t[1] for t in self.far])
        self.in_z = ring_step(ring)
        low_y, low_x = rounded_sum(*self.part(4, 6), self.in_x), rounded_sum(*self.part(12, 14))
        low_y, low_x = hold((low_y, low_x), ring)
        self.out = (ring, low_y, low_x)
        self.near = (*self.part(0, 2), swap(low_y, BIT_Y), swap(low_x, BIT_X))

    def fourth(self, *after):
        in_z = hold((self.in_z,), *after)[0]
        self.out = (rounded_sum(*[t[0] for t in self.far], in_z),)
        self.in_z = ring_step(self.out[0])

    def fifth(self, *after):
        in_z = hold((self.in_z,), *after)[0]
        self.out = (rounded_sum(*[t[1] for t in self.near], in_z),)
        self.in_z = ring_step(self.out[0])

    def result(self, *after):
        total = hold((self.in_z,), *after)[0].astype(F32)
        for term in self.near:
            total = total + term[0].astype(F32)
        return total


def per_device(tuned, *args):
    (
        inputs, segment_ids, pre_attn_gain, pre_attn_bias, w_qkv, b_query, b_value, w_out, b_out,
        pre_mlp_gain, pre_mlp_bias, w_up, b_up, w_down, b_down, cotangent,
    ) = args
    tokens = inputs.shape[0]
    n_rows = tokens // ROW_LEN
    wide, narrow = lax.axis_index("wide"), lax.axis_index("narrow")
    weights = (w_qkv, w_out, w_up, w_down)
    values = (
        pre_attn_gain, pre_attn_bias, b_query, b_value, b_out, pre_mlp_gain, pre_mlp_bias, b_up, b_down,
    )
    per, per_up = pre_attn_gain.shape[0], b_up.shape[0]
    position = jnp.arange(ROW_LEN, dtype=jnp.int32)[None]
    own_id = jnp.where(segment_ids != 0, segment_ids, -1 - position)
    segr = own_id.reshape(n_rows, 1, ROW_LEN)
    segc = own_id.reshape(tokens, 1)
    layer = Layer(tokens)

    if not tuned:
        place = wide * lax.axis_size("narrow") + narrow
        pos = jnp.zeros((2,), jnp.int32)
        attn, up, down = gather_plain(weights, values)
        vec, n1, qkv = layer.qkv_forward(pos, inputs, attn)
        soft, mixed = layer.attention(pos, segr, segc, qkv)
        gbd, n2, mid, act, slope, gout = layer.mlp_up(pos, segc, vec, inputs, mixed, cotangent, up)
        pair_down = layer.down_grad(pos, act, gout)
        gbu, gpre, *pair_up = layer.mlp_down(pos, gout, slope, n2, down)
        sums, gmid, gmixed, *pair_up = layer.mid_backward(
            pos, vec, gbd, gbu, gpre, gout, mid, mixed, up, *pair_up
        )
        gbq, gqkv = layer.attn_backward(pos, gmixed, qkv, soft)
        input_grad, *pair_attn = layer.qkv_grad(pos, vec, sums, gbq, gmid, gqkv, n1, inputs, attn)
        layer_out = layer.layer_out(pos, vec, act, mid, down)
        grad_w_down = scatter_plain(pair_down, "down")
        grad_w_up, grad_w_out = scatter_plain(pair_up, "up")
        grad_w_qkv, sums = scatter_plain(pair_attn, "attn")
        eight, grad_b_up, grad_b_down = small_grads(sums, place, per, per_up)
    else:
        core = (narrow & 1).astype(jnp.int32)
        pos = jnp.stack([wide * 2 + (narrow >> 1), core]).astype(jnp.int32)
        block1, block2, block3 = layer.chip_blocks(pos, weights, values)

        near1 = swap(block1, BIT_Z0)
        lo1 = jnp.stack([block1, near1])
        hi1 = swap(lo1, BIT_Z1)
        y_lo1, x_lo1 = swap(lo1, BIT_Y), swap(lo1, BIT_X)
        near2 = swap(tie(block2, near1), BIT_Z0)
        d_lo1 = swap(y_lo1, BIT_X)
        y_hi1, x_hi1 = swap(hi1, BIT_Y), swap(hi1, BIT_X)
        lo2 = jnp.stack([block2, near2])
        hi2 = swap(tie(lo2, hi1), BIT_Z1)
        d_hi1 = swap(x_hi1, BIT_Y)
        lo2b = tie(lo2, d_lo1, x_hi1)
        y_lo2, x_lo2 = swap(lo2b, BIT_Y), swap(lo2b, BIT_X)
        near3 = swap(tie(block3, d_hi1), BIT_Z0)
        attn = gathered(lo1, hi1, y_lo1, y_hi1, x_lo1, x_hi1, d_lo1, d_hi1)
        lo3 = jnp.stack([block3, near3])
        hi3 = swap(tie(lo3, hi2), BIT_Z1)
        d_lo2 = swap(y_lo2, BIT_X)
        y_hi2, x_hi2 = swap(hi2, BIT_Y), swap(hi2, BIT_X)
        vec, n1, qkv = layer.qkv_forward(tie(pos, hi2, y_lo2, x_lo2), inputs, attn)

        y_hi2, x_hi2, d_lo2 = hold((y_hi2, x_hi2, d_lo2), vec)
        d_hi2 = swap(x_hi2, BIT_Y)
        lo3b = tie(lo3, y_hi2, x_hi2, d_lo2)
        y_lo3, x_lo3 = swap(lo3b, BIT_Y), swap(lo3b, BIT_X)
        soft, mixed = layer.attention(tie(pos, lo3b), segr, segc, qkv)

        d_hi2, y_lo3, x_lo3, hi3 = hold((d_hi2, y_lo3, x_lo3, hi3), mixed)
        d_lo3 = swap(y_lo3, BIT_X)
        y_hi3, x_hi3 = swap(hi3, BIT_Y), swap(hi3, BIT_X)
        lo2, hi2, y_lo2, y_hi2, x_lo2, x_hi2, d_lo2 = hold(
            (lo2, hi2, y_lo2, y_hi2, x_lo2, x_hi2, d_lo2), x_lo3, hi3
        )
        up = gathered(lo2, hi2, y_lo2, y_hi2, x_lo2, x_hi2, d_lo2, d_hi2)
        gbd, n2, mid, act, slope, gout = layer.mlp_up(
            tie(pos, hi3, y_lo3, x_lo3), segc, vec, inputs, mixed, cotangent, up
        )
        y_hi3, x_hi3, d_lo3 = hold((y_hi3, x_hi3, d_lo3), gbd)
        d_hi3 = swap(x_hi3, BIT_Y)
        pair_down = layer.down_grad(tie(pos, y_hi3, x_hi3, d_lo3), act, gout)
        d_hi3 = tie(d_hi3, pair_down[0])
        down = gathered(lo3, hi3, y_lo3, y_hi3, x_lo3, x_hi3, d_lo3, d_hi3)
        scatter1 = Scatter(*pair_down, *down)
        gbu, gpre, *pair_up = layer.mlp_down(pos, gout, slope, n2, down)
        scatter1.first(gbu)
        sums, gmid, gmixed, *pair_up = layer.mid_backward(
            tie(pos, *scatter1.out), vec, gbd, gbu, gpre, gout, mid, mixed, up, *pair_up
        )
        scatter1.second(sums)
        scatter2 = Scatter(*pair_up, scatter1.in_y, scatter1.in_x)
        gbq, gqkv = layer.attn_backward(tie(pos, *scatter1.out), gmixed, qkv, soft)
        scatter2.first(gbq)
        scatter1.third(gbq)
        input_grad, *pair_attn = layer.qkv_grad(
            tie(pos, *scatter2.out, *scatter1.out), vec, sums, gbq, gmid, gqkv, n1, inputs, attn
        )
        scatter2.second(input_grad)
        scatter1.fourth(input_grad)
        scatter3 = Scatter(*pair_attn, scatter2.in_y, scatter2.in_x, *scatter1.out)
        scatter3.diagonal(*scatter2.out, *scatter1.out)
        layer_out = layer.layer_out(tie(pos, *scatter3.out), vec, act, mid, down)
        scatter2.third(layer_out)
        scatter1.fifth(layer_out)
        scatter3.hi(*scatter2.out)
        scatter2.fourth(*scatter3.out)
        scatter3.lo(*scatter2.out)
        scatter2.fifth(*scatter3.out)
        scatter3.fourth(*scatter2.out)
        scatter3.fifth()

        def exchange(blocks, axis):
            first, second = jnp.split(blocks, 2, axis=axis)
            keep = jnp.where(core == 0, first, second)
            got = swap(jnp.where(core == 0, second, first), 0)
            return jnp.where(core == 0, keep, got), jnp.where(core == 0, got, keep)

        grad_w_down = jnp.concatenate(exchange(scatter1.result(*scatter3.out), 0), axis=1)
        lo, hi = exchange(scatter2.result(*scatter3.out), 1)
        both = jnp.stack([lo, hi])
        grad_w_up = both[:, :4].reshape(2, 2, 2, per, HALF).transpose(3, 0, 2, 1, 4).reshape(per, FF)
        grad_w_out = both[:, 4].transpose(1, 0, 2).reshape(per, D)
        grad_w_qkv, eight, grad_b_up, grad_b_down = layer.finish(
            pos, scatter3.in_z, [scatter3.mine, scatter3.got, *scatter3.near[2:]]
        )
        grad_b_up, grad_b_down = grad_b_up[0], grad_b_down[0]
    return (
        layer_out, input_grad, eight[0], eight[1], grad_w_qkv, eight[2], eight[4], grad_w_out, eight[5],
        eight[6], eight[7], grad_w_up, grad_b_up, grad_w_down, grad_b_down,
    )


def solution(mesh):
    both = P(AXES, None)
    one = P(AXES)
    tuned = dict(mesh.shape) == {"wide": 8, "narrow": 4}
    in_specs = (both, both, one, one, both, one, one, both, one, one, one, both, one, both, one, both)
    out_specs = (both, both, one, one, both, one, one, both, one, one, one, both, one, both, one)
    return jax.shard_map(
        functools.partial(per_device, tuned),
        mesh=mesh,
        in_specs=in_specs,
        out_specs=out_specs,
        check_vma=False,
    )
```

```python
import functools
import math

import jax
import jax.numpy as jnp
from jax import lax
from jax.experimental import pallas as pl
from jax.experimental.pallas import tpu as pltpu
from jax.sharding import PartitionSpec as P

HEADS = 12
HEAD_DIM = 64
D = 768
FF = 3072
ROW_LEN = 256
HALF = 384
CHIPS = 16
BLK = 48
PAIRS = HEADS // 2
AXES = ("wide", "narrow")

EPS = 1e-06
MASKED = -1e30
F32 = jnp.float32
BF16 = jnp.bfloat16

BIT_Y, BIT_X, BIT_Z0, BIT_Z1 = 1, 2, 4, 8
Z_OFFSETS = (0, 4, 8, 12)

GATHER = tuple((o + z, o + z + BIT_Z1) for o in (0, BIT_Y, BIT_X, BIT_X + BIT_Y) for z in (0, BIT_Z0))
PIECES = 2 * len(GATHER)

SCATTER = (0, 8, 4, 12, 1, 9, 6, 14, 5, 13, 7, 15, 2, 10, 3, 11)


def nt(a, b):
    return lax.dot_general(a, b, (((1,), (1,)), ((), ())), preferred_element_type=F32)


def tn(a, b):
    return lax.dot_general(a, b, (((0,), (0,)), ((), ())), preferred_element_type=F32)


def nn(a, b):
    return lax.dot_general(a, b, (((1,), (0,)), ((), ())), preferred_element_type=F32)


def chunks(tokens, step, body):
    def one(i, carry):
        body(pl.ds(pl.multiple_of(i * step, step), step))
        return carry

    lax.fori_loop(0, tokens // step, one, 0)


def norm_parts(v):
    centre = jnp.mean(v, axis=-1, keepdims=True)
    centred = v - centre
    scale = lax.rsqrt(jnp.mean(centred * centred, axis=-1, keepdims=True) + EPS)
    return centred * scale, scale


def start(src, dst, sem):
    copy = pltpu.make_async_copy(src, dst, sem)
    copy.start()
    return copy


def whole_wait(ref, sem):
    pltpu.make_async_copy(ref, ref, sem).wait()


def each_block(pos_ref, pieces):
    for other in range(2):
        for ref, offsets in zip(pieces[other * len(GATHER) :], GATHER):
            for b, offset in enumerate(offsets):
                yield ref, b, pos_ref[0] ^ offset, other, offset


def chip_rows(chip, size):
    return pl.ds(pl.multiple_of(chip * size, 16), size)


def half_cols(pos_ref, other):
    return pl.ds(pl.multiple_of((pos_ref[1] ^ other) * HALF, 128), HALF)


def fetch_qkv(pos_ref, pieces, w_qkv, sems):
    for t in range(3):
        for ref, b, chip, other, _ in each_block(pos_ref, pieces):
            dst = w_qkv.at[t, chip_rows(chip, BLK), half_cols(pos_ref, other)]
            start(ref.at[b, pl.ds(t * BLK, BLK)], dst, sems.at[t])


def fetch_out(pos_ref, pieces, w_out, sem):
    for ref, b, chip, other, _ in each_block(pos_ref, pieces):
        dst = w_out.at[chip_rows(chip, BLK), half_cols(pos_ref, other)]
        start(ref.at[b, 4], dst, sem)


def fetch_small(pos_ref, pieces, small, sem):
    for ref, b, chip, other, _ in each_block(pos_ref, pieces):
        start(ref.at[b, pl.ds(3 * BLK, 16)], small.at[pos_ref[1] ^ other, chip], sem)


def fetch_up(pos_ref, pieces, w_up, sems):
    for ref, b, chip, other, _ in each_block(pos_ref, pieces):
        for u in range(2):
            dst = w_up.at[other, pl.ds(0, 2), chip_rows(chip, BLK), pl.ds(u * HALF, HALF)]
            start(ref.at[b, pl.ds(2 * u, 2)], dst, sems.at[other])


def fetch_down(pos_ref, pieces, w_down, sems):
    for q in range(4):
        for ref, b, chip, other, offset in each_block(pos_ref, pieces):
            if offset // 4 == q:
                dst = w_down.at[chip_rows(chip, 4 * BLK), half_cols(pos_ref, other)]
                start(ref.at[b], dst, sems.at[q])


def scatter_place(pos_ref, chip):
    offset = pos_ref[0] ^ chip
    xy, z = offset & 3, ((offset >> 2) & 1) * 2 + (offset >> 3)
    near = jnp.where(xy == 1, 4, jnp.where(xy == 2, 12, 14)) + z
    far = jnp.where(xy == 1, 6, jnp.where(xy == 2, 4, 8)) + z
    return jnp.where(xy == 0, z, jnp.where(z < 2, near, far))


def head_masks():
    lane = lax.broadcasted_iota(jnp.int32, (1, 2 * HEAD_DIM), 1)
    return [(lane // HEAD_DIM == hh).astype(F32).astype(BF16) for hh in range(2)]


def pair_cols(t, i):
    return pl.ds(pl.multiple_of(t * D + i * 128, 128), 128)


def attn_forward_kernel(pos_ref, segr_ref, segc_ref, x_any, *refs):
    pieces, refs = refs[:PIECES], refs[PIECES:]
    vec_ref, n1_ref, qkv_ref, soft_ref, mixed_ref, x_ref, w_qkv, small, bias, sems = refs
    tokens = x_ref.shape[0]
    n_rows = tokens // ROW_LEN
    load_x = start(x_any, x_ref, sems.at[4])
    fetch_small(pos_ref, pieces, small, sems.at[0])
    fetch_qkv(pos_ref, pieces, w_qkv, sems.at[pl.ds(1, 3)])
    for r in range(n_rows):
        same = segc_ref[r * ROW_LEN : (r + 1) * ROW_LEN] == segr_ref[r]
        bias[r] = jnp.where(same, 0.0, MASKED)
    whole_wait(small, sems.at[0])
    for h in range(2):
        vec_ref[:, h * HALF : (h + 1) * HALF] = jnp.sum(small[h].astype(F32), axis=0)
    load_x.wait()

    def norm_one(rows):
        xhat, _ = norm_parts(x_ref[rows, :].astype(F32))
        n1_ref[rows, :] = (xhat * vec_ref[0:1, :] + vec_ref[1:2, :]).astype(BF16)

    chunks(tokens, 128, norm_one)
    for t in range(3):
        whole_wait(w_qkv.at[t], sems.at[1 + t])
        y = (nn(n1_ref[...], w_qkv[t]) + vec_ref[2 + t : 3 + t, :]).astype(BF16)
        if t == 0:
            y = y * BF16(HEAD_DIM**-0.5)
        qkv_ref[:, t * D : (t + 1) * D] = y
    masks = head_masks()
    for r in range(n_rows):
        rows = slice(r * ROW_LEN, (r + 1) * ROW_LEN)

        def pair(i, carry):
            q, k, v = (qkv_ref[rows, pair_cols(t, i)] for t in range(3))
            mixed = jnp.zeros((ROW_LEN, 128), F32)
            for hh, keep in enumerate(masks):
                s = nt(q, k * keep) + bias[r]
                e = jnp.exp(s - jnp.max(s, axis=-1, keepdims=True))
                p = (e * (1.0 / jnp.sum(e, axis=-1, keepdims=True))).astype(BF16)
                soft_ref[r * HEADS + 2 * i + hh] = p
                mixed = mixed + nn(p, v * keep)
            mixed_ref[rows, pair_cols(0, i)] = mixed.astype(BF16)
            return carry

        lax.fori_loop(0, PAIRS, pair, 0)


GELU_A = 0.7978845608028654
GELU_B = 0.044715


def quarter(pos_ref, other, s):
    return (pos_ref[1] ^ other) * 2 + s


def quarter_cols(z):
    return pl.ds(pl.multiple_of(z * D, 128), D)


QUARTERS = ((0, 0), (0, 1), (1, 0), (1, 1))


def mlp_up_kernel(pos_ref, segc_ref, vec_ref, mixed_ref, x_any, cot_any, *refs):
    pieces, refs = refs[:PIECES], refs[PIECES:]
    gb_ref, n2_ref, mid_ref, act_ref, slope_ref, gout_ref, x_ref, cot_ref, w_out, w_up, sems = refs
    tokens = n2_ref.shape[0]
    load_cot = start(cot_any, cot_ref, sems.at[3])
    load_x = start(x_any, x_ref, sems.at[4])
    fetch_out(pos_ref, pieces, w_out, sems.at[2])
    fetch_up(pos_ref, pieces, w_up, sems)
    load_cot.wait()
    valid = segc_ref[...] > 0
    gout = jnp.where(valid, cot_ref[...].astype(F32), 0.0)
    gout_ref[...] = gout.astype(BF16)
    gb_ref[...] = jnp.broadcast_to(jnp.sum(gout, axis=0, keepdims=True), gb_ref.shape)
    load_x.wait()
    whole_wait(w_out, sems.at[2])
    mid_ref[...] = x_ref[...].astype(F32) + nn(mixed_ref[...], w_out[...]) + vec_ref[5:6, :]

    def norm_two(rows):
        xhat, _ = norm_parts(mid_ref[rows, :])
        n2_ref[rows, :] = (xhat * vec_ref[6:7, :] + vec_ref[7:8, :]).astype(BF16)

    chunks(tokens, 128, norm_two)
    for other, s in QUARTERS:
        if s == 0:
            whole_wait(w_up.at[other], sems.at[other])
        z = quarter(pos_ref, other, s)
        b_up = vec_ref[pl.ds(8 + z, 1), :]
        cols = quarter_cols(z)

        def part(rows):
            u = nn(n2_ref[rows, :], w_up[other, s]) + b_up
            sq = u * u
            t = jnp.tanh(u * (GELU_A + GELU_A * GELU_B * sq))
            half_up = 0.5 + 0.5 * t
            act_ref[rows, cols] = (u * half_up).astype(BF16)
            slope_ref[rows, cols] = (
                half_up + u * (0.5 - 0.5 * t * t) * (GELU_A + 3.0 * GELU_A * GELU_B * sq)
            ).astype(BF16)

        chunks(tokens, 256, part)


def down_grad_kernel(pos_ref, act_ref, gout_ref, mine, theirs, grad, sem):
    for z in range(4):
        grad[z] = tn(act_ref[:, z * D : (z + 1) * D], gout_ref[...]).astype(BF16)
        for j in range(4):
            place = scatter_place(pos_ref, 4 * z + j)
            for other, out in enumerate((mine, theirs)):
                src = grad.at[z, pl.ds(j * 4 * BLK, 4 * BLK), half_cols(pos_ref, other)]
                start(src, out.at[place], sem.at[0])
    whole_wait(grad, sem.at[0])


def mlp_down_kernel(pos_ref, gout_ref, slope_ref, n2_ref, *refs):
    pieces, refs = refs[:PIECES], refs[PIECES:]
    gb_ref, gpre_ref, mine, theirs, n2t, w_down, grad, sems = refs
    fetch_down(pos_ref, pieces, w_down, sems)
    gb_ref[...] = jnp.zeros(gb_ref.shape, F32)
    n2t[...] = n2_ref[...].T
    for other, s in QUARTERS:
        z = quarter(pos_ref, other, s)
        cols = quarter_cols(z)
        whole_wait(w_down.at[cols], sems.at[z ^ (pos_ref[0] >> 2)])
        ga = nt(gout_ref[...], w_down[cols, :])
        gp = (ga * slope_ref[:, cols].astype(F32)).astype(BF16)
        gpre_ref[:, cols] = gp
        gb_ref[pl.ds(z, 1), :] = jnp.sum(gp.astype(F32), axis=0, keepdims=True)
        grad[other, s] = nn(n2t[...], gp).astype(BF16)
        if s == 1:
            for chip in range(CHIPS):
                place = scatter_place(pos_ref, chip)
                for u in range(2):
                    src = grad.at[other, pl.ds(0, 2), pl.ds(chip * BLK, BLK), pl.ds(u * HALF, HALF)]
                    start(src, (mine, theirs)[other].at[place, pl.ds(2 * u, 2)], sems.at[4])
    whole_wait(grad, sems.at[4])


def norm_back(grad, xhat, scale, gain):
    gn = grad * gain
    mean_gn = jnp.mean(gn, axis=-1, keepdims=True)
    mean_gx = jnp.mean(gn * xhat, axis=-1, keepdims=True)
    return scale * (gn - mean_gn - xhat * mean_gx)


def mid_backward_kernel(
    pos_ref, vec_ref, gbd_ref, gbu_ref, gpre_ref, gout_ref, mid_ref, mixed_ref, *refs
):
    pieces, refs = refs[:PIECES], refs[PIECES + 2 :]
    sums, gmid, gmixed, mine, theirs, w_up, w_out, acc, gbr, mixt, grad, sems = refs
    tokens = mid_ref.shape[0]
    fetch_up(pos_ref, pieces, w_up, sems)
    fetch_out(pos_ref, pieces, w_out, sems.at[2])
    sums[...] = jnp.zeros(sums.shape, F32)
    sums[8:12, :] = gbu_ref[0:4, :]
    sums[12:13, :] = gbd_ref[0:1, :]
    mixt[...] = mixed_ref[...].T
    for other, s in QUARTERS:
        if s == 0:
            whole_wait(w_up.at[other], sems.at[other])
        part = nt(gpre_ref[:, quarter_cols(quarter(pos_ref, other, s))], w_up[other, s])
        acc[...] = part if other + s == 0 else acc[...] + part

    def back_two(rows):
        xhat, scale = norm_parts(mid_ref[rows, :])
        g = acc[rows, :]
        sums[6:7, :] += jnp.sum(g * xhat, axis=0, keepdims=True)
        sums[7:8, :] += jnp.sum(g, axis=0, keepdims=True)
        gm = gout_ref[rows, :].astype(F32) + norm_back(g, xhat, scale, vec_ref[6:7, :])
        gmid[rows, :] = gm
        low = gm.astype(BF16)
        gbr[rows, :] = low
        sums[5:6, :] += jnp.sum(low.astype(F32), axis=0, keepdims=True)

    chunks(tokens, 128, back_two)
    grad[...] = nn(mixt[...], gbr[...]).astype(BF16)
    for chip in range(CHIPS):
        place = scatter_place(pos_ref, chip)
        for other, out in enumerate((mine, theirs)):
            src = grad.at[pl.ds(chip * BLK, BLK), half_cols(pos_ref, other)]
            start(src, out.at[place, 4], sems.at[3])
    whole_wait(w_out, sems.at[2])
    gmixed[...] = nt(gbr[...], w_out[...]).astype(BF16)
    whole_wait(grad, sems.at[3])


def attn_backward_kernel(pos_ref, gmixed, qkv_ref, soft_ref, gb_ref, gqkv):
    masks = head_masks()
    for r in range(gmixed.shape[0] // ROW_LEN):
        rows = slice(r * ROW_LEN, (r + 1) * ROW_LEN)

        def pair(i, carry):
            q, k, v = (qkv_ref[rows, pair_cols(t, i)] for t in range(3))
            gm = gmixed[rows, pair_cols(0, i)]
            dq = jnp.zeros((ROW_LEN, 128), F32)
            dk = jnp.zeros((ROW_LEN, 128), F32)
            dv = jnp.zeros((ROW_LEN, 128), F32)
            for hh, keep in enumerate(masks):
                p_low = soft_ref[r * HEADS + 2 * i + hh]
                p = p_low.astype(F32)
                gmk = gm * keep
                gs = nt(gmk, v)
                inner = jnp.sum(p * gs, axis=-1, keepdims=True)
                ds = (p * (gs - inner)).astype(BF16)
                dq = dq + nn(ds, k * keep)
                dk = dk + tn(ds, q * keep)
                dv = dv + tn(p_low, gmk)
            gqkv[rows, pair_cols(0, i)] = (dq * (HEAD_DIM**-0.5)).astype(BF16)
            gqkv[rows, pair_cols(1, i)] = dk.astype(BF16)
            gqkv[rows, pair_cols(2, i)] = dv.astype(BF16)
            return carry

        lax.fori_loop(0, PAIRS, pair, 0)
    gb_ref[...] = jnp.zeros(gb_ref.shape, F32)
    gb_ref[0:1, :] = jnp.sum(gqkv[:, :D].astype(F32), axis=0, keepdims=True)
    gb_ref[2:3, :] = jnp.sum(gqkv[:, 2 * D :].astype(F32), axis=0, keepdims=True)


def qkv_grad_kernel(
    pos_ref, vec_ref, sums_ref, gbq_ref, gmid, gqkv, n1_ref, x_any, *refs
):
    pieces, refs = refs[:PIECES], refs[PIECES:]
    igrad, mine, theirs, x_ref, w_qkv, acc, n1t, grad, sums, small, sems = refs
    fetch_qkv(pos_ref, pieces, w_qkv, sems.at[pl.ds(0, 3)])
    load_x = start(x_any, x_ref, sems.at[5])
    sums[...] = sums_ref[...]
    sums[2:3, :] = gbq_ref[0:1, :]
    sums[4:5, :] = gbq_ref[2:3, :]
    n1t[...] = n1_ref[...].T
    for t in range(3):
        grad[t] = nn(n1t[...], gqkv[:, t * D : (t + 1) * D]).astype(BF16)
        for chip in range(CHIPS):
            place = scatter_place(pos_ref, chip)
            for other, out in enumerate((mine, theirs)):
                src = grad.at[t, pl.ds(chip * BLK, BLK), half_cols(pos_ref, other)]
                start(src, out.at[place, pl.ds(t * BLK, BLK)], sems.at[3])
    for t in range(3):
        whole_wait(w_qkv.at[t], sems.at[t])
        part = nt(gqkv[:, t * D : (t + 1) * D], w_qkv[t])
        acc[...] = part if t == 0 else acc[...] + part
    load_x.wait()

    def back_one(rows):
        xhat, scale = norm_parts(x_ref[rows, :].astype(F32))
        g = acc[rows, :]
        sums[0:1, :] += jnp.sum(g * xhat, axis=0, keepdims=True)
        sums[1:2, :] += jnp.sum(g, axis=0, keepdims=True)
        igrad[rows, :] = (gmid[rows, :] + norm_back(g, xhat, scale, vec_ref[0:1, :])).astype(BF16)

    chunks(x_ref.shape[0], 128, back_one)
    for p in range(CHIPS):
        small[0, p] = sums[:, :HALF].astype(BF16)
        small[1, p] = sums[:, HALF:].astype(BF16)
    for other, out in enumerate((mine, theirs)):
        for p in range(CHIPS):
            start(small.at[pos_ref[1] ^ other, p], out.at[p, pl.ds(3 * BLK, 16)], sems.at[4])
    whole_wait(small, sems.at[4])
    whole_wait(grad, sems.at[3])


def layer_out_kernel(pos_ref, vec_ref, act_ref, mid_ref, *refs):
    pieces, refs = refs[:PIECES], refs[PIECES:]
    out_ref, w_down, acc, sems = refs
    fetch_down(pos_ref, pieces, w_down, sems)
    for q in range(4):
        rows = quarter_cols((pos_ref[0] >> 2) ^ q)
        whole_wait(w_down.at[rows], sems.at[q])
        part = nn(act_ref[:, rows], w_down[rows, :])
        if q == 0:
            acc[...] = part + (mid_ref[...] + vec_ref[12:13, :])
        elif q < 3:
            acc[...] = acc[...] + part
        else:
            out_ref[...] = (acc[...] + part).astype(BF16)


PER = D // (2 * CHIPS)
SEND_ROWS = (3 * PER, 16, 5 * PER, 4 * PER)


def pack_kernel(pos_ref, w_qkv, w_out, w_up, w_down, bu_ref, *refs):
    values, (mine, theirs, rows, last, wide) = refs[:8], refs[8:]
    place = pos_ref[0] * 2 + pos_ref[1]
    rows[...] = jnp.zeros(rows.shape, F32)
    last[...] = jnp.zeros(last.shape, F32)
    for r, value in zip((0, 1, 2, 4, 5, 6, 7, 12), values):
        rows[r : r + 1, 0:PER] = value[...].astype(F32)
    last[0:1, 0 : 4 * PER] = bu_ref[...].astype(F32)
    at = place * (4 * PER)
    up = pltpu.roll(last[...], at % D, 1)[0:1]
    here = lax.broadcasted_iota(jnp.int32, (16, 1), 0) == 8 + at // D
    rows[...] = pltpu.roll(rows[...], place * PER, 1) + jnp.where(here, up, 0.0)
    for out, other in ((mine, 0), (theirs, 1)):
        half = pos_ref[1] ^ other

        def cols(first):
            return pl.ds(pl.multiple_of(first + half * HALF, 128), HALF)

        at = 0
        for t in range(3):
            wide[at : at + PER, :] = w_qkv[:, cols(t * D)].astype(F32)
            at += PER
        wide[at : at + 16, :] = rows[:, cols(0)]
        at += 16
        for n in range(4):
            u, s = n // 2, n % 2
            first = pl.multiple_of(half * (2 * D) + s * D + u * HALF, 128)
            wide[at : at + PER, :] = w_up[:, pl.ds(first, HALF)].astype(F32)
            at += PER
        wide[at : at + PER, :] = w_out[:, cols(0)].astype(F32)
        at += PER
        wide[at : at + 4 * PER, :] = w_down[:, cols(0)].astype(F32)
        out[...] = wide[...].astype(BF16)


def combine_kernel(pos_ref, mine, got, one, two, upper, lower, wide):
    first = pos_ref[1] == 0
    m, g = mine[...].astype(F32), got[...].astype(F32)
    upper[...] = jnp.where(first, m, g)
    lower[...] = jnp.where(first, g, m)

    def pair(at, size):
        wide[0:size, :] = upper[at : at + size, :]
        wide[size : 2 * size, :] = lower[at : at + size, :]
        return wide[0 : 2 * size, :].astype(BF16)

    for t in range(3):
        one[t * BLK : (t + 1) * BLK, :] = pair(t * PER, PER)
    at = 3 * PER
    one[3 * BLK :, :] = (upper[at : at + 16, :] + lower[at : at + 16, :]).astype(BF16)
    at += 16
    for n in range(5):
        two[n] = pair(at + n * PER, PER)
    low = pair(at + 5 * PER, 4 * PER)
    for n in range(4):
        two[5 + n] = low[n * BLK : (n + 1) * BLK]


def finish_kernel(pos_ref, last, *refs):
    terms, (keep, send, held, sems) = refs[:5], refs[5:]
    for i, term in enumerate(terms):
        start(term.at[0], held.at[i], sems.at[i])
    total = last[...].astype(F32)
    for i in range(5):
        whole_wait(held.at[i], sems.at[i])
        total = total + held[i].astype(F32)
    first = pos_ref[1] == 0
    for t in range(3):
        upper, lower = total[t * BLK : t * BLK + PER], total[t * BLK + PER : (t + 1) * BLK]
        keep[t * PER : (t + 1) * PER, :] = jnp.where(first, upper, lower)
        send[t * PER : (t + 1) * PER, :] = jnp.where(first, lower, upper)
    keep[3 * PER :, :] = total[3 * BLK :]
    send[3 * PER :, :] = total[3 * BLK :]


def spread_kernel(pos_ref, keep, got, w_ref, eight_ref, up_ref, down_ref, rows):
    place = pos_ref[0] * 2 + pos_ref[1]
    for ref, other in ((keep, 0), (got, 1)):
        half = pos_ref[1] ^ other
        for t in range(3):
            cols = pl.ds(pl.multiple_of(t * D + half * HALF, 128), HALF)
            w_ref[:, cols] = ref[t * PER : (t + 1) * PER, :]
        rows[:, pl.ds(pl.multiple_of(half * HALF, 128), HALF)] = ref[3 * PER :, :]
    mine = pltpu.roll(rows[...], lax.rem(D - place * PER, D), 1)
    eight_ref[...] = mine[0:8, 0:PER]
    down_ref[...] = mine[12:13, 0:PER]
    at = place * (4 * PER)
    here = lax.broadcasted_iota(jnp.int32, (16, 1), 0) == 8 + at // D
    row = jnp.sum(jnp.where(here, rows[...], 0.0), axis=0, keepdims=True)
    turned = pltpu.roll(jnp.broadcast_to(row, (8, D)), lax.rem(D - at % D, D), 1)
    up_ref[...] = turned[0:1, 0 : 4 * PER]


def spread_up_kernel(pos_ref, keep, got, up_ref, out_ref):
    for ref, other in ((keep, 0), (got, 1)):
        half = pos_ref[1] ^ other
        for n in range(4):
            first = half * (2 * D) + (n % 2) * D + (n // 2) * HALF
            up_ref[:, pl.ds(pl.multiple_of(first, 128), HALF)] = ref[n]
        out_ref[:, pl.ds(pl.multiple_of(half * HALF, 128), HALF)] = ref[4]


def call(kernel, name, near, far, near_outs, far_outs, scratch, flops, aliases=None, limit=26):
    far = [in_hbm(a) for a in far]
    space = pl.BlockSpec(memory_space=pltpu.VMEM)
    anyspec = pl.BlockSpec(memory_space=pl.ANY)
    outs = tuple(near_outs) + tuple(far_outs)
    moved = sum(math.prod(a.shape) * a.dtype.itemsize for a in (*near, *far, *outs))
    return pl.pallas_call(
        kernel,
        out_shape=outs,
        in_specs=[pl.BlockSpec(memory_space=pltpu.SMEM)]
        + [space] * (len(near) - 1)
        + [anyspec] * len(far),
        out_specs=[space] * len(near_outs) + [anyspec] * len(far_outs),
        scratch_shapes=scratch,
        input_output_aliases=aliases or {},
        compiler_params=pltpu.CompilerParams(vmem_limit_bytes=limit << 20),
        cost_estimate=pl.CostEstimate(flops=flops, bytes_accessed=moved, transcendentals=0),
        name=name,
    )(*near, *far)


def in_hbm(array):
    return pltpu.with_memory_space_constraint(array, pltpu.HBM)


def keep(*arrays):
    return [pltpu.with_memory_space_constraint(a, pltpu.VMEM) for a in arrays]


def swap(value, chip_bit):
    flip = chip_bit * 2 if chip_bit else 1
    return lax.ppermute(value, AXES, [(i, i ^ flip) for i in range(2 * CHIPS)])


def tie(value, *after):
    return lax.optimization_barrier((value,) + after)[0]


def gathered(*own_half):
    return list(own_half) + [swap(piece, 0) for piece in own_half]


def hold(pieces, *after):
    return lax.optimization_barrier((*pieces, *after))[: len(pieces)] if after else pieces


def rounded_sum(*terms):
    total = terms[0].astype(F32)
    for term in terms[1:]:
        total = total + term.astype(F32)
    return total.astype(BF16)


def small_grads(sums, place, per, per_up):
    eight = lax.dynamic_slice(sums, (0, place * per), (8, per))
    at = place * per_up
    up = lax.dynamic_slice(sums, (8 + at // D, at % D), (1, per_up))[0]
    down = lax.dynamic_slice(sums, (12, place * per), (1, per))[0]
    return eight, up, down


def halves(w_qkv, w_out, w_up, w_down):
    rows = w_qkv.shape[0]
    qkv = w_qkv.reshape(rows, 3, 2, HALF)
    up = w_up.reshape(rows, 2, 4, HALF)
    for h in range(2):
        cols = slice(h * HALF, (h + 1) * HALF)
        up_h = up[:, h].reshape(rows, 2, 2, HALF).transpose(2, 1, 0, 3).reshape(4, rows, HALF)
        yield (
            qkv[:, :, h].transpose(1, 0, 2),
            jnp.concatenate([up_h, w_out[None, :, cols]]),
            w_down[:, cols],
        )


def gather_plain(weights, values):
    def whole(w):
        return lax.all_gather(w, AXES, axis=0, tiled=True)

    gain1, bias1, bq, bv, bo, gain2, bias2, bu, bd = [whole(v) for v in values]
    rest = jnp.zeros((3, D), BF16)
    small = jnp.stack([gain1, bias1, bq, jnp.zeros_like(bq), bv, bo, gain2, bias2])
    small = jnp.concatenate([small, bu.reshape(4, D), bd[None], rest])
    groups = ([], [], [])
    for h, (attn, up, down) in enumerate(halves(*[whole(w) for w in weights])):
        attn = attn.reshape(3, CHIPS, BLK, HALF).transpose(1, 0, 2, 3).reshape(CHIPS, 3 * BLK, HALF)
        up = up.reshape(5, CHIPS, BLK, HALF).transpose(1, 0, 2, 3)
        down = down.reshape(CHIPS, 4 * BLK, HALF)
        extra = jnp.zeros((CHIPS, 16, HALF), BF16).at[0].set(small[:, h * HALF : (h + 1) * HALF])
        for group, blocks in zip(groups, (jnp.concatenate([attn, extra], axis=1), up, down)):
            group.extend(jnp.stack([blocks[o] for o in piece]) for piece in GATHER)
    return groups


def scatter_plain(pair, group):
    both = [jnp.stack([part[SCATTER.index(chip)] for chip in range(CHIPS)]) for part in pair]

    def scatter(v):
        return lax.psum_scatter(v.astype(F32), AXES, scatter_dimension=0, tiled=True)

    def matrix(units):
        return jnp.stack(units, axis=3).transpose(0, 2, 1, 3, 4).reshape(D, -1, 2, HALF)

    if group == "attn":
        sums = jnp.concatenate([b[0, 3 * BLK :] for b in both], axis=1)
        qkv = matrix([b[:, : 3 * BLK].reshape(CHIPS, 3, BLK, HALF) for b in both])
        return scatter(qkv.reshape(D, 3 * D)), lax.psum(sums.astype(F32), AXES)
    if group == "up":
        up = matrix(both)
        order = up[:, :4].reshape(D, 2, 2, 2, HALF).transpose(0, 3, 2, 1, 4)
        return scatter(order.reshape(D, FF)), scatter(up[:, 4].reshape(D, D))
    return scatter(jnp.concatenate([b.reshape(FF, HALF) for b in both], axis=1))


def shape(dims, kind=BF16):
    return jax.ShapeDtypeStruct(dims, kind)


def far_shape(*dims):
    return pltpu.HBM(dims, BF16)


def dma(n):
    return pltpu.SemaphoreType.DMA((n,))


def vmem(*dims, kind=BF16):
    return pltpu.VMEM(dims, kind)


class Layer:
    def __init__(self, tokens):
        self.tokens = tokens
        self.rows = tokens // ROW_LEN
        self.out = shape((tokens, D))
        self.wide = vmem(tokens, FF)
        self.one = vmem(tokens, D)
        self.one_f32 = vmem(tokens, D, kind=F32)
        self.qkv = vmem(tokens, 3 * D)
        self.soft = vmem(self.rows * HEADS, ROW_LEN, ROW_LEN)
        self.turned = vmem(D, tokens)
        self.square = vmem(D, D)
        self.three = vmem(3, D, D)
        self.four = vmem(2, 2, D, D)
        self.sums = vmem(8, D, kind=F32)
        self.vec = vmem(16, D, kind=F32)

    def chip_blocks(self, pos, weights, values):
        *rest, bu, bd = [in_hbm(v.reshape(1, -1)) for v in values]
        weights = [in_hbm(w) for w in weights]
        sent = shape((sum(SEND_ROWS), HALF))
        wide = vmem(sum(SEND_ROWS), HALF, kind=F32)
        mine, theirs = call(
            pack_kernel, "pack", (pos, *weights, bu, *rest, bd), (), (sent, sent), (),
            [vmem(16, D, kind=F32), vmem(8, D, kind=F32), wide], 0,
        )
        return call(
            combine_kernel, "combine", (pos, mine, swap(theirs, 0)), (),
            (shape((3 * BLK + 16, HALF)), shape((9, BLK, HALF))), (),
            [wide, wide, vmem(4 * BLK, HALF, kind=F32)], 0,
        )

    def finish(self, pos, last, low):
        sent = shape((3 * PER + 16, HALF), F32)
        keep, send = call(
            finish_kernel, "finish", (pos, last), low, (sent, sent), (),
            [vmem(5, 3 * PER * 2 + 16, HALF), dma(5)], 0,
        )
        return call(
            spread_kernel, "spread", (pos, keep, swap(send, 0)), (),
            (shape((PER, 3 * D), F32), shape((8, PER), F32), shape((1, 4 * PER), F32), shape((1, PER), F32)),
            (), [vmem(16, D, kind=F32)], 0,
        )

    def spread_up(self, pos, keep, got):
        return call(
            spread_up_kernel, "spread_up", (pos, keep, got), (),
            (shape((PER, FF), F32), shape((PER, D), F32)), (), [], 0,
        )

    def attn_forward(self, pos, segr, segc, inputs, attn):
        return call(
            attn_forward_kernel, "attn_forward", (pos, segr, segc), [in_hbm(inputs)] + attn,
            (self.vec, self.one, self.qkv, self.soft, self.one), (),
            [
                self.one, self.three, vmem(2, CHIPS, 16, HALF),
                vmem(self.rows, ROW_LEN, ROW_LEN, kind=F32), dma(5),
            ],
            2 * self.tokens * D * D * 3 + 8 * self.tokens * D * ROW_LEN,
        )

    def mlp_up(self, pos, segc, vec, inputs, mixed, cotangent, up):
        vec, mixed = keep(vec, mixed)
        return call(
            mlp_up_kernel, "mlp_up", (pos, segc, vec, mixed), [inputs, cotangent] + up,
            (self.sums, self.one, self.one_f32, self.wide, self.wide, self.one), (),
            [self.one, self.one, self.square, self.four, dma(5)],
            2 * self.tokens * D * (FF + D),
        )

    def down_grad(self, pos, act, gout):
        buffer = far_shape(CHIPS, 4 * BLK, HALF)
        return call(
            down_grad_kernel, "down_grad", (pos, *keep(act, gout)), [], (), (buffer, buffer),
            [vmem(4, D, D), dma(1)],
            2 * self.tokens * D * FF,
        )

    def mlp_down(self, pos, gout, slope, n2, down):
        buffer = far_shape(CHIPS, 5, BLK, HALF)
        return call(
            mlp_down_kernel, "mlp_down", (pos, *keep(gout, slope, n2)), down,
            (self.sums, self.wide), (buffer, buffer),
            [self.turned, vmem(FF, D), self.four, dma(5)],
            4 * self.tokens * D * FF,
        )

    def mid_backward(self, pos, vec, gbd, gbu, gpre, gout, mid, mixed, up, mine, theirs):
        buffer = far_shape(*mine.shape)
        far = up + [mine, theirs]
        near = (pos, *keep(vec, gbd, gbu, gpre, gout, mid, mixed))
        return call(
            mid_backward_kernel, "mid_backward", near, far,
            (self.vec, self.one_f32, self.one), (buffer, buffer),
            [self.four, self.square, self.one_f32, self.one, self.turned, self.square, dma(4)],
            2 * self.tokens * D * (FF + 2 * D),
            {len(near) + len(up): 3, len(near) + len(up) + 1: 4},
        )

    def attn_backward(self, pos, gmixed, qkv, soft):
        return call(
            attn_backward_kernel, "attn_backward", (pos, *keep(gmixed, qkv, soft)), [],
            (self.sums, self.qkv), (), [], 20 * self.tokens * D * ROW_LEN,
        )

    def qkv_grad(self, pos, vec, sums, gbq, gmid, gqkv, n1, inputs, attn):
        buffer = far_shape(CHIPS, 3 * BLK + 16, HALF)
        return call(
            qkv_grad_kernel, "qkv_grad", (pos, *keep(vec, sums, gbq, gmid, gqkv, n1)), [inputs] + attn,
            (self.out,), (buffer, buffer),
            [
                self.one, self.three, self.one_f32, self.turned, self.three,
                vmem(16, D, kind=F32), vmem(2, CHIPS, 16, HALF), dma(6),
            ],
            2 * self.tokens * D * 6 * D,
        )

    def layer_out(self, pos, vec, act, mid, down):
        (out,) = call(
            layer_out_kernel, "layer_out", (pos, *keep(vec, act, mid)), down, (self.out,), (),
            [vmem(FF, D), self.one_f32, dma(4)],
            2 * self.tokens * D * FF,
        )
        return out


class Scatter:
    def __init__(self, mine, theirs, *after):
        self.mine = mine
        self.got = swap(tie(theirs, *after), 0)

    def part(self, first, last):
        return self.mine[first:last], self.got[first:last]

    def first(self, *after):
        self.got = hold((self.got,), *after)[0]
        self.out = (rounded_sum(*self.part(8, 12)), rounded_sum(*self.part(12, 16)))
        self.in_y, self.in_x = swap(self.out[0], BIT_Y), swap(self.out[1], BIT_X)

    def second(self, *after):
        in_y, in_x = hold((self.in_y, self.in_x), *after)
        self.out = (
            rounded_sum(*self.part(4, 6), in_x[2:]),
            rounded_sum(*self.part(6, 8), in_y[2:]),
        )
        self.in_y, self.in_x = in_y, in_x
        self.in_y2, self.in_x2 = swap(self.out[0], BIT_Y), swap(self.out[1], BIT_X)

    def third(self, *after):
        in_y2, in_x2 = hold((self.in_y2, self.in_x2), *after)
        self.near = (*self.part(0, 2), self.in_x[:2], in_y2)
        self.out = (rounded_sum(*self.part(2, 4), self.in_y[:2], in_x2),)
        self.in_z = swap(self.out[0], BIT_Z0)

    def diagonal(self, *after):
        self.got = hold((self.got,), *after)[0]
        self.out = (rounded_sum(*self.part(10, 12)), rounded_sum(*self.part(14, 16)))
        self.in_y, self.in_x = swap(self.out[0], BIT_Y), swap(self.out[1], BIT_X)

    def hi(self, *after):
        in_y, self.in_x = hold((self.in_y, self.in_x), *after)
        self.out = (rounded_sum(*self.part(8, 10)), rounded_sum(*self.part(6, 8), in_y))
        self.in_y2, self.in_x2 = swap(self.out[0], BIT_Y), swap(self.out[1], BIT_X)

    def lo(self, *after):
        in_y2, in_x2 = hold((self.in_y2, self.in_x2), *after)
        far = rounded_sum(*self.part(2, 4), in_y2, in_x2)
        self.in_z = swap(far, BIT_Z0)
        low_y, low_x = rounded_sum(*self.part(4, 6), self.in_x), rounded_sum(*self.part(12, 14))
        low_y, low_x = hold((low_y, low_x), far)
        self.out = (far, low_y, low_x)
        self.near = (*self.part(0, 2), swap(low_y, BIT_Y), swap(low_x, BIT_X))

    def fourth(self, *after):
        self.near = (*self.near, *hold((self.in_z,), *after))
        self.out = (rounded_sum(*[t[1] for t in self.near]),)
        self.in_z = swap(self.out[0], BIT_Z1)

    def result(self, *after):
        total = hold((self.in_z,), *after)[0].astype(F32)
        for term in self.near:
            total = total + term[0].astype(F32)
        return total


def per_device(tuned, *args):
    (
        inputs, segment_ids, pre_attn_gain, pre_attn_bias, w_qkv, b_query, b_value, w_out, b_out,
        pre_mlp_gain, pre_mlp_bias, w_up, b_up, w_down, b_down, cotangent,
    ) = args
    tokens = inputs.shape[0]
    n_rows = tokens // ROW_LEN
    wide, narrow = lax.axis_index("wide"), lax.axis_index("narrow")
    weights = (w_qkv, w_out, w_up, w_down)
    values = (
        pre_attn_gain, pre_attn_bias, b_query, b_value, b_out, pre_mlp_gain, pre_mlp_bias, b_up, b_down,
    )
    per, per_up = pre_attn_gain.shape[0], b_up.shape[0]
    position = jnp.arange(ROW_LEN, dtype=jnp.int32)[None]
    own_id = jnp.where(segment_ids != 0, segment_ids, -1 - position)
    segr = own_id.reshape(n_rows, 1, ROW_LEN)
    segc = own_id.reshape(tokens, 1)
    layer = Layer(tokens)

    if not tuned:
        place = wide * lax.axis_size("narrow") + narrow
        pos = jnp.zeros((2,), jnp.int32)
        attn, up, down = gather_plain(weights, values)
        vec, n1, qkv, soft, mixed = layer.attn_forward(pos, segr, segc, inputs, attn)
        gbd, n2, mid, act, slope, gout = layer.mlp_up(pos, segc, vec, inputs, mixed, cotangent, up)
        pair_down = layer.down_grad(pos, act, gout)
        gbu, gpre, *pair_up = layer.mlp_down(pos, gout, slope, n2, down)
        sums, gmid, gmixed, *pair_up = layer.mid_backward(
            pos, vec, gbd, gbu, gpre, gout, mid, mixed, up, *pair_up
        )
        gbq, gqkv = layer.attn_backward(pos, gmixed, qkv, soft)
        input_grad, *pair_attn = layer.qkv_grad(pos, vec, sums, gbq, gmid, gqkv, n1, inputs, attn)
        layer_out = layer.layer_out(pos, vec, act, mid, down)
        grad_w_down = scatter_plain(pair_down, "down")
        grad_w_up, grad_w_out = scatter_plain(pair_up, "up")
        grad_w_qkv, sums = scatter_plain(pair_attn, "attn")
        eight, grad_b_up, grad_b_down = small_grads(sums, place, per, per_up)
    else:
        core = (narrow & 1).astype(jnp.int32)
        pos = jnp.stack([wide * 2 + (narrow >> 1), core]).astype(jnp.int32)
        block1, block23 = layer.chip_blocks(pos, weights, values)
        flat = (4 * BLK, HALF)

        near1 = swap(block1, BIT_Z1)
        lo1 = jnp.stack([block1, near1])
        hi1 = swap(lo1, BIT_Z0)
        y_lo1, x_lo1 = swap(lo1, BIT_Y), swap(lo1, BIT_X)
        near23 = swap(tie(block23, near1), BIT_Z1)
        d_lo1 = swap(y_lo1, BIT_X)
        y_hi1, x_hi1 = swap(hi1, BIT_Y), swap(hi1, BIT_X)
        lo2 = jnp.stack([block23[:5], near23[:5]])
        lo3 = jnp.stack([block23[5:].reshape(flat), near23[5:].reshape(flat)])
        hi2 = swap(tie(lo2, hi1), BIT_Z0)
        d_hi1 = swap(tie(x_hi1, y_hi1), BIT_Y)
        lo2b = tie(lo2, d_lo1, x_hi1, y_hi1)
        y_lo2, x_lo2 = swap(lo2b, BIT_Y), swap(lo2b, BIT_X)
        attn = gathered(lo1, hi1, y_lo1, y_hi1, x_lo1, x_hi1, d_lo1, d_hi1)
        hi3 = swap(tie(lo3, hi2), BIT_Z0)
        y_hi2, x_hi2 = swap(hi2, BIT_Y), swap(hi2, BIT_X)
        d_lo2, d_hi2 = swap(y_lo2, BIT_X), swap(tie(x_hi2, y_hi2), BIT_Y)
        lo3b = tie(lo3, y_lo2, x_lo2, y_hi2)
        y_lo3, x_lo3 = swap(lo3b, BIT_Y), swap(lo3b, BIT_X)
        vec, n1, qkv, soft, mixed = layer.attn_forward(
            tie(pos, y_hi2, x_hi2, lo3b, d_lo2), segr, segc, inputs, attn
        )

        d_hi2, y_lo3, x_lo3, hi3 = hold((d_hi2, y_lo3, x_lo3, hi3), mixed)
        d_lo3 = swap(y_lo3, BIT_X)
        y_hi3, x_hi3 = swap(hi3, BIT_Y), swap(hi3, BIT_X)
        lo2, hi2, y_lo2, y_hi2, x_lo2, x_hi2, d_lo2 = hold(
            (lo2, hi2, y_lo2, y_hi2, x_lo2, x_hi2, d_lo2), x_lo3, hi3
        )
        up = gathered(lo2, hi2, y_lo2, y_hi2, x_lo2, x_hi2, d_lo2, d_hi2)
        gbd, n2, mid, act, slope, gout = layer.mlp_up(
            tie(pos, hi3, y_lo3, x_lo3), segc, vec, inputs, mixed, cotangent, up
        )
        y_hi3, x_hi3, d_lo3 = hold((y_hi3, x_hi3, d_lo3), gbd)
        d_hi3 = swap(x_hi3, BIT_Y)
        pair_down = layer.down_grad(tie(pos, y_hi3, x_hi3, d_lo3), act, gout)
        d_hi3 = tie(d_hi3, pair_down[0])
        down = gathered(lo3, hi3, y_lo3, y_hi3, x_lo3, x_hi3, d_lo3, d_hi3)
        scatter1 = Scatter(*pair_down, *down)
        gbu, gpre, *pair_up = layer.mlp_down(pos, gout, slope, n2, down)
        scatter1.first(gbu)
        sums, gmid, gmixed, *pair_up = layer.mid_backward(
            tie(pos, *scatter1.out), vec, gbd, gbu, gpre, gout, mid, mixed, up, *pair_up
        )
        scatter1.second(sums)
        scatter2 = Scatter(*pair_up, scatter1.in_y, scatter1.in_x)
        gbq, gqkv = layer.attn_backward(tie(pos, *scatter1.out), gmixed, qkv, soft)
        scatter2.first(gbq)
        scatter1.third(gbq)
        input_grad, *pair_attn = layer.qkv_grad(
            tie(pos, *scatter2.out, *scatter1.out), vec, sums, gbq, gmid, gqkv, n1, inputs, attn
        )
        scatter2.second(input_grad)
        scatter1.fourth(input_grad)
        scatter3 = Scatter(*pair_attn, scatter2.in_y, scatter2.in_x, *scatter1.out)
        scatter3.diagonal(*scatter2.out, *scatter1.out)
        layer_out = layer.layer_out(tie(pos, *scatter3.out), vec, act, mid, down)
        scatter2.third(layer_out)
        scatter3.hi(*scatter2.out)
        scatter3.lo()
        scatter2.fourth(*scatter3.out)
        scatter3.fourth(*scatter2.out)

        def exchange(blocks, axis):
            first, second = jnp.split(blocks, 2, axis=axis)
            keep = jnp.where(core == 0, first, second)
            got = swap(jnp.where(core == 0, second, first), 0)
            return jnp.where(core == 0, keep, got), jnp.where(core == 0, got, keep)

        grad_w_down = jnp.concatenate(exchange(scatter1.result(*scatter3.out), 0), axis=1)
        total = scatter2.result(*scatter3.out)
        upper, lower = total[:, :PER], total[:, PER:]
        got = swap(jnp.where(core == 0, lower, upper), 0)
        grad_w_up, grad_w_out = layer.spread_up(pos, jnp.where(core == 0, upper, lower), got)
        grad_w_qkv, eight, grad_b_up, grad_b_down = layer.finish(
            pos, scatter3.in_z, [scatter3.mine, scatter3.got, *scatter3.near[2:]]
        )
        grad_b_up, grad_b_down = grad_b_up[0], grad_b_down[0]
    return (
        layer_out, input_grad, eight[0], eight[1], grad_w_qkv, eight[2], eight[4], grad_w_out, eight[5],
        eight[6], eight[7], grad_w_up, grad_b_up, grad_w_down, grad_b_down,
    )


def solution(mesh):
    both = P(AXES, None)
    one = P(AXES)
    tuned = dict(mesh.shape) == {"wide": 8, "narrow": 4}
    in_specs = (both, both, one, one, both, one, one, both, one, one, one, both, one, both, one, both)
    out_specs = (both, both, one, one, both, one, one, both, one, one, one, both, one, both, one)
    return jax.shard_map(
        functools.partial(per_device, tuned),
        mesh=mesh,
        in_specs=in_specs,
        out_specs=out_specs,
        check_vma=False,
    )
```

```python
import functools
import math

import jax
import jax.numpy as jnp
from jax import lax
from jax.experimental import pallas as pl
from jax.experimental.pallas import tpu as pltpu
from jax.sharding import PartitionSpec as P

HEADS = 12
HEAD_DIM = 64
D = 768
FF = 3072
ROW_LEN = 256
HALF = 384
CHIPS = 16
BLK = 48
PAIRS = HEADS // 2
AXES = ("wide", "narrow")

EPS = 1e-06
MASKED = -1e30
F32 = jnp.float32
BF16 = jnp.bfloat16

BIT_Y, BIT_X, BIT_Z0, BIT_Z1 = 1, 2, 4, 8
Z_OFFSETS = (0, 4, 8, 12)

GATHER = tuple((o + z, o + z + BIT_Z1) for o in (0, BIT_Y, BIT_X, BIT_X + BIT_Y) for z in (0, BIT_Z0))
PIECES = 2 * len(GATHER)

SCATTER = (0, 8, 4, 12, 1, 9, 6, 14, 5, 13, 7, 15, 2, 10, 3, 11)


def nt(a, b):
    return lax.dot_general(a, b, (((1,), (1,)), ((), ())), preferred_element_type=F32)


def tn(a, b):
    return lax.dot_general(a, b, (((0,), (0,)), ((), ())), preferred_element_type=F32)


def nn(a, b):
    return lax.dot_general(a, b, (((1,), (0,)), ((), ())), preferred_element_type=F32)


def chunks(tokens, step, body):
    def one(i, carry):
        body(pl.ds(pl.multiple_of(i * step, step), step))
        return carry

    lax.fori_loop(0, tokens // step, one, 0)


def norm_parts(v):
    centre = jnp.mean(v, axis=-1, keepdims=True)
    centred = v - centre
    scale = lax.rsqrt(jnp.mean(centred * centred, axis=-1, keepdims=True) + EPS)
    return centred * scale, scale


def start(src, dst, sem):
    copy = pltpu.make_async_copy(src, dst, sem)
    copy.start()
    return copy


def whole_wait(ref, sem):
    pltpu.make_async_copy(ref, ref, sem).wait()


def each_block(pos_ref, pieces):
    for other in range(2):
        for ref, offsets in zip(pieces[other * len(GATHER) :], GATHER):
            for b, offset in enumerate(offsets):
                yield ref, b, pos_ref[0] ^ offset, other, offset


def chip_rows(chip, size):
    return pl.ds(pl.multiple_of(chip * size, 16), size)


def half_cols(pos_ref, other):
    return pl.ds(pl.multiple_of((pos_ref[1] ^ other) * HALF, 128), HALF)


def fetch_qkv(pos_ref, pieces, w_qkv, sems):
    for t in range(3):
        for ref, b, chip, other, _ in each_block(pos_ref, pieces):
            dst = w_qkv.at[t, chip_rows(chip, BLK), half_cols(pos_ref, other)]
            start(ref.at[b, pl.ds(t * BLK, BLK)], dst, sems.at[t])


def fetch_out(pos_ref, pieces, w_out, sem):
    for ref, b, chip, other, _ in each_block(pos_ref, pieces):
        dst = w_out.at[chip_rows(chip, BLK), half_cols(pos_ref, other)]
        start(ref.at[b, 4], dst, sem)


def fetch_small(pos_ref, pieces, small, sem):
    for ref, b, chip, other, _ in each_block(pos_ref, pieces):
        start(ref.at[b, pl.ds(3 * BLK, 16)], small.at[pos_ref[1] ^ other, chip], sem)


def fetch_up(pos_ref, pieces, w_up, sems):
    for ref, b, chip, other, _ in each_block(pos_ref, pieces):
        for u in range(2):
            dst = w_up.at[other, pl.ds(0, 2), chip_rows(chip, BLK), pl.ds(u * HALF, HALF)]
            start(ref.at[b, pl.ds(2 * u, 2)], dst, sems.at[other])


def fetch_down(pos_ref, pieces, w_down, sems):
    for q in range(4):
        for ref, b, chip, other, offset in each_block(pos_ref, pieces):
            if offset // 4 == q:
                dst = w_down.at[chip_rows(chip, 4 * BLK), half_cols(pos_ref, other)]
                start(ref.at[b], dst, sems.at[q])


def scatter_place(pos_ref, chip):
    offset = pos_ref[0] ^ chip
    xy, z = offset & 3, ((offset >> 2) & 1) * 2 + (offset >> 3)
    near = jnp.where(xy == 1, 4, jnp.where(xy == 2, 12, 14)) + z
    far = jnp.where(xy == 1, 6, jnp.where(xy == 2, 4, 8)) + z
    return jnp.where(xy == 0, z, jnp.where(z < 2, near, far))


def head_masks():
    lane = lax.broadcasted_iota(jnp.int32, (1, 2 * HEAD_DIM), 1)
    return [(lane // HEAD_DIM == hh).astype(F32).astype(BF16) for hh in range(2)]


def pair_cols(t, i):
    return pl.ds(pl.multiple_of(t * D + i * 128, 128), 128)


def attn_forward_kernel(pos_ref, segr_ref, segc_ref, x_any, *refs):
    pieces, refs = refs[:PIECES], refs[PIECES:]
    vec_ref, n1_ref, qkv_ref, soft_ref, mixed_ref, w_qkv, x_ref, small, bias, sems = refs
    tokens = x_ref.shape[0]
    n_rows = tokens // ROW_LEN
    load_x = start(x_any, x_ref, sems.at[4])
    fetch_small(pos_ref, pieces, small, sems.at[0])
    fetch_qkv(pos_ref, pieces, w_qkv, sems.at[pl.ds(1, 3)])
    for r in range(n_rows):
        same = segc_ref[r * ROW_LEN : (r + 1) * ROW_LEN] == segr_ref[r]
        bias[r] = jnp.where(same, 0.0, MASKED)
    whole_wait(small, sems.at[0])
    for h in range(2):
        vec_ref[:, h * HALF : (h + 1) * HALF] = jnp.sum(small[h].astype(F32), axis=0)
    load_x.wait()

    def norm_one(rows):
        xhat, _ = norm_parts(x_ref[rows, :].astype(F32))
        n1_ref[rows, :] = (xhat * vec_ref[0:1, :] + vec_ref[1:2, :]).astype(BF16)

    chunks(tokens, 128, norm_one)
    for t in range(3):
        whole_wait(w_qkv.at[t], sems.at[1 + t])
        y = (nn(n1_ref[...], w_qkv[t]) + vec_ref[2 + t : 3 + t, :]).astype(BF16)
        if t == 0:
            y = y * BF16(HEAD_DIM**-0.5)
        qkv_ref[:, t * D : (t + 1) * D] = y
    masks = head_masks()
    for r in range(n_rows):
        rows = slice(r * ROW_LEN, (r + 1) * ROW_LEN)

        def pair(i, carry):
            q, k, v = (qkv_ref[rows, pair_cols(t, i)] for t in range(3))
            mixed = jnp.zeros((ROW_LEN, 128), F32)
            for hh, keep in enumerate(masks):
                s = nt(q, k * keep) + bias[r]
                e = jnp.exp(s - jnp.max(s, axis=-1, keepdims=True))
                p = (e * (1.0 / jnp.sum(e, axis=-1, keepdims=True))).astype(BF16)
                soft_ref[r * HEADS + 2 * i + hh] = p
                mixed = mixed + nn(p, v * keep)
            mixed_ref[rows, pair_cols(0, i)] = mixed.astype(BF16)
            return carry

        lax.fori_loop(0, PAIRS, pair, 0)


GELU_A = 0.7978845608028654
GELU_B = 0.044715


def quarter(pos_ref, other, s):
    return (pos_ref[1] ^ other) * 2 + s


def quarter_cols(z):
    return pl.ds(pl.multiple_of(z * D, 128), D)


QUARTERS = ((0, 0), (0, 1), (1, 0), (1, 1))


def mlp_up_kernel(pos_ref, segc_ref, vec_ref, mixed_ref, x_any, cot_any, *refs):
    pieces, refs = refs[:PIECES], refs[PIECES:]
    gb_ref, n2_ref, mid_ref, act_ref, slope_ref, gout_ref, w_out, w_up, x_ref, cot_ref, sems = refs
    tokens = n2_ref.shape[0]
    load_cot = start(cot_any, cot_ref, sems.at[3])
    load_x = start(x_any, x_ref, sems.at[4])
    fetch_out(pos_ref, pieces, w_out, sems.at[2])
    fetch_up(pos_ref, pieces, w_up, sems)
    load_cot.wait()
    valid = segc_ref[...] > 0
    gout = jnp.where(valid, cot_ref[...].astype(F32), 0.0)
    gout_ref[...] = gout.astype(BF16)
    gb_ref[...] = jnp.broadcast_to(jnp.sum(gout, axis=0, keepdims=True), gb_ref.shape)
    load_x.wait()
    whole_wait(w_out, sems.at[2])
    mid_ref[...] = x_ref[...].astype(F32) + nn(mixed_ref[...], w_out[...]) + vec_ref[5:6, :]

    def norm_two(rows):
        xhat, _ = norm_parts(mid_ref[rows, :])
        n2_ref[rows, :] = (xhat * vec_ref[6:7, :] + vec_ref[7:8, :]).astype(BF16)

    chunks(tokens, 128, norm_two)
    for other, s in QUARTERS:
        if s == 0:
            whole_wait(w_up.at[other], sems.at[other])
        z = quarter(pos_ref, other, s)
        b_up = vec_ref[pl.ds(8 + z, 1), :]
        cols = quarter_cols(z)

        def part(rows):
            u = nn(n2_ref[rows, :], w_up[other, s]) + b_up
            sq = u * u
            t = jnp.tanh(u * (GELU_A + GELU_A * GELU_B * sq))
            half_up = 0.5 + 0.5 * t
            act_ref[rows, cols] = (u * half_up).astype(BF16)
            slope_ref[rows, cols] = (
                half_up + u * (0.5 - 0.5 * t * t) * (GELU_A + 3.0 * GELU_A * GELU_B * sq)
            ).astype(BF16)

        chunks(tokens, 256, part)


def down_grad_kernel(pos_ref, act_ref, gout_ref, mine, theirs, grad, sem):
    for z in range(4):
        grad[z] = tn(act_ref[:, z * D : (z + 1) * D], gout_ref[...]).astype(BF16)
        for j in range(4):
            place = scatter_place(pos_ref, 4 * z + j)
            for other, out in enumerate((mine, theirs)):
                src = grad.at[z, pl.ds(j * 4 * BLK, 4 * BLK), half_cols(pos_ref, other)]
                start(src, out.at[place], sem.at[0])
    whole_wait(grad, sem.at[0])


def mlp_down_kernel(pos_ref, gout_ref, slope_ref, n2_ref, *refs):
    pieces, refs = refs[:PIECES], refs[PIECES:]
    gb_ref, gpre_ref, w_down, mine, theirs, n2t, grad, sems = refs
    fetch_down(pos_ref, pieces, w_down, sems)
    gb_ref[...] = jnp.zeros(gb_ref.shape, F32)
    n2t[...] = n2_ref[...].T
    for other, s in QUARTERS:
        z = quarter(pos_ref, other, s)
        cols = quarter_cols(z)
        whole_wait(w_down.at[cols], sems.at[z ^ (pos_ref[0] >> 2)])
        ga = nt(gout_ref[...], w_down[cols, :])
        gp = (ga * slope_ref[:, cols].astype(F32)).astype(BF16)
        gpre_ref[:, cols] = gp
        gb_ref[pl.ds(z, 1), :] = jnp.sum(gp.astype(F32), axis=0, keepdims=True)
        grad[other, s] = nn(n2t[...], gp).astype(BF16)
        if s == 1:
            for chip in range(CHIPS):
                place = scatter_place(pos_ref, chip)
                for u in range(2):
                    src = grad.at[other, pl.ds(0, 2), pl.ds(chip * BLK, BLK), pl.ds(u * HALF, HALF)]
                    start(src, (mine, theirs)[other].at[place, pl.ds(2 * u, 2)], sems.at[4])
    whole_wait(grad, sems.at[4])


def norm_back(grad, xhat, scale, gain):
    gn = grad * gain
    mean_gn = jnp.mean(gn, axis=-1, keepdims=True)
    mean_gx = jnp.mean(gn * xhat, axis=-1, keepdims=True)
    return scale * (gn - mean_gn - xhat * mean_gx)


def mid_backward_kernel(
    pos_ref, vec_ref, gbd_ref, gbu_ref, gpre_ref, gout_ref, mid_ref, mixed_ref, w_out, w_up, _, __,
    sums, gmid, gmixed, mine, theirs, acc, gbr, mixt, grad, sem,
):
    tokens = mid_ref.shape[0]
    sums[...] = jnp.zeros(sums.shape, F32)
    sums[8:12, :] = gbu_ref[0:4, :]
    sums[12:13, :] = gbd_ref[0:1, :]
    mixt[...] = mixed_ref[...].T
    for other, s in QUARTERS:
        part = nt(gpre_ref[:, quarter_cols(quarter(pos_ref, other, s))], w_up[other, s])
        acc[...] = part if other + s == 0 else acc[...] + part

    def back_two(rows):
        xhat, scale = norm_parts(mid_ref[rows, :])
        g = acc[rows, :]
        sums[6:7, :] += jnp.sum(g * xhat, axis=0, keepdims=True)
        sums[7:8, :] += jnp.sum(g, axis=0, keepdims=True)
        gm = gout_ref[rows, :].astype(F32) + norm_back(g, xhat, scale, vec_ref[6:7, :])
        gmid[rows, :] = gm
        low = gm.astype(BF16)
        gbr[rows, :] = low
        sums[5:6, :] += jnp.sum(low.astype(F32), axis=0, keepdims=True)

    chunks(tokens, 128, back_two)
    grad[...] = nn(mixt[...], gbr[...]).astype(BF16)
    for chip in range(CHIPS):
        place = scatter_place(pos_ref, chip)
        for other, out in enumerate((mine, theirs)):
            src = grad.at[pl.ds(chip * BLK, BLK), half_cols(pos_ref, other)]
            start(src, out.at[place, 4], sem.at[0])
    gmixed[...] = nt(gbr[...], w_out[...]).astype(BF16)
    whole_wait(grad, sem.at[0])


def attn_backward_kernel(pos_ref, gmixed, qkv_ref, soft_ref, gb_ref, gqkv, give):
    masks = head_masks()
    for r in range(gmixed.shape[0] // ROW_LEN):
        rows = slice(r * ROW_LEN, (r + 1) * ROW_LEN)

        def pair(i, carry):
            q, k, v = (qkv_ref[rows, pair_cols(t, i)] for t in range(3))
            gm = gmixed[rows, pair_cols(0, i)]
            dq = jnp.zeros((ROW_LEN, 128), F32)
            dk = jnp.zeros((ROW_LEN, 128), F32)
            dv = jnp.zeros((ROW_LEN, 128), F32)
            for hh, keep in enumerate(masks):
                p_low = soft_ref[r * HEADS + 2 * i + hh]
                p = p_low.astype(F32)
                gmk = gm * keep
                gs = nt(gmk, v)
                inner = jnp.sum(p * gs, axis=-1, keepdims=True)
                ds = (p * (gs - inner)).astype(BF16)
                dq = dq + nn(ds, k * keep)
                dk = dk + tn(ds, q * keep)
                dv = dv + tn(p_low, gmk)
            gqkv[rows, pair_cols(0, i)] = (dq * (HEAD_DIM**-0.5)).astype(BF16)
            gqkv[rows, pair_cols(1, i)] = dk.astype(BF16)
            gqkv[rows, pair_cols(2, i)] = dv.astype(BF16)
            return carry

        lax.fori_loop(0, PAIRS, pair, 0)
    for t in range(3):
        cols = pl.ds(pl.multiple_of(t * D + (1 - pos_ref[1]) * HALF, 128), HALF)
        give[:, t * HALF : (t + 1) * HALF] = gqkv[:, cols]
    gb_ref[...] = jnp.zeros(gb_ref.shape, F32)
    gb_ref[0:1, :] = jnp.sum(gqkv[:, :D].astype(F32), axis=0, keepdims=True)
    gb_ref[2:3, :] = jnp.sum(gqkv[:, 2 * D :].astype(F32), axis=0, keepdims=True)


def qkv_grad_kernel(
    pos_ref, vec_ref, sums_ref, gbq_ref, gmid, gqkv, n1_ref, w_qkv, n1_got, g_got, x_any,
    igrad, mine, x_ref, acc, n1t, both, grad, sums, small, sems,
):
    tokens = x_ref.shape[0]
    load_x = start(x_any, x_ref, sems.at[0])
    sums[...] = sums_ref[...]
    sums[2:3, :] = gbq_ref[0:1, :]
    sums[4:5, :] = gbq_ref[2:3, :]
    n1t[:, :tokens] = n1_ref[...].T
    n1t[:, tokens:] = n1_got[...].T
    for t in range(3):
        cols = pl.ds(pl.multiple_of(t * D + pos_ref[1] * HALF, 128), HALF)
        both[:tokens, t * HALF : (t + 1) * HALF] = gqkv[:, cols]
    both[tokens:, :] = g_got[...]
    for z in range(4):
        rows = slice(z * 4 * BLK, (z + 1) * 4 * BLK)
        grad[rows, :] = nn(n1t[rows, :], both[...]).astype(BF16)
        for chip in range(4 * z, 4 * z + 4):
            place = scatter_place(pos_ref, chip)
            for t in range(3):
                src = grad.at[pl.ds(chip * BLK, BLK), pl.ds(t * HALF, HALF)]
                start(src, mine.at[place, pl.ds(t * BLK, BLK)], sems.at[1])
    for t in range(3):
        part = nt(gqkv[:, t * D : (t + 1) * D], w_qkv[t])
        acc[...] = part if t == 0 else acc[...] + part
    load_x.wait()

    def back_one(rows):
        xhat, scale = norm_parts(x_ref[rows, :].astype(F32))
        g = acc[rows, :]
        sums[0:1, :] += jnp.sum(g * xhat, axis=0, keepdims=True)
        sums[1:2, :] += jnp.sum(g, axis=0, keepdims=True)
        igrad[rows, :] = (gmid[rows, :] + norm_back(g, xhat, scale, vec_ref[0:1, :])).astype(BF16)

    chunks(tokens, 128, back_one)
    for p in range(CHIPS):
        small[p, 0:16] = sums[:, :HALF].astype(BF16)
        small[p, 16:32] = sums[:, HALF:].astype(BF16)
        start(small.at[p], mine.at[p, pl.ds(3 * BLK, 32)], sems.at[2])
    whole_wait(small, sems.at[2])
    whole_wait(grad, sems.at[1])


def layer_out_kernel(pos_ref, vec_ref, act_ref, mid_ref, w_down, out_ref):
    out_ref[...] = (
        mid_ref[...] + nn(act_ref[...], w_down[...]) + vec_ref[12:13, :]
    ).astype(BF16)


PER = D // (2 * CHIPS)
SEND_ROWS = (3 * PER, 16, 5 * PER, 4 * PER)


def pack_kernel(pos_ref, w_qkv, w_out, w_up, w_down, bu_ref, *refs):
    values, (mine, theirs, rows, last, wide) = refs[:8], refs[8:]
    place = pos_ref[0] * 2 + pos_ref[1]
    rows[...] = jnp.zeros(rows.shape, F32)
    last[...] = jnp.zeros(last.shape, F32)
    for r, value in zip((0, 1, 2, 4, 5, 6, 7, 12), values):
        rows[r : r + 1, 0:PER] = value[...].astype(F32)
    last[0:1, 0 : 4 * PER] = bu_ref[...].astype(F32)
    at = place * (4 * PER)
    up = pltpu.roll(last[...], at % D, 1)[0:1]
    here = lax.broadcasted_iota(jnp.int32, (16, 1), 0) == 8 + at // D
    rows[...] = pltpu.roll(rows[...], place * PER, 1) + jnp.where(here, up, 0.0)
    for out, other in ((mine, 0), (theirs, 1)):
        half = pos_ref[1] ^ other

        def cols(first):
            return pl.ds(pl.multiple_of(first + half * HALF, 128), HALF)

        at = 0
        for t in range(3):
            wide[at : at + PER, :] = w_qkv[:, cols(t * D)].astype(F32)
            at += PER
        wide[at : at + 16, :] = rows[:, cols(0)]
        at += 16
        for n in range(4):
            u, s = n // 2, n % 2
            first = pl.multiple_of(half * (2 * D) + s * D + u * HALF, 128)
            wide[at : at + PER, :] = w_up[:, pl.ds(first, HALF)].astype(F32)
            at += PER
        wide[at : at + PER, :] = w_out[:, cols(0)].astype(F32)
        at += PER
        wide[at : at + 4 * PER, :] = w_down[:, cols(0)].astype(F32)
        out[...] = wide[...].astype(BF16)


def combine_kernel(pos_ref, mine, got, one, two, upper, lower, wide):
    first = pos_ref[1] == 0
    m, g = mine[...].astype(F32), got[...].astype(F32)
    upper[...] = jnp.where(first, m, g)
    lower[...] = jnp.where(first, g, m)

    def pair(at, size):
        wide[0:size, :] = upper[at : at + size, :]
        wide[size : 2 * size, :] = lower[at : at + size, :]
        return wide[0 : 2 * size, :].astype(BF16)

    for t in range(3):
        one[t * BLK : (t + 1) * BLK, :] = pair(t * PER, PER)
    at = 3 * PER
    one[3 * BLK :, :] = (upper[at : at + 16, :] + lower[at : at + 16, :]).astype(BF16)
    at += 16
    for n in range(5):
        two[n] = pair(at + n * PER, PER)
    low = pair(at + 5 * PER, 4 * PER)
    for n in range(4):
        two[5 + n] = low[n * BLK : (n + 1) * BLK]


def finish_kernel(pos_ref, last, *refs):
    terms, (keep, send, held, sems) = refs[:4], refs[4:]
    for i, term in enumerate(terms):
        start(term.at[0], held.at[i], sems.at[i])
    total = last[...].astype(F32)
    for i in range(4):
        whole_wait(held.at[i], sems.at[i])
        total = total + held[i].astype(F32)
    first = pos_ref[1] == 0
    for t in range(3):
        upper, lower = total[t * BLK : t * BLK + PER], total[t * BLK + PER : (t + 1) * BLK]
        keep[t * PER : (t + 1) * PER, :] = jnp.where(first, upper, lower)
        send[t * PER : (t + 1) * PER, :] = jnp.where(first, lower, upper)
    keep[3 * PER :, :] = total[3 * BLK :]
    send[3 * PER :, :] = total[3 * BLK :]


def spread_kernel(pos_ref, keep, got, w_ref, eight_ref, up_ref, down_ref, rows):
    place = pos_ref[0] * 2 + pos_ref[1]
    for ref, other in ((keep, 0), (got, 1)):
        half = pos_ref[1] ^ other
        for t in range(3):
            cols = pl.ds(pl.multiple_of(t * D + half * HALF, 128), HALF)
            w_ref[:, cols] = ref[t * PER : (t + 1) * PER, :]
    for h in range(2):
        at = 3 * PER + 16 * h
        rows[:, h * HALF : (h + 1) * HALF] = keep[at : at + 16, :] + got[at : at + 16, :]
    mine = pltpu.roll(rows[...], lax.rem(D - place * PER, D), 1)
    eight_ref[...] = mine[0:8, 0:PER]
    down_ref[...] = mine[12:13, 0:PER]
    at = place * (4 * PER)
    here = lax.broadcasted_iota(jnp.int32, (16, 1), 0) == 8 + at // D
    row = jnp.sum(jnp.where(here, rows[...], 0.0), axis=0, keepdims=True)
    turned = pltpu.roll(jnp.broadcast_to(row, (8, D)), lax.rem(D - at % D, D), 1)
    up_ref[...] = turned[0:1, 0 : 4 * PER]


def spread_up_kernel(pos_ref, keep, got, up_ref, out_ref):
    for ref, other in ((keep, 0), (got, 1)):
        half = pos_ref[1] ^ other
        for n in range(4):
            first = half * (2 * D) + (n % 2) * D + (n // 2) * HALF
            up_ref[:, pl.ds(pl.multiple_of(first, 128), HALF)] = ref[n]
        out_ref[:, pl.ds(pl.multiple_of(half * HALF, 128), HALF)] = ref[4]


def call(kernel, name, near, far, near_outs, far_outs, scratch, flops, aliases=None, limit=18):
    far = [in_hbm(a) for a in far]
    space = pl.BlockSpec(memory_space=pltpu.VMEM)
    anyspec = pl.BlockSpec(memory_space=pl.ANY)
    outs = tuple(near_outs) + tuple(far_outs)
    moved = sum(math.prod(a.shape) * a.dtype.itemsize for a in (*near, *far, *outs))
    return pl.pallas_call(
        kernel,
        out_shape=outs,
        in_specs=[pl.BlockSpec(memory_space=pltpu.SMEM)]
        + [space] * (len(near) - 1)
        + [anyspec] * len(far),
        out_specs=[space] * len(near_outs) + [anyspec] * len(far_outs),
        scratch_shapes=scratch,
        input_output_aliases=aliases or {},
        compiler_params=pltpu.CompilerParams(vmem_limit_bytes=limit << 20),
        cost_estimate=pl.CostEstimate(flops=flops, bytes_accessed=moved, transcendentals=0),
        name=name,
    )(*near, *far)


def in_hbm(array):
    return pltpu.with_memory_space_constraint(array, pltpu.HBM)


def keep(*arrays):
    return [pltpu.with_memory_space_constraint(a, pltpu.VMEM) for a in arrays]


def swap(value, chip_bit):
    flip = chip_bit * 2 if chip_bit else 1
    return lax.ppermute(value, AXES, [(i, i ^ flip) for i in range(2 * CHIPS)])


def tie(value, *after):
    return lax.optimization_barrier((value,) + after)[0]


def gathered(*own_half):
    return list(own_half) + [swap(piece, 0) for piece in own_half]


def hold(pieces, *after):
    return lax.optimization_barrier((*pieces, *after))[: len(pieces)] if after else pieces


def rounded_sum(*terms):
    total = terms[0].astype(F32)
    for term in terms[1:]:
        total = total + term.astype(F32)
    return total.astype(BF16)


def small_grads(sums, place, per, per_up):
    eight = lax.dynamic_slice(sums, (0, place * per), (8, per))
    at = place * per_up
    up = lax.dynamic_slice(sums, (8 + at // D, at % D), (1, per_up))[0]
    down = lax.dynamic_slice(sums, (12, place * per), (1, per))[0]
    return eight, up, down


def halves(w_qkv, w_out, w_up, w_down):
    rows = w_qkv.shape[0]
    qkv = w_qkv.reshape(rows, 3, 2, HALF)
    up = w_up.reshape(rows, 2, 4, HALF)
    for h in range(2):
        cols = slice(h * HALF, (h + 1) * HALF)
        up_h = up[:, h].reshape(rows, 2, 2, HALF).transpose(2, 1, 0, 3).reshape(4, rows, HALF)
        yield (
            qkv[:, :, h].transpose(1, 0, 2),
            jnp.concatenate([up_h, w_out[None, :, cols]]),
            w_down[:, cols],
        )


def gather_plain(weights, values):
    def whole(w):
        return lax.all_gather(w, AXES, axis=0, tiled=True)

    gain1, bias1, bq, bv, bo, gain2, bias2, bu, bd = [whole(v) for v in values]
    rest = jnp.zeros((3, D), BF16)
    small = jnp.stack([gain1, bias1, bq, jnp.zeros_like(bq), bv, bo, gain2, bias2])
    small = jnp.concatenate([small, bu.reshape(4, D), bd[None], rest])
    groups = ([], [], [])
    for h, (attn, up, down) in enumerate(halves(*[whole(w) for w in weights])):
        attn = attn.reshape(3, CHIPS, BLK, HALF).transpose(1, 0, 2, 3).reshape(CHIPS, 3 * BLK, HALF)
        up = up.reshape(5, CHIPS, BLK, HALF).transpose(1, 0, 2, 3)
        down = down.reshape(CHIPS, 4 * BLK, HALF)
        extra = jnp.zeros((CHIPS, 16, HALF), BF16).at[0].set(small[:, h * HALF : (h + 1) * HALF])
        for group, blocks in zip(groups, (jnp.concatenate([attn, extra], axis=1), up, down)):
            group.extend(jnp.stack([blocks[o] for o in piece]) for piece in GATHER)
    return groups


def scatter_plain(pair, group):
    both = [jnp.stack([part[SCATTER.index(chip)] for chip in range(CHIPS)]) for part in pair]

    def scatter(v):
        return lax.psum_scatter(v.astype(F32), AXES, scatter_dimension=0, tiled=True)

    def matrix(units):
        return jnp.stack(units, axis=3).transpose(0, 2, 1, 3, 4).reshape(D, -1, 2, HALF)

    if group == "attn":
        sums = jnp.concatenate([both[0][0, 3 * BLK + 16 * h :][:16] for h in range(2)], axis=1)
        qkv = matrix([b[:, : 3 * BLK].reshape(CHIPS, 3, BLK, HALF) for b in both])
        return scatter(qkv.reshape(D, 3 * D)), lax.psum(sums.astype(F32), AXES)
    if group == "up":
        up = matrix(both)
        order = up[:, :4].reshape(D, 2, 2, 2, HALF).transpose(0, 3, 2, 1, 4)
        return scatter(order.reshape(D, FF)), scatter(up[:, 4].reshape(D, D))
    return scatter(jnp.concatenate([b.reshape(FF, HALF) for b in both], axis=1))


def shape(dims, kind=BF16):
    return jax.ShapeDtypeStruct(dims, kind)


def far_shape(*dims):
    return pltpu.HBM(dims, BF16)


def dma(n):
    return pltpu.SemaphoreType.DMA((n,))


def vmem(*dims, kind=BF16):
    return pltpu.VMEM(dims, kind)


class Layer:
    def __init__(self, tokens):
        self.tokens = tokens
        self.rows = tokens // ROW_LEN
        self.out = shape((tokens, D))
        self.wide = vmem(tokens, FF)
        self.one = vmem(tokens, D)
        self.one_f32 = vmem(tokens, D, kind=F32)
        self.qkv = vmem(tokens, 3 * D)
        self.soft = vmem(self.rows * HEADS, ROW_LEN, ROW_LEN)
        self.turned = vmem(D, tokens)
        self.square = vmem(D, D)
        self.three = vmem(3, D, D)
        self.four = vmem(2, 2, D, D)
        self.sums = vmem(8, D, kind=F32)
        self.vec = vmem(16, D, kind=F32)

    def chip_blocks(self, pos, weights, values):
        *rest, bu, bd = [in_hbm(v.reshape(1, -1)) for v in values]
        weights = [in_hbm(w) for w in weights]
        sent = shape((sum(SEND_ROWS), HALF))
        wide = vmem(sum(SEND_ROWS), HALF, kind=F32)
        mine, theirs = call(
            pack_kernel, "pack", (pos, *weights, bu, *rest, bd), (), (sent, sent), (),
            [vmem(16, D, kind=F32), vmem(8, D, kind=F32), wide], 0,
        )
        return call(
            combine_kernel, "combine", (pos, mine, swap(theirs, 0)), (),
            (shape((3 * BLK + 16, HALF)), shape((9, BLK, HALF))), (),
            [wide, wide, vmem(4 * BLK, HALF, kind=F32)], 0,
        )

    def finish(self, pos, last, low):
        sent = shape((3 * PER + 32, HALF), F32)
        keep, send = call(
            finish_kernel, "finish", (pos, last), low, (sent, sent), (),
            [vmem(4, 3 * BLK + 32, HALF), dma(4)], 0,
        )
        return call(
            spread_kernel, "spread", (pos, keep, swap(send, 0)), (),
            (shape((PER, 3 * D), F32), shape((8, PER), F32), shape((1, 4 * PER), F32), shape((1, PER), F32)),
            (), [vmem(16, D, kind=F32)], 0,
        )

    def spread_up(self, pos, keep, got):
        return call(
            spread_up_kernel, "spread_up", (pos, keep, got), (),
            (shape((PER, FF), F32), shape((PER, D), F32)), (), [], 0,
        )

    def attn_forward(self, pos, segr, segc, inputs, attn):
        return call(
            attn_forward_kernel, "attn_forward", (pos, segr, segc), [in_hbm(inputs)] + attn,
            (self.vec, self.one, self.qkv, self.soft, self.one, self.three), (),
            [
                self.one, vmem(2, CHIPS, 16, HALF),
                vmem(self.rows, ROW_LEN, ROW_LEN, kind=F32), dma(5),
            ],
            2 * self.tokens * D * D * 3 + 8 * self.tokens * D * ROW_LEN,
        )

    def mlp_up(self, pos, segc, vec, inputs, mixed, cotangent, up):
        vec, mixed = keep(vec, mixed)
        return call(
            mlp_up_kernel, "mlp_up", (pos, segc, vec, mixed), [inputs, cotangent] + up,
            (self.sums, self.one, self.one_f32, self.wide, self.wide, self.one, self.square, self.four), (),
            [self.one, self.one, dma(5)],
            2 * self.tokens * D * (FF + D),
        )

    def down_grad(self, pos, act, gout):
        buffer = far_shape(CHIPS, 4 * BLK, HALF)
        return call(
            down_grad_kernel, "down_grad", (pos, *keep(act, gout)), [], (), (buffer, buffer),
            [vmem(4, D, D), dma(1)],
            2 * self.tokens * D * FF,
        )

    def mlp_down(self, pos, gout, slope, n2, down):
        buffer = far_shape(CHIPS, 5, BLK, HALF)
        return call(
            mlp_down_kernel, "mlp_down", (pos, *keep(gout, slope, n2)), down,
            (self.sums, self.wide, vmem(FF, D)), (buffer, buffer),
            [self.turned, self.four, dma(5)],
            4 * self.tokens * D * FF,
        )

    def mid_backward(self, pos, vec, gbd, gbu, gpre, gout, mid, mixed, w_out, w_up, mine, theirs):
        buffer = far_shape(*mine.shape)
        near = (pos, *keep(vec, gbd, gbu, gpre, gout, mid, mixed, w_out, w_up))
        return call(
            mid_backward_kernel, "mid_backward", near, [mine, theirs],
            (self.vec, self.one_f32, self.one), (buffer, buffer),
            [self.one_f32, self.one, self.turned, self.square, dma(1)],
            2 * self.tokens * D * (FF + 2 * D),
            {len(near): 3, len(near) + 1: 4},
        )

    def attn_backward(self, pos, gmixed, qkv, soft):
        return call(
            attn_backward_kernel, "attn_backward", (pos, *keep(gmixed, qkv, soft)), [],
            (self.sums, self.qkv, vmem(self.tokens, 3 * HALF)), (), [], 20 * self.tokens * D * ROW_LEN,
        )

    def qkv_grad(self, pos, vec, sums, gbq, gmid, gqkv, n1, w_qkv, n1_got, g_got, inputs):
        return call(
            qkv_grad_kernel, "qkv_grad", (pos, *keep(vec, sums, gbq, gmid, gqkv, n1, w_qkv, n1_got, g_got)),
            [inputs], (self.out,), (far_shape(CHIPS, 3 * BLK + 32, HALF),),
            [
                self.one, self.one_f32, vmem(D, 2 * self.tokens), vmem(2 * self.tokens, 3 * HALF),
                vmem(D, 3 * HALF), vmem(16, D, kind=F32), vmem(CHIPS, 32, HALF), dma(3),
            ],
            2 * self.tokens * D * 6 * D,
        )

    def layer_out(self, pos, vec, act, mid, w_down):
        (out,) = call(
            layer_out_kernel, "layer_out", (pos, *keep(vec, act, mid, w_down)), [], (self.out,), (), [],
            2 * self.tokens * D * FF,
        )
        return out


class Scatter:
    def __init__(self, mine, theirs=None, *after):
        self.both = [mine] if theirs is None else [mine, swap(tie(theirs, *after), 0)]

    def part(self, first, last):
        return [ref[first:last] for ref in self.both]

    def hold_back(self, *after):
        self.both[-1] = hold((self.both[-1],), *after)[0]

    def first(self, *after):
        self.hold_back(*after)
        self.out = (rounded_sum(*self.part(8, 12)), rounded_sum(*self.part(12, 16)))
        self.in_y, self.in_x = swap(self.out[0], BIT_Y), swap(self.out[1], BIT_X)

    def second(self, *after):
        in_y, in_x = hold((self.in_y, self.in_x), *after)
        self.out = (
            rounded_sum(*self.part(4, 6), in_x[2:]),
            rounded_sum(*self.part(6, 8), in_y[2:]),
        )
        self.in_y, self.in_x = in_y, in_x
        self.in_y2, self.in_x2 = swap(self.out[0], BIT_Y), swap(self.out[1], BIT_X)

    def third(self, *after):
        in_y2, in_x2 = hold((self.in_y2, self.in_x2), *after)
        self.near = (*self.part(0, 2), self.in_x[:2], in_y2)
        self.out = (rounded_sum(*self.part(2, 4), self.in_y[:2], in_x2),)
        self.in_z = swap(self.out[0], BIT_Z0)

    def diagonal(self, *after):
        self.hold_back(*after)
        self.out = (rounded_sum(*self.part(10, 12)), rounded_sum(*self.part(14, 16)))
        self.in_y, self.in_x = swap(self.out[0], BIT_Y), swap(self.out[1], BIT_X)

    def hi(self, *after):
        in_y, self.in_x = hold((self.in_y, self.in_x), *after)
        self.out = (rounded_sum(*self.part(8, 10)), rounded_sum(*self.part(6, 8), in_y))
        self.in_y2, self.in_x2 = swap(self.out[0], BIT_Y), swap(self.out[1], BIT_X)

    def lo(self, *after):
        in_y2, in_x2 = hold((self.in_y2, self.in_x2), *after)
        far = rounded_sum(*self.part(2, 4), in_y2, in_x2)
        self.in_z = swap(far, BIT_Z0)
        low_y, low_x = rounded_sum(*self.part(4, 6), self.in_x), rounded_sum(*self.part(12, 14))
        low_y, low_x = hold((low_y, low_x), far)
        self.out = (far, low_y, low_x)
        self.near = (*self.part(0, 2), swap(low_y, BIT_Y), swap(low_x, BIT_X))

    def fourth(self, *after):
        self.near = (*self.near, *hold((self.in_z,), *after))
        self.out = (rounded_sum(*[t[1] for t in self.near]),)
        self.in_z = swap(self.out[0], BIT_Z1)

    def result(self, *after):
        total = hold((self.in_z,), *after)[0].astype(F32)
        for term in self.near:
            total = total + term[0].astype(F32)
        return total


def per_device(tuned, *args):
    (
        inputs, segment_ids, pre_attn_gain, pre_attn_bias, w_qkv, b_query, b_value, w_out, b_out,
        pre_mlp_gain, pre_mlp_bias, w_up, b_up, w_down, b_down, cotangent,
    ) = args
    tokens = inputs.shape[0]
    n_rows = tokens // ROW_LEN
    wide, narrow = lax.axis_index("wide"), lax.axis_index("narrow")
    weights = (w_qkv, w_out, w_up, w_down)
    values = (
        pre_attn_gain, pre_attn_bias, b_query, b_value, b_out, pre_mlp_gain, pre_mlp_bias, b_up, b_down,
    )
    per, per_up = pre_attn_gain.shape[0], b_up.shape[0]
    position = jnp.arange(ROW_LEN, dtype=jnp.int32)[None]
    own_id = jnp.where(segment_ids != 0, segment_ids, -1 - position)
    segr = own_id.reshape(n_rows, 1, ROW_LEN)
    segc = own_id.reshape(tokens, 1)
    layer = Layer(tokens)

    if not tuned:
        place = wide * lax.axis_size("narrow") + narrow
        pos = jnp.zeros((2,), jnp.int32)
        attn, up, down = gather_plain(weights, values)
        vec, n1, qkv, soft, mixed, w_qkv_all = layer.attn_forward(pos, segr, segc, inputs, attn)
        gbd, n2, mid, act, slope, gout, *w_mid = layer.mlp_up(pos, segc, vec, inputs, mixed, cotangent, up)
        pair_down = layer.down_grad(pos, act, gout)
        gbu, gpre, w_down_all, *pair_up = layer.mlp_down(pos, gout, slope, n2, down)
        sums, gmid, gmixed, *pair_up = layer.mid_backward(
            pos, vec, gbd, gbu, gpre, gout, mid, mixed, *w_mid, *pair_up
        )
        gbq, gqkv, give = layer.attn_backward(pos, gmixed, qkv, soft)
        pair_attn = []
        for half in range(2):
            input_grad, blocks = layer.qkv_grad(
                jnp.array([0, half], jnp.int32), vec, sums, gbq, gmid, gqkv, n1, w_qkv_all,
                jnp.zeros_like(n1), jnp.zeros_like(give), inputs,
            )
            pair_attn.append(blocks)
        layer_out = layer.layer_out(pos, vec, act, mid, w_down_all)
        grad_w_down = scatter_plain(pair_down, "down")
        grad_w_up, grad_w_out = scatter_plain(pair_up, "up")
        grad_w_qkv, sums = scatter_plain(pair_attn, "attn")
        eight, grad_b_up, grad_b_down = small_grads(sums, place, per, per_up)
    else:
        core = (narrow & 1).astype(jnp.int32)
        pos = jnp.stack([wide * 2 + (narrow >> 1), core]).astype(jnp.int32)
        block1, block23 = layer.chip_blocks(pos, weights, values)
        flat = (4 * BLK, HALF)

        near1 = swap(block1, BIT_Z1)
        lo1 = jnp.stack([block1, near1])
        hi1 = swap(lo1, BIT_Z0)
        y_lo1, x_lo1 = swap(lo1, BIT_Y), swap(lo1, BIT_X)
        near23 = swap(tie(block23, near1), BIT_Z1)
        d_lo1 = swap(y_lo1, BIT_X)
        y_hi1, x_hi1 = swap(hi1, BIT_Y), swap(hi1, BIT_X)
        lo2 = jnp.stack([block23[:5], near23[:5]])
        lo3 = jnp.stack([block23[5:].reshape(flat), near23[5:].reshape(flat)])
        hi2 = swap(tie(lo2, hi1), BIT_Z0)
        d_hi1 = swap(tie(x_hi1, y_hi1), BIT_Y)
        lo2b = tie(lo2, d_lo1, x_hi1, y_hi1)
        y_lo2, x_lo2 = swap(lo2b, BIT_Y), swap(lo2b, BIT_X)
        attn = gathered(lo1, hi1, y_lo1, y_hi1, x_lo1, x_hi1, d_lo1, d_hi1)
        hi3 = swap(tie(lo3, hi2), BIT_Z0)
        y_hi2, x_hi2 = swap(hi2, BIT_Y), swap(hi2, BIT_X)
        d_lo2, d_hi2 = swap(y_lo2, BIT_X), swap(tie(x_hi2, y_hi2), BIT_Y)
        lo3b = tie(lo3, y_lo2, x_lo2, y_hi2)
        y_lo3, x_lo3 = swap(lo3b, BIT_Y), swap(lo3b, BIT_X)
        vec, n1, qkv, soft, mixed, w_qkv_all = layer.attn_forward(
            tie(pos, y_hi2, x_hi2, lo3b, d_lo2), segr, segc, inputs, attn
        )

        d_hi2, y_lo3, x_lo3, hi3 = hold((d_hi2, y_lo3, x_lo3, hi3), mixed)
        d_lo3 = swap(y_lo3, BIT_X)
        y_hi3, x_hi3 = swap(hi3, BIT_Y), swap(hi3, BIT_X)
        lo2, hi2, y_lo2, y_hi2, x_lo2, x_hi2, d_lo2 = hold(
            (lo2, hi2, y_lo2, y_hi2, x_lo2, x_hi2, d_lo2), x_lo3, hi3
        )
        up = gathered(lo2, hi2, y_lo2, y_hi2, x_lo2, x_hi2, d_lo2, d_hi2)
        gbd, n2, mid, act, slope, gout, *w_mid = layer.mlp_up(
            tie(pos, hi3, y_lo3, x_lo3), segc, vec, inputs, mixed, cotangent, up
        )
        y_hi3, x_hi3, d_lo3 = hold((y_hi3, x_hi3, d_lo3), gbd)
        d_hi3 = swap(x_hi3, BIT_Y)
        pair_down = layer.down_grad(tie(pos, y_hi3, x_hi3, d_lo3), act, gout)
        d_hi3 = tie(d_hi3, pair_down[0])
        down = gathered(lo3, hi3, y_lo3, y_hi3, x_lo3, x_hi3, d_lo3, d_hi3)
        scatter1 = Scatter(*pair_down, *down)
        gbu, gpre, w_down_all, *pair_up = layer.mlp_down(pos, gout, slope, n2, down)
        scatter1.first(gbu)
        sums, gmid, gmixed, *pair_up = layer.mid_backward(
            tie(pos, *scatter1.out), vec, gbd, gbu, gpre, gout, mid, mixed, *w_mid, *pair_up
        )
        scatter1.second(sums)
        scatter2 = Scatter(*pair_up, scatter1.in_y, scatter1.in_x)
        gbq, gqkv, give = layer.attn_backward(tie(pos, *scatter1.out), gmixed, qkv, soft)
        scatter1.third(gbq)
        n1, give = hold((n1, give), *scatter1.out)
        n1_got, g_got = swap(n1, 0), swap(give, 0)
        scatter2.diagonal(gbq)
        input_grad, sums_attn = layer.qkv_grad(
            tie(pos, *scatter2.out, *scatter1.out),
            vec, sums, gbq, gmid, gqkv, n1, w_qkv_all, n1_got, g_got, inputs,
        )
        scatter2.hi(input_grad)
        scatter1.fourth(input_grad)
        scatter3 = Scatter(tie(sums_attn, *scatter2.out))
        scatter3.diagonal()
        layer_out = layer.layer_out(
            tie(pos, *scatter3.out, *scatter1.out), vec, act, mid, w_down_all
        )
        scatter1.in_z = tie(scatter1.in_z, layer_out)
        scatter3.hi(layer_out, scatter1.in_z)
        scatter2.lo(*scatter3.out)
        scatter3.lo(*scatter2.out)
        scatter2.fourth(*scatter3.out)
        scatter3.fourth(*scatter2.out)

        def exchange(blocks, axis):
            first, second = jnp.split(blocks, 2, axis=axis)
            keep = jnp.where(core == 0, first, second)
            got = swap(jnp.where(core == 0, second, first), 0)
            return jnp.where(core == 0, keep, got), jnp.where(core == 0, got, keep)

        grad_w_down = jnp.concatenate(exchange(scatter1.result(*scatter3.out), 0), axis=1)
        total = scatter2.result(*scatter3.out)
        upper, lower = total[:, :PER], total[:, PER:]
        got = swap(jnp.where(core == 0, lower, upper), 0)
        grad_w_up, grad_w_out = layer.spread_up(pos, jnp.where(core == 0, upper, lower), got)
        grad_w_qkv, eight, grad_b_up, grad_b_down = layer.finish(
            pos, scatter3.in_z, [*scatter3.both, *scatter3.near[1:]]
        )
        grad_b_up, grad_b_down = grad_b_up[0], grad_b_down[0]
    return (
        layer_out, input_grad, eight[0], eight[1], grad_w_qkv, eight[2], eight[4], grad_w_out, eight[5],
        eight[6], eight[7], grad_w_up, grad_b_up, grad_w_down, grad_b_down,
    )


def solution(mesh):
    both = P(AXES, None)
    one = P(AXES)
    tuned = dict(mesh.shape) == {"wide": 8, "narrow": 4}
    in_specs = (both, both, one, one, both, one, one, both, one, one, one, both, one, both, one, both)
    out_specs = (both, both, one, one, both, one, one, both, one, one, one, both, one, both, one)
    return jax.shard_map(
        functools.partial(per_device, tuned),
        mesh=mesh,
        in_specs=in_specs,
        out_specs=out_specs,
        check_vma=False,
    )
```

```python
import functools
import math

import jax
import jax.numpy as jnp
from jax import lax
from jax.experimental import pallas as pl
from jax.experimental.pallas import tpu as pltpu
from jax.sharding import PartitionSpec as P

HEADS = 12
HEAD_DIM = 64
D = 768
FF = 3072
ROW_LEN = 256
HALF = 384
CHIPS = 16
BLK = 48
PAIRS = HEADS // 2
AXES = ("wide", "narrow")

EPS = 1e-06
MASKED = -1e30
F32 = jnp.float32
BF16 = jnp.bfloat16

BIT_Y, BIT_X, BIT_Z0, BIT_Z1 = 1, 2, 4, 8
Z_OFFSETS = (0, 4, 8, 12)

GATHER = tuple((o + z, o + z + BIT_Z1) for o in (0, BIT_Y, BIT_X, BIT_X + BIT_Y) for z in (0, BIT_Z0))
PIECES = 2 * len(GATHER)

SCATTER = (0, 8, 4, 12, 1, 9, 6, 14, 5, 13, 7, 15, 2, 10, 3, 11)


def nt(a, b):
    return lax.dot_general(a, b, (((1,), (1,)), ((), ())), preferred_element_type=F32)


def tn(a, b):
    return lax.dot_general(a, b, (((0,), (0,)), ((), ())), preferred_element_type=F32)


def nn(a, b):
    return lax.dot_general(a, b, (((1,), (0,)), ((), ())), preferred_element_type=F32)


def chunks(tokens, step, body):
    def one(i, carry):
        body(pl.ds(pl.multiple_of(i * step, step), step))
        return carry

    lax.fori_loop(0, tokens // step, one, 0)


def norm_parts(v):
    centre = jnp.mean(v, axis=-1, keepdims=True)
    centred = v - centre
    scale = lax.rsqrt(jnp.mean(centred * centred, axis=-1, keepdims=True) + EPS)
    return centred * scale, scale


def start(src, dst, sem):
    copy = pltpu.make_async_copy(src, dst, sem)
    copy.start()
    return copy


def whole_wait(ref, sem):
    pltpu.make_async_copy(ref, ref, sem).wait()


def each_block(pos_ref, pieces):
    for other in range(2):
        for ref, offsets in zip(pieces[other * len(GATHER) :], GATHER):
            for b, offset in enumerate(offsets):
                yield ref, b, pos_ref[0] ^ offset, other, offset


def chip_rows(chip, size):
    return pl.ds(pl.multiple_of(chip * size, 16), size)


def half_cols(pos_ref, other):
    return pl.ds(pl.multiple_of((pos_ref[1] ^ other) * HALF, 128), HALF)


def fetch_qkv(pos_ref, pieces, w_qkv, sems):
    for t in range(3):
        for ref, b, chip, other, _ in each_block(pos_ref, pieces):
            dst = w_qkv.at[t, chip_rows(chip, BLK), half_cols(pos_ref, other)]
            start(ref.at[b, pl.ds(t * BLK, BLK)], dst, sems.at[t])


def fetch_out(pos_ref, pieces, w_out, sem):
    for ref, b, chip, other, _ in each_block(pos_ref, pieces):
        dst = w_out.at[chip_rows(chip, BLK), half_cols(pos_ref, other)]
        start(ref.at[b, 4], dst, sem)


def fetch_small(pos_ref, pieces, small, sem):
    for ref, b, chip, other, _ in each_block(pos_ref, pieces):
        start(ref.at[b, pl.ds(3 * BLK, 16)], small.at[pos_ref[1] ^ other, chip], sem)


def fetch_up(pos_ref, pieces, w_up, sems):
    for ref, b, chip, other, _ in each_block(pos_ref, pieces):
        for u in range(2):
            dst = w_up.at[other, pl.ds(0, 2), chip_rows(chip, BLK), pl.ds(u * HALF, HALF)]
            start(ref.at[b, pl.ds(2 * u, 2)], dst, sems.at[other])


def fetch_down(pos_ref, pieces, w_down, sems):
    for q in range(4):
        for ref, b, chip, other, offset in each_block(pos_ref, pieces):
            if offset // 4 == q:
                dst = w_down.at[chip_rows(chip, 4 * BLK), half_cols(pos_ref, other)]
                start(ref.at[b], dst, sems.at[q])


def scatter_place(pos_ref, chip):
    offset = pos_ref[0] ^ chip
    xy, z = offset & 3, ((offset >> 2) & 1) * 2 + (offset >> 3)
    near = jnp.where(xy == 1, 4, jnp.where(xy == 2, 12, 14)) + z
    far = jnp.where(xy == 1, 6, jnp.where(xy == 2, 4, 8)) + z
    return jnp.where(xy == 0, z, jnp.where(z < 2, near, far))


def head_masks():
    lane = lax.broadcasted_iota(jnp.int32, (1, 2 * HEAD_DIM), 1)
    return [(lane // HEAD_DIM == hh).astype(F32).astype(BF16) for hh in range(2)]


def pair_cols(t, i):
    return pl.ds(pl.multiple_of(t * D + i * 128, 128), 128)


def attn_forward_kernel(pos_ref, segr_ref, segc_ref, x_any, *refs):
    pieces, refs = refs[:PIECES], refs[PIECES:]
    vec_ref, n1_ref, qkv_ref, soft_ref, mixed_ref, w_qkv, x_ref, small, bias, sems = refs
    tokens = x_ref.shape[0]
    n_rows = tokens // ROW_LEN
    load_x = start(x_any, x_ref, sems.at[4])
    fetch_small(pos_ref, pieces, small, sems.at[0])
    fetch_qkv(pos_ref, pieces, w_qkv, sems.at[pl.ds(1, 3)])
    for r in range(n_rows):
        same = segc_ref[r * ROW_LEN : (r + 1) * ROW_LEN] == segr_ref[r]
        bias[r] = jnp.where(same, 0.0, MASKED)
    whole_wait(small, sems.at[0])
    for h in range(2):
        vec_ref[:, h * HALF : (h + 1) * HALF] = jnp.sum(small[h].astype(F32), axis=0)
    load_x.wait()

    def norm_one(rows):
        xhat, _ = norm_parts(x_ref[rows, :].astype(F32))
        n1_ref[rows, :] = (xhat * vec_ref[0:1, :] + vec_ref[1:2, :]).astype(BF16)

    chunks(tokens, 128, norm_one)
    for t in range(3):
        whole_wait(w_qkv.at[t], sems.at[1 + t])
        y = (nn(n1_ref[...], w_qkv[t]) + vec_ref[2 + t : 3 + t, :]).astype(BF16)
        if t == 0:
            y = y * BF16(HEAD_DIM**-0.5)
        qkv_ref[:, t * D : (t + 1) * D] = y
    masks = head_masks()
    for r in range(n_rows):
        rows = slice(r * ROW_LEN, (r + 1) * ROW_LEN)

        def pair(i, carry):
            q, k, v = (qkv_ref[rows, pair_cols(t, i)] for t in range(3))
            mixed = jnp.zeros((ROW_LEN, 128), F32)
            for hh, keep in enumerate(masks):
                s = nt(q, k * keep) + bias[r]
                e = jnp.exp(s - jnp.max(s, axis=-1, keepdims=True))
                p = (e * (1.0 / jnp.sum(e, axis=-1, keepdims=True))).astype(BF16)
                soft_ref[r * HEADS + 2 * i + hh] = p
                mixed = mixed + nn(p, v * keep)
            mixed_ref[rows, pair_cols(0, i)] = mixed.astype(BF16)
            return carry

        lax.fori_loop(0, PAIRS, pair, 0)


GELU_A = 0.7978845608028654
GELU_B = 0.044715


def quarter(pos_ref, other, s):
    return (pos_ref[1] ^ other) * 2 + s


def quarter_cols(z):
    return pl.ds(pl.multiple_of(z * D, 128), D)


QUARTERS = ((0, 0), (0, 1), (1, 0), (1, 1))


def mlp_up_kernel(pos_ref, segc_ref, vec_ref, mixed_ref, x_any, cot_any, *refs):
    pieces, refs = refs[:PIECES], refs[PIECES:]
    gb_ref, n2_ref, mid_ref, act_ref, slope_ref, gout_ref, w_out, w_up, x_ref, cot_ref, sems = refs
    tokens = n2_ref.shape[0]
    load_cot = start(cot_any, cot_ref, sems.at[3])
    load_x = start(x_any, x_ref, sems.at[4])
    fetch_out(pos_ref, pieces, w_out, sems.at[2])
    fetch_up(pos_ref, pieces, w_up, sems)
    load_cot.wait()
    valid = segc_ref[...] > 0
    gout = jnp.where(valid, cot_ref[...].astype(F32), 0.0)
    gout_ref[...] = gout.astype(BF16)
    gb_ref[...] = jnp.broadcast_to(jnp.sum(gout, axis=0, keepdims=True), gb_ref.shape)
    load_x.wait()
    whole_wait(w_out, sems.at[2])
    mid_ref[...] = x_ref[...].astype(F32) + nn(mixed_ref[...], w_out[...]) + vec_ref[5:6, :]

    def norm_two(rows):
        xhat, _ = norm_parts(mid_ref[rows, :])
        n2_ref[rows, :] = (xhat * vec_ref[6:7, :] + vec_ref[7:8, :]).astype(BF16)

    chunks(tokens, 128, norm_two)
    for other, s in QUARTERS:
        if s == 0:
            whole_wait(w_up.at[other], sems.at[other])
        z = quarter(pos_ref, other, s)
        b_up = vec_ref[pl.ds(8 + z, 1), :]
        cols = quarter_cols(z)

        def part(rows):
            u = nn(n2_ref[rows, :], w_up[other, s]) + b_up
            sq = u * u
            t = jnp.tanh(u * (GELU_A + GELU_A * GELU_B * sq))
            half_up = 0.5 + 0.5 * t
            act_ref[rows, cols] = (u * half_up).astype(BF16)
            slope_ref[rows, cols] = (
                half_up + u * (0.5 - 0.5 * t * t) * (GELU_A + 3.0 * GELU_A * GELU_B * sq)
            ).astype(BF16)

        chunks(tokens, 256, part)


def down_grad_kernel(pos_ref, act_ref, gout_ref, mine, theirs, grad, sem):
    for z in range(4):
        grad[z] = tn(act_ref[:, z * D : (z + 1) * D], gout_ref[...]).astype(BF16)
        for j in range(4):
            place = scatter_place(pos_ref, 4 * z + j)
            for other, out in enumerate((mine, theirs)):
                src = grad.at[z, pl.ds(j * 4 * BLK, 4 * BLK), half_cols(pos_ref, other)]
                start(src, out.at[place], sem.at[0])
    whole_wait(grad, sem.at[0])


def mlp_down_kernel(pos_ref, gout_ref, slope_ref, n2_ref, *refs):
    pieces, refs = refs[:PIECES], refs[PIECES:]
    gb_ref, gpre_ref, w_down, mine, theirs, n2t, grad, sems = refs
    fetch_down(pos_ref, pieces, w_down, sems)
    gb_ref[...] = jnp.zeros(gb_ref.shape, F32)
    n2t[...] = n2_ref[...].T
    for other, s in QUARTERS:
        z = quarter(pos_ref, other, s)
        cols = quarter_cols(z)
        whole_wait(w_down.at[cols], sems.at[z ^ (pos_ref[0] >> 2)])
        ga = nt(gout_ref[...], w_down[cols, :])
        gp = (ga * slope_ref[:, cols].astype(F32)).astype(BF16)
        gpre_ref[:, cols] = gp
        gb_ref[pl.ds(z, 1), :] = jnp.sum(gp.astype(F32), axis=0, keepdims=True)
        grad[other, s] = nn(n2t[...], gp).astype(BF16)
        if s == 1:
            for chip in range(CHIPS):
                place = scatter_place(pos_ref, chip)
                for u in range(2):
                    src = grad.at[other, pl.ds(0, 2), pl.ds(chip * BLK, BLK), pl.ds(u * HALF, HALF)]
                    start(src, (mine, theirs)[other].at[place, pl.ds(2 * u, 2)], sems.at[4])
    whole_wait(grad, sems.at[4])


def norm_back(grad, xhat, scale, gain):
    gn = grad * gain
    mean_gn = jnp.mean(gn, axis=-1, keepdims=True)
    mean_gx = jnp.mean(gn * xhat, axis=-1, keepdims=True)
    return scale * (gn - mean_gn - xhat * mean_gx)


def mid_backward_kernel(
    pos_ref, vec_ref, gbd_ref, gbu_ref, gpre_ref, gout_ref, mid_ref, mixed_ref, w_out, w_up, _, __,
    sums, gmid, gmixed, mine, theirs, acc, gbr, mixt, grad, sem,
):
    tokens = mid_ref.shape[0]
    sums[...] = jnp.zeros(sums.shape, F32)
    sums[8:12, :] = gbu_ref[0:4, :]
    sums[12:13, :] = gbd_ref[0:1, :]
    mixt[...] = mixed_ref[...].T
    for other, s in QUARTERS:
        part = nt(gpre_ref[:, quarter_cols(quarter(pos_ref, other, s))], w_up[other, s])
        acc[...] = part if other + s == 0 else acc[...] + part

    def back_two(rows):
        xhat, scale = norm_parts(mid_ref[rows, :])
        g = acc[rows, :]
        sums[6:7, :] += jnp.sum(g * xhat, axis=0, keepdims=True)
        sums[7:8, :] += jnp.sum(g, axis=0, keepdims=True)
        gm = gout_ref[rows, :].astype(F32) + norm_back(g, xhat, scale, vec_ref[6:7, :])
        gmid[rows, :] = gm
        low = gm.astype(BF16)
        gbr[rows, :] = low
        sums[5:6, :] += jnp.sum(low.astype(F32), axis=0, keepdims=True)

    chunks(tokens, 128, back_two)
    grad[...] = nn(mixt[...], gbr[...]).astype(BF16)
    for chip in range(CHIPS):
        place = scatter_place(pos_ref, chip)
        for other, out in enumerate((mine, theirs)):
            src = grad.at[pl.ds(chip * BLK, BLK), half_cols(pos_ref, other)]
            start(src, out.at[place, 4], sem.at[0])
    gmixed[...] = nt(gbr[...], w_out[...]).astype(BF16)
    whole_wait(grad, sem.at[0])


def attn_backward_kernel(pos_ref, gmixed, qkv_ref, soft_ref, gb_ref, gqkv, give):
    masks = head_masks()
    for r in range(gmixed.shape[0] // ROW_LEN):
        rows = slice(r * ROW_LEN, (r + 1) * ROW_LEN)

        def pair(i, carry):
            q, k, v = (qkv_ref[rows, pair_cols(t, i)] for t in range(3))
            gm = gmixed[rows, pair_cols(0, i)]
            dq = jnp.zeros((ROW_LEN, 128), F32)
            dk = jnp.zeros((ROW_LEN, 128), F32)
            dv = jnp.zeros((ROW_LEN, 128), F32)
            for hh, keep in enumerate(masks):
                p_low = soft_ref[r * HEADS + 2 * i + hh]
                p = p_low.astype(F32)
                gmk = gm * keep
                gs = nt(gmk, v)
                inner = jnp.sum(p * gs, axis=-1, keepdims=True)
                ds = (p * (gs - inner)).astype(BF16)
                dq = dq + nn(ds, k * keep)
                dk = dk + tn(ds, q * keep)
                dv = dv + tn(p_low, gmk)
            gqkv[rows, pair_cols(0, i)] = (dq * (HEAD_DIM**-0.5)).astype(BF16)
            gqkv[rows, pair_cols(1, i)] = dk.astype(BF16)
            gqkv[rows, pair_cols(2, i)] = dv.astype(BF16)
            return carry

        lax.fori_loop(0, PAIRS, pair, 0)
    for t in range(3):
        cols = pl.ds(pl.multiple_of(t * D + (1 - pos_ref[1]) * HALF, 128), HALF)
        give[:, t * HALF : (t + 1) * HALF] = gqkv[:, cols]
    gb_ref[...] = jnp.zeros(gb_ref.shape, F32)
    gb_ref[0:1, :] = jnp.sum(gqkv[:, :D].astype(F32), axis=0, keepdims=True)
    gb_ref[2:3, :] = jnp.sum(gqkv[:, 2 * D :].astype(F32), axis=0, keepdims=True)


def qkv_grad_kernel(
    pos_ref, vec_ref, sums_ref, gbq_ref, gmid, gqkv, n1_ref, w_qkv, n1_got, g_got, x_any,
    igrad, mine, x_ref, acc, n1t, both, grad, sums, small, sems,
):
    tokens = x_ref.shape[0]
    load_x = start(x_any, x_ref, sems.at[0])
    sums[...] = sums_ref[...]
    sums[2:3, :] = gbq_ref[0:1, :]
    sums[4:5, :] = gbq_ref[2:3, :]
    n1t[:, :tokens] = n1_ref[...].T
    n1t[:, tokens:] = n1_got[...].T
    for t in range(3):
        cols = pl.ds(pl.multiple_of(t * D + pos_ref[1] * HALF, 128), HALF)
        both[:tokens, t * HALF : (t + 1) * HALF] = gqkv[:, cols]
    both[tokens:, :] = g_got[...]
    for z in range(4):
        rows = slice(z * 4 * BLK, (z + 1) * 4 * BLK)
        grad[rows, :] = nn(n1t[rows, :], both[...]).astype(BF16)
        for chip in range(4 * z, 4 * z + 4):
            place = scatter_place(pos_ref, chip)
            for t in range(3):
                src = grad.at[pl.ds(chip * BLK, BLK), pl.ds(t * HALF, HALF)]
                start(src, mine.at[place, pl.ds(t * BLK, BLK)], sems.at[1])
    for t in range(3):
        part = nt(gqkv[:, t * D : (t + 1) * D], w_qkv[t])
        acc[...] = part if t == 0 else acc[...] + part
    load_x.wait()

    def back_one(rows):
        xhat, scale = norm_parts(x_ref[rows, :].astype(F32))
        g = acc[rows, :]
        sums[0:1, :] += jnp.sum(g * xhat, axis=0, keepdims=True)
        sums[1:2, :] += jnp.sum(g, axis=0, keepdims=True)
        igrad[rows, :] = (gmid[rows, :] + norm_back(g, xhat, scale, vec_ref[0:1, :])).astype(BF16)

    chunks(tokens, 128, back_one)
    for p in range(CHIPS):
        small[p, 0:16] = sums[:, :HALF].astype(BF16)
        small[p, 16:32] = sums[:, HALF:].astype(BF16)
        start(small.at[p], mine.at[p, pl.ds(3 * BLK, 32)], sems.at[2])
    whole_wait(small, sems.at[2])
    whole_wait(grad, sems.at[1])


def layer_out_kernel(pos_ref, vec_ref, act_ref, mid_ref, w_down, out_ref):
    out_ref[...] = (
        mid_ref[...] + nn(act_ref[...], w_down[...]) + vec_ref[12:13, :]
    ).astype(BF16)


PER = D // (2 * CHIPS)
SEND_ROWS = (3 * PER, 16, 5 * PER, 4 * PER)


def pack_kernel(pos_ref, w_qkv, w_out, w_up, w_down, bu_ref, *refs):
    values, (mine, theirs, rows, last, wide) = refs[:8], refs[8:]
    place = pos_ref[0] * 2 + pos_ref[1]
    rows[...] = jnp.zeros(rows.shape, F32)
    last[...] = jnp.zeros(last.shape, F32)
    for r, value in zip((0, 1, 2, 4, 5, 6, 7, 12), values):
        rows[r : r + 1, 0:PER] = value[...].astype(F32)
    last[0:1, 0 : 4 * PER] = bu_ref[...].astype(F32)
    at = place * (4 * PER)
    up = pltpu.roll(last[...], at % D, 1)[0:1]
    here = lax.broadcasted_iota(jnp.int32, (16, 1), 0) == 8 + at // D
    rows[...] = pltpu.roll(rows[...], place * PER, 1) + jnp.where(here, up, 0.0)
    for out, other in ((mine, 0), (theirs, 1)):
        half = pos_ref[1] ^ other

        def cols(first):
            return pl.ds(pl.multiple_of(first + half * HALF, 128), HALF)

        at = 0
        for t in range(3):
            wide[at : at + PER, :] = w_qkv[:, cols(t * D)].astype(F32)
            at += PER
        wide[at : at + 16, :] = rows[:, cols(0)]
        at += 16
        for n in range(4):
            u, s = n // 2, n % 2
            first = pl.multiple_of(half * (2 * D) + s * D + u * HALF, 128)
            wide[at : at + PER, :] = w_up[:, pl.ds(first, HALF)].astype(F32)
            at += PER
        wide[at : at + PER, :] = w_out[:, cols(0)].astype(F32)
        at += PER
        wide[at : at + 4 * PER, :] = w_down[:, cols(0)].astype(F32)
        out[...] = wide[...].astype(BF16)


def combine_kernel(pos_ref, mine, got, one, two, upper, lower, wide):
    first = pos_ref[1] == 0
    m, g = mine[...].astype(F32), got[...].astype(F32)
    upper[...] = jnp.where(first, m, g)
    lower[...] = jnp.where(first, g, m)

    def pair(at, size):
        wide[0:size, :] = upper[at : at + size, :]
        wide[size : 2 * size, :] = lower[at : at + size, :]
        return wide[0 : 2 * size, :].astype(BF16)

    for t in range(3):
        one[t * BLK : (t + 1) * BLK, :] = pair(t * PER, PER)
    at = 3 * PER
    one[3 * BLK :, :] = (upper[at : at + 16, :] + lower[at : at + 16, :]).astype(BF16)
    at += 16
    for n in range(5):
        two[n] = pair(at + n * PER, PER)
    low = pair(at + 5 * PER, 4 * PER)
    for n in range(4):
        two[5 + n] = low[n * BLK : (n + 1) * BLK]


def finish_kernel(pos_ref, last, *refs):
    terms, (keep, send, held, sems) = refs[:4], refs[4:]
    for i, term in enumerate(terms):
        start(term.at[0], held.at[i], sems.at[i])
    total = last[...].astype(F32)
    for i in range(4):
        whole_wait(held.at[i], sems.at[i])
        total = total + held[i].astype(F32)
    first = pos_ref[1] == 0
    for t in range(3):
        upper, lower = total[t * BLK : t * BLK + PER], total[t * BLK + PER : (t + 1) * BLK]
        keep[t * PER : (t + 1) * PER, :] = jnp.where(first, upper, lower)
        send[t * PER : (t + 1) * PER, :] = jnp.where(first, lower, upper)
    keep[3 * PER :, :] = total[3 * BLK :]
    send[3 * PER :, :] = total[3 * BLK :]


def spread_kernel(pos_ref, keep, got, w_ref, eight_ref, up_ref, down_ref, rows):
    place = pos_ref[0] * 2 + pos_ref[1]
    for ref, other in ((keep, 0), (got, 1)):
        half = pos_ref[1] ^ other
        for t in range(3):
            cols = pl.ds(pl.multiple_of(t * D + half * HALF, 128), HALF)
            w_ref[:, cols] = ref[t * PER : (t + 1) * PER, :]
    for h in range(2):
        at = 3 * PER + 16 * h
        rows[:, h * HALF : (h + 1) * HALF] = keep[at : at + 16, :] + got[at : at + 16, :]
    mine = pltpu.roll(rows[...], lax.rem(D - place * PER, D), 1)
    eight_ref[...] = mine[0:8, 0:PER]
    down_ref[...] = mine[12:13, 0:PER]
    at = place * (4 * PER)
    here = lax.broadcasted_iota(jnp.int32, (16, 1), 0) == 8 + at // D
    row = jnp.sum(jnp.where(here, rows[...], 0.0), axis=0, keepdims=True)
    turned = pltpu.roll(jnp.broadcast_to(row, (8, D)), lax.rem(D - at % D, D), 1)
    up_ref[...] = turned[0:1, 0 : 4 * PER]


def spread_up_kernel(pos_ref, keep, got, up_ref, out_ref):
    for ref, other in ((keep, 0), (got, 1)):
        half = pos_ref[1] ^ other
        for n in range(4):
            first = half * (2 * D) + (n % 2) * D + (n // 2) * HALF
            up_ref[:, pl.ds(pl.multiple_of(first, 128), HALF)] = ref[n]
        out_ref[:, pl.ds(pl.multiple_of(half * HALF, 128), HALF)] = ref[4]


def call(kernel, name, near, far, near_outs, far_outs, scratch, flops, aliases=None, limit=18):
    far = [in_hbm(a) for a in far]
    space = pl.BlockSpec(memory_space=pltpu.VMEM)
    anyspec = pl.BlockSpec(memory_space=pl.ANY)
    outs = tuple(near_outs) + tuple(far_outs)
    moved = sum(math.prod(a.shape) * a.dtype.itemsize for a in (*near, *far, *outs))
    return pl.pallas_call(
        kernel,
        out_shape=outs,
        in_specs=[pl.BlockSpec(memory_space=pltpu.SMEM)]
        + [space] * (len(near) - 1)
        + [anyspec] * len(far),
        out_specs=[space] * len(near_outs) + [anyspec] * len(far_outs),
        scratch_shapes=scratch,
        input_output_aliases=aliases or {},
        compiler_params=pltpu.CompilerParams(vmem_limit_bytes=limit << 20),
        cost_estimate=pl.CostEstimate(flops=flops, bytes_accessed=moved, transcendentals=0),
        name=name,
    )(*near, *far)


def in_hbm(array):
    return pltpu.with_memory_space_constraint(array, pltpu.HBM)


def keep(*arrays):
    return [pltpu.with_memory_space_constraint(a, pltpu.VMEM) for a in arrays]


def swap(value, chip_bit):
    flip = chip_bit * 2 if chip_bit else 1
    return lax.ppermute(value, AXES, [(i, i ^ flip) for i in range(2 * CHIPS)])


def tie(value, *after):
    return lax.optimization_barrier((value,) + after)[0]


def gathered(*own_half):
    return list(own_half) + [swap(piece, 0) for piece in own_half]


def hold(pieces, *after):
    return lax.optimization_barrier((*pieces, *after))[: len(pieces)] if after else pieces


def rounded_sum(*terms):
    total = terms[0].astype(F32)
    for term in terms[1:]:
        total = total + term.astype(F32)
    return total.astype(BF16)


def small_grads(sums, place, per, per_up):
    eight = lax.dynamic_slice(sums, (0, place * per), (8, per))
    at = place * per_up
    up = lax.dynamic_slice(sums, (8 + at // D, at % D), (1, per_up))[0]
    down = lax.dynamic_slice(sums, (12, place * per), (1, per))[0]
    return eight, up, down


def halves(w_qkv, w_out, w_up, w_down):
    rows = w_qkv.shape[0]
    qkv = w_qkv.reshape(rows, 3, 2, HALF)
    up = w_up.reshape(rows, 2, 4, HALF)
    for h in range(2):
        cols = slice(h * HALF, (h + 1) * HALF)
        up_h = up[:, h].reshape(rows, 2, 2, HALF).transpose(2, 1, 0, 3).reshape(4, rows, HALF)
        yield (
            qkv[:, :, h].transpose(1, 0, 2),
            jnp.concatenate([up_h, w_out[None, :, cols]]),
            w_down[:, cols],
        )


def gather_plain(weights, values):
    def whole(w):
        return lax.all_gather(w, AXES, axis=0, tiled=True)

    gain1, bias1, bq, bv, bo, gain2, bias2, bu, bd = [whole(v) for v in values]
    rest = jnp.zeros((3, D), BF16)
    small = jnp.stack([gain1, bias1, bq, jnp.zeros_like(bq), bv, bo, gain2, bias2])
    small = jnp.concatenate([small, bu.reshape(4, D), bd[None], rest])
    groups = ([], [], [])
    for h, (attn, up, down) in enumerate(halves(*[whole(w) for w in weights])):
        attn = attn.reshape(3, CHIPS, BLK, HALF).transpose(1, 0, 2, 3).reshape(CHIPS, 3 * BLK, HALF)
        up = up.reshape(5, CHIPS, BLK, HALF).transpose(1, 0, 2, 3)
        down = down.reshape(CHIPS, 4 * BLK, HALF)
        extra = jnp.zeros((CHIPS, 16, HALF), BF16).at[0].set(small[:, h * HALF : (h + 1) * HALF])
        for group, blocks in zip(groups, (jnp.concatenate([attn, extra], axis=1), up, down)):
            group.extend(jnp.stack([blocks[o] for o in piece]) for piece in GATHER)
    return groups


def scatter_plain(pair, group):
    both = [jnp.stack([part[SCATTER.index(chip)] for chip in range(CHIPS)]) for part in pair]

    def scatter(v):
        return lax.psum_scatter(v.astype(F32), AXES, scatter_dimension=0, tiled=True)

    def matrix(units):
        return jnp.stack(units, axis=3).transpose(0, 2, 1, 3, 4).reshape(D, -1, 2, HALF)

    if group == "attn":
        sums = jnp.concatenate([both[0][0, 3 * BLK + 16 * h :][:16] for h in range(2)], axis=1)
        qkv = matrix([b[:, : 3 * BLK].reshape(CHIPS, 3, BLK, HALF) for b in both])
        return scatter(qkv.reshape(D, 3 * D)), lax.psum(sums.astype(F32), AXES)
    if group == "up":
        up = matrix(both)
        order = up[:, :4].reshape(D, 2, 2, 2, HALF).transpose(0, 3, 2, 1, 4)
        return scatter(order.reshape(D, FF)), scatter(up[:, 4].reshape(D, D))
    return scatter(jnp.concatenate([b.reshape(FF, HALF) for b in both], axis=1))


def shape(dims, kind=BF16):
    return jax.ShapeDtypeStruct(dims, kind)


def far_shape(*dims):
    return pltpu.HBM(dims, BF16)


def dma(n):
    return pltpu.SemaphoreType.DMA((n,))


def vmem(*dims, kind=BF16):
    return pltpu.VMEM(dims, kind)


class Layer:
    def __init__(self, tokens):
        self.tokens = tokens
        self.rows = tokens // ROW_LEN
        self.out = shape((tokens, D))
        self.wide = vmem(tokens, FF)
        self.one = vmem(tokens, D)
        self.one_f32 = vmem(tokens, D, kind=F32)
        self.qkv = vmem(tokens, 3 * D)
        self.soft = vmem(self.rows * HEADS, ROW_LEN, ROW_LEN)
        self.turned = vmem(D, tokens)
        self.square = vmem(D, D)
        self.three = vmem(3, D, D)
        self.four = vmem(2, 2, D, D)
        self.sums = vmem(8, D, kind=F32)
        self.vec = vmem(16, D, kind=F32)

    def chip_blocks(self, pos, weights, values):
        *rest, bu, bd = [in_hbm(v.reshape(1, -1)) for v in values]
        weights = [in_hbm(w) for w in weights]
        sent = shape((sum(SEND_ROWS), HALF))
        wide = vmem(sum(SEND_ROWS), HALF, kind=F32)
        mine, theirs = call(
            pack_kernel, "pack", (pos, *weights, bu, *rest, bd), (), (sent, sent), (),
            [vmem(16, D, kind=F32), vmem(8, D, kind=F32), wide], 0,
        )
        return call(
            combine_kernel, "combine", (pos, mine, swap(theirs, 0)), (),
            (shape((3 * BLK + 16, HALF)), shape((9, BLK, HALF))), (),
            [wide, wide, vmem(4 * BLK, HALF, kind=F32)], 0,
        )

    def finish(self, pos, last, low):
        sent = shape((3 * PER + 32, HALF), F32)
        keep, send = call(
            finish_kernel, "finish", (pos, last), low, (sent, sent), (),
            [vmem(4, 3 * BLK + 32, HALF), dma(4)], 0,
        )
        return call(
            spread_kernel, "spread", (pos, keep, swap(send, 0)), (),
            (shape((PER, 3 * D), F32), shape((8, PER), F32), shape((1, 4 * PER), F32), shape((1, PER), F32)),
            (), [vmem(16, D, kind=F32)], 0,
        )

    def spread_up(self, pos, keep, got):
        return call(
            spread_up_kernel, "spread_up", (pos, keep, got), (),
            (shape((PER, FF), F32), shape((PER, D), F32)), (), [], 0,
        )

    def attn_forward(self, pos, segr, segc, inputs, attn):
        return call(
            attn_forward_kernel, "attn_forward", (pos, segr, segc), [in_hbm(inputs)] + attn,
            (self.vec, self.one, self.qkv, self.soft, self.one, self.three), (),
            [
                self.one, vmem(2, CHIPS, 16, HALF),
                vmem(self.rows, ROW_LEN, ROW_LEN, kind=F32), dma(5),
            ],
            2 * self.tokens * D * D * 3 + 8 * self.tokens * D * ROW_LEN,
        )

    def mlp_up(self, pos, segc, vec, inputs, mixed, cotangent, up):
        vec, mixed = keep(vec, mixed)
        return call(
            mlp_up_kernel, "mlp_up", (pos, segc, vec, mixed), [inputs, cotangent] + up,
            (self.sums, self.one, self.one_f32, self.wide, self.wide, self.one, self.square, self.four), (),
            [self.one, self.one, dma(5)],
            2 * self.tokens * D * (FF + D),
        )

    def down_grad(self, pos, act, gout):
        buffer = far_shape(CHIPS, 4 * BLK, HALF)
        return call(
            down_grad_kernel, "down_grad", (pos, *keep(act, gout)), [], (), (buffer, buffer),
            [vmem(4, D, D), dma(1)],
            2 * self.tokens * D * FF,
        )

    def mlp_down(self, pos, gout, slope, n2, down):
        buffer = far_shape(CHIPS, 5, BLK, HALF)
        return call(
            mlp_down_kernel, "mlp_down", (pos, *keep(gout, slope, n2)), down,
            (self.sums, self.wide, vmem(FF, D)), (buffer, buffer),
            [self.turned, self.four, dma(5)],
            4 * self.tokens * D * FF,
        )

    def mid_backward(self, pos, vec, gbd, gbu, gpre, gout, mid, mixed, w_out, w_up, mine, theirs):
        buffer = far_shape(*mine.shape)
        near = (pos, *keep(vec, gbd, gbu, gpre, gout, mid, mixed, w_out, w_up))
        return call(
            mid_backward_kernel, "mid_backward", near, [mine, theirs],
            (self.vec, self.one_f32, self.one), (buffer, buffer),
            [self.one_f32, self.one, self.turned, self.square, dma(1)],
            2 * self.tokens * D * (FF + 2 * D),
            {len(near): 3, len(near) + 1: 4},
        )

    def attn_backward(self, pos, gmixed, qkv, soft):
        return call(
            attn_backward_kernel, "attn_backward", (pos, *keep(gmixed, qkv, soft)), [],
            (self.sums, self.qkv, vmem(self.tokens, 3 * HALF)), (), [], 20 * self.tokens * D * ROW_LEN,
        )

    def qkv_grad(self, pos, vec, sums, gbq, gmid, gqkv, n1, w_qkv, n1_got, g_got, inputs):
        return call(
            qkv_grad_kernel, "qkv_grad", (pos, *keep(vec, sums, gbq, gmid, gqkv, n1, w_qkv, n1_got, g_got)),
            [inputs], (self.out,), (far_shape(CHIPS, 3 * BLK + 32, HALF),),
            [
                self.one, self.one_f32, vmem(D, 2 * self.tokens), vmem(2 * self.tokens, 3 * HALF),
                vmem(D, 3 * HALF), vmem(16, D, kind=F32), vmem(CHIPS, 32, HALF), dma(3),
            ],
            2 * self.tokens * D * 6 * D,
        )

    def layer_out(self, pos, vec, act, mid, w_down):
        (out,) = call(
            layer_out_kernel, "layer_out", (pos, *keep(vec, act, mid, w_down)), [], (self.out,), (), [],
            2 * self.tokens * D * FF,
        )
        return out


class Scatter:
    def __init__(self, mine, theirs=None, *after):
        self.both = [mine] if theirs is None else [mine, swap(tie(theirs, *after), 0)]

    def part(self, first, last):
        return [ref[first:last] for ref in self.both]

    def hold_back(self, *after):
        self.both[-1] = hold((self.both[-1],), *after)[0]

    def first(self, *after):
        self.hold_back(*after)
        self.out = (rounded_sum(*self.part(8, 12)), rounded_sum(*self.part(12, 16)))
        self.in_y, self.in_x = swap(self.out[0], BIT_Y), swap(self.out[1], BIT_X)

    def second(self, *after):
        in_y, in_x = hold((self.in_y, self.in_x), *after)
        self.out = (
            rounded_sum(*self.part(4, 6), in_x[2:]),
            rounded_sum(*self.part(6, 8), in_y[2:]),
        )
        self.in_y, self.in_x = in_y, in_x
        self.in_y2, self.in_x2 = swap(self.out[0], BIT_Y), swap(self.out[1], BIT_X)

    def third(self, *after):
        in_y2, in_x2 = hold((self.in_y2, self.in_x2), *after)
        self.near = (*self.part(0, 2), self.in_x[:2], in_y2)
        self.out = (rounded_sum(*self.part(2, 4), self.in_y[:2], in_x2),)
        self.in_z = swap(self.out[0], BIT_Z0)

    def diagonal(self, *after):
        self.hold_back(*after)
        self.out = (rounded_sum(*self.part(10, 12)), rounded_sum(*self.part(14, 16)))
        self.in_y, self.in_x = swap(self.out[0], BIT_Y), swap(self.out[1], BIT_X)

    def hi(self, *after):
        in_y, self.in_x = hold((self.in_y, self.in_x), *after)
        self.out = (rounded_sum(*self.part(8, 10)), rounded_sum(*self.part(6, 8), in_y))
        self.in_y2, self.in_x2 = swap(self.out[0], BIT_Y), swap(self.out[1], BIT_X)

    def lo(self, *after):
        in_y2, in_x2 = hold((self.in_y2, self.in_x2), *after)
        far = rounded_sum(*self.part(2, 4), in_y2, in_x2)
        self.in_z = swap(far, BIT_Z0)
        low_y, low_x = rounded_sum(*self.part(4, 6), self.in_x), rounded_sum(*self.part(12, 14))
        low_y, low_x = hold((low_y, low_x), far)
        self.out = (far, low_y, low_x)
        self.near = (*self.part(0, 2), swap(low_y, BIT_Y), swap(low_x, BIT_X))

    def fourth(self, *after):
        self.near = (*self.near, *hold((self.in_z,), *after))
        self.out = (rounded_sum(*[t[1] for t in self.near]),)
        self.in_z = swap(self.out[0], BIT_Z1)

    def result(self, *after):
        total = hold((self.in_z,), *after)[0].astype(F32)
        for term in self.near:
            total = total + term[0].astype(F32)
        return total


def per_device(tuned, *args):
    (
        inputs, segment_ids, pre_attn_gain, pre_attn_bias, w_qkv, b_query, b_value, w_out, b_out,
        pre_mlp_gain, pre_mlp_bias, w_up, b_up, w_down, b_down, cotangent,
    ) = args
    tokens = inputs.shape[0]
    n_rows = tokens // ROW_LEN
    wide, narrow = lax.axis_index("wide"), lax.axis_index("narrow")
    weights = (w_qkv, w_out, w_up, w_down)
    values = (
        pre_attn_gain, pre_attn_bias, b_query, b_value, b_out, pre_mlp_gain, pre_mlp_bias, b_up, b_down,
    )
    per, per_up = pre_attn_gain.shape[0], b_up.shape[0]
    position = jnp.arange(ROW_LEN, dtype=jnp.int32)[None]
    own_id = jnp.where(segment_ids != 0, segment_ids, -1 - position)
    segr = own_id.reshape(n_rows, 1, ROW_LEN)
    segc = own_id.reshape(tokens, 1)
    layer = Layer(tokens)

    if not tuned:
        place = wide * lax.axis_size("narrow") + narrow
        pos = jnp.zeros((2,), jnp.int32)
        attn, up, down = gather_plain(weights, values)
        vec, n1, qkv, soft, mixed, w_qkv_all = layer.attn_forward(pos, segr, segc, inputs, attn)
        gbd, n2, mid, act, slope, gout, *w_mid = layer.mlp_up(pos, segc, vec, inputs, mixed, cotangent, up)
        pair_down = layer.down_grad(pos, act, gout)
        gbu, gpre, w_down_all, *pair_up = layer.mlp_down(pos, gout, slope, n2, down)
        sums, gmid, gmixed, *pair_up = layer.mid_backward(
            pos, vec, gbd, gbu, gpre, gout, mid, mixed, *w_mid, *pair_up
        )
        gbq, gqkv, give = layer.attn_backward(pos, gmixed, qkv, soft)
        pair_attn = []
        for half in range(2):
            input_grad, blocks = layer.qkv_grad(
                jnp.array([0, half], jnp.int32), vec, sums, gbq, gmid, gqkv, n1, w_qkv_all,
                jnp.zeros_like(n1), jnp.zeros_like(give), inputs,
            )
            pair_attn.append(blocks)
        layer_out = layer.layer_out(pos, vec, act, mid, w_down_all)
        grad_w_down = scatter_plain(pair_down, "down")
        grad_w_up, grad_w_out = scatter_plain(pair_up, "up")
        grad_w_qkv, sums = scatter_plain(pair_attn, "attn")
        eight, grad_b_up, grad_b_down = small_grads(sums, place, per, per_up)
    else:
        core = (narrow & 1).astype(jnp.int32)
        pos = jnp.stack([wide * 2 + (narrow >> 1), core]).astype(jnp.int32)
        block1, block23 = layer.chip_blocks(pos, weights, values)
        flat = (4 * BLK, HALF)

        near1 = swap(block1, BIT_Z1)
        lo1 = jnp.stack([block1, near1])
        hi1 = swap(lo1, BIT_Z0)
        y_lo1, x_lo1 = swap(lo1, BIT_Y), swap(lo1, BIT_X)
        near23 = swap(tie(block23, near1), BIT_Z1)
        d_lo1 = swap(y_lo1, BIT_X)
        y_hi1, x_hi1 = swap(hi1, BIT_Y), swap(hi1, BIT_X)
        lo2 = jnp.stack([block23[:5], near23[:5]])
        lo3 = jnp.stack([block23[5:].reshape(flat), near23[5:].reshape(flat)])
        hi2 = swap(tie(lo2, hi1), BIT_Z0)
        d_hi1 = swap(tie(x_hi1, y_hi1), BIT_Y)
        lo2b = tie(lo2, d_lo1, x_hi1, y_hi1)
        y_lo2, x_lo2 = swap(lo2b, BIT_Y), swap(lo2b, BIT_X)
        attn = gathered(lo1, hi1, y_lo1, y_hi1, x_lo1, x_hi1, d_lo1, d_hi1)
        hi3 = swap(tie(lo3, hi2), BIT_Z0)
        y_hi2, x_hi2 = swap(hi2, BIT_Y), swap(hi2, BIT_X)
        d_lo2, d_hi2 = swap(y_lo2, BIT_X), swap(tie(x_hi2, y_hi2), BIT_Y)
        lo3b = tie(lo3, y_lo2, x_lo2, y_hi2)
        y_lo3, x_lo3 = swap(lo3b, BIT_Y), swap(lo3b, BIT_X)
        vec, n1, qkv, soft, mixed, w_qkv_all = layer.attn_forward(
            tie(pos, y_hi2, x_hi2, lo3b, d_lo2), segr, segc, inputs, attn
        )

        d_hi2, y_lo3, x_lo3, hi3 = hold((d_hi2, y_lo3, x_lo3, hi3), mixed)
        d_lo3 = swap(y_lo3, BIT_X)
        y_hi3, x_hi3 = swap(hi3, BIT_Y), swap(hi3, BIT_X)
        lo2, hi2, y_lo2, y_hi2, x_lo2, x_hi2, d_lo2 = hold(
            (lo2, hi2, y_lo2, y_hi2, x_lo2, x_hi2, d_lo2), x_lo3, hi3
        )
        up = gathered(lo2, hi2, y_lo2, y_hi2, x_lo2, x_hi2, d_lo2, d_hi2)
        gbd, n2, mid, act, slope, gout, *w_mid = layer.mlp_up(
            tie(pos, hi3, y_lo3, x_lo3), segc, vec, inputs, mixed, cotangent, up
        )
        y_hi3, x_hi3, d_lo3 = hold((y_hi3, x_hi3, d_lo3), gbd)
        d_hi3 = swap(x_hi3, BIT_Y)
        pair_down = layer.down_grad(tie(pos, y_hi3, x_hi3, d_lo3), act, gout)
        d_hi3 = tie(d_hi3, pair_down[0])
        down = gathered(lo3, hi3, y_lo3, y_hi3, x_lo3, x_hi3, d_lo3, d_hi3)
        scatter1 = Scatter(*pair_down, *down)
        gbu, gpre, w_down_all, *pair_up = layer.mlp_down(pos, gout, slope, n2, down)
        scatter1.diagonal(gbu)
        sums, gmid, gmixed, *pair_up = layer.mid_backward(
            tie(pos, *scatter1.out), vec, gbd, gbu, gpre, gout, mid, mixed, *w_mid, *pair_up
        )
        scatter1.hi(sums)
        scatter2 = Scatter(*pair_up, scatter1.in_x)
        gbq, gqkv, give = layer.attn_backward(tie(pos, *scatter1.out), gmixed, qkv, soft)
        scatter1.lo(gbq)
        n1, give = hold((n1, give), *scatter1.out)
        n1_got, g_got = swap(n1, 0), swap(give, 0)
        scatter2.diagonal(gbq)
        input_grad, sums_attn = layer.qkv_grad(
            tie(pos, *scatter2.out, *scatter1.out),
            vec, sums, gbq, gmid, gqkv, n1, w_qkv_all, n1_got, g_got, inputs,
        )
        scatter2.hi(input_grad)
        scatter1.fourth(input_grad)
        scatter3 = Scatter(tie(sums_attn, *scatter2.out))
        scatter3.diagonal()
        layer_out = layer.layer_out(
            tie(pos, *scatter3.out, *scatter1.out), vec, act, mid, w_down_all
        )
        scatter1.in_z = tie(scatter1.in_z, layer_out)
        scatter3.hi(layer_out, scatter1.in_z)
        scatter2.lo(*scatter3.out)
        scatter3.lo(*scatter2.out)
        scatter2.fourth(*scatter3.out)
        scatter3.fourth(*scatter2.out)

        def exchange(blocks, axis):
            first, second = jnp.split(blocks, 2, axis=axis)
            keep = jnp.where(core == 0, first, second)
            got = swap(jnp.where(core == 0, second, first), 0)
            return jnp.where(core == 0, keep, got), jnp.where(core == 0, got, keep)

        grad_w_down = jnp.concatenate(exchange(scatter1.result(*scatter3.out), 0), axis=1)
        total = scatter2.result(*scatter3.out)
        upper, lower = total[:, :PER], total[:, PER:]
        got = swap(jnp.where(core == 0, lower, upper), 0)
        grad_w_up, grad_w_out = layer.spread_up(pos, jnp.where(core == 0, upper, lower), got)
        grad_w_qkv, eight, grad_b_up, grad_b_down = layer.finish(
            pos, scatter3.in_z, [*scatter3.both, *scatter3.near[1:]]
        )
        grad_b_up, grad_b_down = grad_b_up[0], grad_b_down[0]
    return (
        layer_out, input_grad, eight[0], eight[1], grad_w_qkv, eight[2], eight[4], grad_w_out, eight[5],
        eight[6], eight[7], grad_w_up, grad_b_up, grad_w_down, grad_b_down,
    )


def solution(mesh):
    both = P(AXES, None)
    one = P(AXES)
    tuned = dict(mesh.shape) == {"wide": 8, "narrow": 4}
    in_specs = (both, both, one, one, both, one, one, both, one, one, one, both, one, both, one, both)
    out_specs = (both, both, one, one, both, one, one, both, one, one, one, both, one, both, one)
    return jax.shard_map(
        functools.partial(per_device, tuned),
        mesh=mesh,
        in_specs=in_specs,
        out_specs=out_specs,
        check_vma=False,
    )
```

```python
import functools
import math

import jax
import jax.numpy as jnp
from jax import lax
from jax.experimental import pallas as pl
from jax.experimental.pallas import tpu as pltpu
from jax.sharding import PartitionSpec as P

HEADS = 12
HEAD_DIM = 64
D = 768
FF = 3072
ROW_LEN = 256
HALF = 384
CHIPS = 16
BLK = 48
PAIRS = HEADS // 2
AXES = ("wide", "narrow")

EPS = 1e-06
MASKED = -1e30
F32 = jnp.float32
BF16 = jnp.bfloat16

BIT_Y, BIT_X, BIT_Z0, BIT_Z1 = 1, 2, 4, 8
Z_OFFSETS = (0, 4, 8, 12)

GATHER = tuple((o + z, o + z + BIT_Z1) for o in (0, BIT_Y, BIT_X, BIT_X + BIT_Y) for z in (0, BIT_Z0))
PIECES = 2 * len(GATHER)

SCATTER = (0, 8, 4, 12, 1, 9, 6, 14, 5, 13, 7, 15, 2, 10, 3, 11)


def nt(a, b):
    return lax.dot_general(a, b, (((1,), (1,)), ((), ())), preferred_element_type=F32)


def tn(a, b):
    return lax.dot_general(a, b, (((0,), (0,)), ((), ())), preferred_element_type=F32)


def nn(a, b):
    return lax.dot_general(a, b, (((1,), (0,)), ((), ())), preferred_element_type=F32)


def chunks(tokens, step, body):
    def one(i, carry):
        body(pl.ds(pl.multiple_of(i * step, step), step))
        return carry

    lax.fori_loop(0, tokens // step, one, 0)


def norm_parts(v):
    centre = jnp.mean(v, axis=-1, keepdims=True)
    centred = v - centre
    scale = lax.rsqrt(jnp.mean(centred * centred, axis=-1, keepdims=True) + EPS)
    return centred * scale, scale


def start(src, dst, sem):
    copy = pltpu.make_async_copy(src, dst, sem)
    copy.start()
    return copy


def whole_wait(ref, sem):
    pltpu.make_async_copy(ref, ref, sem).wait()


def each_block(pos_ref, pieces):
    for other in range(2):
        for ref, offsets in zip(pieces[other * len(GATHER) :], GATHER):
            for b, offset in enumerate(offsets):
                yield ref, b, pos_ref[0] ^ offset, other, offset


def chip_rows(chip, size):
    return pl.ds(pl.multiple_of(chip * size, 16), size)


def half_cols(pos_ref, other):
    return pl.ds(pl.multiple_of((pos_ref[1] ^ other) * HALF, 128), HALF)


def fetch_qkv(pos_ref, pieces, w_qkv, sems):
    for t in range(3):
        for ref, b, chip, other, _ in each_block(pos_ref, pieces):
            dst = w_qkv.at[t, chip_rows(chip, BLK), half_cols(pos_ref, other)]
            start(ref.at[b, pl.ds(t * BLK, BLK)], dst, sems.at[t])


def fetch_out(pos_ref, pieces, w_out, sem):
    for ref, b, chip, other, _ in each_block(pos_ref, pieces):
        dst = w_out.at[chip_rows(chip, BLK), half_cols(pos_ref, other)]
        start(ref.at[b, 4], dst, sem)


def fetch_small(pos_ref, pieces, small, sem):
    for ref, b, chip, other, _ in each_block(pos_ref, pieces):
        start(ref.at[b, pl.ds(3 * BLK, 16)], small.at[pos_ref[1] ^ other, chip], sem)


def fetch_up(pos_ref, pieces, w_up, sems):
    for ref, b, chip, other, _ in each_block(pos_ref, pieces):
        for u in range(2):
            dst = w_up.at[other, pl.ds(0, 2), chip_rows(chip, BLK), pl.ds(u * HALF, HALF)]
            start(ref.at[b, pl.ds(2 * u, 2)], dst, sems.at[other])


def fetch_down(pos_ref, pieces, w_down, sems):
    for q in range(4):
        for ref, b, chip, other, offset in each_block(pos_ref, pieces):
            if offset // 4 == q:
                dst = w_down.at[chip_rows(chip, 4 * BLK), half_cols(pos_ref, other)]
                start(ref.at[b], dst, sems.at[q])


def scatter_place(pos_ref, chip):
    offset = pos_ref[0] ^ chip
    xy, z = offset & 3, ((offset >> 2) & 1) * 2 + (offset >> 3)
    near = jnp.where(xy == 1, 4, jnp.where(xy == 2, 12, 14)) + z
    far = jnp.where(xy == 1, 6, jnp.where(xy == 2, 4, 8)) + z
    return jnp.where(xy == 0, z, jnp.where(z < 2, near, far))


def head_masks():
    lane = lax.broadcasted_iota(jnp.int32, (1, 2 * HEAD_DIM), 1)
    return [(lane // HEAD_DIM == hh).astype(F32).astype(BF16) for hh in range(2)]


def pair_cols(t, i):
    return pl.ds(pl.multiple_of(t * D + i * 128, 128), 128)


def attn_forward_kernel(pos_ref, segr_ref, segc_ref, x_any, *refs):
    pieces, refs = refs[:PIECES], refs[PIECES:]
    vec_ref, n1_ref, qkv_ref, soft_ref, mixed_ref, w_qkv, x_ref, small, bias, sems = refs
    tokens = x_ref.shape[0]
    n_rows = tokens // ROW_LEN
    load_x = start(x_any, x_ref, sems.at[4])
    fetch_small(pos_ref, pieces, small, sems.at[0])
    fetch_qkv(pos_ref, pieces, w_qkv, sems.at[pl.ds(1, 3)])
    for r in range(n_rows):
        same = segc_ref[r * ROW_LEN : (r + 1) * ROW_LEN] == segr_ref[r]
        bias[r] = jnp.where(same, 0.0, MASKED)
    whole_wait(small, sems.at[0])
    for h in range(2):
        vec_ref[:, h * HALF : (h + 1) * HALF] = jnp.sum(small[h].astype(F32), axis=0)
    load_x.wait()

    def norm_one(rows):
        xhat, _ = norm_parts(x_ref[rows, :].astype(F32))
        n1_ref[rows, :] = (xhat * vec_ref[0:1, :] + vec_ref[1:2, :]).astype(BF16)

    chunks(tokens, 256, norm_one)
    for t in range(3):
        whole_wait(w_qkv.at[t], sems.at[1 + t])
        y = (nn(n1_ref[...], w_qkv[t]) + vec_ref[2 + t : 3 + t, :]).astype(BF16)
        if t == 0:
            y = y * BF16(HEAD_DIM**-0.5)
        qkv_ref[:, t * D : (t + 1) * D] = y
    masks = head_masks()
    for r in range(n_rows):
        rows = slice(r * ROW_LEN, (r + 1) * ROW_LEN)

        def pair(i, carry):
            q, k, v = (qkv_ref[rows, pair_cols(t, i)] for t in range(3))
            mixed = jnp.zeros((ROW_LEN, 128), F32)
            for hh, keep in enumerate(masks):
                s = nt(q, k * keep) + bias[r]
                e = jnp.exp(s - jnp.max(s, axis=-1, keepdims=True))
                p = (e * (1.0 / jnp.sum(e, axis=-1, keepdims=True))).astype(BF16)
                soft_ref[r * HEADS + 2 * i + hh] = p
                mixed = mixed + nn(p, v * keep)
            mixed_ref[rows, pair_cols(0, i)] = mixed.astype(BF16)
            return carry

        lax.fori_loop(0, PAIRS, pair, 0, unroll=PAIRS)


GELU_A = 0.7978845608028654
GELU_B = 0.044715


def quarter(pos_ref, other, s):
    return (pos_ref[1] ^ other) * 2 + s


def quarter_cols(z):
    return pl.ds(pl.multiple_of(z * D, 128), D)


QUARTERS = ((0, 0), (0, 1), (1, 0), (1, 1))


def mlp_up_kernel(pos_ref, segc_ref, vec_ref, mixed_ref, x_any, cot_any, *refs):
    pieces, refs = refs[:PIECES], refs[PIECES:]
    gb_ref, n2_ref, mid_ref, act_ref, slope_ref, gout_ref, w_out, w_up, x_ref, cot_ref, sems = refs
    tokens = n2_ref.shape[0]
    load_cot = start(cot_any, cot_ref, sems.at[3])
    load_x = start(x_any, x_ref, sems.at[4])
    fetch_out(pos_ref, pieces, w_out, sems.at[2])
    fetch_up(pos_ref, pieces, w_up, sems)
    load_cot.wait()
    valid = segc_ref[...] > 0
    gout = jnp.where(valid, cot_ref[...].astype(F32), 0.0)
    gout_ref[...] = gout.astype(BF16)
    gb_ref[...] = jnp.broadcast_to(jnp.sum(gout, axis=0, keepdims=True), gb_ref.shape)
    load_x.wait()
    whole_wait(w_out, sems.at[2])
    mid_ref[...] = x_ref[...].astype(F32) + nn(mixed_ref[...], w_out[...]) + vec_ref[5:6, :]

    def norm_two(rows):
        xhat, _ = norm_parts(mid_ref[rows, :])
        n2_ref[rows, :] = (xhat * vec_ref[6:7, :] + vec_ref[7:8, :]).astype(BF16)

    chunks(tokens, 256, norm_two)
    for other, s in QUARTERS:
        if s == 0:
            whole_wait(w_up.at[other], sems.at[other])
        z = quarter(pos_ref, other, s)
        b_up = vec_ref[pl.ds(8 + z, 1), :]
        cols = quarter_cols(z)

        def part(rows):
            u = nn(n2_ref[rows, :], w_up[other, s]) + b_up
            sq = u * u
            t = jnp.tanh(u * (GELU_A + GELU_A * GELU_B * sq))
            half_up = 0.5 + 0.5 * t
            act_ref[rows, cols] = (u * half_up).astype(BF16)
            slope_ref[rows, cols] = (
                half_up + u * (0.5 - 0.5 * t * t) * (GELU_A + 3.0 * GELU_A * GELU_B * sq)
            ).astype(BF16)

        chunks(tokens, 512, part)


def down_grad_kernel(pos_ref, act_ref, gout_ref, mine, theirs, grad, sem):
    for z in range(4):
        grad[z] = tn(act_ref[:, z * D : (z + 1) * D], gout_ref[...]).astype(BF16)
        for j in range(4):
            place = scatter_place(pos_ref, 4 * z + j)
            for other, out in enumerate((mine, theirs)):
                src = grad.at[z, pl.ds(j * 4 * BLK, 4 * BLK), half_cols(pos_ref, other)]
                start(src, out.at[place], sem.at[0])
    whole_wait(grad, sem.at[0])


def mlp_down_kernel(pos_ref, gout_ref, slope_ref, n2_ref, *refs):
    pieces, refs = refs[:PIECES], refs[PIECES:]
    gb_ref, gpre_ref, w_down, mine, theirs, n2t, grad, sems = refs
    fetch_down(pos_ref, pieces, w_down, sems)
    gb_ref[...] = jnp.zeros(gb_ref.shape, F32)
    n2t[...] = n2_ref[...].T
    for other, s in QUARTERS:
        z = quarter(pos_ref, other, s)
        cols = quarter_cols(z)
        whole_wait(w_down.at[cols], sems.at[z ^ (pos_ref[0] >> 2)])
        ga = nt(gout_ref[...], w_down[cols, :])
        gp = (ga * slope_ref[:, cols].astype(F32)).astype(BF16)
        gpre_ref[:, cols] = gp
        gb_ref[pl.ds(z, 1), :] = jnp.sum(gp.astype(F32), axis=0, keepdims=True)
        grad[other, s] = nn(n2t[...], gp).astype(BF16)
        if s == 1:
            for chip in range(CHIPS):
                place = scatter_place(pos_ref, chip)
                for u in range(2):
                    src = grad.at[other, pl.ds(0, 2), pl.ds(chip * BLK, BLK), pl.ds(u * HALF, HALF)]
                    start(src, (mine, theirs)[other].at[place, pl.ds(2 * u, 2)], sems.at[4])
    whole_wait(grad, sems.at[4])


def norm_back(grad, xhat, scale, gain):
    gn = grad * gain
    mean_gn = jnp.mean(gn, axis=-1, keepdims=True)
    mean_gx = jnp.mean(gn * xhat, axis=-1, keepdims=True)
    return scale * (gn - mean_gn - xhat * mean_gx)


def mid_backward_kernel(
    pos_ref, vec_ref, gbd_ref, gbu_ref, gpre_ref, gout_ref, mid_ref, mixed_ref, w_out, w_up, _, __,
    sums, gmid, gmixed, mine, theirs, acc, gbr, mixt, grad, sem,
):
    tokens = mid_ref.shape[0]
    sums[...] = jnp.zeros(sums.shape, F32)
    sums[8:12, :] = gbu_ref[0:4, :]
    sums[12:13, :] = gbd_ref[0:1, :]
    mixt[...] = mixed_ref[...].T
    for other, s in QUARTERS:
        part = nt(gpre_ref[:, quarter_cols(quarter(pos_ref, other, s))], w_up[other, s])
        acc[...] = part if other + s == 0 else acc[...] + part

    def back_two(rows):
        xhat, scale = norm_parts(mid_ref[rows, :])
        g = acc[rows, :]
        sums[6:7, :] += jnp.sum(g * xhat, axis=0, keepdims=True)
        sums[7:8, :] += jnp.sum(g, axis=0, keepdims=True)
        gm = gout_ref[rows, :].astype(F32) + norm_back(g, xhat, scale, vec_ref[6:7, :])
        gmid[rows, :] = gm
        low = gm.astype(BF16)
        gbr[rows, :] = low
        sums[5:6, :] += jnp.sum(low.astype(F32), axis=0, keepdims=True)

    chunks(tokens, 256, back_two)
    grad[...] = nn(mixt[...], gbr[...]).astype(BF16)
    for chip in range(CHIPS):
        place = scatter_place(pos_ref, chip)
        for other, out in enumerate((mine, theirs)):
            src = grad.at[pl.ds(chip * BLK, BLK), half_cols(pos_ref, other)]
            start(src, out.at[place, 4], sem.at[0])
    gmixed[...] = nt(gbr[...], w_out[...]).astype(BF16)
    whole_wait(grad, sem.at[0])


def attn_backward_kernel(pos_ref, gmixed, qkv_ref, soft_ref, gb_ref, gqkv, give):
    masks = head_masks()
    for r in range(gmixed.shape[0] // ROW_LEN):
        rows = slice(r * ROW_LEN, (r + 1) * ROW_LEN)

        def pair(i, carry):
            q, k, v = (qkv_ref[rows, pair_cols(t, i)] for t in range(3))
            gm = gmixed[rows, pair_cols(0, i)]
            dq = jnp.zeros((ROW_LEN, 128), F32)
            dk = jnp.zeros((ROW_LEN, 128), F32)
            dv = jnp.zeros((ROW_LEN, 128), F32)
            for hh, keep in enumerate(masks):
                p_low = soft_ref[r * HEADS + 2 * i + hh]
                p = p_low.astype(F32)
                gmk = gm * keep
                gs = nt(gmk, v)
                inner = jnp.sum(p * gs, axis=-1, keepdims=True)
                ds = (p * (gs - inner)).astype(BF16)
                dq = dq + nn(ds, k * keep)
                dk = dk + tn(ds, q * keep)
                dv = dv + tn(p_low, gmk)
            gqkv[rows, pair_cols(0, i)] = (dq * (HEAD_DIM**-0.5)).astype(BF16)
            gqkv[rows, pair_cols(1, i)] = dk.astype(BF16)
            gqkv[rows, pair_cols(2, i)] = dv.astype(BF16)
            return carry

        lax.fori_loop(0, PAIRS, pair, 0, unroll=PAIRS)
    for t in range(3):
        cols = pl.ds(pl.multiple_of(t * D + (1 - pos_ref[1]) * HALF, 128), HALF)
        give[:, t * HALF : (t + 1) * HALF] = gqkv[:, cols]
    gb_ref[...] = jnp.zeros(gb_ref.shape, F32)
    gb_ref[0:1, :] = jnp.sum(gqkv[:, :D].astype(F32), axis=0, keepdims=True)
    gb_ref[2:3, :] = jnp.sum(gqkv[:, 2 * D :].astype(F32), axis=0, keepdims=True)


def up_rows():
    row = lax.broadcasted_iota(jnp.int32, (16, 1), 0)
    return (row >= 8) & (row < 12)


def qkv_grad_kernel(
    pos_ref, vec_ref, sums_ref, gbq_ref, gmid, gqkv, n1_ref, w_qkv, n1_got, g_got, x_any,
    igrad, mine, x_ref, acc, n1t, both, grad, sums, small, sems,
):
    tokens = x_ref.shape[0]
    load_x = start(x_any, x_ref, sems.at[0])
    sums[...] = sums_ref[...]
    sums[2:3, :] = gbq_ref[0:1, :]
    sums[4:5, :] = gbq_ref[2:3, :]
    n1t[:, :tokens] = n1_ref[...].T
    n1t[:, tokens:] = n1_got[...].T
    for t in range(3):
        cols = pl.ds(pl.multiple_of(t * D + pos_ref[1] * HALF, 128), HALF)
        both[:tokens, t * HALF : (t + 1) * HALF] = gqkv[:, cols]
    both[tokens:, :] = g_got[...]
    for z in range(4):
        rows = slice(z * 4 * BLK, (z + 1) * 4 * BLK)
        grad[rows, :] = nn(n1t[rows, :], both[...]).astype(BF16)
        for chip in range(4 * z, 4 * z + 4):
            place = scatter_place(pos_ref, chip)
            for t in range(3):
                src = grad.at[pl.ds(chip * BLK, BLK), pl.ds(t * HALF, HALF)]
                start(src, mine.at[place, pl.ds(t * BLK, BLK)], sems.at[1])
    for t in range(3):
        part = nt(gqkv[:, t * D : (t + 1) * D], w_qkv[t])
        acc[...] = part if t == 0 else acc[...] + part
    load_x.wait()

    def back_one(rows):
        xhat, scale = norm_parts(x_ref[rows, :].astype(F32))
        g = acc[rows, :]
        sums[0:1, :] += jnp.sum(g * xhat, axis=0, keepdims=True)
        sums[1:2, :] += jnp.sum(g, axis=0, keepdims=True)
        igrad[rows, :] = (gmid[rows, :] + norm_back(g, xhat, scale, vec_ref[0:1, :])).astype(BF16)

    chunks(tokens, 256, back_one)
    is_up = up_rows()
    for chip in range(CHIPS):
        one, up = chip // 8 * HALF, chip % 4 // 2 * HALF
        block = jnp.where(is_up, sums[:, up : up + HALF], sums[:, one : one + HALF])
        place = scatter_place(pos_ref, chip)
        small[place] = block.astype(BF16)
        start(small.at[place], mine.at[place, pl.ds(3 * BLK, 16)], sems.at[2])
    whole_wait(small, sems.at[2])
    whole_wait(grad, sems.at[1])


def layer_out_kernel(pos_ref, vec_ref, act_ref, mid_ref, w_down, out_ref):
    out_ref[...] = (
        mid_ref[...] + nn(act_ref[...], w_down[...]) + vec_ref[12:13, :]
    ).astype(BF16)


PER = D // (2 * CHIPS)
SEND_ROWS = (3 * PER, 16, 5 * PER, 4 * PER)


def pack_kernel(pos_ref, w_qkv, w_out, w_up, w_down, bu_ref, *refs):
    values, (mine, theirs, rows, last, wide) = refs[:8], refs[8:]
    place = pos_ref[0] * 2 + pos_ref[1]
    rows[...] = jnp.zeros(rows.shape, F32)
    last[...] = jnp.zeros(last.shape, F32)
    for r, value in zip((0, 1, 2, 4, 5, 6, 7, 12), values):
        rows[r : r + 1, 0:PER] = value[...].astype(F32)
    last[0:1, 0 : 4 * PER] = bu_ref[...].astype(F32)
    at = place * (4 * PER)
    up = pltpu.roll(last[...], at % D, 1)[0:1]
    here = lax.broadcasted_iota(jnp.int32, (16, 1), 0) == 8 + at // D
    rows[...] = pltpu.roll(rows[...], place * PER, 1) + jnp.where(here, up, 0.0)
    for out, other in ((mine, 0), (theirs, 1)):
        half = pos_ref[1] ^ other

        def cols(first):
            return pl.ds(pl.multiple_of(first + half * HALF, 128), HALF)

        at = 0
        for t in range(3):
            wide[at : at + PER, :] = w_qkv[:, cols(t * D)].astype(F32)
            at += PER
        wide[at : at + 16, :] = rows[:, cols(0)]
        at += 16
        for n in range(4):
            u, s = n // 2, n % 2
            first = pl.multiple_of(half * (2 * D) + s * D + u * HALF, 128)
            wide[at : at + PER, :] = w_up[:, pl.ds(first, HALF)].astype(F32)
            at += PER
        wide[at : at + PER, :] = w_out[:, cols(0)].astype(F32)
        at += PER
        wide[at : at + 4 * PER, :] = w_down[:, cols(0)].astype(F32)
        out[...] = wide[...].astype(BF16)


def combine_kernel(pos_ref, mine, got, one, two, upper, lower, wide):
    first = pos_ref[1] == 0
    m, g = mine[...].astype(F32), got[...].astype(F32)
    upper[...] = jnp.where(first, m, g)
    lower[...] = jnp.where(first, g, m)

    def pair(at, size):
        wide[0:size, :] = upper[at : at + size, :]
        wide[size : 2 * size, :] = lower[at : at + size, :]
        return wide[0 : 2 * size, :].astype(BF16)

    for t in range(3):
        one[t * BLK : (t + 1) * BLK, :] = pair(t * PER, PER)
    at = 3 * PER
    one[3 * BLK :, :] = (upper[at : at + 16, :] + lower[at : at + 16, :]).astype(BF16)
    at += 16
    for n in range(5):
        two[n] = pair(at + n * PER, PER)
    low = pair(at + 5 * PER, 4 * PER)
    for n in range(4):
        two[5 + n] = low[n * BLK : (n + 1) * BLK]


def finish_kernel(pos_ref, last, *refs):
    terms, (keep, send, held, sems) = refs[:4], refs[4:]
    for i, term in enumerate(terms):
        start(term.at[0], held.at[i], sems.at[i])
    total = last[...].astype(F32)
    for i in range(4):
        whole_wait(held.at[i], sems.at[i])
        total = total + held[i].astype(F32)
    first = pos_ref[1] == 0
    for t in range(3):
        upper, lower = total[t * BLK : t * BLK + PER], total[t * BLK + PER : (t + 1) * BLK]
        keep[t * PER : (t + 1) * PER, :] = jnp.where(first, upper, lower)
        send[t * PER : (t + 1) * PER, :] = jnp.where(first, lower, upper)
    keep[3 * PER :, :] = total[3 * BLK :]
    send[3 * PER :, :] = total[3 * BLK :]


def spread_kernel(pos_ref, keep, got, w_ref, eight_ref, up_ref, down_ref, rows):
    place = pos_ref[0] * 2 + pos_ref[1]
    for ref, other in ((keep, 0), (got, 1)):
        half = pos_ref[1] ^ other
        for t in range(3):
            cols = pl.ds(pl.multiple_of(t * D + half * HALF, 128), HALF)
            w_ref[:, cols] = ref[t * PER : (t + 1) * PER, :]
    rows[...] = keep[3 * PER :, :] + got[3 * PER :, :]
    mine = pltpu.roll(rows[...], (HALF - place * PER % HALF) % HALF, 1)
    eight_ref[...] = mine[0:8, 0:PER]
    down_ref[...] = mine[12:13, 0:PER]
    at = place * (4 * PER)
    here = lax.broadcasted_iota(jnp.int32, (16, 1), 0) == 8 + at // D
    row = jnp.sum(jnp.where(here, rows[...], 0.0), axis=0, keepdims=True)
    turned = pltpu.roll(jnp.broadcast_to(row, (8, HALF)), (HALF - at % HALF) % HALF, 1)
    up_ref[...] = turned[0:1, 0 : 4 * PER]


def spread_up_kernel(pos_ref, keep, got, up_ref, out_ref):
    for ref, other in ((keep, 0), (got, 1)):
        half = pos_ref[1] ^ other
        for n in range(4):
            first = half * (2 * D) + (n % 2) * D + (n // 2) * HALF
            up_ref[:, pl.ds(pl.multiple_of(first, 128), HALF)] = ref[n]
        out_ref[:, pl.ds(pl.multiple_of(half * HALF, 128), HALF)] = ref[4]


def call(kernel, name, near, far, near_outs, far_outs, scratch, flops, aliases=None, limit=18):
    far = [in_hbm(a) for a in far]
    space = pl.BlockSpec(memory_space=pltpu.VMEM)
    anyspec = pl.BlockSpec(memory_space=pl.ANY)
    outs = tuple(near_outs) + tuple(far_outs)
    moved = sum(math.prod(a.shape) * a.dtype.itemsize for a in (*near, *far, *outs))
    return pl.pallas_call(
        kernel,
        out_shape=outs,
        in_specs=[pl.BlockSpec(memory_space=pltpu.SMEM)]
        + [space] * (len(near) - 1)
        + [anyspec] * len(far),
        out_specs=[space] * len(near_outs) + [anyspec] * len(far_outs),
        scratch_shapes=scratch,
        input_output_aliases=aliases or {},
        compiler_params=pltpu.CompilerParams(vmem_limit_bytes=limit << 20),
        cost_estimate=pl.CostEstimate(flops=flops, bytes_accessed=moved, transcendentals=0),
        name=name,
    )(*near, *far)


def in_hbm(array):
    return pltpu.with_memory_space_constraint(array, pltpu.HBM)


def keep(*arrays):
    return [pltpu.with_memory_space_constraint(a, pltpu.VMEM) for a in arrays]


def swap(value, chip_bit):
    flip = chip_bit * 2 if chip_bit else 1
    return lax.ppermute(value, AXES, [(i, i ^ flip) for i in range(2 * CHIPS)])


def tie(value, *after):
    return lax.optimization_barrier((value,) + after)[0]


def gathered(*own_half):
    return list(own_half) + [swap(piece, 0) for piece in own_half]


def hold(pieces, *after):
    return lax.optimization_barrier((*pieces, *after))[: len(pieces)] if after else pieces


def rounded_sum(*terms):
    total = terms[0].astype(F32)
    for term in terms[1:]:
        total = total + term.astype(F32)
    return total.astype(BF16)


def small_grads(sums, place, per, per_up):
    eight = lax.dynamic_slice(sums, (0, place * per), (8, per))
    at = place * per_up
    up = lax.dynamic_slice(sums, (8 + at // D, at % D), (1, per_up))[0]
    down = lax.dynamic_slice(sums, (12, place * per), (1, per))[0]
    return eight, up, down


def halves(w_qkv, w_out, w_up, w_down):
    rows = w_qkv.shape[0]
    qkv = w_qkv.reshape(rows, 3, 2, HALF)
    up = w_up.reshape(rows, 2, 4, HALF)
    for h in range(2):
        cols = slice(h * HALF, (h + 1) * HALF)
        up_h = up[:, h].reshape(rows, 2, 2, HALF).transpose(2, 1, 0, 3).reshape(4, rows, HALF)
        yield (
            qkv[:, :, h].transpose(1, 0, 2),
            jnp.concatenate([up_h, w_out[None, :, cols]]),
            w_down[:, cols],
        )


def gather_plain(weights, values):
    def whole(w):
        return lax.all_gather(w, AXES, axis=0, tiled=True)

    gain1, bias1, bq, bv, bo, gain2, bias2, bu, bd = [whole(v) for v in values]
    rest = jnp.zeros((3, D), BF16)
    small = jnp.stack([gain1, bias1, bq, jnp.zeros_like(bq), bv, bo, gain2, bias2])
    small = jnp.concatenate([small, bu.reshape(4, D), bd[None], rest])
    groups = ([], [], [])
    for h, (attn, up, down) in enumerate(halves(*[whole(w) for w in weights])):
        attn = attn.reshape(3, CHIPS, BLK, HALF).transpose(1, 0, 2, 3).reshape(CHIPS, 3 * BLK, HALF)
        up = up.reshape(5, CHIPS, BLK, HALF).transpose(1, 0, 2, 3)
        down = down.reshape(CHIPS, 4 * BLK, HALF)
        extra = jnp.zeros((CHIPS, 16, HALF), BF16).at[0].set(small[:, h * HALF : (h + 1) * HALF])
        for group, blocks in zip(groups, (jnp.concatenate([attn, extra], axis=1), up, down)):
            group.extend(jnp.stack([blocks[o] for o in piece]) for piece in GATHER)
    return groups


def scatter_plain(pair, group):
    both = [jnp.stack([part[SCATTER.index(chip)] for chip in range(CHIPS)]) for part in pair]

    def scatter(v):
        return lax.psum_scatter(v.astype(F32), AXES, scatter_dimension=0, tiled=True)

    def matrix(units):
        return jnp.stack(units, axis=3).transpose(0, 2, 1, 3, 4).reshape(D, -1, 2, HALF)

    if group == "attn":
        near, far, far_up = (both[0][chip, 3 * BLK :] for chip in (0, 8, 2))
        sums = jnp.concatenate([near, far.at[8:12].set(far_up[8:12])], axis=1)
        qkv = matrix([b[:, : 3 * BLK].reshape(CHIPS, 3, BLK, HALF) for b in both])
        return scatter(qkv.reshape(D, 3 * D)), lax.psum(sums.astype(F32), AXES)
    if group == "up":
        up = matrix(both)
        order = up[:, :4].reshape(D, 2, 2, 2, HALF).transpose(0, 3, 2, 1, 4)
        return scatter(order.reshape(D, FF)), scatter(up[:, 4].reshape(D, D))
    return scatter(jnp.concatenate([b.reshape(FF, HALF) for b in both], axis=1))


def shape(dims, kind=BF16):
    return jax.ShapeDtypeStruct(dims, kind)


def far_shape(*dims):
    return pltpu.HBM(dims, BF16)


def dma(n):
    return pltpu.SemaphoreType.DMA((n,))


def vmem(*dims, kind=BF16):
    return pltpu.VMEM(dims, kind)


class Layer:
    def __init__(self, tokens):
        self.tokens = tokens
        self.rows = tokens // ROW_LEN
        self.out = shape((tokens, D))
        self.wide = vmem(tokens, FF)
        self.one = vmem(tokens, D)
        self.one_f32 = vmem(tokens, D, kind=F32)
        self.qkv = vmem(tokens, 3 * D)
        self.soft = vmem(self.rows * HEADS, ROW_LEN, ROW_LEN)
        self.turned = vmem(D, tokens)
        self.square = vmem(D, D)
        self.three = vmem(3, D, D)
        self.four = vmem(2, 2, D, D)
        self.sums = vmem(8, D, kind=F32)
        self.vec = vmem(16, D, kind=F32)

    def chip_blocks(self, pos, weights, values):
        *rest, bu, bd = [in_hbm(v.reshape(1, -1)) for v in values]
        weights = [in_hbm(w) for w in weights]
        sent = shape((sum(SEND_ROWS), HALF))
        wide = vmem(sum(SEND_ROWS), HALF, kind=F32)
        mine, theirs = call(
            pack_kernel, "pack", (pos, *weights, bu, *rest, bd), (), (sent, sent), (),
            [vmem(16, D, kind=F32), vmem(8, D, kind=F32), wide], 0,
        )
        return call(
            combine_kernel, "combine", (pos, mine, swap(theirs, 0)), (),
            (shape((3 * BLK + 16, HALF)), shape((9, BLK, HALF))), (),
            [wide, wide, vmem(4 * BLK, HALF, kind=F32)], 0,
        )

    def finish(self, pos, last, low):
        sent = shape((3 * PER + 16, HALF), F32)
        keep, send = call(
            finish_kernel, "finish", (pos, last), low, (sent, sent), (),
            [vmem(4, 3 * BLK + 16, HALF), dma(4)], 0,
        )
        return call(
            spread_kernel, "spread", (pos, keep, swap(send, 0)), (),
            (shape((PER, 3 * D), F32), shape((8, PER), F32), shape((1, 4 * PER), F32), shape((1, PER), F32)),
            (), [vmem(16, HALF, kind=F32)], 0,
        )

    def spread_up(self, pos, keep, got):
        return call(
            spread_up_kernel, "spread_up", (pos, keep, got), (),
            (shape((PER, FF), F32), shape((PER, D), F32)), (), [], 0,
        )

    def attn_forward(self, pos, segr, segc, inputs, attn):
        return call(
            attn_forward_kernel, "attn_forward", (pos, segr, segc), [in_hbm(inputs)] + attn,
            (self.vec, self.one, self.qkv, self.soft, self.one, self.three), (),
            [
                self.one, vmem(2, CHIPS, 16, HALF),
                vmem(self.rows, ROW_LEN, ROW_LEN, kind=F32), dma(5),
            ],
            2 * self.tokens * D * D * 3 + 8 * self.tokens * D * ROW_LEN,
        )

    def mlp_up(self, pos, segc, vec, inputs, mixed, cotangent, up):
        vec, mixed = keep(vec, mixed)
        return call(
            mlp_up_kernel, "mlp_up", (pos, segc, vec, mixed), [inputs, cotangent] + up,
            (self.sums, self.one, self.one_f32, self.wide, self.wide, self.one, self.square, self.four), (),
            [self.one, self.one, dma(5)],
            2 * self.tokens * D * (FF + D),
        )

    def down_grad(self, pos, act, gout):
        buffer = far_shape(CHIPS, 4 * BLK, HALF)
        return call(
            down_grad_kernel, "down_grad", (pos, *keep(act, gout)), [], (), (buffer, buffer),
            [vmem(4, D, D), dma(1)],
            2 * self.tokens * D * FF,
        )

    def mlp_down(self, pos, gout, slope, n2, down):
        buffer = far_shape(CHIPS, 5, BLK, HALF)
        return call(
            mlp_down_kernel, "mlp_down", (pos, *keep(gout, slope, n2)), down,
            (self.sums, self.wide, vmem(FF, D)), (buffer, buffer),
            [self.turned, self.four, dma(5)],
            4 * self.tokens * D * FF,
        )

    def mid_backward(self, pos, vec, gbd, gbu, gpre, gout, mid, mixed, w_out, w_up, mine, theirs):
        buffer = far_shape(*mine.shape)
        near = (pos, *keep(vec, gbd, gbu, gpre, gout, mid, mixed, w_out, w_up))
        return call(
            mid_backward_kernel, "mid_backward", near, [mine, theirs],
            (self.vec, self.one_f32, self.one), (buffer, buffer),
            [self.one_f32, self.one, self.turned, self.square, dma(1)],
            2 * self.tokens * D * (FF + 2 * D),
            {len(near): 3, len(near) + 1: 4},
        )

    def attn_backward(self, pos, gmixed, qkv, soft):
        return call(
            attn_backward_kernel, "attn_backward", (pos, *keep(gmixed, qkv, soft)), [],
            (self.sums, self.qkv, vmem(self.tokens, 3 * HALF)), (), [], 20 * self.tokens * D * ROW_LEN,
        )

    def qkv_grad(self, pos, vec, sums, gbq, gmid, gqkv, n1, w_qkv, n1_got, g_got, inputs):
        return call(
            qkv_grad_kernel, "qkv_grad", (pos, *keep(vec, sums, gbq, gmid, gqkv, n1, w_qkv, n1_got, g_got)),
            [inputs], (self.out,), (far_shape(CHIPS, 3 * BLK + 16, HALF),),
            [
                self.one, self.one_f32, vmem(D, 2 * self.tokens), vmem(2 * self.tokens, 3 * HALF),
                vmem(D, 3 * HALF), vmem(16, D, kind=F32), vmem(CHIPS, 16, HALF), dma(3),
            ],
            2 * self.tokens * D * 6 * D,
        )

    def layer_out(self, pos, vec, act, mid, w_down):
        (out,) = call(
            layer_out_kernel, "layer_out", (pos, *keep(vec, act, mid, w_down)), [], (self.out,), (), [],
            2 * self.tokens * D * FF,
        )
        return out


class Scatter:
    def __init__(self, mine, theirs=None, *after):
        self.both = [mine] if theirs is None else [mine, swap(tie(theirs, *after), 0)]

    def part(self, first, last):
        return [ref[first:last] for ref in self.both]

    def hold_back(self, *after):
        self.both[-1] = hold((self.both[-1],), *after)[0]

    def first(self, *after):
        self.hold_back(*after)
        self.out = (rounded_sum(*self.part(8, 12)), rounded_sum(*self.part(12, 16)))
        self.in_y, self.in_x = swap(self.out[0], BIT_Y), swap(self.out[1], BIT_X)

    def second(self, *after):
        in_y, in_x = hold((self.in_y, self.in_x), *after)
        self.out = (
            rounded_sum(*self.part(4, 6), in_x[2:]),
            rounded_sum(*self.part(6, 8), in_y[2:]),
        )
        self.in_y, self.in_x = in_y, in_x
        self.in_y2, self.in_x2 = swap(self.out[0], BIT_Y), swap(self.out[1], BIT_X)

    def third(self, *after):
        in_y2, in_x2 = hold((self.in_y2, self.in_x2), *after)
        self.near = (*self.part(0, 2), self.in_x[:2], in_y2)
        self.out = (rounded_sum(*self.part(2, 4), self.in_y[:2], in_x2),)
        self.in_z = swap(self.out[0], BIT_Z0)

    def diagonal(self, *after):
        self.hold_back(*after)
        self.out = (rounded_sum(*self.part(10, 12)), rounded_sum(*self.part(14, 16)))
        self.in_y, self.in_x = swap(self.out[0], BIT_Y), swap(self.out[1], BIT_X)

    def hi(self, *after):
        in_y, self.in_x = hold((self.in_y, self.in_x), *after)
        self.out = (rounded_sum(*self.part(8, 10)), rounded_sum(*self.part(6, 8), in_y))
        self.in_y2, self.in_x2 = swap(self.out[0], BIT_Y), swap(self.out[1], BIT_X)

    def lo(self, *after):
        in_y2, in_x2 = hold((self.in_y2, self.in_x2), *after)
        far = rounded_sum(*self.part(2, 4), in_y2, in_x2)
        self.in_z = swap(far, BIT_Z0)
        low_y, low_x = rounded_sum(*self.part(4, 6), self.in_x), rounded_sum(*self.part(12, 14))
        low_y, low_x = hold((low_y, low_x), far)
        self.out = (far, low_y, low_x)
        self.near = (*self.part(0, 2), swap(low_y, BIT_Y), swap(low_x, BIT_X))

    def fourth(self, *after):
        self.near = (*self.near, *hold((self.in_z,), *after))
        self.out = (rounded_sum(*[t[1] for t in self.near]),)
        self.in_z = swap(self.out[0], BIT_Z1)

    def result(self, *after):
        total = hold((self.in_z,), *after)[0].astype(F32)
        for term in self.near:
            total = total + term[0].astype(F32)
        return total


def per_device(tuned, *args):
    (
        inputs, segment_ids, pre_attn_gain, pre_attn_bias, w_qkv, b_query, b_value, w_out, b_out,
        pre_mlp_gain, pre_mlp_bias, w_up, b_up, w_down, b_down, cotangent,
    ) = args
    tokens = inputs.shape[0]
    n_rows = tokens // ROW_LEN
    wide, narrow = lax.axis_index("wide"), lax.axis_index("narrow")
    weights = (w_qkv, w_out, w_up, w_down)
    values = (
        pre_attn_gain, pre_attn_bias, b_query, b_value, b_out, pre_mlp_gain, pre_mlp_bias, b_up, b_down,
    )
    per, per_up = pre_attn_gain.shape[0], b_up.shape[0]
    position = jnp.arange(ROW_LEN, dtype=jnp.int32)[None]
    own_id = jnp.where(segment_ids != 0, segment_ids, -1 - position)
    segr = own_id.reshape(n_rows, 1, ROW_LEN)
    segc = own_id.reshape(tokens, 1)
    layer = Layer(tokens)

    if not tuned:
        place = wide * lax.axis_size("narrow") + narrow
        pos = jnp.zeros((2,), jnp.int32)
        attn, up, down = gather_plain(weights, values)
        vec, n1, qkv, soft, mixed, w_qkv_all = layer.attn_forward(pos, segr, segc, inputs, attn)
        gbd, n2, mid, act, slope, gout, *w_mid = layer.mlp_up(pos, segc, vec, inputs, mixed, cotangent, up)
        pair_down = layer.down_grad(pos, act, gout)
        gbu, gpre, w_down_all, *pair_up = layer.mlp_down(pos, gout, slope, n2, down)
        sums, gmid, gmixed, *pair_up = layer.mid_backward(
            pos, vec, gbd, gbu, gpre, gout, mid, mixed, *w_mid, *pair_up
        )
        gbq, gqkv, give = layer.attn_backward(pos, gmixed, qkv, soft)
        pair_attn = []
        for half in range(2):
            input_grad, blocks = layer.qkv_grad(
                jnp.array([0, half], jnp.int32), vec, sums, gbq, gmid, gqkv, n1, w_qkv_all,
                jnp.zeros_like(n1), jnp.zeros_like(give), inputs,
            )
            pair_attn.append(blocks)
        layer_out = layer.layer_out(pos, vec, act, mid, w_down_all)
        grad_w_down = scatter_plain(pair_down, "down")
        grad_w_up, grad_w_out = scatter_plain(pair_up, "up")
        grad_w_qkv, sums = scatter_plain(pair_attn, "attn")
        eight, grad_b_up, grad_b_down = small_grads(sums, place, per, per_up)
    else:
        core = (narrow & 1).astype(jnp.int32)
        pos = jnp.stack([wide * 2 + (narrow >> 1), core]).astype(jnp.int32)
        block1, block23 = layer.chip_blocks(pos, weights, values)
        flat = (4 * BLK, HALF)

        near1 = swap(block1, BIT_Z1)
        lo1 = jnp.stack([block1, near1])
        hi1 = swap(lo1, BIT_Z0)
        y_lo1, x_lo1 = swap(lo1, BIT_Y), swap(lo1, BIT_X)
        near23 = swap(tie(block23, near1), BIT_Z1)
        d_lo1 = swap(y_lo1, BIT_X)
        y_hi1, x_hi1 = swap(hi1, BIT_Y), swap(hi1, BIT_X)
        lo2 = jnp.stack([block23[:5], near23[:5]])
        lo3 = jnp.stack([block23[5:].reshape(flat), near23[5:].reshape(flat)])
        hi2 = swap(tie(lo2, hi1), BIT_Z0)
        d_hi1 = swap(tie(x_hi1, y_hi1), BIT_Y)
        lo2b = tie(lo2, d_lo1, x_hi1, y_hi1)
        y_lo2, x_lo2 = swap(lo2b, BIT_Y), swap(lo2b, BIT_X)
        attn = gathered(lo1, hi1, y_lo1, y_hi1, x_lo1, x_hi1, d_lo1, d_hi1)
        hi3 = swap(tie(lo3, hi2), BIT_Z0)
        y_hi2, x_hi2 = swap(hi2, BIT_Y), swap(hi2, BIT_X)
        d_lo2, d_hi2 = swap(y_lo2, BIT_X), swap(tie(x_hi2, y_hi2), BIT_Y)
        lo3b = tie(lo3, y_lo2, x_lo2, y_hi2)
        y_lo3, x_lo3 = swap(lo3b, BIT_Y), swap(lo3b, BIT_X)
        vec, n1, qkv, soft, mixed, w_qkv_all = layer.attn_forward(
            tie(pos, y_hi2, x_hi2, lo3b, d_lo2), segr, segc, inputs, attn
        )

        d_hi2, y_lo3, x_lo3, hi3 = hold((d_hi2, y_lo3, x_lo3, hi3), mixed)
        d_lo3 = swap(y_lo3, BIT_X)
        y_hi3, x_hi3 = swap(hi3, BIT_Y), swap(hi3, BIT_X)
        lo2, hi2, y_lo2, y_hi2, x_lo2, x_hi2, d_lo2 = hold(
            (lo2, hi2, y_lo2, y_hi2, x_lo2, x_hi2, d_lo2), x_lo3, hi3
        )
        up = gathered(lo2, hi2, y_lo2, y_hi2, x_lo2, x_hi2, d_lo2, d_hi2)
        gbd, n2, mid, act, slope, gout, *w_mid = layer.mlp_up(
            tie(pos, hi3, y_lo3, x_lo3), segc, vec, inputs, mixed, cotangent, up
        )
        y_hi3, x_hi3, d_lo3 = hold((y_hi3, x_hi3, d_lo3), gbd)
        d_hi3 = swap(x_hi3, BIT_Y)
        pair_down = layer.down_grad(tie(pos, y_hi3, x_hi3, d_lo3), act, gout)
        d_hi3 = tie(d_hi3, pair_down[0])
        down = gathered(lo3, hi3, y_lo3, y_hi3, x_lo3, x_hi3, d_lo3, d_hi3)
        scatter1 = Scatter(*pair_down, *down)
        gbu, gpre, w_down_all, *pair_up = layer.mlp_down(pos, gout, slope, n2, down)
        scatter1.diagonal(gbu)
        sums, gmid, gmixed, *pair_up = layer.mid_backward(
            tie(pos, *scatter1.out), vec, gbd, gbu, gpre, gout, mid, mixed, *w_mid, *pair_up
        )
        scatter1.hi(sums)
        scatter2 = Scatter(*pair_up, scatter1.in_x)
        gbq, gqkv, give = layer.attn_backward(tie(pos, *scatter1.out), gmixed, qkv, soft)
        scatter1.lo(gbq)
        n1, give = hold((n1, give), *scatter1.out)
        n1_got, g_got = swap(n1, 0), swap(give, 0)
        scatter2.diagonal(gbq)
        input_grad, sums_attn = layer.qkv_grad(
            tie(pos, *scatter2.out, *scatter1.out),
            vec, sums, gbq, gmid, gqkv, n1, w_qkv_all, n1_got, g_got, inputs,
        )
        scatter1.fourth(input_grad)
        scatter2.hi(input_grad)
        scatter3 = Scatter(tie(sums_attn, *scatter2.out))
        scatter3.diagonal()
        layer_out = layer.layer_out(tie(pos, *scatter3.out, *scatter1.out), vec, act, mid, w_down_all)
        scatter1.in_z = tie(scatter1.in_z, layer_out)
        scatter3.hi(layer_out, scatter1.in_z)
        scatter2.lo(*scatter3.out)
        scatter3.lo(*scatter2.out)
        scatter2.fourth(scatter3.in_z)
        scatter3.fourth()

        def exchange(blocks, axis):
            first, second = jnp.split(blocks, 2, axis=axis)
            keep = jnp.where(core == 0, first, second)
            got = swap(jnp.where(core == 0, second, first), 0)
            return jnp.where(core == 0, keep, got), jnp.where(core == 0, got, keep)

        grad_w_down = jnp.concatenate(exchange(scatter1.result(scatter2.in_z), 0), axis=1)
        total = scatter2.result(*scatter3.out)
        upper, lower = total[:, :PER], total[:, PER:]
        got = swap(jnp.where(core == 0, lower, upper), 0)
        grad_w_up, grad_w_out = layer.spread_up(pos, jnp.where(core == 0, upper, lower), got)
        grad_w_qkv, eight, grad_b_up, grad_b_down = layer.finish(
            tie(pos, total), scatter3.in_z, [*scatter3.both, *scatter3.near[1:]]
        )
        grad_b_up, grad_b_down = grad_b_up[0], grad_b_down[0]
    return (
        layer_out, input_grad, eight[0], eight[1], grad_w_qkv, eight[2], eight[4], grad_w_out, eight[5],
        eight[6], eight[7], grad_w_up, grad_b_up, grad_w_down, grad_b_down,
    )


def solution(mesh):
    both = P(AXES, None)
    one = P(AXES)
    tuned = dict(mesh.shape) == {"wide": 8, "narrow": 4}
    in_specs = (both, both, one, one, both, one, one, both, one, one, one, both, one, both, one, both)
    out_specs = (both, both, one, one, both, one, one, both, one, one, one, both, one, both, one)
    return jax.shard_map(
        functools.partial(per_device, tuned),
        mesh=mesh,
        in_specs=in_specs,
        out_specs=out_specs,
        check_vma=False,
    )
```

```python
import functools
import math

import jax
import jax.numpy as jnp
from jax import lax
from jax.experimental import pallas as pl
from jax.experimental.pallas import tpu as pltpu
from jax.sharding import PartitionSpec as P

HEADS = 12
HEAD_DIM = 64
D = 768
FF = 3072
ROW_LEN = 256
HALF = 384
CHIPS = 16
BLK = 48
PAIRS = HEADS // 2
AXES = ("wide", "narrow")

EPS = 1e-06
MASKED = -1e30
F32 = jnp.float32
BF16 = jnp.bfloat16

BIT_Y, BIT_X, BIT_Z0, BIT_Z1 = 1, 2, 4, 8
Z_OFFSETS = (0, 4, 8, 12)

GATHER = tuple((o + z, o + z + BIT_Z1) for o in (0, BIT_Y, BIT_X, BIT_X + BIT_Y) for z in (0, BIT_Z0))
PIECES = 2 * len(GATHER)

SCATTER = (0, 8, 4, 12, 1, 9, 6, 14, 5, 13, 7, 15, 2, 10, 3, 11)


def nt(a, b):
    return lax.dot_general(a, b, (((1,), (1,)), ((), ())), preferred_element_type=F32)


def tn(a, b):
    return lax.dot_general(a, b, (((0,), (0,)), ((), ())), preferred_element_type=F32)


def nn(a, b):
    return lax.dot_general(a, b, (((1,), (0,)), ((), ())), preferred_element_type=F32)


def chunks(tokens, step, body):
    def one(i, carry):
        body(pl.ds(pl.multiple_of(i * step, step), step))
        return carry

    lax.fori_loop(0, tokens // step, one, 0)


def norm_parts(v):
    centre = jnp.mean(v, axis=-1, keepdims=True)
    centred = v - centre
    scale = lax.rsqrt(jnp.mean(centred * centred, axis=-1, keepdims=True) + EPS)
    return centred * scale, scale


def start(src, dst, sem):
    copy = pltpu.make_async_copy(src, dst, sem)
    copy.start()
    return copy


def whole_wait(ref, sem):
    pltpu.make_async_copy(ref, ref, sem).wait()


def each_block(pos_ref, pieces):
    for other in range(2):
        for ref, offsets in zip(pieces[other * len(GATHER) :], GATHER):
            for b, offset in enumerate(offsets):
                yield ref, b, pos_ref[0] ^ offset, other, offset


def chip_rows(chip, size):
    return pl.ds(pl.multiple_of(chip * size, 16), size)


def half_cols(pos_ref, other):
    return pl.ds(pl.multiple_of((pos_ref[1] ^ other) * HALF, 128), HALF)


def fetch_qkv(pos_ref, pieces, w_qkv, sems):
    for t in range(3):
        for ref, b, chip, other, _ in each_block(pos_ref, pieces):
            dst = w_qkv.at[t, chip_rows(chip, BLK), half_cols(pos_ref, other)]
            start(ref.at[b, pl.ds(t * BLK, BLK)], dst, sems.at[t])


def fetch_out(pos_ref, pieces, w_out, sem):
    for ref, b, chip, other, _ in each_block(pos_ref, pieces):
        dst = w_out.at[chip_rows(chip, BLK), half_cols(pos_ref, other)]
        start(ref.at[b, 4], dst, sem)


def fetch_small(pos_ref, pieces, small, sem):
    for ref, b, chip, other, _ in each_block(pos_ref, pieces):
        start(ref.at[b, pl.ds(3 * BLK, 16)], small.at[pos_ref[1] ^ other, chip], sem)


def fetch_up(pos_ref, pieces, w_up, sems):
    for ref, b, chip, other, _ in each_block(pos_ref, pieces):
        for u in range(2):
            dst = w_up.at[other, pl.ds(0, 2), chip_rows(chip, BLK), pl.ds(u * HALF, HALF)]
            start(ref.at[b, pl.ds(2 * u, 2)], dst, sems.at[other])


def fetch_down(pos_ref, pieces, w_down, sems):
    for q in range(4):
        for ref, b, chip, other, offset in each_block(pos_ref, pieces):
            if offset // 4 == q:
                dst = w_down.at[chip_rows(chip, 4 * BLK), half_cols(pos_ref, other)]
                start(ref.at[b], dst, sems.at[q])


def scatter_place(pos_ref, chip):
    offset = pos_ref[0] ^ chip
    xy, z = offset & 3, ((offset >> 2) & 1) * 2 + (offset >> 3)
    near = jnp.where(xy == 1, 4, jnp.where(xy == 2, 12, 14)) + z
    far = jnp.where(xy == 1, 6, jnp.where(xy == 2, 4, 8)) + z
    return jnp.where(xy == 0, z, jnp.where(z < 2, near, far))


def head_masks():
    lane = lax.broadcasted_iota(jnp.int32, (1, 2 * HEAD_DIM), 1)
    return [(lane // HEAD_DIM == hh).astype(F32).astype(BF16) for hh in range(2)]


def pair_cols(t, i):
    return pl.ds(pl.multiple_of(t * D + i * 128, 128), 128)


def attn_forward_kernel(pos_ref, segr_ref, segc_ref, x_any, *refs):
    pieces, refs = refs[:PIECES], refs[PIECES:]
    vec_ref, n1_ref, qkv_ref, soft_ref, mixed_ref, w_qkv, x_ref, small, bias, sems = refs
    tokens = x_ref.shape[0]
    n_rows = tokens // ROW_LEN
    load_x = start(x_any, x_ref, sems.at[4])
    fetch_small(pos_ref, pieces, small, sems.at[0])
    fetch_qkv(pos_ref, pieces, w_qkv, sems.at[pl.ds(1, 3)])
    for r in range(n_rows):
        same = segc_ref[r * ROW_LEN : (r + 1) * ROW_LEN] == segr_ref[r]
        bias[r] = jnp.where(same, 0.0, MASKED)
    whole_wait(small, sems.at[0])
    for h in range(2):
        vec_ref[:, h * HALF : (h + 1) * HALF] = jnp.sum(small[h].astype(F32), axis=0)
    load_x.wait()

    def norm_one(rows):
        xhat, _ = norm_parts(x_ref[rows, :].astype(F32))
        n1_ref[rows, :] = (xhat * vec_ref[0:1, :] + vec_ref[1:2, :]).astype(BF16)

    chunks(tokens, 256, norm_one)
    for t in range(3):
        whole_wait(w_qkv.at[t], sems.at[1 + t])
        y = (nn(n1_ref[...], w_qkv[t]) + vec_ref[2 + t : 3 + t, :]).astype(BF16)
        if t == 0:
            y = y * BF16(HEAD_DIM**-0.5)
        qkv_ref[:, t * D : (t + 1) * D] = y
    masks = head_masks()
    for r in range(n_rows):
        rows = slice(r * ROW_LEN, (r + 1) * ROW_LEN)

        def pair(i, carry):
            q, k, v = (qkv_ref[rows, pair_cols(t, i)] for t in range(3))
            mixed = jnp.zeros((ROW_LEN, 128), F32)
            for hh, keep in enumerate(masks):
                s = nt(q, k * keep) + bias[r]
                e = jnp.exp(s - jnp.max(s, axis=-1, keepdims=True))
                p = (e * (1.0 / jnp.sum(e, axis=-1, keepdims=True))).astype(BF16)
                soft_ref[r * HEADS + 2 * i + hh] = p
                mixed = mixed + nn(p, v * keep)
            mixed_ref[rows, pair_cols(0, i)] = mixed.astype(BF16)
            return carry

        lax.fori_loop(0, PAIRS, pair, 0, unroll=3)


GELU_A = 0.7978845608028654
GELU_B = 0.044715


def quarter(pos_ref, other, s):
    return (pos_ref[1] ^ other) * 2 + s


def quarter_cols(z):
    return pl.ds(pl.multiple_of(z * D, 128), D)


QUARTERS = ((0, 0), (0, 1), (1, 0), (1, 1))


def mlp_up_kernel(pos_ref, segc_ref, vec_ref, mixed_ref, x_any, cot_any, *refs):
    pieces, refs = refs[:PIECES], refs[PIECES:]
    gb_ref, n2_ref, mid_ref, act_ref, slope_ref, gout_ref, w_out, w_up, x_ref, cot_ref, sems = refs
    tokens = n2_ref.shape[0]
    load_cot = start(cot_any, cot_ref, sems.at[3])
    load_x = start(x_any, x_ref, sems.at[4])
    fetch_out(pos_ref, pieces, w_out, sems.at[2])
    fetch_up(pos_ref, pieces, w_up, sems)
    load_cot.wait()
    valid = segc_ref[...] > 0
    gout = jnp.where(valid, cot_ref[...].astype(F32), 0.0)
    gout_ref[...] = gout.astype(BF16)
    gb_ref[...] = jnp.broadcast_to(jnp.sum(gout, axis=0, keepdims=True), gb_ref.shape)
    load_x.wait()
    whole_wait(w_out, sems.at[2])
    mid_ref[...] = x_ref[...].astype(F32) + nn(mixed_ref[...], w_out[...]) + vec_ref[5:6, :]

    def norm_two(rows):
        xhat, _ = norm_parts(mid_ref[rows, :])
        n2_ref[rows, :] = (xhat * vec_ref[6:7, :] + vec_ref[7:8, :]).astype(BF16)

    chunks(tokens, 256, norm_two)
    for other, s in QUARTERS:
        if s == 0:
            whole_wait(w_up.at[other], sems.at[other])
        z = quarter(pos_ref, other, s)
        b_up = vec_ref[pl.ds(8 + z, 1), :]
        cols = quarter_cols(z)

        def part(rows):
            u = nn(n2_ref[rows, :], w_up[other, s]) + b_up
            sq = u * u
            t = jnp.tanh(u * (GELU_A + GELU_A * GELU_B * sq))
            half_up = 0.5 + 0.5 * t
            act_ref[rows, cols] = (u * half_up).astype(BF16)
            slope_ref[rows, cols] = (
                half_up + u * (0.5 - 0.5 * t * t) * (GELU_A + 3.0 * GELU_A * GELU_B * sq)
            ).astype(BF16)

        chunks(tokens, 512, part)


def down_grad_kernel(pos_ref, act_ref, gout_ref, mine, theirs, grad, sem):
    for z in range(4):
        grad[z] = tn(act_ref[:, z * D : (z + 1) * D], gout_ref[...]).astype(BF16)
        for j in range(4):
            place = scatter_place(pos_ref, 4 * z + j)
            for other, out in enumerate((mine, theirs)):
                src = grad.at[z, pl.ds(j * 4 * BLK, 4 * BLK), half_cols(pos_ref, other)]
                start(src, out.at[place], sem.at[0])
    whole_wait(grad, sem.at[0])


def mlp_down_kernel(pos_ref, gout_ref, slope_ref, n2_ref, *refs):
    pieces, refs = refs[:PIECES], refs[PIECES:]
    gb_ref, gpre_ref, w_down, mine, theirs, n2t, grad, sems = refs
    fetch_down(pos_ref, pieces, w_down, sems)
    gb_ref[...] = jnp.zeros(gb_ref.shape, F32)
    n2t[...] = n2_ref[...].T
    for other, s in QUARTERS:
        z = quarter(pos_ref, other, s)
        cols = quarter_cols(z)
        whole_wait(w_down.at[cols], sems.at[z ^ (pos_ref[0] >> 2)])
        ga = nt(gout_ref[...], w_down[cols, :])
        gp = (ga * slope_ref[:, cols].astype(F32)).astype(BF16)
        gpre_ref[:, cols] = gp
        gb_ref[pl.ds(z, 1), :] = jnp.sum(gp.astype(F32), axis=0, keepdims=True)
        grad[other, s] = nn(n2t[...], gp).astype(BF16)
        if s == 1:
            for chip in range(CHIPS):
                place = scatter_place(pos_ref, chip)
                for u in range(2):
                    src = grad.at[other, pl.ds(0, 2), pl.ds(chip * BLK, BLK), pl.ds(u * HALF, HALF)]
                    start(src, (mine, theirs)[other].at[place, pl.ds(2 * u, 2)], sems.at[4])
    whole_wait(grad, sems.at[4])


def norm_back(grad, xhat, scale, gain):
    gn = grad * gain
    mean_gn = jnp.mean(gn, axis=-1, keepdims=True)
    mean_gx = jnp.mean(gn * xhat, axis=-1, keepdims=True)
    return scale * (gn - mean_gn - xhat * mean_gx)


def mid_backward_kernel(
    pos_ref, vec_ref, gbd_ref, gbu_ref, gpre_ref, gout_ref, mid_ref, mixed_ref, w_out, w_up, _, __,
    sums, gmid, gmixed, mine, theirs, acc, gbr, mixt, grad, sem,
):
    tokens = mid_ref.shape[0]
    sums[...] = jnp.zeros(sums.shape, F32)
    sums[8:12, :] = gbu_ref[0:4, :]
    sums[12:13, :] = gbd_ref[0:1, :]
    mixt[...] = mixed_ref[...].T
    for other, s in QUARTERS:
        part = nt(gpre_ref[:, quarter_cols(quarter(pos_ref, other, s))], w_up[other, s])
        acc[...] = part if other + s == 0 else acc[...] + part

    def back_two(rows):
        xhat, scale = norm_parts(mid_ref[rows, :])
        g = acc[rows, :]
        sums[6:7, :] += jnp.sum(g * xhat, axis=0, keepdims=True)
        sums[7:8, :] += jnp.sum(g, axis=0, keepdims=True)
        gm = gout_ref[rows, :].astype(F32) + norm_back(g, xhat, scale, vec_ref[6:7, :])
        gmid[rows, :] = gm
        low = gm.astype(BF16)
        gbr[rows, :] = low
        sums[5:6, :] += jnp.sum(low.astype(F32), axis=0, keepdims=True)

    chunks(tokens, 256, back_two)
    grad[...] = nn(mixt[...], gbr[...]).astype(BF16)
    for chip in range(CHIPS):
        place = scatter_place(pos_ref, chip)
        for other, out in enumerate((mine, theirs)):
            src = grad.at[pl.ds(chip * BLK, BLK), half_cols(pos_ref, other)]
            start(src, out.at[place, 4], sem.at[0])
    gmixed[...] = nt(gbr[...], w_out[...]).astype(BF16)
    whole_wait(grad, sem.at[0])


def attn_backward_kernel(pos_ref, gmixed, qkv_ref, soft_ref, gb_ref, gqkv, give):
    masks = head_masks()
    for r in range(gmixed.shape[0] // ROW_LEN):
        rows = slice(r * ROW_LEN, (r + 1) * ROW_LEN)

        def pair(i, carry):
            q, k, v = (qkv_ref[rows, pair_cols(t, i)] for t in range(3))
            gm = gmixed[rows, pair_cols(0, i)]
            dq = jnp.zeros((ROW_LEN, 128), F32)
            dk = jnp.zeros((ROW_LEN, 128), F32)
            dv = jnp.zeros((ROW_LEN, 128), F32)
            for hh, keep in enumerate(masks):
                p_low = soft_ref[r * HEADS + 2 * i + hh]
                p = p_low.astype(F32)
                gmk = gm * keep
                gs = nt(gmk, v)
                inner = jnp.sum(p * gs, axis=-1, keepdims=True)
                ds = (p * (gs - inner)).astype(BF16)
                dq = dq + nn(ds, k * keep)
                dk = dk + tn(ds, q * keep)
                dv = dv + tn(p_low, gmk)
            gqkv[rows, pair_cols(0, i)] = (dq * (HEAD_DIM**-0.5)).astype(BF16)
            gqkv[rows, pair_cols(1, i)] = dk.astype(BF16)
            gqkv[rows, pair_cols(2, i)] = dv.astype(BF16)
            return carry

        lax.fori_loop(0, PAIRS, pair, 0, unroll=3)
    for t in range(3):
        cols = pl.ds(pl.multiple_of(t * D + (1 - pos_ref[1]) * HALF, 128), HALF)
        give[:, t * HALF : (t + 1) * HALF] = gqkv[:, cols]
    gb_ref[...] = jnp.zeros(gb_ref.shape, F32)
    gb_ref[0:1, :] = jnp.sum(gqkv[:, :D].astype(F32), axis=0, keepdims=True)
    gb_ref[2:3, :] = jnp.sum(gqkv[:, 2 * D :].astype(F32), axis=0, keepdims=True)


def qkv_grad_kernel(
    pos_ref, vec_ref, sums_ref, gbq_ref, gmid, gqkv, n1_ref, w_qkv, n1_got, g_got, x_any,
    igrad, mine, x_ref, acc, n1t, both, grad, sums, small, sems,
):
    tokens = x_ref.shape[0]
    load_x = start(x_any, x_ref, sems.at[0])
    sums[...] = sums_ref[...]
    sums[2:3, :] = gbq_ref[0:1, :]
    sums[4:5, :] = gbq_ref[2:3, :]
    n1t[:, :tokens] = n1_ref[...].T
    n1t[:, tokens:] = n1_got[...].T
    for t in range(3):
        cols = pl.ds(pl.multiple_of(t * D + pos_ref[1] * HALF, 128), HALF)
        both[:tokens, t * HALF : (t + 1) * HALF] = gqkv[:, cols]
    both[tokens:, :] = g_got[...]
    for z in range(4):
        rows = slice(z * 4 * BLK, (z + 1) * 4 * BLK)
        grad[rows, :] = nn(n1t[rows, :], both[...]).astype(BF16)
        for chip in range(4 * z, 4 * z + 4):
            place = scatter_place(pos_ref, chip)
            for t in range(3):
                src = grad.at[pl.ds(chip * BLK, BLK), pl.ds(t * HALF, HALF)]
                start(src, mine.at[place, pl.ds(t * BLK, BLK)], sems.at[1])
    for t in range(3):
        part = nt(gqkv[:, t * D : (t + 1) * D], w_qkv[t])
        acc[...] = part if t == 0 else acc[...] + part
    load_x.wait()

    def back_one(rows):
        xhat, scale = norm_parts(x_ref[rows, :].astype(F32))
        g = acc[rows, :]
        sums[0:1, :] += jnp.sum(g * xhat, axis=0, keepdims=True)
        sums[1:2, :] += jnp.sum(g, axis=0, keepdims=True)
        igrad[rows, :] = (gmid[rows, :] + norm_back(g, xhat, scale, vec_ref[0:1, :])).astype(BF16)

    chunks(tokens, 256, back_one)
    for p in range(CHIPS):
        small[p, 0:16] = sums[:, :HALF].astype(BF16)
        small[p, 16:32] = sums[:, HALF:].astype(BF16)
        start(small.at[p], mine.at[p, pl.ds(3 * BLK, 32)], sems.at[2])
    whole_wait(small, sems.at[2])
    whole_wait(grad, sems.at[1])


def layer_out_kernel(pos_ref, vec_ref, act_ref, mid_ref, w_down, out_ref):
    out_ref[...] = (
        mid_ref[...] + nn(act_ref[...], w_down[...]) + vec_ref[12:13, :]
    ).astype(BF16)


PER = D // (2 * CHIPS)
SEND_ROWS = (3 * PER, 16, 5 * PER, 4 * PER)


def pack_kernel(pos_ref, w_qkv, w_out, w_up, w_down, bu_ref, *refs):
    values, (mine, theirs, rows, last, wide) = refs[:8], refs[8:]
    place = pos_ref[0] * 2 + pos_ref[1]
    rows[...] = jnp.zeros(rows.shape, F32)
    last[...] = jnp.zeros(last.shape, F32)
    for r, value in zip((0, 1, 2, 4, 5, 6, 7, 12), values):
        rows[r : r + 1, 0:PER] = value[...].astype(F32)
    last[0:1, 0 : 4 * PER] = bu_ref[...].astype(F32)
    at = place * (4 * PER)
    up = pltpu.roll(last[...], at % D, 1)[0:1]
    here = lax.broadcasted_iota(jnp.int32, (16, 1), 0) == 8 + at // D
    rows[...] = pltpu.roll(rows[...], place * PER, 1) + jnp.where(here, up, 0.0)
    for out, other in ((mine, 0), (theirs, 1)):
        half = pos_ref[1] ^ other

        def cols(first):
            return pl.ds(pl.multiple_of(first + half * HALF, 128), HALF)

        at = 0
        for t in range(3):
            wide[at : at + PER, :] = w_qkv[:, cols(t * D)].astype(F32)
            at += PER
        wide[at : at + 16, :] = rows[:, cols(0)]
        at += 16
        for n in range(4):
            u, s = n // 2, n % 2
            first = pl.multiple_of(half * (2 * D) + s * D + u * HALF, 128)
            wide[at : at + PER, :] = w_up[:, pl.ds(first, HALF)].astype(F32)
            at += PER
        wide[at : at + PER, :] = w_out[:, cols(0)].astype(F32)
        at += PER
        wide[at : at + 4 * PER, :] = w_down[:, cols(0)].astype(F32)
        out[...] = wide[...].astype(BF16)


def combine_kernel(pos_ref, mine, got, one, two, upper, lower, wide):
    first = pos_ref[1] == 0
    m, g = mine[...].astype(F32), got[...].astype(F32)
    upper[...] = jnp.where(first, m, g)
    lower[...] = jnp.where(first, g, m)

    def pair(at, size):
        wide[0:size, :] = upper[at : at + size, :]
        wide[size : 2 * size, :] = lower[at : at + size, :]
        return wide[0 : 2 * size, :].astype(BF16)

    for t in range(3):
        one[t * BLK : (t + 1) * BLK, :] = pair(t * PER, PER)
    at = 3 * PER
    one[3 * BLK :, :] = (upper[at : at + 16, :] + lower[at : at + 16, :]).astype(BF16)
    at += 16
    for n in range(5):
        two[n] = pair(at + n * PER, PER)
    low = pair(at + 5 * PER, 4 * PER)
    for n in range(4):
        two[5 + n] = low[n * BLK : (n + 1) * BLK]


def finish_kernel(pos_ref, last, *refs):
    terms, (keep, send, held, sems) = refs[:4], refs[4:]
    for i, term in enumerate(terms):
        start(term.at[0], held.at[i], sems.at[i])
    total = last[...].astype(F32)
    for i in range(4):
        whole_wait(held.at[i], sems.at[i])
        total = total + held[i].astype(F32)
    first = pos_ref[1] == 0
    for t in range(3):
        upper, lower = total[t * BLK : t * BLK + PER], total[t * BLK + PER : (t + 1) * BLK]
        keep[t * PER : (t + 1) * PER, :] = jnp.where(first, upper, lower)
        send[t * PER : (t + 1) * PER, :] = jnp.where(first, lower, upper)
    keep[3 * PER :, :] = total[3 * BLK :]
    send[3 * PER :, :] = total[3 * BLK :]


def spread_kernel(pos_ref, keep, got, w_ref, eight_ref, up_ref, down_ref, rows):
    place = pos_ref[0] * 2 + pos_ref[1]
    for ref, other in ((keep, 0), (got, 1)):
        half = pos_ref[1] ^ other
        for t in range(3):
            cols = pl.ds(pl.multiple_of(t * D + half * HALF, 128), HALF)
            w_ref[:, cols] = ref[t * PER : (t + 1) * PER, :]
    for h in range(2):
        at = 3 * PER + 16 * h
        rows[:, h * HALF : (h + 1) * HALF] = keep[at : at + 16, :] + got[at : at + 16, :]
    mine = pltpu.roll(rows[...], lax.rem(D - place * PER, D), 1)
    eight_ref[...] = mine[0:8, 0:PER]
    down_ref[...] = mine[12:13, 0:PER]
    at = place * (4 * PER)
    here = lax.broadcasted_iota(jnp.int32, (16, 1), 0) == 8 + at // D
    row = jnp.sum(jnp.where(here, rows[...], 0.0), axis=0, keepdims=True)
    turned = pltpu.roll(jnp.broadcast_to(row, (8, D)), lax.rem(D - at % D, D), 1)
    up_ref[...] = turned[0:1, 0 : 4 * PER]


def spread_up_kernel(pos_ref, keep, got, up_ref, out_ref):
    for ref, other in ((keep, 0), (got, 1)):
        half = pos_ref[1] ^ other
        for n in range(4):
            first = half * (2 * D) + (n % 2) * D + (n // 2) * HALF
            up_ref[:, pl.ds(pl.multiple_of(first, 128), HALF)] = ref[n]
        out_ref[:, pl.ds(pl.multiple_of(half * HALF, 128), HALF)] = ref[4]


def call(kernel, name, near, far, near_outs, far_outs, scratch, flops, aliases=None, limit=18):
    far = [in_hbm(a) for a in far]
    space = pl.BlockSpec(memory_space=pltpu.VMEM)
    anyspec = pl.BlockSpec(memory_space=pl.ANY)
    outs = tuple(near_outs) + tuple(far_outs)
    moved = sum(math.prod(a.shape) * a.dtype.itemsize for a in (*near, *far, *outs))
    return pl.pallas_call(
        kernel,
        out_shape=outs,
        in_specs=[pl.BlockSpec(memory_space=pltpu.SMEM)]
        + [space] * (len(near) - 1)
        + [anyspec] * len(far),
        out_specs=[space] * len(near_outs) + [anyspec] * len(far_outs),
        scratch_shapes=scratch,
        input_output_aliases=aliases or {},
        compiler_params=pltpu.CompilerParams(vmem_limit_bytes=limit << 20),
        cost_estimate=pl.CostEstimate(flops=flops, bytes_accessed=moved, transcendentals=0),
        name=name,
    )(*near, *far)


def in_hbm(array):
    return pltpu.with_memory_space_constraint(array, pltpu.HBM)


def keep(*arrays):
    return [pltpu.with_memory_space_constraint(a, pltpu.VMEM) for a in arrays]


def swap(value, chip_bit):
    flip = chip_bit * 2 if chip_bit else 1
    return lax.ppermute(value, AXES, [(i, i ^ flip) for i in range(2 * CHIPS)])


def tie(value, *after):
    return lax.optimization_barrier((value,) + after)[0]


def gathered(*own_half):
    return list(own_half) + [swap(piece, 0) for piece in own_half]


def hold(pieces, *after):
    return lax.optimization_barrier((*pieces, *after))[: len(pieces)] if after else pieces


def rounded_sum(*terms):
    total = terms[0].astype(F32)
    for term in terms[1:]:
        total = total + term.astype(F32)
    return total.astype(BF16)


def small_grads(sums, place, per, per_up):
    eight = lax.dynamic_slice(sums, (0, place * per), (8, per))
    at = place * per_up
    up = lax.dynamic_slice(sums, (8 + at // D, at % D), (1, per_up))[0]
    down = lax.dynamic_slice(sums, (12, place * per), (1, per))[0]
    return eight, up, down


def halves(w_qkv, w_out, w_up, w_down):
    rows = w_qkv.shape[0]
    qkv = w_qkv.reshape(rows, 3, 2, HALF)
    up = w_up.reshape(rows, 2, 4, HALF)
    for h in range(2):
        cols = slice(h * HALF, (h + 1) * HALF)
        up_h = up[:, h].reshape(rows, 2, 2, HALF).transpose(2, 1, 0, 3).reshape(4, rows, HALF)
        yield (
            qkv[:, :, h].transpose(1, 0, 2),
            jnp.concatenate([up_h, w_out[None, :, cols]]),
            w_down[:, cols],
        )


def gather_plain(weights, values):
    def whole(w):
        return lax.all_gather(w, AXES, axis=0, tiled=True)

    gain1, bias1, bq, bv, bo, gain2, bias2, bu, bd = [whole(v) for v in values]
    rest = jnp.zeros((3, D), BF16)
    small = jnp.stack([gain1, bias1, bq, jnp.zeros_like(bq), bv, bo, gain2, bias2])
    small = jnp.concatenate([small, bu.reshape(4, D), bd[None], rest])
    groups = ([], [], [])
    for h, (attn, up, down) in enumerate(halves(*[whole(w) for w in weights])):
        attn = attn.reshape(3, CHIPS, BLK, HALF).transpose(1, 0, 2, 3).reshape(CHIPS, 3 * BLK, HALF)
        up = up.reshape(5, CHIPS, BLK, HALF).transpose(1, 0, 2, 3)
        down = down.reshape(CHIPS, 4 * BLK, HALF)
        extra = jnp.zeros((CHIPS, 16, HALF), BF16).at[0].set(small[:, h * HALF : (h + 1) * HALF])
        for group, blocks in zip(groups, (jnp.concatenate([attn, extra], axis=1), up, down)):
            group.extend(jnp.stack([blocks[o] for o in piece]) for piece in GATHER)
    return groups


def scatter_plain(pair, group):
    both = [jnp.stack([part[SCATTER.index(chip)] for chip in range(CHIPS)]) for part in pair]

    def scatter(v):
        return lax.psum_scatter(v.astype(F32), AXES, scatter_dimension=0, tiled=True)

    def matrix(units):
        return jnp.stack(units, axis=3).transpose(0, 2, 1, 3, 4).reshape(D, -1, 2, HALF)

    if group == "attn":
        sums = jnp.concatenate([both[0][0, 3 * BLK + 16 * h :][:16] for h in range(2)], axis=1)
        qkv = matrix([b[:, : 3 * BLK].reshape(CHIPS, 3, BLK, HALF) for b in both])
        return scatter(qkv.reshape(D, 3 * D)), lax.psum(sums.astype(F32), AXES)
    if group == "up":
        up = matrix(both)
        order = up[:, :4].reshape(D, 2, 2, 2, HALF).transpose(0, 3, 2, 1, 4)
        return scatter(order.reshape(D, FF)), scatter(up[:, 4].reshape(D, D))
    return scatter(jnp.concatenate([b.reshape(FF, HALF) for b in both], axis=1))


def shape(dims, kind=BF16):
    return jax.ShapeDtypeStruct(dims, kind)


def far_shape(*dims):
    return pltpu.HBM(dims, BF16)


def dma(n):
    return pltpu.SemaphoreType.DMA((n,))


def vmem(*dims, kind=BF16):
    return pltpu.VMEM(dims, kind)


class Layer:
    def __init__(self, tokens):
        self.tokens = tokens
        self.rows = tokens // ROW_LEN
        self.out = shape((tokens, D))
        self.wide = vmem(tokens, FF)
        self.one = vmem(tokens, D)
        self.one_f32 = vmem(tokens, D, kind=F32)
        self.qkv = vmem(tokens, 3 * D)
        self.soft = vmem(self.rows * HEADS, ROW_LEN, ROW_LEN)
        self.turned = vmem(D, tokens)
        self.square = vmem(D, D)
        self.three = vmem(3, D, D)
        self.four = vmem(2, 2, D, D)
        self.sums = vmem(8, D, kind=F32)
        self.vec = vmem(16, D, kind=F32)

    def chip_blocks(self, pos, weights, values):
        *rest, bu, bd = [in_hbm(v.reshape(1, -1)) for v in values]
        weights = [in_hbm(w) for w in weights]
        sent = shape((sum(SEND_ROWS), HALF))
        wide = vmem(sum(SEND_ROWS), HALF, kind=F32)
        mine, theirs = call(
            pack_kernel, "pack", (pos, *weights, bu, *rest, bd), (), (sent, sent), (),
            [vmem(16, D, kind=F32), vmem(8, D, kind=F32), wide], 0,
        )
        return call(
            combine_kernel, "combine", (pos, mine, swap(theirs, 0)), (),
            (shape((3 * BLK + 16, HALF)), shape((9, BLK, HALF))), (),
            [wide, wide, vmem(4 * BLK, HALF, kind=F32)], 0,
        )

    def finish(self, pos, last, low):
        sent = shape((3 * PER + 32, HALF), F32)
        keep, send = call(
            finish_kernel, "finish", (pos, last), low, (sent, sent), (),
            [vmem(4, 3 * BLK + 32, HALF), dma(4)], 0,
        )
        return call(
            spread_kernel, "spread", (pos, keep, swap(send, 0)), (),
            (shape((PER, 3 * D), F32), shape((8, PER), F32), shape((1, 4 * PER), F32), shape((1, PER), F32)),
            (), [vmem(16, D, kind=F32)], 0,
        )

    def spread_up(self, pos, keep, got):
        return call(
            spread_up_kernel, "spread_up", (pos, keep, got), (),
            (shape((PER, FF), F32), shape((PER, D), F32)), (), [], 0,
        )

    def attn_forward(self, pos, segr, segc, inputs, attn):
        return call(
            attn_forward_kernel, "attn_forward", (pos, segr, segc), [in_hbm(inputs)] + attn,
            (self.vec, self.one, self.qkv, self.soft, self.one, self.three), (),
            [
                self.one, vmem(2, CHIPS, 16, HALF),
                vmem(self.rows, ROW_LEN, ROW_LEN, kind=F32), dma(5),
            ],
            2 * self.tokens * D * D * 3 + 8 * self.tokens * D * ROW_LEN,
        )

    def mlp_up(self, pos, segc, vec, inputs, mixed, cotangent, up):
        vec, mixed = keep(vec, mixed)
        return call(
            mlp_up_kernel, "mlp_up", (pos, segc, vec, mixed), [inputs, cotangent] + up,
            (self.sums, self.one, self.one_f32, self.wide, self.wide, self.one, self.square, self.four), (),
            [self.one, self.one, dma(5)],
            2 * self.tokens * D * (FF + D),
        )

    def down_grad(self, pos, act, gout):
        buffer = far_shape(CHIPS, 4 * BLK, HALF)
        return call(
            down_grad_kernel, "down_grad", (pos, *keep(act, gout)), [], (), (buffer, buffer),
            [vmem(4, D, D), dma(1)],
            2 * self.tokens * D * FF,
        )

    def mlp_down(self, pos, gout, slope, n2, down):
        buffer = far_shape(CHIPS, 5, BLK, HALF)
        return call(
            mlp_down_kernel, "mlp_down", (pos, *keep(gout, slope, n2)), down,
            (self.sums, self.wide, vmem(FF, D)), (buffer, buffer),
            [self.turned, self.four, dma(5)],
            4 * self.tokens * D * FF,
        )

    def mid_backward(self, pos, vec, gbd, gbu, gpre, gout, mid, mixed, w_out, w_up, mine, theirs):
        buffer = far_shape(*mine.shape)
        near = (pos, *keep(vec, gbd, gbu, gpre, gout, mid, mixed, w_out, w_up))
        return call(
            mid_backward_kernel, "mid_backward", near, [mine, theirs],
            (self.vec, self.one_f32, self.one), (buffer, buffer),
            [self.one_f32, self.one, self.turned, self.square, dma(1)],
            2 * self.tokens * D * (FF + 2 * D),
            {len(near): 3, len(near) + 1: 4},
        )

    def attn_backward(self, pos, gmixed, qkv, soft):
        return call(
            attn_backward_kernel, "attn_backward", (pos, *keep(gmixed, qkv, soft)), [],
            (self.sums, self.qkv, vmem(self.tokens, 3 * HALF)), (), [], 20 * self.tokens * D * ROW_LEN,
        )

    def qkv_grad(self, pos, vec, sums, gbq, gmid, gqkv, n1, w_qkv, n1_got, g_got, inputs):
        return call(
            qkv_grad_kernel, "qkv_grad", (pos, *keep(vec, sums, gbq, gmid, gqkv, n1, w_qkv, n1_got, g_got)),
            [inputs], (self.out,), (far_shape(CHIPS, 3 * BLK + 32, HALF),),
            [
                self.one, self.one_f32, vmem(D, 2 * self.tokens), vmem(2 * self.tokens, 3 * HALF),
                vmem(D, 3 * HALF), vmem(16, D, kind=F32), vmem(CHIPS, 32, HALF), dma(3),
            ],
            2 * self.tokens * D * 6 * D,
        )

    def layer_out(self, pos, vec, act, mid, w_down):
        (out,) = call(
            layer_out_kernel, "layer_out", (pos, *keep(vec, act, mid, w_down)), [], (self.out,), (), [],
            2 * self.tokens * D * FF,
        )
        return out


class Scatter:
    def __init__(self, mine, theirs=None, *after):
        self.both = [mine] if theirs is None else [mine, swap(tie(theirs, *after), 0)]

    def part(self, first, last):
        return [ref[first:last] for ref in self.both]

    def hold_back(self, *after):
        self.both[-1] = hold((self.both[-1],), *after)[0]

    def first(self, *after):
        self.hold_back(*after)
        self.out = (rounded_sum(*self.part(8, 12)), rounded_sum(*self.part(12, 16)))
        self.in_y, self.in_x = swap(self.out[0], BIT_Y), swap(self.out[1], BIT_X)

    def second(self, *after):
        in_y, in_x = hold((self.in_y, self.in_x), *after)
        self.out = (
            rounded_sum(*self.part(4, 6), in_x[2:]),
            rounded_sum(*self.part(6, 8), in_y[2:]),
        )
        self.in_y, self.in_x = in_y, in_x
        self.in_y2, self.in_x2 = swap(self.out[0], BIT_Y), swap(self.out[1], BIT_X)

    def third(self, *after):
        in_y2, in_x2 = hold((self.in_y2, self.in_x2), *after)
        self.near = (*self.part(0, 2), self.in_x[:2], in_y2)
        self.out = (rounded_sum(*self.part(2, 4), self.in_y[:2], in_x2),)
        self.in_z = swap(self.out[0], BIT_Z0)

    def diagonal(self, *after):
        self.hold_back(*after)
        self.out = (rounded_sum(*self.part(10, 12)), rounded_sum(*self.part(14, 16)))
        self.in_y, self.in_x = swap(self.out[0], BIT_Y), swap(self.out[1], BIT_X)

    def hi(self, *after):
        in_y, self.in_x = hold((self.in_y, self.in_x), *after)
        self.out = (rounded_sum(*self.part(8, 10)), rounded_sum(*self.part(6, 8), in_y))
        self.in_y2, self.in_x2 = swap(self.out[0], BIT_Y), swap(self.out[1], BIT_X)

    def lo(self, *after):
        in_y2, in_x2 = hold((self.in_y2, self.in_x2), *after)
        far = rounded_sum(*self.part(2, 4), in_y2, in_x2)
        self.in_z = swap(far, BIT_Z0)
        low_y, low_x = rounded_sum(*self.part(4, 6), self.in_x), rounded_sum(*self.part(12, 14))
        low_y, low_x = hold((low_y, low_x), far)
        self.out = (far, low_y, low_x)
        self.near = (*self.part(0, 2), swap(low_y, BIT_Y), swap(low_x, BIT_X))

    def fourth(self, *after):
        self.near = (*self.near, *hold((self.in_z,), *after))
        self.out = (rounded_sum(*[t[1] for t in self.near]),)
        self.in_z = swap(self.out[0], BIT_Z1)

    def result(self, *after):
        total = hold((self.in_z,), *after)[0].astype(F32)
        for term in self.near:
            total = total + term[0].astype(F32)
        return total


def per_device(tuned, *args):
    (
        inputs, segment_ids, pre_attn_gain, pre_attn_bias, w_qkv, b_query, b_value, w_out, b_out,
        pre_mlp_gain, pre_mlp_bias, w_up, b_up, w_down, b_down, cotangent,
    ) = args
    tokens = inputs.shape[0]
    n_rows = tokens // ROW_LEN
    wide, narrow = lax.axis_index("wide"), lax.axis_index("narrow")
    weights = (w_qkv, w_out, w_up, w_down)
    values = (
        pre_attn_gain, pre_attn_bias, b_query, b_value, b_out, pre_mlp_gain, pre_mlp_bias, b_up, b_down,
    )
    per, per_up = pre_attn_gain.shape[0], b_up.shape[0]
    position = jnp.arange(ROW_LEN, dtype=jnp.int32)[None]
    own_id = jnp.where(segment_ids != 0, segment_ids, -1 - position)
    segr = own_id.reshape(n_rows, 1, ROW_LEN)
    segc = own_id.reshape(tokens, 1)
    layer = Layer(tokens)

    if not tuned:
        place = wide * lax.axis_size("narrow") + narrow
        pos = jnp.zeros((2,), jnp.int32)
        attn, up, down = gather_plain(weights, values)
        vec, n1, qkv, soft, mixed, w_qkv_all = layer.attn_forward(pos, segr, segc, inputs, attn)
        gbd, n2, mid, act, slope, gout, *w_mid = layer.mlp_up(pos, segc, vec, inputs, mixed, cotangent, up)
        pair_down = layer.down_grad(pos, act, gout)
        gbu, gpre, w_down_all, *pair_up = layer.mlp_down(pos, gout, slope, n2, down)
        sums, gmid, gmixed, *pair_up = layer.mid_backward(
            pos, vec, gbd, gbu, gpre, gout, mid, mixed, *w_mid, *pair_up
        )
        gbq, gqkv, give = layer.attn_backward(pos, gmixed, qkv, soft)
        pair_attn = []
        for half in range(2):
            input_grad, blocks = layer.qkv_grad(
                jnp.array([0, half], jnp.int32), vec, sums, gbq, gmid, gqkv, n1, w_qkv_all,
                jnp.zeros_like(n1), jnp.zeros_like(give), inputs,
            )
            pair_attn.append(blocks)
        layer_out = layer.layer_out(pos, vec, act, mid, w_down_all)
        grad_w_down = scatter_plain(pair_down, "down")
        grad_w_up, grad_w_out = scatter_plain(pair_up, "up")
        grad_w_qkv, sums = scatter_plain(pair_attn, "attn")
        eight, grad_b_up, grad_b_down = small_grads(sums, place, per, per_up)
    else:
        core = (narrow & 1).astype(jnp.int32)
        pos = jnp.stack([wide * 2 + (narrow >> 1), core]).astype(jnp.int32)
        block1, block23 = layer.chip_blocks(pos, weights, values)
        flat = (4 * BLK, HALF)

        near1 = swap(block1, BIT_Z1)
        lo1 = jnp.stack([block1, near1])
        hi1 = swap(lo1, BIT_Z0)
        y_lo1, x_lo1 = swap(lo1, BIT_Y), swap(lo1, BIT_X)
        near23 = swap(tie(block23, near1), BIT_Z1)
        d_lo1 = swap(y_lo1, BIT_X)
        y_hi1, x_hi1 = swap(hi1, BIT_Y), swap(hi1, BIT_X)
        lo2 = jnp.stack([block23[:5], near23[:5]])
        lo3 = jnp.stack([block23[5:].reshape(flat), near23[5:].reshape(flat)])
        hi2 = swap(tie(lo2, hi1), BIT_Z0)
        d_hi1 = swap(tie(x_hi1, y_hi1), BIT_Y)
        lo2b = tie(lo2, d_lo1, x_hi1, y_hi1)
        y_lo2, x_lo2 = swap(lo2b, BIT_Y), swap(lo2b, BIT_X)
        attn = gathered(lo1, hi1, y_lo1, y_hi1, x_lo1, x_hi1, d_lo1, d_hi1)
        hi3 = swap(tie(lo3, hi2), BIT_Z0)
        y_hi2, x_hi2 = swap(hi2, BIT_Y), swap(hi2, BIT_X)
        d_lo2, d_hi2 = swap(y_lo2, BIT_X), swap(tie(x_hi2, y_hi2), BIT_Y)
        lo3b = tie(lo3, y_lo2, x_lo2, y_hi2)
        y_lo3, x_lo3 = swap(lo3b, BIT_Y), swap(lo3b, BIT_X)
        vec, n1, qkv, soft, mixed, w_qkv_all = layer.attn_forward(
            tie(pos, y_hi2, x_hi2, lo3b, d_lo2), segr, segc, inputs, attn
        )

        d_hi2, y_lo3, x_lo3, hi3 = hold((d_hi2, y_lo3, x_lo3, hi3), mixed)
        d_lo3 = swap(y_lo3, BIT_X)
        y_hi3, x_hi3 = swap(hi3, BIT_Y), swap(hi3, BIT_X)
        lo2, hi2, y_lo2, y_hi2, x_lo2, x_hi2, d_lo2 = hold(
            (lo2, hi2, y_lo2, y_hi2, x_lo2, x_hi2, d_lo2), x_lo3, hi3
        )
        up = gathered(lo2, hi2, y_lo2, y_hi2, x_lo2, x_hi2, d_lo2, d_hi2)
        gbd, n2, mid, act, slope, gout, *w_mid = layer.mlp_up(
            tie(pos, hi3, y_lo3, x_lo3), segc, vec, inputs, mixed, cotangent, up
        )
        y_hi3, x_hi3, d_lo3 = hold((y_hi3, x_hi3, d_lo3), gbd)
        d_hi3 = swap(x_hi3, BIT_Y)
        pair_down = layer.down_grad(tie(pos, y_hi3, x_hi3, d_lo3), act, gout)
        d_hi3 = tie(d_hi3, pair_down[0])
        down = gathered(lo3, hi3, y_lo3, y_hi3, x_lo3, x_hi3, d_lo3, d_hi3)
        scatter1 = Scatter(*pair_down, *down)
        gbu, gpre, w_down_all, *pair_up = layer.mlp_down(pos, gout, slope, n2, down)
        scatter1.diagonal(gbu)
        sums, gmid, gmixed, *pair_up = layer.mid_backward(
            tie(pos, *scatter1.out), vec, gbd, gbu, gpre, gout, mid, mixed, *w_mid, *pair_up
        )
        scatter1.hi(sums)
        scatter2 = Scatter(*pair_up, scatter1.in_x)
        gbq, gqkv, give = layer.attn_backward(tie(pos, *scatter1.out), gmixed, qkv, soft)
        scatter1.lo(gbq)
        n1, give = hold((n1, give), *scatter1.out)
        n1_got, g_got = swap(n1, 0), swap(give, 0)
        scatter2.diagonal(gbq)
        input_grad, sums_attn = layer.qkv_grad(
            tie(pos, *scatter2.out, *scatter1.out),
            vec, sums, gbq, gmid, gqkv, n1, w_qkv_all, n1_got, g_got, inputs,
        )
        scatter2.hi(input_grad)
        scatter1.fourth(input_grad)
        scatter3 = Scatter(tie(sums_attn, *scatter2.out))
        scatter3.diagonal()
        layer_out = layer.layer_out(
            tie(pos, *scatter3.out, *scatter1.out), vec, act, mid, w_down_all
        )
        scatter1.in_z = tie(scatter1.in_z, layer_out)
        scatter3.hi(layer_out, scatter1.in_z)
        scatter2.lo(*scatter3.out)
        scatter3.lo(*scatter2.out)
        scatter2.fourth(*scatter3.out)
        scatter3.fourth(*scatter2.out)

        def exchange(blocks, axis):
            first, second = jnp.split(blocks, 2, axis=axis)
            keep = jnp.where(core == 0, first, second)
            got = swap(jnp.where(core == 0, second, first), 0)
            return jnp.where(core == 0, keep, got), jnp.where(core == 0, got, keep)

        grad_w_down = jnp.concatenate(exchange(scatter1.result(*scatter3.out), 0), axis=1)
        total = scatter2.result(*scatter3.out)
        upper, lower = total[:, :PER], total[:, PER:]
        got = swap(jnp.where(core == 0, lower, upper), 0)
        grad_w_up, grad_w_out = layer.spread_up(pos, jnp.where(core == 0, upper, lower), got)
        grad_w_qkv, eight, grad_b_up, grad_b_down = layer.finish(
            pos, scatter3.in_z, [*scatter3.both, *scatter3.near[1:]]
        )
        grad_b_up, grad_b_down = grad_b_up[0], grad_b_down[0]
    return (
        layer_out, input_grad, eight[0], eight[1], grad_w_qkv, eight[2], eight[4], grad_w_out, eight[5],
        eight[6], eight[7], grad_w_up, grad_b_up, grad_w_down, grad_b_down,
    )


def solution(mesh):
    both = P(AXES, None)
    one = P(AXES)
    tuned = dict(mesh.shape) == {"wide": 8, "narrow": 4}
    in_specs = (both, both, one, one, both, one, one, both, one, one, one, both, one, both, one, both)
    out_specs = (both, both, one, one, both, one, one, both, one, one, one, both, one, both, one)
    return jax.shard_map(
        functools.partial(per_device, tuned),
        mesh=mesh,
        in_specs=in_specs,
        out_specs=out_specs,
        check_vma=False,
    )
```

```python
import functools
import math

import jax
import jax.numpy as jnp
from jax import lax
from jax.experimental import pallas as pl
from jax.experimental.pallas import tpu as pltpu
from jax.sharding import PartitionSpec as P

HEADS = 12
HEAD_DIM = 64
D = 768
FF = 3072
ROW_LEN = 256
HALF = 384
CHIPS = 16
BLK = 48
PAIRS = HEADS // 2
AXES = ("wide", "narrow")

EPS = 1e-06
MASKED = -1e30
F32 = jnp.float32
BF16 = jnp.bfloat16

BIT_Y, BIT_X, BIT_Z0, BIT_Z1 = 1, 2, 4, 8
Z_OFFSETS = (0, 4, 8, 12)

GATHER = tuple((o + z, o + z + BIT_Z1) for o in (0, BIT_Y, BIT_X, BIT_X + BIT_Y) for z in (0, BIT_Z0))
PIECES = 2 * len(GATHER)

SCATTER = (0, 8, 4, 12, 1, 9, 6, 14, 5, 13, 7, 15, 2, 10, 3, 11)


def nt(a, b):
    return lax.dot_general(a, b, (((1,), (1,)), ((), ())), preferred_element_type=F32)


def tn(a, b):
    return lax.dot_general(a, b, (((0,), (0,)), ((), ())), preferred_element_type=F32)


def nn(a, b):
    return lax.dot_general(a, b, (((1,), (0,)), ((), ())), preferred_element_type=F32)


def chunks(tokens, step, body):
    def one(i, carry):
        body(pl.ds(pl.multiple_of(i * step, step), step))
        return carry

    lax.fori_loop(0, tokens // step, one, 0)


def norm_parts(v):
    centre = jnp.mean(v, axis=-1, keepdims=True)
    centred = v - centre
    scale = lax.rsqrt(jnp.mean(centred * centred, axis=-1, keepdims=True) + EPS)
    return centred * scale, scale


def start(src, dst, sem):
    copy = pltpu.make_async_copy(src, dst, sem)
    copy.start()
    return copy


def whole_wait(ref, sem):
    pltpu.make_async_copy(ref, ref, sem).wait()


def each_block(pos_ref, pieces):
    for other in range(2):
        for ref, offsets in zip(pieces[other * len(GATHER) :], GATHER):
            for b, offset in enumerate(offsets):
                yield ref, b, pos_ref[0] ^ offset, other, offset


def chip_rows(chip, size):
    return pl.ds(pl.multiple_of(chip * size, 16), size)


def half_cols(pos_ref, other):
    return pl.ds(pl.multiple_of((pos_ref[1] ^ other) * HALF, 128), HALF)


def fetch_qkv(pos_ref, pieces, w_qkv, sems):
    for t in range(3):
        for ref, b, chip, other, _ in each_block(pos_ref, pieces):
            dst = w_qkv.at[t, chip_rows(chip, BLK), half_cols(pos_ref, other)]
            start(ref.at[b, pl.ds(t * BLK, BLK)], dst, sems.at[t])


def fetch_out(pos_ref, pieces, w_out, sem):
    for ref, b, chip, other, _ in each_block(pos_ref, pieces):
        dst = w_out.at[chip_rows(chip, BLK), half_cols(pos_ref, other)]
        start(ref.at[b, 4], dst, sem)


def fetch_small(pos_ref, pieces, small, sem):
    for ref, b, chip, other, _ in each_block(pos_ref, pieces):
        start(ref.at[b, pl.ds(3 * BLK, 16)], small.at[pos_ref[1] ^ other, chip], sem)


def fetch_up(pos_ref, pieces, w_up, sems):
    for ref, b, chip, other, _ in each_block(pos_ref, pieces):
        for u in range(2):
            dst = w_up.at[other, pl.ds(0, 2), chip_rows(chip, BLK), pl.ds(u * HALF, HALF)]
            start(ref.at[b, pl.ds(2 * u, 2)], dst, sems.at[other])


def fetch_down(pos_ref, pieces, w_down, sems):
    for q in range(4):
        for ref, b, chip, other, offset in each_block(pos_ref, pieces):
            if offset // 4 == q:
                dst = w_down.at[chip_rows(chip, 4 * BLK), half_cols(pos_ref, other)]
                start(ref.at[b], dst, sems.at[q])


def scatter_place(pos_ref, chip):
    offset = pos_ref[0] ^ chip
    xy, z = offset & 3, ((offset >> 2) & 1) * 2 + (offset >> 3)
    near = jnp.where(xy == 1, 4, jnp.where(xy == 2, 12, 14)) + z
    far = jnp.where(xy == 1, 6, jnp.where(xy == 2, 4, 8)) + z
    return jnp.where(xy == 0, z, jnp.where(z < 2, near, far))


def head_masks():
    lane = lax.broadcasted_iota(jnp.int32, (1, 2 * HEAD_DIM), 1)
    return [(lane // HEAD_DIM == hh).astype(F32).astype(BF16) for hh in range(2)]


def pair_cols(t, i):
    return pl.ds(pl.multiple_of(t * D + i * 128, 128), 128)


def attn_forward_kernel(pos_ref, segr_ref, segc_ref, x_any, *refs):
    pieces, refs = refs[:PIECES], refs[PIECES:]
    vec_ref, n1_ref, qkv_ref, soft_ref, mixed_ref, w_qkv, x_ref, small, bias, sems = refs
    tokens = x_ref.shape[0]
    n_rows = tokens // ROW_LEN
    load_x = start(x_any, x_ref, sems.at[4])
    fetch_small(pos_ref, pieces, small, sems.at[0])
    fetch_qkv(pos_ref, pieces, w_qkv, sems.at[pl.ds(1, 3)])
    for r in range(n_rows):
        same = segc_ref[r * ROW_LEN : (r + 1) * ROW_LEN] == segr_ref[r]
        bias[r] = jnp.where(same, 0.0, MASKED)
    whole_wait(small, sems.at[0])
    for h in range(2):
        vec_ref[:, h * HALF : (h + 1) * HALF] = jnp.sum(small[h].astype(F32), axis=0)
    load_x.wait()

    def norm_one(rows):
        xhat, _ = norm_parts(x_ref[rows, :].astype(F32))
        n1_ref[rows, :] = (xhat * vec_ref[0:1, :] + vec_ref[1:2, :]).astype(BF16)

    chunks(tokens, 128, norm_one)
    for t in range(3):
        whole_wait(w_qkv.at[t], sems.at[1 + t])
        y = (nn(n1_ref[...], w_qkv[t]) + vec_ref[2 + t : 3 + t, :]).astype(BF16)
        if t == 0:
            y = y * BF16(HEAD_DIM**-0.5)
        qkv_ref[:, t * D : (t + 1) * D] = y
    masks = head_masks()
    for r in range(n_rows):
        rows = slice(r * ROW_LEN, (r + 1) * ROW_LEN)

        def pair(i, carry):
            q, k, v = (qkv_ref[rows, pair_cols(t, i)] for t in range(3))
            mixed = jnp.zeros((ROW_LEN, 128), F32)
            for hh, keep in enumerate(masks):
                s = nt(q, k * keep) + bias[r]
                e = jnp.exp(s - jnp.max(s, axis=-1, keepdims=True))
                p = (e * (1.0 / jnp.sum(e, axis=-1, keepdims=True))).astype(BF16)
                soft_ref[r * HEADS + 2 * i + hh] = p
                mixed = mixed + nn(p, v * keep)
            mixed_ref[rows, pair_cols(0, i)] = mixed.astype(BF16)
            return carry

        lax.fori_loop(0, PAIRS, pair, 0, unroll=3)


GELU_A = 0.7978845608028654
GELU_B = 0.044715


def quarter(pos_ref, other, s):
    return (pos_ref[1] ^ other) * 2 + s


def quarter_cols(z):
    return pl.ds(pl.multiple_of(z * D, 128), D)


QUARTERS = ((0, 0), (0, 1), (1, 0), (1, 1))


def mlp_up_kernel(pos_ref, segc_ref, vec_ref, mixed_ref, x_any, cot_any, *refs):
    pieces, refs = refs[:PIECES], refs[PIECES:]
    gb_ref, n2_ref, mid_ref, act_ref, slope_ref, gout_ref, w_out, w_up, x_ref, cot_ref, sems = refs
    tokens = n2_ref.shape[0]
    load_cot = start(cot_any, cot_ref, sems.at[3])
    load_x = start(x_any, x_ref, sems.at[4])
    fetch_out(pos_ref, pieces, w_out, sems.at[2])
    fetch_up(pos_ref, pieces, w_up, sems)
    load_cot.wait()
    valid = segc_ref[...] > 0
    gout = jnp.where(valid, cot_ref[...].astype(F32), 0.0)
    gout_ref[...] = gout.astype(BF16)
    gb_ref[...] = jnp.broadcast_to(jnp.sum(gout, axis=0, keepdims=True), gb_ref.shape)
    load_x.wait()
    whole_wait(w_out, sems.at[2])
    mid_ref[...] = x_ref[...].astype(F32) + nn(mixed_ref[...], w_out[...]) + vec_ref[5:6, :]

    def norm_two(rows):
        xhat, _ = norm_parts(mid_ref[rows, :])
        n2_ref[rows, :] = (xhat * vec_ref[6:7, :] + vec_ref[7:8, :]).astype(BF16)

    chunks(tokens, 128, norm_two)
    for other, s in QUARTERS:
        if s == 0:
            whole_wait(w_up.at[other], sems.at[other])
        z = quarter(pos_ref, other, s)
        b_up = vec_ref[pl.ds(8 + z, 1), :]
        cols = quarter_cols(z)

        def part(rows):
            u = nn(n2_ref[rows, :], w_up[other, s]) + b_up
            sq = u * u
            t = jnp.tanh(u * (GELU_A + GELU_A * GELU_B * sq))
            half_up = 0.5 + 0.5 * t
            act_ref[rows, cols] = (u * half_up).astype(BF16)
            slope_ref[rows, cols] = (
                half_up + u * (0.5 - 0.5 * t * t) * (GELU_A + 3.0 * GELU_A * GELU_B * sq)
            ).astype(BF16)

        chunks(tokens, 512, part)


def down_grad_kernel(pos_ref, act_ref, gout_ref, mine, theirs, grad, sem):
    for z in range(4):
        grad[z] = tn(act_ref[:, z * D : (z + 1) * D], gout_ref[...]).astype(BF16)
        for j in range(4):
            place = scatter_place(pos_ref, 4 * z + j)
            for other, out in enumerate((mine, theirs)):
                src = grad.at[z, pl.ds(j * 4 * BLK, 4 * BLK), half_cols(pos_ref, other)]
                start(src, out.at[place], sem.at[0])
    whole_wait(grad, sem.at[0])


def mlp_down_kernel(pos_ref, gout_ref, slope_ref, n2_ref, *refs):
    pieces, refs = refs[:PIECES], refs[PIECES:]
    gb_ref, gpre_ref, w_down, mine, theirs, n2t, grad, sems = refs
    fetch_down(pos_ref, pieces, w_down, sems)
    gb_ref[...] = jnp.zeros(gb_ref.shape, F32)
    n2t[...] = n2_ref[...].T
    for other, s in QUARTERS:
        z = quarter(pos_ref, other, s)
        cols = quarter_cols(z)
        whole_wait(w_down.at[cols], sems.at[z ^ (pos_ref[0] >> 2)])
        ga = nt(gout_ref[...], w_down[cols, :])
        gp = (ga * slope_ref[:, cols].astype(F32)).astype(BF16)
        gpre_ref[:, cols] = gp
        gb_ref[pl.ds(z, 1), :] = jnp.sum(gp.astype(F32), axis=0, keepdims=True)
        grad[other, s] = nn(n2t[...], gp).astype(BF16)
        if s == 1:
            for chip in range(CHIPS):
                place = scatter_place(pos_ref, chip)
                for u in range(2):
                    src = grad.at[other, pl.ds(0, 2), pl.ds(chip * BLK, BLK), pl.ds(u * HALF, HALF)]
                    start(src, (mine, theirs)[other].at[place, pl.ds(2 * u, 2)], sems.at[4])
    whole_wait(grad, sems.at[4])


def norm_back(grad, xhat, scale, gain):
    gn = grad * gain
    mean_gn = jnp.mean(gn, axis=-1, keepdims=True)
    mean_gx = jnp.mean(gn * xhat, axis=-1, keepdims=True)
    return scale * (gn - mean_gn - xhat * mean_gx)


def mid_backward_kernel(
    pos_ref, vec_ref, gbd_ref, gbu_ref, gpre_ref, gout_ref, mid_ref, mixed_ref, w_out, w_up, _, __,
    sums, gmid, gmixed, mine, theirs, acc, gbr, mixt, grad, sem,
):
    tokens = mid_ref.shape[0]
    sums[...] = jnp.zeros(sums.shape, F32)
    sums[8:12, :] = gbu_ref[0:4, :]
    sums[12:13, :] = gbd_ref[0:1, :]
    mixt[...] = mixed_ref[...].T
    for other, s in QUARTERS:
        part = nt(gpre_ref[:, quarter_cols(quarter(pos_ref, other, s))], w_up[other, s])
        acc[...] = part if other + s == 0 else acc[...] + part

    def back_two(rows):
        xhat, scale = norm_parts(mid_ref[rows, :])
        g = acc[rows, :]
        sums[6:7, :] += jnp.sum(g * xhat, axis=0, keepdims=True)
        sums[7:8, :] += jnp.sum(g, axis=0, keepdims=True)
        gm = gout_ref[rows, :].astype(F32) + norm_back(g, xhat, scale, vec_ref[6:7, :])
        gmid[rows, :] = gm
        low = gm.astype(BF16)
        gbr[rows, :] = low
        sums[5:6, :] += jnp.sum(low.astype(F32), axis=0, keepdims=True)

    chunks(tokens, 128, back_two)
    grad[...] = nn(mixt[...], gbr[...]).astype(BF16)
    for chip in range(CHIPS):
        place = scatter_place(pos_ref, chip)
        for other, out in enumerate((mine, theirs)):
            src = grad.at[pl.ds(chip * BLK, BLK), half_cols(pos_ref, other)]
            start(src, out.at[place, 4], sem.at[0])
    gmixed[...] = nt(gbr[...], w_out[...]).astype(BF16)
    whole_wait(grad, sem.at[0])


def attn_backward_kernel(pos_ref, gmixed, qkv_ref, soft_ref, gb_ref, gqkv, give):
    masks = head_masks()
    for r in range(gmixed.shape[0] // ROW_LEN):
        rows = slice(r * ROW_LEN, (r + 1) * ROW_LEN)

        def pair(i, carry):
            q, k, v = (qkv_ref[rows, pair_cols(t, i)] for t in range(3))
            gm = gmixed[rows, pair_cols(0, i)]
            dq = jnp.zeros((ROW_LEN, 128), F32)
            dk = jnp.zeros((ROW_LEN, 128), F32)
            dv = jnp.zeros((ROW_LEN, 128), F32)
            for hh, keep in enumerate(masks):
                p_low = soft_ref[r * HEADS + 2 * i + hh]
                p = p_low.astype(F32)
                gmk = gm * keep
                gs = nt(gmk, v)
                inner = jnp.sum(p * gs, axis=-1, keepdims=True)
                ds = (p * (gs - inner)).astype(BF16)
                dq = dq + nn(ds, k * keep)
                dk = dk + tn(ds, q * keep)
                dv = dv + tn(p_low, gmk)
            gqkv[rows, pair_cols(0, i)] = (dq * (HEAD_DIM**-0.5)).astype(BF16)
            gqkv[rows, pair_cols(1, i)] = dk.astype(BF16)
            gqkv[rows, pair_cols(2, i)] = dv.astype(BF16)
            return carry

        lax.fori_loop(0, PAIRS, pair, 0)
    for t in range(3):
        cols = pl.ds(pl.multiple_of(t * D + (1 - pos_ref[1]) * HALF, 128), HALF)
        give[:, t * HALF : (t + 1) * HALF] = gqkv[:, cols]
    gb_ref[...] = jnp.zeros(gb_ref.shape, F32)
    gb_ref[0:1, :] = jnp.sum(gqkv[:, :D].astype(F32), axis=0, keepdims=True)
    gb_ref[2:3, :] = jnp.sum(gqkv[:, 2 * D :].astype(F32), axis=0, keepdims=True)


def qkv_grad_kernel(
    pos_ref, vec_ref, sums_ref, gbq_ref, gmid, gqkv, n1_ref, w_qkv, n1_got, g_got, x_any,
    igrad, mine, x_ref, acc, n1t, both, grad, sums, small, sems,
):
    tokens = x_ref.shape[0]
    load_x = start(x_any, x_ref, sems.at[0])
    sums[...] = sums_ref[...]
    sums[2:3, :] = gbq_ref[0:1, :]
    sums[4:5, :] = gbq_ref[2:3, :]
    n1t[:, :tokens] = n1_ref[...].T
    n1t[:, tokens:] = n1_got[...].T
    for t in range(3):
        cols = pl.ds(pl.multiple_of(t * D + pos_ref[1] * HALF, 128), HALF)
        both[:tokens, t * HALF : (t + 1) * HALF] = gqkv[:, cols]
    both[tokens:, :] = g_got[...]
    for z in range(4):
        rows = slice(z * 4 * BLK, (z + 1) * 4 * BLK)
        grad[rows, :] = nn(n1t[rows, :], both[...]).astype(BF16)
        for chip in range(4 * z, 4 * z + 4):
            place = scatter_place(pos_ref, chip)
            for t in range(3):
                src = grad.at[pl.ds(chip * BLK, BLK), pl.ds(t * HALF, HALF)]
                start(src, mine.at[place, pl.ds(t * BLK, BLK)], sems.at[1])
    for t in range(3):
        part = nt(gqkv[:, t * D : (t + 1) * D], w_qkv[t])
        acc[...] = part if t == 0 else acc[...] + part
    load_x.wait()

    def back_one(rows):
        xhat, scale = norm_parts(x_ref[rows, :].astype(F32))
        g = acc[rows, :]
        sums[0:1, :] += jnp.sum(g * xhat, axis=0, keepdims=True)
        sums[1:2, :] += jnp.sum(g, axis=0, keepdims=True)
        igrad[rows, :] = (gmid[rows, :] + norm_back(g, xhat, scale, vec_ref[0:1, :])).astype(BF16)

    chunks(tokens, 128, back_one)
    for p in range(CHIPS):
        small[p, 0:16] = sums[:, :HALF].astype(BF16)
        small[p, 16:32] = sums[:, HALF:].astype(BF16)
        start(small.at[p], mine.at[p, pl.ds(3 * BLK, 32)], sems.at[2])
    whole_wait(small, sems.at[2])
    whole_wait(grad, sems.at[1])


def layer_out_kernel(pos_ref, vec_ref, act_ref, mid_ref, w_down, out_ref):
    out_ref[...] = (
        mid_ref[...] + nn(act_ref[...], w_down[...]) + vec_ref[12:13, :]
    ).astype(BF16)


PER = D // (2 * CHIPS)
SEND_ROWS = (3 * PER, 16, 5 * PER, 4 * PER)


def pack_kernel(pos_ref, w_qkv, w_out, w_up, w_down, bu_ref, *refs):
    values, (mine, theirs, rows, last, wide) = refs[:8], refs[8:]
    place = pos_ref[0] * 2 + pos_ref[1]
    rows[...] = jnp.zeros(rows.shape, F32)
    last[...] = jnp.zeros(last.shape, F32)
    for r, value in zip((0, 1, 2, 4, 5, 6, 7, 12), values):
        rows[r : r + 1, 0:PER] = value[...].astype(F32)
    last[0:1, 0 : 4 * PER] = bu_ref[...].astype(F32)
    at = place * (4 * PER)
    up = pltpu.roll(last[...], at % D, 1)[0:1]
    here = lax.broadcasted_iota(jnp.int32, (16, 1), 0) == 8 + at // D
    rows[...] = pltpu.roll(rows[...], place * PER, 1) + jnp.where(here, up, 0.0)
    for out, other in ((mine, 0), (theirs, 1)):
        half = pos_ref[1] ^ other

        def cols(first):
            return pl.ds(pl.multiple_of(first + half * HALF, 128), HALF)

        at = 0
        for t in range(3):
            wide[at : at + PER, :] = w_qkv[:, cols(t * D)].astype(F32)
            at += PER
        wide[at : at + 16, :] = rows[:, cols(0)]
        at += 16
        for n in range(4):
            u, s = n // 2, n % 2
            first = pl.multiple_of(half * (2 * D) + s * D + u * HALF, 128)
            wide[at : at + PER, :] = w_up[:, pl.ds(first, HALF)].astype(F32)
            at += PER
        wide[at : at + PER, :] = w_out[:, cols(0)].astype(F32)
        at += PER
        wide[at : at + 4 * PER, :] = w_down[:, cols(0)].astype(F32)
        out[...] = wide[...].astype(BF16)


def combine_kernel(pos_ref, mine, got, one, two, upper, lower, wide):
    first = pos_ref[1] == 0
    m, g = mine[...].astype(F32), got[...].astype(F32)
    upper[...] = jnp.where(first, m, g)
    lower[...] = jnp.where(first, g, m)

    def pair(at, size):
        wide[0:size, :] = upper[at : at + size, :]
        wide[size : 2 * size, :] = lower[at : at + size, :]
        return wide[0 : 2 * size, :].astype(BF16)

    for t in range(3):
        one[t * BLK : (t + 1) * BLK, :] = pair(t * PER, PER)
    at = 3 * PER
    one[3 * BLK :, :] = (upper[at : at + 16, :] + lower[at : at + 16, :]).astype(BF16)
    at += 16
    for n in range(5):
        two[n] = pair(at + n * PER, PER)
    low = pair(at + 5 * PER, 4 * PER)
    for n in range(4):
        two[5 + n] = low[n * BLK : (n + 1) * BLK]


def finish_kernel(pos_ref, last, *refs):
    terms, (keep, send, held, sems) = refs[:4], refs[4:]
    for i, term in enumerate(terms):
        start(term.at[0], held.at[i], sems.at[i])
    total = last[...].astype(F32)
    for i in range(4):
        whole_wait(held.at[i], sems.at[i])
        total = total + held[i].astype(F32)
    first = pos_ref[1] == 0
    for t in range(3):
        upper, lower = total[t * BLK : t * BLK + PER], total[t * BLK + PER : (t + 1) * BLK]
        keep[t * PER : (t + 1) * PER, :] = jnp.where(first, upper, lower)
        send[t * PER : (t + 1) * PER, :] = jnp.where(first, lower, upper)
    keep[3 * PER :, :] = total[3 * BLK :]
    send[3 * PER :, :] = total[3 * BLK :]


def spread_kernel(pos_ref, keep, got, w_ref, eight_ref, up_ref, down_ref, rows):
    place = pos_ref[0] * 2 + pos_ref[1]
    for ref, other in ((keep, 0), (got, 1)):
        half = pos_ref[1] ^ other
        for t in range(3):
            cols = pl.ds(pl.multiple_of(t * D + half * HALF, 128), HALF)
            w_ref[:, cols] = ref[t * PER : (t + 1) * PER, :]
    for h in range(2):
        at = 3 * PER + 16 * h
        rows[:, h * HALF : (h + 1) * HALF] = keep[at : at + 16, :] + got[at : at + 16, :]
    mine = pltpu.roll(rows[...], lax.rem(D - place * PER, D), 1)
    eight_ref[...] = mine[0:8, 0:PER]
    down_ref[...] = mine[12:13, 0:PER]
    at = place * (4 * PER)
    here = lax.broadcasted_iota(jnp.int32, (16, 1), 0) == 8 + at // D
    row = jnp.sum(jnp.where(here, rows[...], 0.0), axis=0, keepdims=True)
    turned = pltpu.roll(jnp.broadcast_to(row, (8, D)), lax.rem(D - at % D, D), 1)
    up_ref[...] = turned[0:1, 0 : 4 * PER]


def spread_up_kernel(pos_ref, keep, got, up_ref, out_ref):
    for ref, other in ((keep, 0), (got, 1)):
        half = pos_ref[1] ^ other
        for n in range(4):
            first = half * (2 * D) + (n % 2) * D + (n // 2) * HALF
            up_ref[:, pl.ds(pl.multiple_of(first, 128), HALF)] = ref[n]
        out_ref[:, pl.ds(pl.multiple_of(half * HALF, 128), HALF)] = ref[4]


def call(kernel, name, near, far, near_outs, far_outs, scratch, flops, aliases=None, limit=18):
    far = [in_hbm(a) for a in far]
    space = pl.BlockSpec(memory_space=pltpu.VMEM)
    anyspec = pl.BlockSpec(memory_space=pl.ANY)
    outs = tuple(near_outs) + tuple(far_outs)
    moved = sum(math.prod(a.shape) * a.dtype.itemsize for a in (*near, *far, *outs))
    return pl.pallas_call(
        kernel,
        out_shape=outs,
        in_specs=[pl.BlockSpec(memory_space=pltpu.SMEM)]
        + [space] * (len(near) - 1)
        + [anyspec] * len(far),
        out_specs=[space] * len(near_outs) + [anyspec] * len(far_outs),
        scratch_shapes=scratch,
        input_output_aliases=aliases or {},
        compiler_params=pltpu.CompilerParams(vmem_limit_bytes=limit << 20),
        cost_estimate=pl.CostEstimate(flops=flops, bytes_accessed=moved, transcendentals=0),
        name=name,
    )(*near, *far)


def in_hbm(array):
    return pltpu.with_memory_space_constraint(array, pltpu.HBM)


def keep(*arrays):
    return [pltpu.with_memory_space_constraint(a, pltpu.VMEM) for a in arrays]


def swap(value, chip_bit):
    flip = chip_bit * 2 if chip_bit else 1
    return lax.ppermute(value, AXES, [(i, i ^ flip) for i in range(2 * CHIPS)])


def tie(value, *after):
    return lax.optimization_barrier((value,) + after)[0]


def gathered(*own_half):
    return list(own_half) + [swap(piece, 0) for piece in own_half]


def hold(pieces, *after):
    return lax.optimization_barrier((*pieces, *after))[: len(pieces)] if after else pieces


def rounded_sum(*terms):
    total = terms[0].astype(F32)
    for term in terms[1:]:
        total = total + term.astype(F32)
    return total.astype(BF16)


def small_grads(sums, place, per, per_up):
    eight = lax.dynamic_slice(sums, (0, place * per), (8, per))
    at = place * per_up
    up = lax.dynamic_slice(sums, (8 + at // D, at % D), (1, per_up))[0]
    down = lax.dynamic_slice(sums, (12, place * per), (1, per))[0]
    return eight, up, down


def halves(w_qkv, w_out, w_up, w_down):
    rows = w_qkv.shape[0]
    qkv = w_qkv.reshape(rows, 3, 2, HALF)
    up = w_up.reshape(rows, 2, 4, HALF)
    for h in range(2):
        cols = slice(h * HALF, (h + 1) * HALF)
        up_h = up[:, h].reshape(rows, 2, 2, HALF).transpose(2, 1, 0, 3).reshape(4, rows, HALF)
        yield (
            qkv[:, :, h].transpose(1, 0, 2),
            jnp.concatenate([up_h, w_out[None, :, cols]]),
            w_down[:, cols],
        )


def gather_plain(weights, values):
    def whole(w):
        return lax.all_gather(w, AXES, axis=0, tiled=True)

    gain1, bias1, bq, bv, bo, gain2, bias2, bu, bd = [whole(v) for v in values]
    rest = jnp.zeros((3, D), BF16)
    small = jnp.stack([gain1, bias1, bq, jnp.zeros_like(bq), bv, bo, gain2, bias2])
    small = jnp.concatenate([small, bu.reshape(4, D), bd[None], rest])
    groups = ([], [], [])
    for h, (attn, up, down) in enumerate(halves(*[whole(w) for w in weights])):
        attn = attn.reshape(3, CHIPS, BLK, HALF).transpose(1, 0, 2, 3).reshape(CHIPS, 3 * BLK, HALF)
        up = up.reshape(5, CHIPS, BLK, HALF).transpose(1, 0, 2, 3)
        down = down.reshape(CHIPS, 4 * BLK, HALF)
        extra = jnp.zeros((CHIPS, 16, HALF), BF16).at[0].set(small[:, h * HALF : (h + 1) * HALF])
        for group, blocks in zip(groups, (jnp.concatenate([attn, extra], axis=1), up, down)):
            group.extend(jnp.stack([blocks[o] for o in piece]) for piece in GATHER)
    return groups


def scatter_plain(pair, group):
    both = [jnp.stack([part[SCATTER.index(chip)] for chip in range(CHIPS)]) for part in pair]

    def scatter(v):
        return lax.psum_scatter(v.astype(F32), AXES, scatter_dimension=0, tiled=True)

    def matrix(units):
        return jnp.stack(units, axis=3).transpose(0, 2, 1, 3, 4).reshape(D, -1, 2, HALF)

    if group == "attn":
        sums = jnp.concatenate([both[0][0, 3 * BLK + 16 * h :][:16] for h in range(2)], axis=1)
        qkv = matrix([b[:, : 3 * BLK].reshape(CHIPS, 3, BLK, HALF) for b in both])
        return scatter(qkv.reshape(D, 3 * D)), lax.psum(sums.astype(F32), AXES)
    if group == "up":
        up = matrix(both)
        order = up[:, :4].reshape(D, 2, 2, 2, HALF).transpose(0, 3, 2, 1, 4)
        return scatter(order.reshape(D, FF)), scatter(up[:, 4].reshape(D, D))
    return scatter(jnp.concatenate([b.reshape(FF, HALF) for b in both], axis=1))


def shape(dims, kind=BF16):
    return jax.ShapeDtypeStruct(dims, kind)


def far_shape(*dims):
    return pltpu.HBM(dims, BF16)


def dma(n):
    return pltpu.SemaphoreType.DMA((n,))


def vmem(*dims, kind=BF16):
    return pltpu.VMEM(dims, kind)


class Layer:
    def __init__(self, tokens):
        self.tokens = tokens
        self.rows = tokens // ROW_LEN
        self.out = shape((tokens, D))
        self.wide = vmem(tokens, FF)
        self.one = vmem(tokens, D)
        self.one_f32 = vmem(tokens, D, kind=F32)
        self.qkv = vmem(tokens, 3 * D)
        self.soft = vmem(self.rows * HEADS, ROW_LEN, ROW_LEN)
        self.turned = vmem(D, tokens)
        self.square = vmem(D, D)
        self.three = vmem(3, D, D)
        self.four = vmem(2, 2, D, D)
        self.sums = vmem(8, D, kind=F32)
        self.vec = vmem(16, D, kind=F32)

    def chip_blocks(self, pos, weights, values):
        *rest, bu, bd = [in_hbm(v.reshape(1, -1)) for v in values]
        weights = [in_hbm(w) for w in weights]
        sent = shape((sum(SEND_ROWS), HALF))
        wide = vmem(sum(SEND_ROWS), HALF, kind=F32)
        mine, theirs = call(
            pack_kernel, "pack", (pos, *weights, bu, *rest, bd), (), (sent, sent), (),
            [vmem(16, D, kind=F32), vmem(8, D, kind=F32), wide], 0,
        )
        return call(
            combine_kernel, "combine", (pos, mine, swap(theirs, 0)), (),
            (shape((3 * BLK + 16, HALF)), shape((9, BLK, HALF))), (),
            [wide, wide, vmem(4 * BLK, HALF, kind=F32)], 0,
        )

    def finish(self, pos, last, low):
        sent = shape((3 * PER + 32, HALF), F32)
        keep, send = call(
            finish_kernel, "finish", (pos, last), low, (sent, sent), (),
            [vmem(4, 3 * BLK + 32, HALF), dma(4)], 0,
        )
        return call(
            spread_kernel, "spread", (pos, keep, swap(send, 0)), (),
            (shape((PER, 3 * D), F32), shape((8, PER), F32), shape((1, 4 * PER), F32), shape((1, PER), F32)),
            (), [vmem(16, D, kind=F32)], 0,
        )

    def spread_up(self, pos, keep, got):
        return call(
            spread_up_kernel, "spread_up", (pos, keep, got), (),
            (shape((PER, FF), F32), shape((PER, D), F32)), (), [], 0,
        )

    def attn_forward(self, pos, segr, segc, inputs, attn):
        return call(
            attn_forward_kernel, "attn_forward", (pos, segr, segc), [in_hbm(inputs)] + attn,
            (self.vec, self.one, self.qkv, self.soft, self.one, self.three), (),
            [
                self.one, vmem(2, CHIPS, 16, HALF),
                vmem(self.rows, ROW_LEN, ROW_LEN, kind=F32), dma(5),
            ],
            2 * self.tokens * D * D * 3 + 8 * self.tokens * D * ROW_LEN,
        )

    def mlp_up(self, pos, segc, vec, inputs, mixed, cotangent, up):
        vec, mixed = keep(vec, mixed)
        return call(
            mlp_up_kernel, "mlp_up", (pos, segc, vec, mixed), [inputs, cotangent] + up,
            (self.sums, self.one, self.one_f32, self.wide, self.wide, self.one, self.square, self.four), (),
            [self.one, self.one, dma(5)],
            2 * self.tokens * D * (FF + D),
        )

    def down_grad(self, pos, act, gout):
        buffer = far_shape(CHIPS, 4 * BLK, HALF)
        return call(
            down_grad_kernel, "down_grad", (pos, *keep(act, gout)), [], (), (buffer, buffer),
            [vmem(4, D, D), dma(1)],
            2 * self.tokens * D * FF,
        )

    def mlp_down(self, pos, gout, slope, n2, down):
        buffer = far_shape(CHIPS, 5, BLK, HALF)
        return call(
            mlp_down_kernel, "mlp_down", (pos, *keep(gout, slope, n2)), down,
            (self.sums, self.wide, vmem(FF, D)), (buffer, buffer),
            [self.turned, self.four, dma(5)],
            4 * self.tokens * D * FF,
        )

    def mid_backward(self, pos, vec, gbd, gbu, gpre, gout, mid, mixed, w_out, w_up, mine, theirs):
        buffer = far_shape(*mine.shape)
        near = (pos, *keep(vec, gbd, gbu, gpre, gout, mid, mixed, w_out, w_up))
        return call(
            mid_backward_kernel, "mid_backward", near, [mine, theirs],
            (self.vec, self.one_f32, self.one), (buffer, buffer),
            [self.one_f32, self.one, self.turned, self.square, dma(1)],
            2 * self.tokens * D * (FF + 2 * D),
            {len(near): 3, len(near) + 1: 4},
        )

    def attn_backward(self, pos, gmixed, qkv, soft):
        return call(
            attn_backward_kernel, "attn_backward", (pos, *keep(gmixed, qkv, soft)), [],
            (self.sums, self.qkv, vmem(self.tokens, 3 * HALF)), (), [], 20 * self.tokens * D * ROW_LEN,
        )

    def qkv_grad(self, pos, vec, sums, gbq, gmid, gqkv, n1, w_qkv, n1_got, g_got, inputs):
        return call(
            qkv_grad_kernel, "qkv_grad", (pos, *keep(vec, sums, gbq, gmid, gqkv, n1, w_qkv, n1_got, g_got)),
            [inputs], (self.out,), (far_shape(CHIPS, 3 * BLK + 32, HALF),),
            [
                self.one, self.one_f32, vmem(D, 2 * self.tokens), vmem(2 * self.tokens, 3 * HALF),
                vmem(D, 3 * HALF), vmem(16, D, kind=F32), vmem(CHIPS, 32, HALF), dma(3),
            ],
            2 * self.tokens * D * 6 * D,
        )

    def layer_out(self, pos, vec, act, mid, w_down):
        (out,) = call(
            layer_out_kernel, "layer_out", (pos, *keep(vec, act, mid, w_down)), [], (self.out,), (), [],
            2 * self.tokens * D * FF,
        )
        return out


class Scatter:
    def __init__(self, mine, theirs=None, *after):
        self.both = [mine] if theirs is None else [mine, swap(tie(theirs, *after), 0)]

    def part(self, first, last):
        return [ref[first:last] for ref in self.both]

    def hold_back(self, *after):
        self.both[-1] = hold((self.both[-1],), *after)[0]

    def first(self, *after):
        self.hold_back(*after)
        self.out = (rounded_sum(*self.part(8, 12)), rounded_sum(*self.part(12, 16)))
        self.in_y, self.in_x = swap(self.out[0], BIT_Y), swap(self.out[1], BIT_X)

    def second(self, *after):
        in_y, in_x = hold((self.in_y, self.in_x), *after)
        self.out = (
            rounded_sum(*self.part(4, 6), in_x[2:]),
            rounded_sum(*self.part(6, 8), in_y[2:]),
        )
        self.in_y, self.in_x = in_y, in_x
        self.in_y2, self.in_x2 = swap(self.out[0], BIT_Y), swap(self.out[1], BIT_X)

    def third(self, *after):
        in_y2, in_x2 = hold((self.in_y2, self.in_x2), *after)
        self.near = (*self.part(0, 2), self.in_x[:2], in_y2)
        self.out = (rounded_sum(*self.part(2, 4), self.in_y[:2], in_x2),)
        self.in_z = swap(self.out[0], BIT_Z0)

    def diagonal(self, *after):
        self.hold_back(*after)
        self.out = (rounded_sum(*self.part(10, 12)), rounded_sum(*self.part(14, 16)))
        self.in_y, self.in_x = swap(self.out[0], BIT_Y), swap(self.out[1], BIT_X)

    def hi(self, *after):
        in_y, self.in_x = hold((self.in_y, self.in_x), *after)
        self.out = (rounded_sum(*self.part(8, 10)), rounded_sum(*self.part(6, 8), in_y))
        self.in_y2, self.in_x2 = swap(self.out[0], BIT_Y), swap(self.out[1], BIT_X)

    def lo(self, *after):
        in_y2, in_x2 = hold((self.in_y2, self.in_x2), *after)
        far = rounded_sum(*self.part(2, 4), in_y2, in_x2)
        self.in_z = swap(far, BIT_Z0)
        low_y, low_x = rounded_sum(*self.part(4, 6), self.in_x), rounded_sum(*self.part(12, 14))
        low_y, low_x = hold((low_y, low_x), far)
        self.out = (far, low_y, low_x)
        self.near = (*self.part(0, 2), swap(low_y, BIT_Y), swap(low_x, BIT_X))

    def fourth(self, *after):
        self.near = (*self.near, *hold((self.in_z,), *after))
        self.out = (rounded_sum(*[t[1] for t in self.near]),)
        self.in_z = swap(self.out[0], BIT_Z1)

    def result(self, *after):
        total = hold((self.in_z,), *after)[0].astype(F32)
        for term in self.near:
            total = total + term[0].astype(F32)
        return total


def per_device(tuned, *args):
    (
        inputs, segment_ids, pre_attn_gain, pre_attn_bias, w_qkv, b_query, b_value, w_out, b_out,
        pre_mlp_gain, pre_mlp_bias, w_up, b_up, w_down, b_down, cotangent,
    ) = args
    tokens = inputs.shape[0]
    n_rows = tokens // ROW_LEN
    wide, narrow = lax.axis_index("wide"), lax.axis_index("narrow")
    weights = (w_qkv, w_out, w_up, w_down)
    values = (
        pre_attn_gain, pre_attn_bias, b_query, b_value, b_out, pre_mlp_gain, pre_mlp_bias, b_up, b_down,
    )
    per, per_up = pre_attn_gain.shape[0], b_up.shape[0]
    position = jnp.arange(ROW_LEN, dtype=jnp.int32)[None]
    own_id = jnp.where(segment_ids != 0, segment_ids, -1 - position)
    segr = own_id.reshape(n_rows, 1, ROW_LEN)
    segc = own_id.reshape(tokens, 1)
    layer = Layer(tokens)

    if not tuned:
        place = wide * lax.axis_size("narrow") + narrow
        pos = jnp.zeros((2,), jnp.int32)
        attn, up, down = gather_plain(weights, values)
        vec, n1, qkv, soft, mixed, w_qkv_all = layer.attn_forward(pos, segr, segc, inputs, attn)
        gbd, n2, mid, act, slope, gout, *w_mid = layer.mlp_up(pos, segc, vec, inputs, mixed, cotangent, up)
        pair_down = layer.down_grad(pos, act, gout)
        gbu, gpre, w_down_all, *pair_up = layer.mlp_down(pos, gout, slope, n2, down)
        sums, gmid, gmixed, *pair_up = layer.mid_backward(
            pos, vec, gbd, gbu, gpre, gout, mid, mixed, *w_mid, *pair_up
        )
        gbq, gqkv, give = layer.attn_backward(pos, gmixed, qkv, soft)
        pair_attn = []
        for half in range(2):
            input_grad, blocks = layer.qkv_grad(
                jnp.array([0, half], jnp.int32), vec, sums, gbq, gmid, gqkv, n1, w_qkv_all,
                jnp.zeros_like(n1), jnp.zeros_like(give), inputs,
            )
            pair_attn.append(blocks)
        layer_out = layer.layer_out(pos, vec, act, mid, w_down_all)
        grad_w_down = scatter_plain(pair_down, "down")
        grad_w_up, grad_w_out = scatter_plain(pair_up, "up")
        grad_w_qkv, sums = scatter_plain(pair_attn, "attn")
        eight, grad_b_up, grad_b_down = small_grads(sums, place, per, per_up)
    else:
        core = (narrow & 1).astype(jnp.int32)
        pos = jnp.stack([wide * 2 + (narrow >> 1), core]).astype(jnp.int32)
        block1, block23 = layer.chip_blocks(pos, weights, values)
        flat = (4 * BLK, HALF)

        near1 = swap(block1, BIT_Z1)
        lo1 = jnp.stack([block1, near1])
        hi1 = swap(lo1, BIT_Z0)
        y_lo1, x_lo1 = swap(lo1, BIT_Y), swap(lo1, BIT_X)
        near23 = swap(tie(block23, near1), BIT_Z1)
        d_lo1 = swap(y_lo1, BIT_X)
        y_hi1, x_hi1 = swap(hi1, BIT_Y), swap(hi1, BIT_X)
        lo2 = jnp.stack([block23[:5], near23[:5]])
        lo3 = jnp.stack([block23[5:].reshape(flat), near23[5:].reshape(flat)])
        hi2 = swap(tie(lo2, hi1), BIT_Z0)
        d_hi1 = swap(tie(x_hi1, y_hi1), BIT_Y)
        lo2b = tie(lo2, d_lo1, x_hi1, y_hi1)
        y_lo2, x_lo2 = swap(lo2b, BIT_Y), swap(lo2b, BIT_X)
        attn = gathered(lo1, hi1, y_lo1, y_hi1, x_lo1, x_hi1, d_lo1, d_hi1)
        hi3 = swap(tie(lo3, hi2), BIT_Z0)
        y_hi2, x_hi2 = swap(hi2, BIT_Y), swap(hi2, BIT_X)
        d_lo2, d_hi2 = swap(y_lo2, BIT_X), swap(tie(x_hi2, y_hi2), BIT_Y)
        lo3b = tie(lo3, y_lo2, x_lo2, y_hi2)
        y_lo3, x_lo3 = swap(lo3b, BIT_Y), swap(lo3b, BIT_X)
        vec, n1, qkv, soft, mixed, w_qkv_all = layer.attn_forward(
            tie(pos, y_hi2, x_hi2, lo3b, d_lo2), segr, segc, inputs, attn
        )

        d_hi2, y_lo3, x_lo3, hi3 = hold((d_hi2, y_lo3, x_lo3, hi3), mixed)
        d_lo3 = swap(y_lo3, BIT_X)
        y_hi3, x_hi3 = swap(hi3, BIT_Y), swap(hi3, BIT_X)
        lo2, hi2, y_lo2, y_hi2, x_lo2, x_hi2, d_lo2 = hold(
            (lo2, hi2, y_lo2, y_hi2, x_lo2, x_hi2, d_lo2), x_lo3, hi3
        )
        up = gathered(lo2, hi2, y_lo2, y_hi2, x_lo2, x_hi2, d_lo2, d_hi2)
        gbd, n2, mid, act, slope, gout, *w_mid = layer.mlp_up(
            tie(pos, hi3, y_lo3, x_lo3), segc, vec, inputs, mixed, cotangent, up
        )
        y_hi3, x_hi3, d_lo3 = hold((y_hi3, x_hi3, d_lo3), gbd)
        d_hi3 = swap(x_hi3, BIT_Y)
        pair_down = layer.down_grad(tie(pos, y_hi3, x_hi3, d_lo3), act, gout)
        d_hi3 = tie(d_hi3, pair_down[0])
        down = gathered(lo3, hi3, y_lo3, y_hi3, x_lo3, x_hi3, d_lo3, d_hi3)
        scatter1 = Scatter(*pair_down, *down)
        gbu, gpre, w_down_all, *pair_up = layer.mlp_down(pos, gout, slope, n2, down)
        scatter1.diagonal(gbu)
        sums, gmid, gmixed, *pair_up = layer.mid_backward(
            tie(pos, *scatter1.out), vec, gbd, gbu, gpre, gout, mid, mixed, *w_mid, *pair_up
        )
        scatter1.hi(sums)
        scatter2 = Scatter(*pair_up, scatter1.in_x)
        gbq, gqkv, give = layer.attn_backward(tie(pos, *scatter1.out), gmixed, qkv, soft)
        scatter1.lo(gbq)
        n1, give = hold((n1, give), *scatter1.out)
        n1_got, g_got = swap(n1, 0), swap(give, 0)
        scatter2.diagonal(gbq)
        input_grad, sums_attn = layer.qkv_grad(
            tie(pos, *scatter2.out, *scatter1.out),
            vec, sums, gbq, gmid, gqkv, n1, w_qkv_all, n1_got, g_got, inputs,
        )
        scatter2.hi(input_grad)
        scatter1.fourth(input_grad)
        scatter3 = Scatter(tie(sums_attn, *scatter2.out))
        scatter3.diagonal()
        layer_out = layer.layer_out(
            tie(pos, *scatter3.out, *scatter1.out), vec, act, mid, w_down_all
        )
        scatter1.in_z = tie(scatter1.in_z, layer_out)
        scatter3.hi(layer_out, scatter1.in_z)
        scatter2.lo(*scatter3.out)
        scatter3.lo(*scatter2.out)
        scatter2.fourth(*scatter3.out)
        scatter3.fourth(*scatter2.out)

        def exchange(blocks, axis):
            first, second = jnp.split(blocks, 2, axis=axis)
            keep = jnp.where(core == 0, first, second)
            got = swap(jnp.where(core == 0, second, first), 0)
            return jnp.where(core == 0, keep, got), jnp.where(core == 0, got, keep)

        grad_w_down = jnp.concatenate(exchange(scatter1.result(*scatter3.out), 0), axis=1)
        total = scatter2.result(*scatter3.out)
        upper, lower = total[:, :PER], total[:, PER:]
        got = swap(jnp.where(core == 0, lower, upper), 0)
        grad_w_up, grad_w_out = layer.spread_up(pos, jnp.where(core == 0, upper, lower), got)
        grad_w_qkv, eight, grad_b_up, grad_b_down = layer.finish(
            pos, scatter3.in_z, [*scatter3.both, *scatter3.near[1:]]
        )
        grad_b_up, grad_b_down = grad_b_up[0], grad_b_down[0]
    return (
        layer_out, input_grad, eight[0], eight[1], grad_w_qkv, eight[2], eight[4], grad_w_out, eight[5],
        eight[6], eight[7], grad_w_up, grad_b_up, grad_w_down, grad_b_down,
    )


def solution(mesh):
    both = P(AXES, None)
    one = P(AXES)
    tuned = dict(mesh.shape) == {"wide": 8, "narrow": 4}
    in_specs = (both, both, one, one, both, one, one, both, one, one, one, both, one, both, one, both)
    out_specs = (both, both, one, one, both, one, one, both, one, one, one, both, one, both, one)
    return jax.shard_map(
        functools.partial(per_device, tuned),
        mesh=mesh,
        in_specs=in_specs,
        out_specs=out_specs,
        check_vma=False,
    )
```
